32 devices in a mesh: pipe: 2 (over core), dp: 4 (over y, x), tensor: 4 (over z).
Axes of the slice: x: 2, y: 2, z: 4, core: 2. Of those that a mesh axis runs over, the one named last changes fastest.
Arguments:
- acts: bfloat16 [2, 2048, 4096], P('pipe', 'dp', 'tensor'), may hold values from -6 to 6
- out_grad: bfloat16 [2, 2048, 1024], P('pipe', 'dp', 'tensor'), may hold values from -6 to 6
- old_factor: float32 [2, 4, 1024, 1024], P('pipe', 'tensor', 'dp'), may hold values from -2 to 4, as said below
- old_root: bfloat16 [2, 4, 1024, 1024], P('pipe', 'tensor', 'dp'), may hold values from -2 to 2, as said below
- iter_count: int32 [2, 4], P('pipe', 'tensor'), may hold values from 1 to 2
Outputs:
- new_factor: float32 [2, 4, 1024, 1024], P('pipe', 'tensor', 'dp')
- new_root: bfloat16 [2, 4, 1024, 1024], P('pipe', 'tensor', 'dp')
- step: bfloat16 [2, 4, 256, 1024], P('pipe', 'tensor', None, 'dp')
The draws below stay inside these ranges and needn't reach their ends.
Inputs may be any that keep to these rules, and one draw needn't show every extreme that they name: Every block of old_factor is symmetric, with diagonal entries of 0.5 or more. Every block of old_root is symmetric.
All inputs are finite; a program needn't handle non-finite values.
Results may differ from the reference program's by a relative error of at most 0.0056.
Values may be sent and summed in bfloat16 or wider, within the bound.
No kernel may reach another device: no remote copies, remote signals or barrier semaphores. Data moves between devices by JAX's collectives and lax.ppermute only.
A program may use at most 64 MiB of HBM per device.

```python
import math
import jax
import jax.numpy as jnp
from jax import lax

BS = 1024
GROWS = 256
ITERS = 2
SECTIONS = 2
BLOCKS = 4
TOKENS = 2048


def symmetric_blocks(key, spread, high):
    key_diag, key_off = jax.random.split(jax.random.fold_in(key, 17))
    logs = jax.random.uniform(key_diag, (SECTIONS, BLOCKS, BS), jnp.float32, math.log(0.5), math.log(high))
    noise = jax.random.normal(key_off, (SECTIONS, BLOCKS, BS, BS), jnp.float32) * (spread / math.sqrt(BS))
    sym = 0.5 * (noise + jnp.swapaxes(noise, -1, -2))
    eye = jnp.eye(BS, dtype=jnp.float32)
    return sym * (1.0 - eye) + eye * jnp.exp(logs)[..., None]


def draw_old_factor(key, part):
    return symmetric_blocks(key, 1.0, 2.0)


def draw_old_root(key, part):
    return symmetric_blocks(key, 0.45, 2.0).astype(jnp.bfloat16)


def place_ends(entries, key, least, high):
    longest = entries.shape.index(max(entries.shape))
    spots = []
    for shift in (0, 1):
        where = [jax.random.randint(jax.random.fold_in(key, axis), (), 0, length) for axis, length in enumerate(entries.shape)]
        where[longest] = (where[longest] + shift) % entries.shape[longest]
        spots.append(tuple(where))
    return entries.at[spots[0]].set(least).at[spots[1]].set(high)


def shard_levels(stream_key, shape, pieces, low, top_value):
    factor_of, own = 1.0, jax.random.fold_in(stream_key, 6)
    for position, parts in pieces:
        steps = jnp.exp(jax.random.uniform(jax.random.fold_in(own, position), (parts,), jnp.float32, low / len(pieces), top_value / len(pieces)))
        factor_of = factor_of * jnp.repeat(steps, shape[position] // parts).reshape([-1 if axis == position else 1 for axis in range(len(shape))])
    return factor_of


def normal_values(key, shape, width, bound, cuts=(), kind=jnp.bfloat16):
    result = width * jax.random.normal(key, shape, jnp.float32)
    if cuts:
        result = result * shard_levels(key, shape, cuts, -0.22, 0.18)
    return jnp.clip(result, -bound, bound).astype(kind)


def setup_inputs(seed: int = 0) -> dict:
    key_list = jax.random.split(jax.random.key(seed), 6)
    return {
        "acts": normal_values(key_list[0], (SECTIONS, TOKENS, BLOCKS * BS), 1.0, 6.0, ((0, 2), (1, 4), (2, 4))),
        "out_grad": normal_values(key_list[1], (SECTIONS, TOKENS, BLOCKS * GROWS), 1.0, 6.0, ((0, 2), (1, 4), (2, 4))),
        "old_factor": draw_old_factor(jax.random.fold_in(key_list[5], 71), 0),
        "old_root": draw_old_root(jax.random.fold_in(key_list[5], 71), 0),
        "iter_count": place_ends(jax.random.randint(key_list[4], (SECTIONS, BLOCKS), 1, ITERS + 1), jax.random.fold_in(key_list[4], 1), 1, ITERS).astype(jnp.int32),
    }


DECAY = 0.75
DAMPING = 0.1
EPSILON = 1e-06

def reference(acts, out_grad, old_factor, old_root, iter_count):
    received = jnp.roll(out_grad, -1, axis=0)
    eye = jnp.eye(BS, dtype=jnp.float32)

    def one_block(index):
        section = index // BLOCKS
        block = index % BLOCKS
        inputs = lax.dynamic_slice(acts, (section, jnp.int32(0), (block * BS).astype(jnp.int32)), (1, TOKENS, BS))[0]
        grads_in = lax.dynamic_slice(received, (section, jnp.int32(0), (block * GROWS).astype(jnp.int32)), (1, TOKENS, GROWS))[0]
        f_old = old_factor[section, block]
        r_old = old_root[section, block]
        count = iter_count[section, block]
        batch = jnp.dot(inputs.T, inputs, preferred_element_type=jnp.float32) / TOKENS
        factor = DECAY * f_old + (1.0 - DECAY) * batch + DAMPING * eye
        grad = (jnp.dot(grads_in.T, inputs, preferred_element_type=jnp.float32) / math.sqrt(TOKENS)).astype(jnp.bfloat16)
        step_block = jnp.dot(grad, r_old, preferred_element_type=jnp.float32).astype(jnp.bfloat16)
        scale = jnp.sqrt(jnp.sum(factor * factor) / BS + EPSILON)
        first = (factor / scale).astype(jnp.bfloat16)
        turn_one = (1.5 * eye - 0.5 * first.astype(jnp.float32)).astype(jnp.bfloat16)
        second = jnp.dot(first, turn_one, preferred_element_type=jnp.float32).astype(jnp.bfloat16)
        turn_two = (1.5 * eye - 0.5 * jnp.dot(turn_one, second, preferred_element_type=jnp.float32)).astype(jnp.bfloat16)
        inverse = jnp.dot(turn_two, turn_one, preferred_element_type=jnp.float32)
        chosen = jnp.where(count == 1, turn_one.astype(jnp.float32), inverse)
        root = (chosen / jnp.sqrt(scale)).astype(jnp.bfloat16)
        return (factor, root, step_block)
    indices = jnp.arange(SECTIONS * BLOCKS, dtype=jnp.int32)
    factors, roots, steps = lax.map(one_block, indices)
    new_factor = factors.reshape(SECTIONS, BLOCKS, BS, BS)
    new_root = roots.reshape(SECTIONS, BLOCKS, BS, BS)
    step = steps.reshape(SECTIONS, BLOCKS, GROWS, BS)
    return (new_factor, new_root, step)
```

```python
import functools
import math

import jax
import jax.numpy as jnp
from jax import lax
from jax.experimental import pallas as pl
from jax.experimental.pallas import tpu as pltpu
from jax.sharding import PartitionSpec as P

DECAY = 0.75
DAMPING = 0.1
EPSILON = 1e-06
BF16 = jnp.bfloat16
F32 = jnp.float32
VMEM_LIMIT = 28 * 1024 * 1024


def passed_along(block, axis, distance):
    devices = range(lax.axis_size(axis))
    route = [((i - distance) % len(devices), i) for i in devices]
    return lax.ppermute(block, axis, route)


def swapped(block, offset):
    return lax.ppermute(block, "dp", [(i, i ^ offset) for i in range(lax.axis_size("dp"))])


def eye_of(rows, cols, shift=0):
    row_ids = lax.broadcasted_iota(jnp.int32, (rows, cols), 0) + shift
    col_ids = lax.broadcasted_iota(jnp.int32, (rows, cols), 1)
    return (row_ids == col_ids).astype(F32)


def whole(count):
    return [pl.BlockSpec(memory_space=pltpu.VMEM)] * count


def products_kernel(replicas, tokens_all, acts, grads, own, *rest):
    sends, grad_sum = rest[:-1], rest[-1]
    order = acts.shape[1]
    share = order // replicas
    strip = grads.shape[1] // replicas
    mine = lax.axis_index("dp")
    everything = acts[...]
    grad_sum[...] = lax.dot_general(
        grads[...], everything, (((0,), (0,)), ((), ())), preferred_element_type=F32
    ) * (1.0 / math.sqrt(tokens_all))
    for offset in reversed(range(replicas)):
        other = mine ^ offset
        columns = acts[:, pl.ds(pl.multiple_of(other * share, share), share)]
        batch = lax.dot_general(
            columns, everything, (((0,), (0,)), ((), ())), preferred_element_type=F32
        ) * (1.0 / tokens_all)
        part = grad_sum[pl.ds(pl.multiple_of(other * strip, strip), strip), :]
        target = own if offset == 0 else sends[offset - 1]
        target[0:share, :] = batch.astype(target.dtype)
        target[share:, :] = part.astype(target.dtype)


def factor_kernel(replicas, own, *rest):
    got, old, factor_out = rest[: replicas - 1], rest[replicas - 1], rest[replicas]
    rows_out, sends = rest[replicas + 1], rest[replicas + 2 :]
    share, order = old.shape
    strip = own.shape[0] - share
    half = share // 2
    mine = lax.axis_index("dp")
    total = own[...]
    for message in got:
        total = total + message[...].astype(F32)
    eye = (
        lax.broadcasted_iota(jnp.int32, (share, order), 0) + mine * share
        == lax.broadcasted_iota(jnp.int32, (share, order), 1)
    ).astype(F32)
    factor = DECAY * old[...] + (1.0 - DECAY) * total[0:share] + DAMPING * eye
    factor_out[...] = factor
    grad16 = total[share:].astype(BF16)
    squares = jnp.sum(factor * factor, axis=0, keepdims=True)
    lanes = squares[:, 0:share]
    for offset in range(1, replicas):
        lanes = lanes + squares[:, offset * share : (offset + 1) * share]
    high = lanes.astype(BF16).astype(F32)
    middle = (lanes - high).astype(BF16).astype(F32)
    low = lanes - high - middle
    spot = lax.broadcasted_iota(jnp.int32, (16, share), 0)
    digits = jnp.where(spot == 0, high, jnp.where(spot == 1, middle, jnp.where(spot == 2, low, 0.0)))
    digits16 = digits.astype(BF16)
    for offset in range(replicas):
        other = mine ^ offset
        block = factor_out[:, pl.ds(pl.multiple_of(other * share, share), share)].astype(BF16)
        rows_out[0:share, offset * share : (offset + 1) * share] = block
    rows_out[share : share + strip, :] = grad16
    rows_out[share + strip :, 0:share] = digits16
    rows_out[share + strip :, share:] = jnp.zeros((16, order - share), BF16)

    def block_of(offset):
        return rows_out[0:share, offset * share : (offset + 1) * share]

    for offset, send in zip(range(1, replicas), sends):
        pieces = [block_of(0)]
        if offset == 1:
            pieces += [block_of(2), block_of(3)[0:half, :]]
        if offset == 2:
            pieces += [block_of(1), block_of(3)[:, half:].astype(F32).T.astype(BF16)]
        for chunk in range(replicas):
            pieces.append(grad16[:, chunk * share : (chunk + 1) * share])
        pieces.append(digits16)
        start = 0
        for piece in pieces:
            send[start : start + piece.shape[0], :] = piece
            start += piece.shape[0]


def root_kernel(replicas, count, rows, near, side, far, old_root, root_out, step_out, factor, turn, grads, result):
    share = rows.shape[1] // replicas
    order = rows.shape[1]
    strip = rows.shape[0] - share - 16
    half = share // 2
    mine = lax.axis_index("dp")

    def put(row, col, block):
        factor[row * share : (row + 1) * share, col * share : (col + 1) * share] = block

    def mirror(row, col, block):
        put(row, col, block)
        put(col, row, block.astype(F32).T.astype(BF16))

    factor[0:share, :] = rows[0:share, :]
    for offset in range(1, replicas):
        put(offset, 0, rows[0:share, offset * share : (offset + 1) * share].astype(F32).T.astype(BF16))
    put(1, 1, near[0:share, :])
    put(2, 2, side[0:share, :])
    put(3, 3, far[0:share, :])
    mirror(1, 3, near[share : 2 * share, :])
    mirror(2, 3, side[share : 2 * share, :])
    middle = jnp.concatenate(
        [near[2 * share : 2 * share + half, :], side[2 * share : 2 * share + half, :]], axis=0
    )
    mirror(1, 2, middle)

    squares = rows[share + strip :, 0:share].astype(F32)
    for message in (near, side, far):
        squares = squares + message[message.shape[0] - 16 :, :].astype(F32)
    square_total = jnp.sum(squares, keepdims=True)
    scale = jnp.sqrt(square_total / order + EPSILON)
    inverse = 1.0 / scale

    for offset in range(replicas):
        band = slice(offset * share, (offset + 1) * share)
        first = (factor[band, :].astype(F32) * inverse).astype(BF16)
        factor[band, :] = first
        eye = eye_of(share, order, offset * share)
        turn[band, :] = (1.5 * eye - 0.5 * first.astype(F32)).astype(BF16)
    eye = eye_of(share, order)
    turn_rows = turn[0:share, :]
    second = jnp.dot(turn_rows, factor[...], preferred_element_type=F32).astype(BF16)
    product = jnp.dot(second, turn[...], preferred_element_type=F32)
    turn_two = (1.5 * eye - 0.5 * product).astype(BF16)
    inverse_rows = jnp.dot(turn_two, turn[...], preferred_element_type=F32)
    chosen = jnp.where(count[0, 0] == 1, turn_rows.astype(F32), inverse_rows)
    root = (chosen * lax.rsqrt(scale)).astype(BF16)
    for offset in range(replicas):
        other = mine ^ offset
        root_out[:, pl.ds(pl.multiple_of(other * share, share), share)] = root[
            :, offset * share : (offset + 1) * share
        ]

    grads[0:strip, :] = rows[share : share + strip, :]
    for offset, message in zip(range(1, replicas), (near, side, far)):
        start = message.shape[0] - 16 - replicas * strip
        for chunk in range(replicas):
            grads[offset * strip : (offset + 1) * strip, chunk * share : (chunk + 1) * share] = message[
                start + chunk * strip : start + (chunk + 1) * strip, :
            ]
    result[...] = lax.dot_general(
        grads[...], old_root[...], (((1,), (1,)), ((), ())), preferred_element_type=F32
    ).astype(BF16)
    for offset in range(replicas):
        other = mine ^ offset
        step_out[pl.ds(pl.multiple_of(other * strip, strip), strip), :] = result[
            offset * strip : (offset + 1) * strip, :
        ]


def square_plan(acts, out_grad, old_factor, old_root, iter_count):
    replicas = lax.axis_size("dp")
    inputs = acts[0]
    tokens_all = inputs.shape[0] * replicas
    order = inputs.shape[1]
    share = order // replicas
    grows = out_grad.shape[2]
    strip = grows // replicas
    half = share // 2
    params = pltpu.CompilerParams(vmem_limit_bytes=VMEM_LIMIT)
    offsets = range(1, replicas)

    received = passed_along(out_grad, "pipe", -1)[0]
    own, *sends = pl.pallas_call(
        functools.partial(products_kernel, replicas, tokens_all),
        out_shape=[jax.ShapeDtypeStruct((share + strip, order), F32)]
        + [jax.ShapeDtypeStruct((share + strip, order), BF16)] * (replicas - 1),
        in_specs=whole(2),
        out_specs=whole(replicas),
        scratch_shapes=[pltpu.VMEM((grows, order), F32)],
        compiler_params=params,
        name="products",
    )(inputs, received)
    got = [swapped(sends[offset - 1], offset) for offset in reversed(offsets)][::-1]

    tail = replicas * strip + 16
    lengths = [2 * share + half + tail, 2 * share + half + tail, share + tail]
    factor, rows, *sends = pl.pallas_call(
        functools.partial(factor_kernel, replicas),
        out_shape=[
            jax.ShapeDtypeStruct((share, order), F32),
            jax.ShapeDtypeStruct((share + strip + 16, order), BF16),
        ]
        + [jax.ShapeDtypeStruct((length, share), BF16) for length in lengths],
        in_specs=whole(replicas + 1),
        out_specs=whole(replicas + 1),
        compiler_params=params,
        name="factor",
    )(own, *got, old_factor[0, 0])
    got = [swapped(sends[offset - 1], offset) for offset in reversed(offsets)][::-1]

    root, step = pl.pallas_call(
        functools.partial(root_kernel, replicas),
        out_shape=[
            jax.ShapeDtypeStruct((share, order), BF16),
            jax.ShapeDtypeStruct((grows, share), BF16),
        ],
        in_specs=[pl.BlockSpec(memory_space=pltpu.SMEM)] + whole(replicas + 1),
        out_specs=whole(2),
        scratch_shapes=[
            pltpu.VMEM((order, order), BF16),
            pltpu.VMEM((order, order), BF16),
            pltpu.VMEM((grows, order), BF16),
            pltpu.VMEM((grows, share), BF16),
        ],
        compiler_params=params,
        name="root",
    )(iter_count, rows, *got, old_root[0, 0])
    return (factor[None, None], root[None, None], step[None, None])


def ring_plan(acts, out_grad, old_factor, old_root, iter_count):
    inputs = acts[0]
    replicas = lax.axis_size("dp")
    tokens_all = inputs.shape[0] * replicas
    order = inputs.shape[1]
    share = order // replicas
    offset = lax.axis_index("dp") * share
    received = passed_along(out_grad, "pipe", -1)[0]
    partial_grad = jnp.dot(received.T, inputs, preferred_element_type=F32) / math.sqrt(tokens_all)
    batch = lax.psum_scatter(
        jnp.dot(inputs.T, inputs, preferred_element_type=F32) / tokens_all,
        "dp",
        scatter_dimension=0,
        tiled=True,
    )
    eye_rows = eye_of(share, order, offset)
    factor = DECAY * old_factor[0, 0] + (1.0 - DECAY) * batch + DAMPING * eye_rows
    grad16 = lax.psum(partial_grad, "dp").astype(BF16)
    scale = jnp.sqrt(lax.psum(jnp.sum(factor * factor), "dp") / order + EPSILON)
    step = lax.dot_general(
        grad16, old_root[0, 0], (((1,), (1,)), ((), ())), preferred_element_type=F32
    ).astype(BF16)
    first = lax.all_gather((factor / scale).astype(BF16), "dp", axis=0, tiled=True)
    turn_one = (1.5 * eye_of(order, order) - 0.5 * first.astype(F32)).astype(BF16)
    turn_rows = lax.dynamic_slice_in_dim(turn_one, offset, share, 0)
    second = jnp.dot(turn_rows, first, preferred_element_type=F32).astype(BF16)
    product = jnp.dot(second, turn_one, preferred_element_type=F32)
    turn_two = (1.5 * eye_rows - 0.5 * product).astype(BF16)
    inverse_rows = jnp.dot(turn_two, turn_one, preferred_element_type=F32)
    chosen = jnp.where(iter_count[0, 0] == 1, turn_rows.astype(F32), inverse_rows)
    root = (chosen / jnp.sqrt(scale)).astype(BF16)
    return (factor[None, None], root[None, None], step[None, None])


def solution(mesh):
    return jax.shard_map(
        square_plan if mesh.shape["dp"] == 4 else ring_plan,
        mesh=mesh,
        in_specs=(
            P("pipe", "dp", "tensor"),
            P("pipe", "dp", "tensor"),
            P("pipe", "tensor", "dp", None),
            P("pipe", "tensor", "dp", None),
            P("pipe", "tensor"),
        ),
        out_specs=(
            P("pipe", "tensor", "dp", None),
            P("pipe", "tensor", "dp", None),
            P("pipe", "tensor", None, "dp"),
        ),
        check_vma=False,
    )
```

```python
import functools
import math

import jax
import jax.numpy as jnp
from jax import lax
from jax.experimental import pallas as pl
from jax.experimental.pallas import tpu as pltpu
from jax.sharding import PartitionSpec as P

DECAY = 0.75
DAMPING = 0.1
EPSILON = 1e-06
BF16 = jnp.bfloat16
F32 = jnp.float32
VMEM_LIMIT = 28 * 1024 * 1024


def passed_along(block, axis, distance):
    devices = range(lax.axis_size(axis))
    route = [((i - distance) % len(devices), i) for i in devices]
    return lax.ppermute(block, axis, route)


def swapped(block, offset):
    return lax.ppermute(block, "dp", [(i, i ^ offset) for i in range(lax.axis_size("dp"))])


def eye_of(rows, cols, shift=0):
    row_ids = lax.broadcasted_iota(jnp.int32, (rows, cols), 0) + shift
    col_ids = lax.broadcasted_iota(jnp.int32, (rows, cols), 1)
    return (row_ids == col_ids).astype(F32)


def whole(count):
    return [pl.BlockSpec(memory_space=pltpu.VMEM)] * count


def transposed(block):
    return block.astype(F32).T.astype(block.dtype)


def chunk_rows(share):
    half = share // 2
    return [0, half, half + half // 2] + [half + half // 2 + half * i for i in range(1, 4)]


def shared_half(owner, offset, share):
    other = owner ^ offset
    low, high = jnp.minimum(owner, other), jnp.maximum(owner, other)
    row = low * share + jnp.where(owner > other, share // 2, 0)
    return pl.multiple_of(row, share // 2), pl.multiple_of(high * share, share)


def products_kernel(replicas, tokens_all, acts, grads, relay_x, relay_y, direct_x, direct_y, keep, batch, grad_sum):
    order = acts.shape[1]
    share = order // replicas
    half = share // 2
    strip = grads.shape[1] // replicas
    starts = chunk_rows(share)
    length = relay_x.shape[0]
    mine = lax.axis_index("dp")
    over_rows = (((0,), (0,)), ((), ()))
    for i in range(replicas):
        band = slice(i * share, (i + 1) * share)
        batch[band, i * share :] = lax.dot_general(
            acts[:, band], acts[:, i * share :], over_rows, preferred_element_type=F32
        ) * (1.0 / tokens_all)
    grad_sum[...] = lax.dot_general(grads[...], acts[...], over_rows, preferred_element_type=F32) * (
        1.0 / math.sqrt(tokens_all)
    )

    def pieces(offset):
        owner = mine ^ offset
        base = pl.multiple_of(owner * share, share)
        corner = pl.multiple_of(owner * share + half, half)
        yield 0, batch[pl.ds(base, half), pl.ds(base, share)]
        low = batch[pl.ds(corner, half), pl.ds(corner, half)]
        yield starts[1], jnp.concatenate([low[0 : half // 2], low[half // 2 :]], axis=1)
        for step in range(1, replicas):
            row, col = shared_half(owner, step, share)
            yield starts[1 + step], batch[pl.ds(row, half), pl.ds(col, share)]
        rows = pl.ds(pl.multiple_of(owner * strip, strip), strip)
        for part in range(replicas):
            yield starts[-1] + part * strip, grad_sum[rows, part * share : (part + 1) * share]

    def store(offset, upper, lower):
        for start, piece in pieces(offset):
            stop = start + piece.shape[0]
            for target, low, high in ((upper, 0, length), (lower, length, 2 * length)):
                first, last = max(start, low), min(stop, high)
                if target is not None and first < last:
                    ref, at = target
                    ref[at + first - low : at + last - low, :] = piece[first - start : last - start].astype(ref.dtype)

    store(3, (relay_x, 0), (relay_y, 0))
    store(1, (direct_x, 0), (keep, 3 * length))
    store(2, (keep, 2 * length), (direct_y, 0))
    store(0, (keep, 0), (keep, length))


def relay_kernel(keep, got_x, got_y, send_x, send_y):
    length = send_x.shape[0]
    send_y[...] = (keep[2 * length : 3 * length, :] + got_x[...].astype(F32)).astype(BF16)
    send_x[...] = (keep[3 * length :, :] + got_y[...].astype(F32)).astype(BF16)


def factor_kernel(replicas, keep, direct_x, direct_y, relay_x, relay_y, old, upper, lower, exact):
    share, order = old.shape
    half = share // 2
    starts = chunk_rows(share)
    length = upper.shape[0]
    mine = lax.axis_index("dp")
    total = jnp.concatenate(
        [
            keep[0:length, :] + direct_x[...].astype(F32) + relay_y[...].astype(F32),
            keep[length : 2 * length, :] + direct_y[...].astype(F32) + relay_x[...].astype(F32),
        ],
        axis=0,
    )
    diagonal = old[:, pl.ds(pl.multiple_of(mine * share, share), share)]
    eye = eye_of(half, share)
    low_eye = eye_of(half, half)

    def packed(low):
        return jnp.concatenate([low[0 : half // 2], low[half // 2 :]], axis=1)

    terms = [
        DECAY * diagonal[0:half] + DAMPING * eye,
        packed(DECAY * diagonal[half:, half:] + DAMPING * low_eye),
    ]
    for step in range(1, replicas):
        other = mine ^ step
        block = old[:, pl.ds(pl.multiple_of(other * share, share), share)]
        terms.append(DECAY * jnp.where(mine < other, block[0:half], block[:, half:].T))
    column = lax.broadcasted_iota(jnp.int32, (1, share), 1)
    squares = jnp.zeros((1, share), F32)
    values = []
    for position, (start, term) in enumerate(zip(starts, terms)):
        value = term + (1.0 - DECAY) * total[start : start + term.shape[0]]
        exact[start : start + term.shape[0], :] = value
        summed = jnp.sum(value * value, axis=0, keepdims=True)
        if position == 0:
            summed = jnp.where(column < half, summed, 2.0 * summed)
        squares = squares + (summed if position < 2 else 2.0 * summed)
        values.append(value.astype(BF16))
    values.append(total[starts[-1] :].astype(BF16))
    high = squares.astype(BF16).astype(F32)
    middle = (squares - high).astype(BF16).astype(F32)
    rest = squares - high - middle
    spot = lax.broadcasted_iota(jnp.int32, (16, share), 0)
    digits = jnp.where(spot == 0, high, jnp.where(spot == 1, middle, jnp.where(spot == 2, rest, 0.0)))
    values.append(digits.astype(BF16))
    chunk = jnp.concatenate(values, axis=0)
    upper[...] = chunk[0:length]
    lower[...] = chunk[length:]


def root_kernel(replicas, count, exact, *rest):
    chunks = [rest[2 * i : 2 * i + 2] for i in range(replicas)]
    old_root, factor_out, root_out, step_out, factor, grads, diagonal, result = rest[2 * replicas :]
    share = root_out.shape[0]
    order = root_out.shape[1]
    half = share // 2
    strip = step_out.shape[0] // replicas
    starts = chunk_rows(share)
    length = chunks[0][0].shape[0]
    mine = lax.axis_index("dp")

    def rows_of(offset, start, count):
        upper, lower = chunks[offset]
        if start + count <= length:
            return upper[start : start + count, :]
        if start >= length:
            return lower[start - length : start - length + count, :]
        return jnp.concatenate([upper[start:, :], lower[0 : start + count - length, :]], axis=0)

    squares = jnp.zeros((16, share), F32)
    for offset in range(replicas):
        owner = mine ^ offset
        base = pl.multiple_of(owner * share, share)
        corner = pl.multiple_of(owner * share + half, half)
        top = rows_of(offset, 0, half)
        low = rows_of(offset, starts[1], half // 2)
        low = jnp.concatenate([low[:, 0:half], low[:, half:]], axis=0)
        factor[pl.ds(base, half), pl.ds(base, share)] = top
        factor[pl.ds(corner, half), pl.ds(base, half)] = transposed(top[:, half:])
        factor[pl.ds(corner, half), pl.ds(corner, half)] = low
        on_diagonal = low_eye = eye_of(half, half)
        diagonal[:, pl.ds(base, half)] = jnp.sum(
            top[:, 0:half].astype(F32) * on_diagonal, axis=0, keepdims=True
        )
        diagonal[:, pl.ds(corner, half)] = jnp.sum(low.astype(F32) * low_eye, axis=0, keepdims=True)
        for step in range(1, replicas):
            row, col = shared_half(owner, step, share)
            block = rows_of(offset, starts[1 + step], half)
            factor[pl.ds(row, half), pl.ds(col, share)] = block
            factor[pl.ds(col, share), pl.ds(row, half)] = transposed(block)
        for part in range(replicas):
            grads[offset * strip : (offset + 1) * strip, part * share : (part + 1) * share] = rows_of(
                offset, starts[-1] + part * strip, strip
            )
        squares = squares + rows_of(offset, starts[-1] + replicas * strip, 16).astype(F32)

    scale = jnp.sqrt(jnp.sum(squares, keepdims=True) / order + EPSILON)
    inverse = 1.0 / scale
    ones = diagonal[...] * inverse
    ones = ones.astype(BF16).astype(F32)
    lift = (1.5 - 0.5 * ones).astype(BF16).astype(F32) + 0.5 * (diagonal[...] * inverse)
    eye = eye_of(share, order, mine * share)
    my_rows = pl.ds(pl.multiple_of(mine * share, share), share)
    first = (factor[my_rows, :].astype(F32) * inverse).astype(BF16).astype(F32)
    turn = (1.5 * eye - 0.5 * first).astype(BF16)
    second = (jnp.dot(turn, factor[...], preferred_element_type=F32) * inverse).astype(BF16)
    product = (-0.5 * inverse) * jnp.dot(second, factor[...], preferred_element_type=F32) + second.astype(F32) * lift
    turn_two = (1.5 * eye - 0.5 * product).astype(BF16)
    inverse_rows = (-0.5 * inverse) * jnp.dot(
        turn_two, factor[...], preferred_element_type=F32
    ) + turn_two.astype(F32) * lift
    chosen = jnp.where(count[0, 0] == 1, turn.astype(F32), inverse_rows)
    root_out[...] = (chosen * lax.rsqrt(scale)).astype(BF16)

    result[...] = lax.dot_general(
        grads[...], old_root[...], (((1,), (1,)), ((), ())), preferred_element_type=F32
    ).astype(BF16)
    for offset in range(replicas):
        owner = mine ^ offset
        step_out[pl.ds(pl.multiple_of(owner * strip, strip), strip), :] = result[
            offset * strip : (offset + 1) * strip, :
        ]

    own_columns = pl.ds(pl.multiple_of(mine * share, share), share)
    top = exact[0:half, :]
    low = exact[starts[1] : starts[2], :]
    low = jnp.concatenate([low[:, 0:half], low[:, half:]], axis=0)
    factor_out[0:half, own_columns] = top
    factor_out[half:, own_columns] = jnp.concatenate([top[:, half:].T, low], axis=1)
    for step in range(1, replicas):
        other = mine ^ step
        columns = pl.ds(pl.multiple_of(other * share, share), share)
        own = exact[starts[1 + step] : starts[1 + step] + half, :]
        theirs = rows_of(step, starts[1 + step], half).astype(F32)

        @pl.when(mine < other)
        def _():
            factor_out[0:half, columns] = own
            factor_out[half:, columns] = theirs

        @pl.when(mine > other)
        def _():
            factor_out[:, columns] = jnp.concatenate([theirs.T, own.T], axis=1)


def square_plan(acts, out_grad, old_factor, old_root, iter_count):
    replicas = lax.axis_size("dp")
    inputs = acts[0]
    tokens_all = inputs.shape[0] * replicas
    order = inputs.shape[1]
    share = order // replicas
    grows = out_grad.shape[2]
    params = pltpu.CompilerParams(vmem_limit_bytes=VMEM_LIMIT)
    whole_rows = chunk_rows(share)[-1] + grows
    length = whole_rows // 2
    piece = jax.ShapeDtypeStruct((length, share), BF16)

    received = passed_along(out_grad, "pipe", -1)[0]
    relay_x, relay_y, direct_x, direct_y, keep = pl.pallas_call(
        functools.partial(products_kernel, replicas, tokens_all),
        out_shape=[piece] * 4 + [jax.ShapeDtypeStruct((4 * length, share), F32)],
        in_specs=whole(2),
        out_specs=whole(5),
        scratch_shapes=[pltpu.VMEM((order, order), F32), pltpu.VMEM((grows, order), F32)],
        compiler_params=params,
        name="products",
    )(inputs, received)
    relay_x, relay_y = swapped(relay_x, 1), swapped(relay_y, 2)
    direct_x, direct_y = swapped(direct_x, 1), swapped(direct_y, 2)
    relay_x, relay_y = pl.pallas_call(
        relay_kernel,
        out_shape=[piece] * 2,
        in_specs=whole(3),
        out_specs=whole(2),
        compiler_params=params,
        name="relay",
    )(keep, relay_x, relay_y)
    relay_x, relay_y = swapped(relay_x, 1), swapped(relay_y, 2)
    upper, lower, exact = pl.pallas_call(
        functools.partial(factor_kernel, replicas),
        out_shape=[
            piece,
            jax.ShapeDtypeStruct((length + 16, share), BF16),
            jax.ShapeDtypeStruct((chunk_rows(share)[-1], share), F32),
        ],
        in_specs=whole(6),
        out_specs=whole(3),
        compiler_params=params,
        name="factor",
    )(keep, direct_x, direct_y, relay_x, relay_y, old_factor[0, 0])
    upper_x, lower_y = swapped(upper, 1), swapped(lower, 2)
    lower_x, upper_y = swapped(lower, 1), swapped(upper, 2)
    upper_far, lower_far = swapped(upper_x, 2), swapped(lower_y, 1)
    factor, root, step = pl.pallas_call(
        functools.partial(root_kernel, replicas),
        out_shape=[
            jax.ShapeDtypeStruct((share, order), F32),
            jax.ShapeDtypeStruct((share, order), BF16),
            jax.ShapeDtypeStruct((grows, share), BF16),
        ],
        in_specs=[pl.BlockSpec(memory_space=pltpu.SMEM)] + whole(2 * replicas + 2),
        out_specs=whole(3),
        scratch_shapes=[
            pltpu.VMEM((order, order), BF16),
            pltpu.VMEM((grows, order), BF16),
            pltpu.VMEM((1, order), F32),
            pltpu.VMEM((grows, share), BF16),
        ],
        compiler_params=params,
        name="root",
    )(iter_count, exact, upper, lower, upper_x, lower_x, upper_y, lower_y, upper_far, lower_far, old_root[0, 0])
    return (factor[None, None], root[None, None], step[None, None])


def ring_plan(acts, out_grad, old_factor, old_root, iter_count):
    inputs = acts[0]
    replicas = lax.axis_size("dp")
    tokens_all = inputs.shape[0] * replicas
    order = inputs.shape[1]
    share = order // replicas
    offset = lax.axis_index("dp") * share
    received = passed_along(out_grad, "pipe", -1)[0]
    partial_grad = jnp.dot(received.T, inputs, preferred_element_type=F32) / math.sqrt(tokens_all)
    batch = lax.psum_scatter(
        jnp.dot(inputs.T, inputs, preferred_element_type=F32) / tokens_all,
        "dp",
        scatter_dimension=0,
        tiled=True,
    )
    eye_rows = eye_of(share, order, offset)
    factor = DECAY * old_factor[0, 0] + (1.0 - DECAY) * batch + DAMPING * eye_rows
    grad16 = lax.psum(partial_grad, "dp").astype(BF16)
    scale = jnp.sqrt(lax.psum(jnp.sum(factor * factor), "dp") / order + EPSILON)
    step = lax.dot_general(
        grad16, old_root[0, 0], (((1,), (1,)), ((), ())), preferred_element_type=F32
    ).astype(BF16)
    first = lax.all_gather((factor / scale).astype(BF16), "dp", axis=0, tiled=True)
    turn_one = (1.5 * eye_of(order, order) - 0.5 * first.astype(F32)).astype(BF16)
    turn_rows = lax.dynamic_slice_in_dim(turn_one, offset, share, 0)
    second = jnp.dot(turn_rows, first, preferred_element_type=F32).astype(BF16)
    product = jnp.dot(second, turn_one, preferred_element_type=F32)
    turn_two = (1.5 * eye_rows - 0.5 * product).astype(BF16)
    inverse_rows = jnp.dot(turn_two, turn_one, preferred_element_type=F32)
    chosen = jnp.where(iter_count[0, 0] == 1, turn_rows.astype(F32), inverse_rows)
    root = (chosen / jnp.sqrt(scale)).astype(BF16)
    return (factor[None, None], root[None, None], step[None, None])


def solution(mesh):
    return jax.shard_map(
        square_plan if mesh.shape["dp"] == 4 else ring_plan,
        mesh=mesh,
        in_specs=(
            P("pipe", "dp", "tensor"),
            P("pipe", "dp", "tensor"),
            P("pipe", "tensor", "dp", None),
            P("pipe", "tensor", "dp", None),
            P("pipe", "tensor"),
        ),
        out_specs=(
            P("pipe", "tensor", "dp", None),
            P("pipe", "tensor", "dp", None),
            P("pipe", "tensor", None, "dp"),
        ),
        check_vma=False,
    )
```

```python
import functools
import math

import jax
import jax.numpy as jnp
from jax import lax
from jax.experimental import pallas as pl
from jax.experimental.pallas import tpu as pltpu
from jax.sharding import PartitionSpec as P

DECAY = 0.75
DAMPING = 0.1
EPSILON = 1e-06
BF16 = jnp.bfloat16
F32 = jnp.float32
VMEM_LIMIT = 28 * 1024 * 1024


def passed_along(block, axis, distance):
    devices = range(lax.axis_size(axis))
    route = [((i - distance) % len(devices), i) for i in devices]
    return lax.ppermute(block, axis, route)


def swapped(block, offset):
    return lax.ppermute(block, "dp", [(i, i ^ offset) for i in range(lax.axis_size("dp"))])


def eye_of(rows, cols, shift=0):
    row_ids = lax.broadcasted_iota(jnp.int32, (rows, cols), 0) + shift
    col_ids = lax.broadcasted_iota(jnp.int32, (rows, cols), 1)
    return (row_ids == col_ids).astype(F32)


def whole(count):
    return [pl.BlockSpec(memory_space=pltpu.VMEM)] * count


def transposed(block):
    return block.astype(F32).T.astype(block.dtype)


def chunk_rows(share):
    half = share // 2
    return [0, half, half + half // 2] + [half + half // 2 + half * i for i in range(1, 4)]


def shared_half(owner, offset, share):
    other = owner ^ offset
    low, high = jnp.minimum(owner, other), jnp.maximum(owner, other)
    row = low * share + jnp.where(owner > other, share // 2, 0)
    return pl.multiple_of(row, share // 2), pl.multiple_of(high * share, share)


def store_chunk(pieces, length, upper, lower):
    for start, piece in pieces:
        stop = start + piece.shape[0]
        for target, low, high in ((upper, 0, length), (lower, length, stop)):
            first, last = max(start, low), min(stop, high)
            if target is not None and first < last:
                ref, at = target
                ref[at + first - low : at + last - low, :] = piece[first - start : last - start].astype(ref.dtype)


def batch_kernel(replicas, tokens_all, acts, relay_x, relay_y, direct_x, direct_y, keep, batch):
    order = acts.shape[1]
    share = order // replicas
    half = share // 2
    starts = chunk_rows(share)
    length = relay_x.shape[0]
    mine = lax.axis_index("dp")
    for i in range(replicas):
        band = slice(i * share, (i + 1) * share)
        batch[band, i * share :] = lax.dot_general(
            acts[:, band], acts[:, i * share :], (((0,), (0,)), ((), ())), preferred_element_type=F32
        ) * (1.0 / tokens_all)

    def pieces(offset):
        owner = mine ^ offset
        base = pl.multiple_of(owner * share, share)
        corner = pl.multiple_of(owner * share + half, half)
        yield 0, batch[pl.ds(base, half), pl.ds(base, share)]
        low = batch[pl.ds(corner, half), pl.ds(corner, half)]
        yield starts[1], jnp.concatenate([low[0 : half // 2], low[half // 2 :]], axis=1)
        for step in range(1, replicas):
            row, col = shared_half(owner, step, share)
            yield starts[1 + step], batch[pl.ds(row, half), pl.ds(col, share)]

    store_chunk(pieces(3), length, (relay_x, 0), (relay_y, 0))
    store_chunk(pieces(1), length, (direct_x, 0), (keep, 3 * length))
    store_chunk(pieces(2), length, (keep, 2 * length), (direct_y, 0))
    store_chunk(pieces(0), length, (keep, 0), (keep, length))


def grad_kernel(replicas, tokens_all, acts, grads, send_x, send_y, keep, total):
    order = acts.shape[1]
    share = order // replicas
    strip = grads.shape[1] // replicas
    length = send_x.shape[0] // 2
    mine = lax.axis_index("dp")
    total[...] = lax.dot_general(
        grads[...], acts[...], (((0,), (0,)), ((), ())), preferred_element_type=F32
    ) * (1.0 / math.sqrt(tokens_all))

    def pieces(offset):
        rows = pl.ds(pl.multiple_of((mine ^ offset) * strip, strip), strip)
        for part in range(replicas):
            yield part * strip, total[rows, part * share : (part + 1) * share]

    store_chunk(pieces(3), length, (send_x, 0), (send_y, 0))
    store_chunk(pieces(1), length, (send_x, length), (keep, 3 * length))
    store_chunk(pieces(2), length, (keep, 2 * length), (send_y, length))
    store_chunk(pieces(0), length, (keep, 0), (keep, length))


def relay_kernel(keep, got_x, got_y, send_x, send_y):
    length = send_x.shape[0]
    send_y[...] = (keep[2 * length : 3 * length, :] + got_x[...].astype(F32)).astype(BF16)
    send_x[...] = (keep[3 * length :, :] + got_y[...].astype(F32)).astype(BF16)


def grad_relay_kernel(keep, got_x, got_y, send_x, send_y):
    length = send_x.shape[0]
    send_y[...] = (keep[2 * length : 3 * length, :] + got_x[0:length, :].astype(F32)).astype(BF16)
    send_x[...] = (keep[3 * length :, :] + got_y[0:length, :].astype(F32)).astype(BF16)


def grad_total_kernel(keep, got_x, got_y, relay_x, relay_y, chunk):
    length = relay_x.shape[0]
    chunk[0:length, :] = (
        keep[0:length, :] + got_x[length:, :].astype(F32) + relay_y[...].astype(F32)
    ).astype(BF16)
    chunk[length:, :] = (
        keep[length : 2 * length, :] + got_y[length:, :].astype(F32) + relay_x[...].astype(F32)
    ).astype(BF16)


def factor_kernel(replicas, keep, direct_x, direct_y, relay_x, relay_y, old, upper, lower, exact):
    share, order = old.shape
    half = share // 2
    starts = chunk_rows(share)
    length = upper.shape[0]
    mine = lax.axis_index("dp")
    total = jnp.concatenate(
        [
            keep[0:length, :] + direct_x[...].astype(F32) + relay_y[...].astype(F32),
            keep[length : 2 * length, :] + direct_y[...].astype(F32) + relay_x[...].astype(F32),
        ],
        axis=0,
    )
    diagonal = old[:, pl.ds(pl.multiple_of(mine * share, share), share)]
    eye = eye_of(half, share)
    low_eye = eye_of(half, half)

    def packed(low):
        return jnp.concatenate([low[0 : half // 2], low[half // 2 :]], axis=1)

    terms = [
        DECAY * diagonal[0:half] + DAMPING * eye,
        packed(DECAY * diagonal[half:, half:] + DAMPING * low_eye),
    ]
    for step in range(1, replicas):
        other = mine ^ step
        block = old[:, pl.ds(pl.multiple_of(other * share, share), share)]
        terms.append(DECAY * jnp.where(mine < other, block[0:half], block[:, half:].T))
    column = lax.broadcasted_iota(jnp.int32, (1, share), 1)
    squares = jnp.zeros((1, share), F32)
    values = []
    for position, (start, term) in enumerate(zip(starts, terms)):
        value = term + (1.0 - DECAY) * total[start : start + term.shape[0]]
        exact[start : start + term.shape[0], :] = value
        summed = jnp.sum(value * value, axis=0, keepdims=True)
        if position == 0:
            summed = jnp.where(column < half, summed, 2.0 * summed)
        squares = squares + (summed if position < 2 else 2.0 * summed)
        values.append(value.astype(BF16))
    high = squares.astype(BF16).astype(F32)
    middle = (squares - high).astype(BF16).astype(F32)
    rest = squares - high - middle
    spot = lax.broadcasted_iota(jnp.int32, (16, share), 0)
    digits = jnp.where(spot == 0, high, jnp.where(spot == 1, middle, jnp.where(spot == 2, rest, 0.0)))
    values.append(digits.astype(BF16))
    chunk = jnp.concatenate(values, axis=0)
    upper[...] = chunk[0:length]
    lower[...] = chunk[length:]


def root_kernel(replicas, count, exact, *rest):
    chunks = [rest[2 * i : 2 * i + 2] for i in range(replicas)]
    factor_out, root_out, finished, factor, diagonal = rest[2 * replicas :]
    share = root_out.shape[0]
    order = root_out.shape[1]
    half = share // 2
    starts = chunk_rows(share)
    length = chunks[0][0].shape[0]
    mine = lax.axis_index("dp")

    def rows_of(offset, start, count):
        upper, lower = chunks[offset]
        if start + count <= length:
            return upper[start : start + count, :]
        if start >= length:
            return lower[start - length : start - length + count, :]
        return jnp.concatenate([upper[start:length, :], lower[0 : start + count - length, :]], axis=0)

    squares = jnp.zeros((16, share), F32)
    low_eye = eye_of(half, half)
    for offset in range(replicas):
        owner = mine ^ offset
        base = pl.multiple_of(owner * share, share)
        corner = pl.multiple_of(owner * share + half, half)
        top = rows_of(offset, 0, half)
        low = rows_of(offset, starts[1], half // 2)
        low = jnp.concatenate([low[:, 0:half], low[:, half:]], axis=0)
        factor[pl.ds(base, half), pl.ds(base, share)] = top
        factor[pl.ds(corner, half), pl.ds(base, half)] = transposed(top[:, half:])
        factor[pl.ds(corner, half), pl.ds(corner, half)] = low
        diagonal[:, pl.ds(base, half)] = jnp.sum(top[:, 0:half].astype(F32) * low_eye, axis=0, keepdims=True)
        diagonal[:, pl.ds(corner, half)] = jnp.sum(low.astype(F32) * low_eye, axis=0, keepdims=True)
        for step in range(1, replicas):
            row, col = shared_half(owner, step, share)
            block = rows_of(offset, starts[1 + step], half)
            factor[pl.ds(row, half), pl.ds(col, share)] = block
            factor[pl.ds(col, share), pl.ds(row, half)] = transposed(block)
        squares = squares + rows_of(offset, starts[-1], 16).astype(F32)

    scale = jnp.sqrt(jnp.sum(squares, keepdims=True) / order + EPSILON)
    inverse = 1.0 / scale
    ones = (diagonal[...] * inverse).astype(BF16).astype(F32)
    lift = (1.5 - 0.5 * ones).astype(BF16).astype(F32) + 0.5 * (diagonal[...] * inverse)
    eye = eye_of(share, order, mine * share)
    my_rows = pl.ds(pl.multiple_of(mine * share, share), share)
    first = (factor[my_rows, :].astype(F32) * inverse).astype(BF16).astype(F32)
    turn = (1.5 * eye - 0.5 * first).astype(BF16)
    second = (jnp.dot(turn, factor[...], preferred_element_type=F32) * inverse).astype(BF16)
    product = (-0.5 * inverse) * jnp.dot(second, factor[...], preferred_element_type=F32) + second.astype(F32) * lift
    turn_two = (1.5 * eye - 0.5 * product).astype(BF16)
    inverse_rows = (-0.5 * inverse) * jnp.dot(
        turn_two, factor[...], preferred_element_type=F32
    ) + turn_two.astype(F32) * lift
    chosen = jnp.where(count[0, 0] == 1, turn.astype(F32), inverse_rows)
    root_out[...] = (chosen * lax.rsqrt(scale)).astype(BF16)
    finished[...] = jnp.zeros_like(finished)

    own_columns = pl.ds(pl.multiple_of(mine * share, share), share)
    top = exact[0:half, :]
    low = exact[starts[1] : starts[2], :]
    low = jnp.concatenate([low[:, 0:half], low[:, half:]], axis=0)
    factor_out[0:half, own_columns] = top
    factor_out[half:, own_columns] = jnp.concatenate([top[:, half:].T, low], axis=1)
    for step in range(1, replicas):
        other = mine ^ step
        columns = pl.ds(pl.multiple_of(other * share, share), share)
        own = exact[starts[1 + step] : starts[1 + step] + half, :]
        theirs = rows_of(step, starts[1 + step], half).astype(F32)

        @pl.when(mine < other)
        def _():
            factor_out[0:half, columns] = own
            factor_out[half:, columns] = theirs

        @pl.when(mine > other)
        def _():
            factor_out[:, columns] = jnp.concatenate([theirs.T, own.T], axis=1)


def step_kernel(replicas, *refs):
    chunks = refs[:replicas]
    old_root, step_out, grads, result = refs[replicas:]
    share = old_root.shape[0]
    strip = step_out.shape[0] // replicas
    mine = lax.axis_index("dp")
    for offset, chunk in enumerate(chunks):
        for part in range(replicas):
            grads[offset * strip : (offset + 1) * strip, part * share : (part + 1) * share] = chunk[
                part * strip : (part + 1) * strip, :
            ]
    result[...] = lax.dot_general(
        grads[...], old_root[...], (((1,), (1,)), ((), ())), preferred_element_type=F32
    ).astype(BF16)
    for offset in range(replicas):
        owner = mine ^ offset
        step_out[pl.ds(pl.multiple_of(owner * strip, strip), strip), :] = result[
            offset * strip : (offset + 1) * strip, :
        ]


def square_plan(acts, out_grad, old_factor, old_root, iter_count):
    replicas = lax.axis_size("dp")
    inputs = acts[0]
    tokens, order = inputs.shape
    share = order // replicas
    grows = out_grad.shape[2]
    params = pltpu.CompilerParams(vmem_limit_bytes=VMEM_LIMIT)
    whole_rows = chunk_rows(share)[-1]
    length = whole_rows // 2

    def shape(rows, kind=BF16, columns=share):
        return jax.ShapeDtypeStruct((rows, columns), kind)

    def call(kernel, outs, name, *operands, first=None, after=(), scratch=()):
        in_specs = whole(len(operands)) + [pl.BlockSpec(memory_space=pl.ANY)] * len(after)
        if first is not None:
            in_specs[0] = pl.BlockSpec(memory_space=first)

        def body(*refs):
            kernel(*refs[: len(operands)], *refs[len(operands) + len(after) :])

        return pl.pallas_call(
            body,
            out_shape=outs,
            in_specs=in_specs,
            out_specs=whole(len(outs)),
            scratch_shapes=scratch,
            compiler_params=params,
            name=name,
        )(*operands, *after)

    received = passed_along(out_grad, "pipe", -1)[0]
    relay_x, relay_y, direct_x, direct_y, keep = call(
        functools.partial(batch_kernel, replicas, tokens * replicas),
        [shape(length)] * 4 + [shape(4 * length, F32)],
        "batch",
        inputs,
        scratch=[pltpu.VMEM((order, order), F32)],
    )
    relay_x, relay_y = swapped(relay_x, 1), swapped(relay_y, 2)
    direct_x, direct_y = swapped(direct_x, 1), swapped(direct_y, 2)
    relay_x, relay_y = call(relay_kernel, [shape(length)] * 2, "relay", keep, relay_x, relay_y)
    grad_x, grad_y, grad_keep = call(
        functools.partial(grad_kernel, replicas, tokens * replicas),
        [shape(grows)] * 2 + [shape(2 * grows, F32)],
        "grad",
        inputs,
        received,
        after=[relay_x, relay_y],
        scratch=[pltpu.VMEM((grows, order), F32)],
    )
    relay_x, relay_y = swapped(relay_x, 1), swapped(relay_y, 2)
    grad_x, grad_y = swapped(grad_x, 1), swapped(grad_y, 2)
    upper, lower, exact = call(
        functools.partial(factor_kernel, replicas),
        [shape(length), shape(length + 16), shape(whole_rows, F32)],
        "factor",
        keep,
        direct_x,
        direct_y,
        relay_x,
        relay_y,
        old_factor[0, 0],
    )
    upper_x, lower_y = swapped(upper, 1), swapped(lower, 2)
    lower_x, upper_y = swapped(lower, 1), swapped(upper, 2)
    strip_x, strip_y = call(
        grad_relay_kernel, [shape(grows // 2)] * 2, "grad_relay", grad_keep, grad_x, grad_y, after=[upper, lower]
    )
    strip_x, strip_y = swapped(strip_x, 1), swapped(strip_y, 2)
    upper_far, lower_far = swapped(upper_x, 2), swapped(lower_y, 1)
    (strip,) = call(
        grad_total_kernel,
        [shape(grows)],
        "grad_total",
        grad_keep,
        grad_x,
        grad_y,
        strip_x,
        strip_y,
        after=[upper_x, lower_y],
    )
    strips = [strip] + [swapped(strip, offset) for offset in range(1, replicas)]
    factor, root, finished = call(
        functools.partial(root_kernel, replicas),
        [shape(share, F32, order), shape(share, BF16, order), shape(8, F32, 128)],
        "root",
        iter_count,
        exact,
        upper,
        lower,
        upper_x,
        lower_x,
        upper_y,
        lower_y,
        upper_far,
        lower_far,
        first=pltpu.SMEM,
        scratch=[pltpu.VMEM((order, order), BF16), pltpu.VMEM((1, order), F32)],
    )
    (step,) = call(
        functools.partial(step_kernel, replicas),
        [shape(grows, BF16, share)],
        "step",
        *strips,
        old_root[0, 0],
        after=[finished],
        scratch=[pltpu.VMEM((grows, order), BF16), pltpu.VMEM((grows, share), BF16)],
    )
    return (factor[None, None], root[None, None], step[None, None])


def ring_plan(acts, out_grad, old_factor, old_root, iter_count):
    inputs = acts[0]
    replicas = lax.axis_size("dp")
    tokens_all = inputs.shape[0] * replicas
    order = inputs.shape[1]
    share = order // replicas
    offset = lax.axis_index("dp") * share
    received = passed_along(out_grad, "pipe", -1)[0]
    partial_grad = jnp.dot(received.T, inputs, preferred_element_type=F32) / math.sqrt(tokens_all)
    batch = lax.psum_scatter(
        jnp.dot(inputs.T, inputs, preferred_element_type=F32) / tokens_all,
        "dp",
        scatter_dimension=0,
        tiled=True,
    )
    eye_rows = eye_of(share, order, offset)
    factor = DECAY * old_factor[0, 0] + (1.0 - DECAY) * batch + DAMPING * eye_rows
    grad16 = lax.psum(partial_grad, "dp").astype(BF16)
    scale = jnp.sqrt(lax.psum(jnp.sum(factor * factor), "dp") / order + EPSILON)
    step = lax.dot_general(
        grad16, old_root[0, 0], (((1,), (1,)), ((), ())), preferred_element_type=F32
    ).astype(BF16)
    first = lax.all_gather((factor / scale).astype(BF16), "dp", axis=0, tiled=True)
    turn_one = (1.5 * eye_of(order, order) - 0.5 * first.astype(F32)).astype(BF16)
    turn_rows = lax.dynamic_slice_in_dim(turn_one, offset, share, 0)
    second = jnp.dot(turn_rows, first, preferred_element_type=F32).astype(BF16)
    product = jnp.dot(second, turn_one, preferred_element_type=F32)
    turn_two = (1.5 * eye_rows - 0.5 * product).astype(BF16)
    inverse_rows = jnp.dot(turn_two, turn_one, preferred_element_type=F32)
    chosen = jnp.where(iter_count[0, 0] == 1, turn_rows.astype(F32), inverse_rows)
    root = (chosen / jnp.sqrt(scale)).astype(BF16)
    return (factor[None, None], root[None, None], step[None, None])


def solution(mesh):
    return jax.shard_map(
        square_plan if mesh.shape["dp"] == 4 else ring_plan,
        mesh=mesh,
        in_specs=(
            P("pipe", "dp", "tensor"),
            P("pipe", "dp", "tensor"),
            P("pipe", "tensor", "dp", None),
            P("pipe", "tensor", "dp", None),
            P("pipe", "tensor"),
        ),
        out_specs=(
            P("pipe", "tensor", "dp", None),
            P("pipe", "tensor", "dp", None),
            P("pipe", "tensor", None, "dp"),
        ),
        check_vma=False,
    )
```

```python
import functools
import math

import jax
import jax.numpy as jnp
from jax import lax
from jax.experimental import pallas as pl
from jax.experimental.pallas import tpu as pltpu
from jax.sharding import PartitionSpec as P

DECAY = 0.75
DAMPING = 0.1
EPSILON = 1e-06
BF16 = jnp.bfloat16
F32 = jnp.float32
VMEM_LIMIT = 28 * 1024 * 1024


def passed_along(block, axis, distance):
    devices = range(lax.axis_size(axis))
    route = [((i - distance) % len(devices), i) for i in devices]
    return lax.ppermute(block, axis, route)


def swapped(block, offset):
    return lax.ppermute(block, "dp", [(i, i ^ offset) for i in range(lax.axis_size("dp"))])


def eye_of(rows, cols, shift=0):
    row_ids = lax.broadcasted_iota(jnp.int32, (rows, cols), 0) + shift
    col_ids = lax.broadcasted_iota(jnp.int32, (rows, cols), 1)
    return (row_ids == col_ids).astype(F32)


def whole(count):
    return [pl.BlockSpec(memory_space=pltpu.VMEM)] * count


def transposed(block):
    return block.astype(F32).T.astype(block.dtype)


def chunk_rows(share):
    half = share // 2
    return [0, half, half + half // 2] + [half + half // 2 + half * i for i in range(1, 4)]


def shared_half(owner, offset, share):
    other = owner ^ offset
    low, high = jnp.minimum(owner, other), jnp.maximum(owner, other)
    row = low * share + jnp.where(owner > other, share // 2, 0)
    return pl.multiple_of(row, share // 2), pl.multiple_of(high * share, share)


def store_chunk(pieces, length, upper, lower):
    for start, piece in pieces:
        stop = start + piece.shape[0]
        for target, low, high in ((upper, 0, length), (lower, length, stop)):
            first, last = max(start, low), min(stop, high)
            if target is not None and first < last:
                ref, at = target
                ref[at + first - low : at + last - low, :] = piece[first - start : last - start].astype(ref.dtype)


def batch_kernel(replicas, tokens_all, acts, relay_x, relay_y, direct_x, direct_y, keep, batch):
    order = acts.shape[1]
    share = order // replicas
    half = share // 2
    starts = chunk_rows(share)
    length = relay_x.shape[0]
    mine = lax.axis_index("dp")
    for i in range(replicas):
        band = slice(i * share, (i + 1) * share)
        batch[band, i * share :] = lax.dot_general(
            acts[:, band], acts[:, i * share :], (((0,), (0,)), ((), ())), preferred_element_type=F32
        ) * (1.0 / tokens_all)

    def pieces(offset):
        owner = mine ^ offset
        base = pl.multiple_of(owner * share, share)
        corner = pl.multiple_of(owner * share + half, half)
        yield 0, batch[pl.ds(base, half), pl.ds(base, share)]
        low = batch[pl.ds(corner, half), pl.ds(corner, half)]
        yield starts[1], jnp.concatenate([low[0 : half // 2], low[half // 2 :]], axis=1)
        for step in range(1, replicas):
            row, col = shared_half(owner, step, share)
            yield starts[1 + step], batch[pl.ds(row, half), pl.ds(col, share)]

    store_chunk(pieces(3), length, (relay_x, 0), (relay_y, 0))
    store_chunk(pieces(1), length, (direct_x, 0), (keep, 3 * length))
    store_chunk(pieces(2), length, (keep, 2 * length), (direct_y, 0))
    store_chunk(pieces(0), length, (keep, 0), (keep, length))


def grad_kernel(tokens_all, acts, grads, partial):
    partial[...] = (
        lax.dot_general(grads[...], acts[...], (((0,), (0,)), ((), ())), preferred_element_type=F32)
        * (1.0 / math.sqrt(tokens_all))
    ).astype(BF16)


def relay_kernel(keep, got_x, got_y, send_x, send_y):
    length = send_x.shape[0]
    send_y[...] = (keep[2 * length : 3 * length, :] + got_x[...].astype(F32)).astype(BF16)
    send_x[...] = (keep[3 * length :, :] + got_y[...].astype(F32)).astype(BF16)


def strip_kernel(replicas, partials, copies):
    strip = partials.shape[0] // replicas
    total = partials[0:strip, :].astype(F32)
    for i in range(1, replicas):
        total = total + partials[i * strip : (i + 1) * strip, :].astype(F32)
    for i in range(replicas):
        copies[i * strip : (i + 1) * strip, :] = total.astype(BF16)


def halves_kernel(got_x, got_y, send_x, send_y):
    send_y[...] = got_x[0 : send_y.shape[0], :]
    send_x[...] = got_y[send_y.shape[0] :, :]


def factor_kernel(replicas, keep, direct_x, direct_y, relay_x, relay_y, old, chunk, exact):
    share, order = old.shape
    half = share // 2
    starts = chunk_rows(share)
    length = direct_x.shape[0]
    mine = lax.axis_index("dp")
    total = jnp.concatenate(
        [
            keep[0:length, :] + direct_x[...].astype(F32) + relay_y[...].astype(F32),
            keep[length : 2 * length, :] + direct_y[...].astype(F32) + relay_x[...].astype(F32),
        ],
        axis=0,
    )
    diagonal = old[:, pl.ds(pl.multiple_of(mine * share, share), share)]
    eye = eye_of(half, share)
    low_eye = eye_of(half, half)

    def packed(low):
        return jnp.concatenate([low[0 : half // 2], low[half // 2 :]], axis=1)

    terms = [
        DECAY * diagonal[0:half] + DAMPING * eye,
        packed(DECAY * diagonal[half:, half:] + DAMPING * low_eye),
    ]
    for step in range(1, replicas):
        other = mine ^ step
        block = old[:, pl.ds(pl.multiple_of(other * share, share), share)]
        terms.append(DECAY * jnp.where(mine < other, block[0:half], block[:, half:].T))
    column = lax.broadcasted_iota(jnp.int32, (1, share), 1)
    squares = jnp.zeros((1, share), F32)
    values = []
    for position, (start, term) in enumerate(zip(starts, terms)):
        value = term + (1.0 - DECAY) * total[start : start + term.shape[0]]
        exact[start : start + term.shape[0], :] = value
        summed = jnp.sum(value * value, axis=0, keepdims=True)
        if position == 0:
            summed = jnp.where(column < half, summed, 2.0 * summed)
        squares = squares + (summed if position < 2 else 2.0 * summed)
        values.append(value.astype(BF16))
    high = squares.astype(BF16).astype(F32)
    middle = (squares - high).astype(BF16).astype(F32)
    rest = squares - high - middle
    spot = lax.broadcasted_iota(jnp.int32, (16, share), 0)
    digits = jnp.where(spot == 0, high, jnp.where(spot == 1, middle, jnp.where(spot == 2, rest, 0.0)))
    values.append(digits.astype(BF16))
    chunk[...] = jnp.concatenate(values, axis=0)


def root_kernel(replicas, count, exact, *rest):
    own, near, side, far_upper, far_lower, factor_out, root_out, finished, factor, diagonal = rest
    share = root_out.shape[0]
    order = root_out.shape[1]
    half = share // 2
    starts = chunk_rows(share)
    length = far_upper.shape[0]
    mine = lax.axis_index("dp")

    def rows_of(offset, start, count):
        if offset < 3:
            return (own, near, side)[offset][start : start + count, :]
        upper, lower = far_upper, far_lower
        if start + count <= length:
            return upper[start : start + count, :]
        if start >= length:
            return lower[start - length : start - length + count, :]
        return jnp.concatenate([upper[start:length, :], lower[0 : start + count - length, :]], axis=0)

    squares = jnp.zeros((16, share), F32)
    low_eye = eye_of(half, half)
    for offset in range(replicas):
        owner = mine ^ offset
        base = pl.multiple_of(owner * share, share)
        corner = pl.multiple_of(owner * share + half, half)
        top = rows_of(offset, 0, half)
        low = rows_of(offset, starts[1], half // 2)
        low = jnp.concatenate([low[:, 0:half], low[:, half:]], axis=0)
        factor[pl.ds(base, half), pl.ds(base, share)] = top
        factor[pl.ds(corner, half), pl.ds(base, half)] = transposed(top[:, half:])
        factor[pl.ds(corner, half), pl.ds(corner, half)] = low
        diagonal[:, pl.ds(base, half)] = jnp.sum(top[:, 0:half].astype(F32) * low_eye, axis=0, keepdims=True)
        diagonal[:, pl.ds(corner, half)] = jnp.sum(low.astype(F32) * low_eye, axis=0, keepdims=True)
        for step in range(1, replicas):
            row, col = shared_half(owner, step, share)
            block = rows_of(offset, starts[1 + step], half)
            factor[pl.ds(row, half), pl.ds(col, share)] = block
            factor[pl.ds(col, share), pl.ds(row, half)] = transposed(block)
        squares = squares + rows_of(offset, starts[-1], 16).astype(F32)

    scale = jnp.sqrt(jnp.sum(squares, keepdims=True) / order + EPSILON)
    inverse = 1.0 / scale
    ones = (diagonal[...] * inverse).astype(BF16).astype(F32)
    lift = (1.5 - 0.5 * ones).astype(BF16).astype(F32) + 0.5 * (diagonal[...] * inverse)
    eye = eye_of(share, order, mine * share)
    my_rows = pl.ds(pl.multiple_of(mine * share, share), share)
    first = (factor[my_rows, :].astype(F32) * inverse).astype(BF16).astype(F32)
    turn = (1.5 * eye - 0.5 * first).astype(BF16)
    second = (jnp.dot(turn, factor[...], preferred_element_type=F32) * inverse).astype(BF16)
    product = (-0.5 * inverse) * jnp.dot(second, factor[...], preferred_element_type=F32) + second.astype(F32) * lift
    turn_two = (1.5 * eye - 0.5 * product).astype(BF16)
    inverse_rows = (-0.5 * inverse) * jnp.dot(
        turn_two, factor[...], preferred_element_type=F32
    ) + turn_two.astype(F32) * lift
    chosen = jnp.where(count[0, 0] == 1, turn.astype(F32), inverse_rows)
    root_out[...] = (chosen * lax.rsqrt(scale)).astype(BF16)
    finished[...] = jnp.zeros_like(finished)

    own_columns = pl.ds(pl.multiple_of(mine * share, share), share)
    top = exact[0:half, :]
    low = exact[starts[1] : starts[2], :]
    low = jnp.concatenate([low[:, 0:half], low[:, half:]], axis=0)
    factor_out[0:half, own_columns] = top
    factor_out[half:, own_columns] = jnp.concatenate([top[:, half:].T, low], axis=1)
    for step in range(1, replicas):
        other = mine ^ step
        columns = pl.ds(pl.multiple_of(other * share, share), share)
        own = exact[starts[1 + step] : starts[1 + step] + half, :]
        theirs = rows_of(step, starts[1 + step], half).astype(F32)

        @pl.when(mine < other)
        def _():
            factor_out[0:half, columns] = own
            factor_out[half:, columns] = theirs

        @pl.when(mine > other)
        def _():
            factor_out[:, columns] = jnp.concatenate([theirs.T, own.T], axis=1)


def step_kernel(grads, old_root, step_out):
    step_out[...] = lax.dot_general(
        grads[...], old_root[...], (((1,), (1,)), ((), ())), preferred_element_type=F32
    ).astype(BF16)


def square_plan(acts, out_grad, old_factor, old_root, iter_count):
    replicas = lax.axis_size("dp")
    inputs = acts[0]
    tokens, order = inputs.shape
    share = order // replicas
    grows = out_grad.shape[2]
    params = pltpu.CompilerParams(vmem_limit_bytes=VMEM_LIMIT)
    whole_rows = chunk_rows(share)[-1]
    length = whole_rows // 2

    def shape(rows, kind=BF16, columns=share):
        return jax.ShapeDtypeStruct((rows, columns), kind)

    def call(kernel, outs, name, *operands, first=None, after=(), scratch=()):
        in_specs = whole(len(operands)) + [pl.BlockSpec(memory_space=pl.ANY)] * len(after)
        if first is not None:
            in_specs[0] = pl.BlockSpec(memory_space=first)

        def body(*refs):
            kernel(*refs[: len(operands)], *refs[len(operands) + len(after) :])

        return pl.pallas_call(
            body,
            out_shape=outs,
            in_specs=in_specs,
            out_specs=whole(len(outs)),
            scratch_shapes=scratch,
            compiler_params=params,
            name=name,
        )(*operands, *after)

    received = passed_along(out_grad, "pipe", -1)[0]
    relay_x, relay_y, direct_x, direct_y, keep = call(
        functools.partial(batch_kernel, replicas, tokens * replicas),
        [shape(length)] * 4 + [shape(4 * length, F32)],
        "batch",
        inputs,
        scratch=[pltpu.VMEM((order, order), F32)],
    )
    relay_x, relay_y = swapped(relay_x, 1), swapped(relay_y, 2)
    direct_x, direct_y = swapped(direct_x, 1), swapped(direct_y, 2)
    relay_x, relay_y = call(relay_kernel, [shape(length)] * 2, "relay", keep, relay_x, relay_y)
    (partial,) = call(
        functools.partial(grad_kernel, tokens * replicas),
        [shape(grows, BF16, order)],
        "grad",
        inputs,
        received,
        after=[relay_x, relay_y],
    )
    relay_x, relay_y = swapped(relay_x, 1), swapped(relay_y, 2)
    partials = lax.all_to_all(partial, "dp", 0, 0, tiled=True)
    chunk, exact = call(
        functools.partial(factor_kernel, replicas),
        [shape(2 * length + 16), shape(whole_rows, F32)],
        "factor",
        keep,
        direct_x,
        direct_y,
        relay_x,
        relay_y,
        old_factor[0, 0],
    )
    near, side = swapped(chunk, 1), swapped(chunk, 2)
    lower, upper = call(halves_kernel, [shape(length + 16), shape(length)], "halves", near, side)
    far_upper, far_lower = swapped(upper, 2), swapped(lower, 1)
    (strips,) = call(
        functools.partial(strip_kernel, replicas), [shape(grows, BF16, order)], "strip", partials, after=[upper]
    )
    grad16 = lax.all_to_all(strips, "dp", 0, 0, tiled=True)
    factor, root, finished = call(
        functools.partial(root_kernel, replicas),
        [shape(share, F32, order), shape(share, BF16, order), shape(8, F32, 128)],
        "root",
        iter_count,
        exact,
        chunk,
        near,
        side,
        far_upper,
        far_lower,
        first=pltpu.SMEM,
        scratch=[pltpu.VMEM((order, order), BF16), pltpu.VMEM((1, order), F32)],
    )
    (step,) = call(step_kernel, [shape(grows, BF16, share)], "step", grad16, old_root[0, 0], after=[finished])
    return (factor[None, None], root[None, None], step[None, None])


def ring_plan(acts, out_grad, old_factor, old_root, iter_count):
    inputs = acts[0]
    replicas = lax.axis_size("dp")
    tokens_all = inputs.shape[0] * replicas
    order = inputs.shape[1]
    share = order // replicas
    offset = lax.axis_index("dp") * share
    received = passed_along(out_grad, "pipe", -1)[0]
    partial_grad = jnp.dot(received.T, inputs, preferred_element_type=F32) / math.sqrt(tokens_all)
    batch = lax.psum_scatter(
        jnp.dot(inputs.T, inputs, preferred_element_type=F32) / tokens_all,
        "dp",
        scatter_dimension=0,
        tiled=True,
    )
    eye_rows = eye_of(share, order, offset)
    factor = DECAY * old_factor[0, 0] + (1.0 - DECAY) * batch + DAMPING * eye_rows
    grad16 = lax.psum(partial_grad, "dp").astype(BF16)
    scale = jnp.sqrt(lax.psum(jnp.sum(factor * factor), "dp") / order + EPSILON)
    step = lax.dot_general(
        grad16, old_root[0, 0], (((1,), (1,)), ((), ())), preferred_element_type=F32
    ).astype(BF16)
    first = lax.all_gather((factor / scale).astype(BF16), "dp", axis=0, tiled=True)
    turn_one = (1.5 * eye_of(order, order) - 0.5 * first.astype(F32)).astype(BF16)
    turn_rows = lax.dynamic_slice_in_dim(turn_one, offset, share, 0)
    second = jnp.dot(turn_rows, first, preferred_element_type=F32).astype(BF16)
    product = jnp.dot(second, turn_one, preferred_element_type=F32)
    turn_two = (1.5 * eye_rows - 0.5 * product).astype(BF16)
    inverse_rows = jnp.dot(turn_two, turn_one, preferred_element_type=F32)
    chosen = jnp.where(iter_count[0, 0] == 1, turn_rows.astype(F32), inverse_rows)
    root = (chosen / jnp.sqrt(scale)).astype(BF16)
    return (factor[None, None], root[None, None], step[None, None])


def solution(mesh):
    return jax.shard_map(
        square_plan if mesh.shape["dp"] == 4 else ring_plan,
        mesh=mesh,
        in_specs=(
            P("pipe", "dp", "tensor"),
            P("pipe", "dp", "tensor"),
            P("pipe", "tensor", "dp", None),
            P("pipe", "tensor", "dp", None),
            P("pipe", "tensor"),
        ),
        out_specs=(
            P("pipe", "tensor", "dp", None),
            P("pipe", "tensor", "dp", None),
            P("pipe", "tensor", None, "dp"),
        ),
        check_vma=False,
    )
```

```python
import functools
import math

import jax
import jax.numpy as jnp
from jax import lax
from jax.experimental import pallas as pl
from jax.experimental.pallas import tpu as pltpu
from jax.sharding import PartitionSpec as P

DECAY = 0.75
DAMPING = 0.1
EPSILON = 1e-06
BF16 = jnp.bfloat16
F32 = jnp.float32
VMEM_LIMIT = 28 * 1024 * 1024


def passed_along(block, axis, distance):
    devices = range(lax.axis_size(axis))
    route = [((i - distance) % len(devices), i) for i in devices]
    return lax.ppermute(block, axis, route)


def swapped(block, offset):
    return lax.ppermute(block, "dp", [(i, i ^ offset) for i in range(lax.axis_size("dp"))])


def eye_of(rows, cols, shift=0):
    row_ids = lax.broadcasted_iota(jnp.int32, (rows, cols), 0) + shift
    col_ids = lax.broadcasted_iota(jnp.int32, (rows, cols), 1)
    return (row_ids == col_ids).astype(F32)


def whole(count):
    return [pl.BlockSpec(memory_space=pltpu.VMEM)] * count


def transposed(block):
    return block.astype(F32).T.astype(block.dtype)


OVER_ROWS = (((0,), (0,)), ((), ()))
FIRST_WAVE = (1, 3)


def first_starts(share):
    half = share // 2
    return 0, half, half + half // 2, 2 * half + half // 2, 3 * half + half // 2


def shared_half(owner, offset, share):
    other = owner ^ offset
    low, high = jnp.minimum(owner, other), jnp.maximum(owner, other)
    row = low * share + jnp.where(owner > other, share // 2, 0)
    return pl.multiple_of(row, share // 2), pl.multiple_of(high * share, share)


def side_by_side(low):
    half = low.shape[0] // 2
    return jnp.concatenate([low[0:half], low[half:]], axis=1)


def stacked(packed):
    half = packed.shape[1] // 2
    return jnp.concatenate([packed[:, 0:half], packed[:, half:]], axis=0)


def store_wave(pieces, length, upper, lower):
    for start, piece in pieces:
        stop = start + piece.shape[0]
        for target, low, high in ((upper, 0, length), (lower, length, stop)):
            first, last = max(start, low), min(stop, high)
            if first < last:
                ref, at = target
                ref[at + first - low : at + last - low, :] = piece[first - start : last - start].astype(ref.dtype)


def store_messages(pieces, send_x, send_y, keep):
    length = send_x.shape[0] // 2
    store_wave(pieces(3), length, (send_x, 0), (send_y, 0))
    store_wave(pieces(1), length, (send_x, length), (keep, 3 * length))
    store_wave(pieces(2), length, (keep, 2 * length), (send_y, length))
    store_wave(pieces(0), length, (keep, 0), (keep, length))


def batch_kernel(replicas, tokens_all, acts, send_x, send_y, keep, rest, batch):
    order = acts.shape[1]
    share = order // replicas
    half = share // 2
    starts = first_starts(share)
    mine = lax.axis_index("dp")
    for i in range(replicas):
        band = slice(i * share, (i + 1) * share)
        batch[band, i * share :] = lax.dot_general(
            acts[:, band], acts[:, i * share :], OVER_ROWS, preferred_element_type=F32
        ) * (1.0 / tokens_all)

    def shared(owner, offset):
        row, col = shared_half(owner, offset, share)
        return batch[pl.ds(row, half), pl.ds(col, share)]

    def pieces(offset):
        owner = mine ^ offset
        base = pl.multiple_of(owner * share, share)
        corner = pl.multiple_of(owner * share + half, half)
        yield starts[0], batch[pl.ds(base, half), pl.ds(base, share)]
        yield starts[1], side_by_side(batch[pl.ds(corner, half), pl.ds(corner, half)])
        for start, step in zip(starts[2:], FIRST_WAVE):
            yield start, shared(owner, step)

    store_messages(pieces, send_x, send_y, keep)
    for offset in range(replicas):
        rest[offset * half : (offset + 1) * half, :] = shared(mine ^ offset, 2)


def grad_kernel(replicas, tokens_all, acts, grads, rest, send_x, send_y, keep, total):
    share = acts.shape[1] // replicas
    half = share // 2
    strip = grads.shape[1] // replicas
    mine = lax.axis_index("dp")
    total[...] = lax.dot_general(grads[...], acts[...], OVER_ROWS, preferred_element_type=F32) * (
        1.0 / math.sqrt(tokens_all)
    )

    def pieces(offset):
        yield 0, rest[offset * half : (offset + 1) * half, :]
        rows = pl.ds(pl.multiple_of((mine ^ offset) * strip, strip), strip)
        for part in range(replicas):
            yield half + part * strip, total[rows, part * share : (part + 1) * share]

    store_messages(pieces, send_x, send_y, keep)


def relay_kernel(keep, got_x, got_y, send_x, send_y):
    length = send_x.shape[0]
    send_y[...] = (keep[2 * length : 3 * length, :] + got_x[0:length, :].astype(F32)).astype(BF16)
    send_x[...] = (keep[3 * length :, :] + got_y[0:length, :].astype(F32)).astype(BF16)


def wave_total(keep, got_x, got_y, relay_x, relay_y):
    length = relay_x.shape[0]
    upper = keep[0:length, :] + got_x[length:, :].astype(F32) + relay_y[...].astype(F32)
    lower = keep[length : 2 * length, :] + got_y[length:, :].astype(F32) + relay_x[...].astype(F32)
    return jnp.concatenate([upper, lower], axis=0)


def old_half(old, mine, offset):
    share = old.shape[0]
    half = share // 2
    other = mine ^ offset
    block = old[:, pl.ds(pl.multiple_of(other * share, share), share)]
    return jnp.where(mine < other, block[0:half], block[:, half:].T)


def column_sums(value):
    return jnp.sum(value * value, axis=0, keepdims=True)


def first_factor_kernel(keep, got_x, got_y, relay_x, relay_y, old, chunk, exact, squares):
    share = old.shape[0]
    half = share // 2
    starts = first_starts(share)
    mine = lax.axis_index("dp")
    total = wave_total(keep, got_x, got_y, relay_x, relay_y)
    diagonal = old[:, pl.ds(pl.multiple_of(mine * share, share), share)]
    terms = [
        DECAY * diagonal[0:half] + DAMPING * eye_of(half, share),
        side_by_side(DECAY * diagonal[half:, half:] + DAMPING * eye_of(half, half)),
    ] + [DECAY * old_half(old, mine, offset) for offset in FIRST_WAVE]
    column = lax.broadcasted_iota(jnp.int32, (1, share), 1)
    weights = [jnp.where(column < half, 1.0, 2.0), 1.0, 2.0, 2.0]
    sums = jnp.zeros((1, share), F32)
    for start, term, weight in zip(starts, terms, weights):
        rows = slice(start, start + term.shape[0])
        value = term + (1.0 - DECAY) * total[rows]
        exact[rows, :] = value
        chunk[rows, :] = value.astype(BF16)
        sums = sums + weight * column_sums(value)
    squares[...] = sums


def second_factor_kernel(keep, got_x, got_y, relay_x, relay_y, old, squares, chunk, exact):
    share = old.shape[0]
    half = share // 2
    total = wave_total(keep, got_x, got_y, relay_x, relay_y)
    length = total.shape[0]
    value = DECAY * old_half(old, lax.axis_index("dp"), 2) + (1.0 - DECAY) * total[0:half]
    exact[...] = value
    chunk[0:half, :] = value.astype(BF16)
    chunk[half:length, :] = total[half:].astype(BF16)
    sums = squares[...] + 2.0 * column_sums(value)
    high = sums.astype(BF16).astype(F32)
    middle = (sums - high).astype(BF16).astype(F32)
    rest = sums - high - middle
    spot = lax.broadcasted_iota(jnp.int32, (chunk.shape[0] - length, share), 0)
    digits = jnp.where(spot == 0, high, jnp.where(spot == 1, middle, jnp.where(spot == 2, rest, 0.0)))
    chunk[length:, :] = digits.astype(BF16)


def halves_kernel(got_x, got_y, send_x, send_y):
    length = send_y.shape[0]
    send_y[...] = got_x[0:length, :]
    send_x[...] = got_y[length:, :]


def place(factor, diagonal, owner, first, second, share):
    half = share // 2
    starts = first_starts(share)
    base = pl.multiple_of(owner * share, share)
    corner = pl.multiple_of(owner * share + half, half)
    top = first(starts[0], half)
    low = stacked(first(starts[1], half // 2))
    factor[pl.ds(base, half), pl.ds(base, share)] = top
    factor[pl.ds(corner, half), pl.ds(base, half)] = transposed(top[:, half:])
    factor[pl.ds(corner, half), pl.ds(corner, half)] = low
    eye = eye_of(half, half)
    diagonal[:, pl.ds(base, half)] = jnp.sum(top[:, 0:half].astype(F32) * eye, axis=0, keepdims=True)
    diagonal[:, pl.ds(corner, half)] = jnp.sum(low.astype(F32) * eye, axis=0, keepdims=True)
    blocks = [(step, first(start, half)) for start, step in zip(starts[2:], FIRST_WAVE)]
    for step, block in blocks + [(2, second(0, half))]:
        row, col = shared_half(owner, step, share)
        factor[pl.ds(row, half), pl.ds(col, share)] = block
        factor[pl.ds(col, share), pl.ds(row, half)] = transposed(block)


def rows_of(upper, lower=None):
    def read(start, count):
        if lower is None:
            return upper[start : start + count, :]
        length = upper.shape[0]
        if start + count <= length:
            return upper[start : start + count, :]
        if start >= length:
            return lower[start - length : start - length + count, :]
        return jnp.concatenate([upper[start:, :], lower[0 : start + count - length, :]], axis=0)

    return read


def near_kernel(own, own_rest, x, x_rest, y, y_rest, factor, diagonal):
    share = own.shape[1]
    mine = lax.axis_index("dp")
    for offset, (first, second) in enumerate([(own, own_rest), (x, x_rest), (y, y_rest)]):
        place(factor, diagonal, mine ^ offset, rows_of(first), rows_of(second), share)


def new_rows_kernel(exact, exact_rest, x, y_rest, far_upper, far_lower, factor_out):
    share = factor_out.shape[0]
    half = share // 2
    starts = first_starts(share)
    mine = lax.axis_index("dp")
    own_columns = pl.ds(pl.multiple_of(mine * share, share), share)
    top = exact[0:half, :]
    factor_out[0:half, own_columns] = top
    factor_out[half:, own_columns] = jnp.concatenate(
        [top[:, half:].T, stacked(exact[starts[1] : starts[2], :])], axis=1
    )
    pairs = [
        (1, exact[starts[2] : starts[3], :], x[starts[2] : starts[3], :]),
        (2, exact_rest[...], y_rest[0:half, :]),
        (3, exact[starts[3] : starts[4], :], rows_of(far_upper, far_lower)(starts[3], half)),
    ]
    for step, own, theirs in pairs:
        other = mine ^ step
        columns = pl.ds(pl.multiple_of(other * share, share), share)
        theirs = theirs.astype(F32)

        @pl.when(mine < other)
        def _():
            factor_out[0:half, columns] = own
            factor_out[half:, columns] = theirs

        @pl.when(mine > other)
        def _():
            factor_out[:, columns] = jnp.concatenate([theirs.T, own.T], axis=1)


def root_kernel(
    replicas, count, known, known_diagonal, upper, lower, own_rest, x_rest, y_rest, upper_rest, lower_rest, old_root,
    root_out, step_out, factor, diagonal, grads, result,
):
    share = root_out.shape[0]
    order = root_out.shape[1]
    half = share // 2
    strip = step_out.shape[0] // replicas
    digits = half + replicas * strip
    mine = lax.axis_index("dp")
    diagonal[...] = known_diagonal[...]
    seconds = [rows_of(own_rest), rows_of(x_rest), rows_of(y_rest), rows_of(upper_rest, lower_rest)]
    place(factor, diagonal, mine ^ 3, rows_of(upper, lower), seconds[3], share)
    squares = jnp.zeros((16, share), F32)
    for second in seconds:
        squares = squares + second(digits, 16).astype(F32)
    scale = jnp.sqrt(jnp.sum(squares, keepdims=True) / order + EPSILON)
    inverse = 1.0 / scale
    ones = (diagonal[...] * inverse).astype(BF16).astype(F32)
    lift = (1.5 - 0.5 * ones).astype(BF16).astype(F32) + 0.5 * (diagonal[...] * inverse)
    eye = eye_of(share, order, mine * share)
    my_rows = pl.ds(pl.multiple_of(mine * share, share), share)
    first = (factor[my_rows, :].astype(F32) * inverse).astype(BF16).astype(F32)
    turn = (1.5 * eye - 0.5 * first).astype(BF16)
    second = (jnp.dot(turn, factor[...], preferred_element_type=F32) * inverse).astype(BF16)
    product = (-0.5 * inverse) * jnp.dot(second, factor[...], preferred_element_type=F32) + second.astype(F32) * lift
    turn_two = (1.5 * eye - 0.5 * product).astype(BF16)
    inverse_rows = (-0.5 * inverse) * jnp.dot(
        turn_two, factor[...], preferred_element_type=F32
    ) + turn_two.astype(F32) * lift
    chosen = jnp.where(count[0, 0] == 1, turn.astype(F32), inverse_rows)
    root_out[...] = (chosen * lax.rsqrt(scale)).astype(BF16)

    for offset, second in enumerate(seconds):
        for part in range(replicas):
            grads[offset * strip : (offset + 1) * strip, part * share : (part + 1) * share] = second(
                half + part * strip, strip
            )
    result[...] = lax.dot_general(
        grads[...], old_root[...], (((1,), (1,)), ((), ())), preferred_element_type=F32
    ).astype(BF16)
    for offset in range(replicas):
        owner = mine ^ offset
        step_out[pl.ds(pl.multiple_of(owner * strip, strip), strip), :] = result[
            offset * strip : (offset + 1) * strip, :
        ]


def square_plan(acts, out_grad, old_factor, old_root, iter_count):
    replicas = lax.axis_size("dp")
    inputs = acts[0]
    tokens, order = inputs.shape
    share = order // replicas
    half = share // 2
    grows = out_grad.shape[2]
    old = old_factor[0, 0]
    params = pltpu.CompilerParams(vmem_limit_bytes=VMEM_LIMIT)
    first = first_starts(share)[-1]
    second = half + grows
    digits = 16

    def shape(rows, kind=BF16, columns=share):
        return jax.ShapeDtypeStruct((rows, columns), kind)

    def call(kernel, outs, name, *operands, in_smem=(), aliases=None, after=(), scratch=()):
        in_specs = whole(len(operands)) + [pl.BlockSpec(memory_space=pl.ANY)] * len(after)
        for i in in_smem:
            in_specs[i] = pl.BlockSpec(memory_space=pltpu.SMEM)

        def body(*refs):
            kernel(*refs[: len(operands)], *refs[len(operands) + len(after) :])

        return pl.pallas_call(
            body,
            out_shape=outs,
            in_specs=in_specs,
            out_specs=whole(len(outs)),
            scratch_shapes=scratch,
            input_output_aliases=aliases or {},
            compiler_params=params,
            name=name,
        )(*operands, *after)

    def both(x, y):
        return swapped(x, 1), swapped(y, 2)

    received = passed_along(out_grad, "pipe", -1)[0]
    x1, y1, keep1, rest = call(
        functools.partial(batch_kernel, replicas, tokens * replicas),
        [shape(first)] * 2 + [shape(2 * first, F32), shape(replicas * half, F32)],
        "batch",
        inputs,
        scratch=[pltpu.VMEM((order, order), F32)],
    )
    x1, y1 = both(x1, y1)
    x2, y2, keep2 = call(
        functools.partial(grad_kernel, replicas, tokens * replicas),
        [shape(second)] * 2 + [shape(2 * second, F32)],
        "grad",
        inputs,
        received,
        rest,
        scratch=[pltpu.VMEM((grows, order), F32)],
    )
    x2, y2 = both(x2, y2)
    relay_x1, relay_y1 = both(*call(relay_kernel, [shape(first // 2)] * 2, "relay", keep1, x1, y1))
    relay_x2, relay_y2 = both(*call(relay_kernel, [shape(second // 2)] * 2, "relay_rest", keep2, x2, y2))
    own1, exact1, squares = call(
        first_factor_kernel,
        [shape(first), shape(first, F32), shape(1, F32)],
        "factor",
        keep1,
        x1,
        y1,
        relay_x1,
        relay_y1,
        old,
    )
    near1, side1 = both(own1, own1)
    own2, exact2 = call(
        second_factor_kernel,
        [shape(second + digits), shape(half, F32)],
        "factor_rest",
        keep2,
        x2,
        y2,
        relay_x2,
        relay_y2,
        old,
        squares,
    )
    near2, side2 = both(own2, own2)
    on_x1, on_y1 = call(halves_kernel, [shape(first // 2)] * 2, "halves", near1, side1)
    lower1, upper1 = both(on_x1, on_y1)
    on_x2, on_y2 = call(
        halves_kernel,
        [shape(second // 2 + digits), shape(second // 2)],
        "halves_rest",
        near2,
        side2,
        after=[on_x1],
    )
    lower2, upper2 = both(on_x2, on_y2)
    known, diagonal = call(
        near_kernel,
        [shape(order, BF16, order), shape(1, F32, order)],
        "near",
        own1,
        own2,
        near1,
        near2,
        side1,
        side2,
        after=[on_x2],
    )
    (factor,) = call(
        new_rows_kernel,
        [shape(share, F32, order)],
        "new_rows",
        exact1,
        exact2,
        near1,
        side2,
        upper1,
        lower1,
        after=[diagonal],
    )
    root, step, _ = call(
        functools.partial(root_kernel, replicas),
        [shape(share, BF16, order), shape(grows), shape(order, BF16, order)],
        "root",
        iter_count,
        known,
        diagonal,
        upper1,
        lower1,
        own2,
        near2,
        side2,
        upper2,
        lower2,
        old_root[0, 0],
        in_smem=[0],
        aliases={1: 2},
        scratch=[
            pltpu.VMEM((1, order), F32),
            pltpu.VMEM((grows, order), BF16),
            pltpu.VMEM((grows, share), BF16),
        ],
    )
    return (factor[None, None], root[None, None], step[None, None])


def ring_plan(acts, out_grad, old_factor, old_root, iter_count):
    inputs = acts[0]
    replicas = lax.axis_size("dp")
    tokens_all = inputs.shape[0] * replicas
    order = inputs.shape[1]
    share = order // replicas
    offset = lax.axis_index("dp") * share
    received = passed_along(out_grad, "pipe", -1)[0]
    partial_grad = jnp.dot(received.T, inputs, preferred_element_type=F32) / math.sqrt(tokens_all)
    batch = lax.psum_scatter(
        jnp.dot(inputs.T, inputs, preferred_element_type=F32) / tokens_all,
        "dp",
        scatter_dimension=0,
        tiled=True,
    )
    eye_rows = eye_of(share, order, offset)
    factor = DECAY * old_factor[0, 0] + (1.0 - DECAY) * batch + DAMPING * eye_rows
    grad16 = lax.psum(partial_grad, "dp").astype(BF16)
    scale = jnp.sqrt(lax.psum(jnp.sum(factor * factor), "dp") / order + EPSILON)
    step = lax.dot_general(
        grad16, old_root[0, 0], (((1,), (1,)), ((), ())), preferred_element_type=F32
    ).astype(BF16)
    first = lax.all_gather((factor / scale).astype(BF16), "dp", axis=0, tiled=True)
    turn_one = (1.5 * eye_of(order, order) - 0.5 * first.astype(F32)).astype(BF16)
    turn_rows = lax.dynamic_slice_in_dim(turn_one, offset, share, 0)
    second = jnp.dot(turn_rows, first, preferred_element_type=F32).astype(BF16)
    product = jnp.dot(second, turn_one, preferred_element_type=F32)
    turn_two = (1.5 * eye_rows - 0.5 * product).astype(BF16)
    inverse_rows = jnp.dot(turn_two, turn_one, preferred_element_type=F32)
    chosen = jnp.where(iter_count[0, 0] == 1, turn_rows.astype(F32), inverse_rows)
    root = (chosen / jnp.sqrt(scale)).astype(BF16)
    return (factor[None, None], root[None, None], step[None, None])


def solution(mesh):
    return jax.shard_map(
        square_plan if mesh.shape["dp"] == 4 else ring_plan,
        mesh=mesh,
        in_specs=(
            P("pipe", "dp", "tensor"),
            P("pipe", "dp", "tensor"),
            P("pipe", "tensor", "dp", None),
            P("pipe", "tensor", "dp", None),
            P("pipe", "tensor"),
        ),
        out_specs=(
            P("pipe", "tensor", "dp", None),
            P("pipe", "tensor", "dp", None),
            P("pipe", "tensor", None, "dp"),
        ),
        check_vma=False,
    )
```

```python
import functools
import math

import jax
import jax.numpy as jnp
from jax import lax
from jax.experimental import pallas as pl
from jax.experimental.pallas import tpu as pltpu
from jax.sharding import PartitionSpec as P

DECAY = 0.75
DAMPING = 0.1
EPSILON = 1e-06
BF16 = jnp.bfloat16
F32 = jnp.float32
VMEM_LIMIT = 28 * 1024 * 1024


def passed_along(block, axis, distance):
    devices = range(lax.axis_size(axis))
    route = [((i - distance) % len(devices), i) for i in devices]
    return lax.ppermute(block, axis, route)


def along(axis_turn):
    return jnp.where(lax.axis_index("pipe") == axis_turn, 1, 2)


def swapped(block, axis_turn):
    replicas = lax.axis_size("dp")
    route = []
    for section in range(lax.axis_size("pipe")):
        offset = 1 if section == axis_turn else 2
        route += [(section * replicas + i, section * replicas + (i ^ offset)) for i in range(replicas)]
    return lax.ppermute(block, ("pipe", "dp"), route)


def eye_of(rows, cols, shift=0):
    row_ids = lax.broadcasted_iota(jnp.int32, (rows, cols), 0) + shift
    col_ids = lax.broadcasted_iota(jnp.int32, (rows, cols), 1)
    return (row_ids == col_ids).astype(F32)


def whole(count):
    return [pl.BlockSpec(memory_space=pltpu.VMEM)] * count


def transposed(block):
    return block.astype(F32).T.astype(block.dtype)


OVER_ROWS = (((0,), (0,)), ((), ()))


def first_starts(share):
    half = share // 2
    return 0, half, half + half // 2, 2 * half + half // 2, 3 * half + half // 2


def shared_half(owner, offset, share):
    other = owner ^ offset
    low, high = jnp.minimum(owner, other), jnp.maximum(owner, other)
    row = low * share + jnp.where(owner > other, share // 2, 0)
    return pl.multiple_of(row, share // 2), pl.multiple_of(high * share, share)


def side_by_side(low):
    half = low.shape[0] // 2
    return jnp.concatenate([low[0:half], low[half:]], axis=1)


def stacked(packed):
    half = packed.shape[1] // 2
    return jnp.concatenate([packed[:, 0:half], packed[:, half:]], axis=0)


def store_messages(pieces, send, keep):
    for ref, offsets in ((send, (along(0), 3)), (keep, (0, along(1)))):
        length = ref.shape[0] // 2
        for at, offset in zip((0, length), offsets):
            for start, piece in pieces(offset):
                ref[at + start : at + start + piece.shape[0], :] = piece.astype(ref.dtype)


def batch_kernel(replicas, tokens_all, acts, send, keep, rest, batch):
    order = acts.shape[1]
    share = order // replicas
    half = share // 2
    starts = first_starts(share)
    mine = lax.axis_index("dp")
    for i in range(replicas):
        band = slice(i * share, (i + 1) * share)
        batch[band, i * share :] = lax.dot_general(
            acts[:, band], acts[:, i * share :], OVER_ROWS, preferred_element_type=F32
        ) * (1.0 / tokens_all)

    def shared(owner, offset):
        row, col = shared_half(owner, offset, share)
        return batch[pl.ds(row, half), pl.ds(col, share)]

    def pieces(offset):
        owner = mine ^ offset
        base = pl.multiple_of(owner * share, share)
        corner = pl.multiple_of(owner * share + half, half)
        yield starts[0], batch[pl.ds(base, half), pl.ds(base, share)]
        yield starts[1], side_by_side(batch[pl.ds(corner, half), pl.ds(corner, half)])
        for start, step in zip(starts[2:], (along(0), 3)):
            yield start, shared(owner, step)

    store_messages(pieces, send, keep)
    for owner in range(replicas):
        rest[owner * half : (owner + 1) * half, :] = shared(owner, along(1))


def grad_kernel(replicas, tokens_all, acts, grads, rest, send, keep, total):
    share = acts.shape[1] // replicas
    half = share // 2
    strip = grads.shape[1] // replicas
    mine = lax.axis_index("dp")
    total[...] = lax.dot_general(grads[...], acts[...], OVER_ROWS, preferred_element_type=F32) * (
        1.0 / math.sqrt(tokens_all)
    )

    def pieces(offset):
        owner = mine ^ offset
        yield 0, rest[pl.ds(pl.multiple_of(owner * half, half), half), :]
        rows = pl.ds(pl.multiple_of(owner * strip, strip), strip)
        for part in range(replicas):
            yield half + part * strip, total[rows, part * share : (part + 1) * share]

    store_messages(pieces, send, keep)


def relay_kernel(keep, got, send):
    length = send.shape[0]
    send[...] = (keep[length:, :] + got[length:, :].astype(F32)).astype(BF16)


def wave_total(keep, got, relayed):
    length = relayed.shape[0]
    return keep[0:length, :] + got[0:length, :].astype(F32) + relayed[...].astype(F32)


def old_half(old, mine, offset):
    share = old.shape[0]
    half = share // 2
    other = mine ^ offset
    block = old[:, pl.ds(pl.multiple_of(other * share, share), share)]
    return jnp.where(mine < other, block[0:half], block[:, half:].T)


def column_sums(value):
    return jnp.sum(value * value, axis=0, keepdims=True)


def first_factor_kernel(keep, got, relayed, old, chunk, exact, squares):
    share = old.shape[0]
    half = share // 2
    starts = first_starts(share)
    mine = lax.axis_index("dp")
    total = wave_total(keep, got, relayed)
    diagonal = old[:, pl.ds(pl.multiple_of(mine * share, share), share)]
    terms = [
        DECAY * diagonal[0:half] + DAMPING * eye_of(half, share),
        side_by_side(DECAY * diagonal[half:, half:] + DAMPING * eye_of(half, half)),
    ] + [DECAY * old_half(old, mine, offset) for offset in (along(0), 3)]
    column = lax.broadcasted_iota(jnp.int32, (1, share), 1)
    weights = [jnp.where(column < half, 1.0, 2.0), 1.0, 2.0, 2.0]
    sums = jnp.zeros((1, share), F32)
    for start, term, weight in zip(starts, terms, weights):
        rows = slice(start, start + term.shape[0])
        value = term + (1.0 - DECAY) * total[rows]
        exact[rows, :] = value
        chunk[rows, :] = value.astype(BF16)
        sums = sums + weight * column_sums(value)
    squares[...] = sums


def second_factor_kernel(keep, got, relayed, old, squares, chunk, exact):
    share = old.shape[0]
    half = share // 2
    total = wave_total(keep, got, relayed)
    length = total.shape[0]
    value = DECAY * old_half(old, lax.axis_index("dp"), along(1)) + (1.0 - DECAY) * total[0:half]
    exact[...] = value
    chunk[0:half, :] = value.astype(BF16)
    chunk[half:length, :] = total[half:].astype(BF16)
    sums = squares[...] + 2.0 * column_sums(value)
    high = sums.astype(BF16).astype(F32)
    middle = (sums - high).astype(BF16).astype(F32)
    rest = sums - high - middle
    spot = lax.broadcasted_iota(jnp.int32, (chunk.shape[0] - length, share), 0)
    digits = jnp.where(spot == 0, high, jnp.where(spot == 1, middle, jnp.where(spot == 2, rest, 0.0)))
    chunk[length:, :] = digits.astype(BF16)


def pair_kernel(own, got, send):
    length = own.shape[0]
    send[0:length, :] = own[...]
    send[length:, :] = got[...]


def place_half(factor, owner, offset, block):
    row, col = shared_half(owner, offset, block.shape[1])
    factor[pl.ds(row, block.shape[0]), pl.ds(col, block.shape[1])] = block
    factor[pl.ds(col, block.shape[1]), pl.ds(row, block.shape[0])] = transposed(block)


def place_first(factor, diagonal, owner, wave, at=0):
    share = wave.shape[1]
    half = share // 2
    starts = [at + start for start in first_starts(share)]
    base = pl.multiple_of(owner * share, share)
    corner = pl.multiple_of(owner * share + half, half)
    top = wave[at : at + half, :]
    low = stacked(wave[starts[1] : starts[2], :])
    factor[pl.ds(base, half), pl.ds(base, share)] = top
    factor[pl.ds(corner, half), pl.ds(base, half)] = transposed(top[:, half:])
    factor[pl.ds(corner, half), pl.ds(corner, half)] = low
    eye = eye_of(half, half)
    diagonal[:, pl.ds(base, half)] = jnp.sum(top[:, 0:half].astype(F32) * eye, axis=0, keepdims=True)
    diagonal[:, pl.ds(corner, half)] = jnp.sum(low.astype(F32) * eye, axis=0, keepdims=True)
    for start, offset in zip(starts[2:], (along(0), 3)):
        place_half(factor, owner, offset, wave[start : start + half, :])


def matrix_kernel(pair, pair_rest, far, factor, diagonal):
    share = pair.shape[1]
    half = share // 2
    mine = lax.axis_index("dp")
    for offset, wave, at in (
        (0, pair, 0),
        (along(1), pair, pair.shape[0] // 2),
        (along(0), far, 0),
        (3, far, far.shape[0] // 2),
    ):
        place_first(factor, diagonal, mine ^ offset, wave, at)
    for i, offset in enumerate((0, along(1))):
        start = i * (pair_rest.shape[0] // 2)
        place_half(factor, mine ^ offset, along(1), pair_rest[start : start + half, :])
    bands = [pl.ds(pl.multiple_of((mine ^ offset) * share, share), share) for offset in (along(0), 3)]
    for rows, columns in (bands, bands[::-1]):
        factor[rows, columns] = jnp.zeros((share, share), BF16)


def new_rows_kernel(exact, exact_rest, far, pair_rest, factor_out):
    share = factor_out.shape[0]
    half = share // 2
    starts = first_starts(share)
    across = far.shape[0] // 2 + starts[3]
    second = pair_rest.shape[0] // 2
    mine = lax.axis_index("dp")
    own_columns = pl.ds(pl.multiple_of(mine * share, share), share)
    top = exact[0:half, :]
    factor_out[0:half, own_columns] = top
    factor_out[half:, own_columns] = jnp.concatenate(
        [top[:, half:].T, stacked(exact[starts[1] : starts[2], :])], axis=1
    )
    shared = [
        (along(0), exact[starts[2] : starts[3], :], far[starts[2] : starts[3], :]),
        (along(1), exact_rest[...], pair_rest[second : second + half, :]),
        (3, exact[starts[3] : starts[4], :], far[across : across + half, :]),
    ]
    for offset, own, theirs in shared:
        other = mine ^ offset
        columns = pl.ds(pl.multiple_of(other * share, share), share)
        theirs = theirs.astype(F32)

        @pl.when(mine < other)
        def _():
            factor_out[0:half, columns] = own
            factor_out[half:, columns] = theirs

        @pl.when(mine > other)
        def _():
            factor_out[:, columns] = jnp.concatenate([theirs.T, own.T], axis=1)


def root_kernel(replicas, count, known, diagonal, pair, far, old_root, root_out, step_out, left, right, grads, result):
    share = root_out.shape[0]
    order = root_out.shape[1]
    half = share // 2
    strip = step_out.shape[0] // replicas
    digits = half + replicas * strip
    length = pair.shape[0] // 2
    mine = lax.axis_index("dp")
    waves = [(pair, 0, 0), (pair, length, along(1)), (far, 0, along(0)), (far, length, 3)]
    squares = jnp.zeros((length - digits, share), F32)
    for wave, at, _ in waves:
        squares = squares + wave[at + digits : at + length, :].astype(F32)
    scale = jnp.sqrt(jnp.sum(squares, keepdims=True) / order + EPSILON)
    inverse = 1.0 / scale
    neighbour, across = mine ^ along(0), mine ^ 3
    ours, theirs = far[0:half, :], far[length : length + half, :]
    ordered = jnp.where(neighbour < across, 1.0, 0.0).astype(F32)
    upper = ordered * ours.astype(F32) + (1.0 - ordered) * theirs.astype(F32)
    lower = ordered * theirs.astype(F32) + (1.0 - ordered) * ours.astype(F32)
    block = jnp.concatenate([upper, lower], axis=0).astype(BF16)
    low = pl.ds(pl.multiple_of(jnp.minimum(neighbour, across) * share, share), share)
    high = pl.ds(pl.multiple_of(jnp.maximum(neighbour, across) * share, share), share)

    def times_factor(value):
        left[...] = value
        right[...] = jnp.dot(value, known[...], preferred_element_type=F32)
        right[:, high] += jnp.dot(left[:, low], block, preferred_element_type=F32)
        right[:, low] += lax.dot_general(
            left[:, high], block, (((1,), (1,)), ((), ())), preferred_element_type=F32
        )
        return right[...]

    ones = (diagonal[...] * inverse).astype(BF16).astype(F32)
    lift = (1.5 - 0.5 * ones).astype(BF16).astype(F32) + 0.5 * (diagonal[...] * inverse)
    eye = eye_of(share, order, mine * share)
    my_rows = pl.ds(pl.multiple_of(mine * share, share), share)
    first = (known[my_rows, :].astype(F32) * inverse).astype(BF16).astype(F32)
    turn = (1.5 * eye - 0.5 * first).astype(BF16)
    second = (times_factor(turn) * inverse).astype(BF16)
    product = (-0.5 * inverse) * times_factor(second) + second.astype(F32) * lift
    turn_two = (1.5 * eye - 0.5 * product).astype(BF16)
    inverse_rows = (-0.5 * inverse) * times_factor(turn_two) + turn_two.astype(F32) * lift
    chosen = jnp.where(count[0, 0] == 1, turn.astype(F32), inverse_rows)
    root_out[...] = (chosen * lax.rsqrt(scale)).astype(BF16)

    for i, (wave, at, _) in enumerate(waves):
        for part in range(replicas):
            start = at + half + part * strip
            grads[i * strip : (i + 1) * strip, part * share : (part + 1) * share] = wave[start : start + strip, :]
    result[...] = lax.dot_general(
        grads[...], old_root[...], (((1,), (1,)), ((), ())), preferred_element_type=F32
    ).astype(BF16)
    for i, (_, _, offset) in enumerate(waves):
        rows = pl.ds(pl.multiple_of((mine ^ offset) * strip, strip), strip)
        step_out[rows, :] = result[i * strip : (i + 1) * strip, :]


def square_plan(acts, out_grad, old_factor, old_root, iter_count):
    replicas = lax.axis_size("dp")
    inputs = acts[0]
    tokens, order = inputs.shape
    share = order // replicas
    half = share // 2
    grows = out_grad.shape[2]
    old = old_factor[0, 0]
    params = pltpu.CompilerParams(vmem_limit_bytes=VMEM_LIMIT)
    first = first_starts(share)[-1]
    second = half + grows
    digits = 16

    def shape(rows, kind=BF16, columns=share):
        return jax.ShapeDtypeStruct((rows, columns), kind)

    def call(kernel, outs, name, *operands, in_smem=(), after=(), scratch=()):
        in_specs = whole(len(operands)) + [pl.BlockSpec(memory_space=pl.ANY)] * len(after)
        for i in in_smem:
            in_specs[i] = pl.BlockSpec(memory_space=pltpu.SMEM)

        def body(*refs):
            kernel(*refs[: len(operands)], *refs[len(operands) + len(after) :])

        return pl.pallas_call(
            body,
            out_shape=outs,
            in_specs=in_specs,
            out_specs=whole(len(outs)),
            scratch_shapes=scratch,
            compiler_params=params,
            name=name,
        )(*operands, *after)

    received = passed_along(out_grad, "pipe", -1)[0]
    send1, keep1, rest = call(
        functools.partial(batch_kernel, replicas, tokens * replicas),
        [shape(2 * first), shape(2 * first, F32), shape(replicas * half, F32)],
        "batch",
        inputs,
        scratch=[pltpu.VMEM((order, order), F32)],
    )
    got1 = swapped(send1, 0)
    send2, keep2 = call(
        functools.partial(grad_kernel, replicas, tokens * replicas),
        [shape(2 * second), shape(2 * second, F32)],
        "grad",
        inputs,
        received,
        rest,
        scratch=[pltpu.VMEM((grows, order), F32)],
    )
    got2 = swapped(send2, 0)
    (send1,) = call(relay_kernel, [shape(first)], "relay", keep1, got1)
    relayed1 = swapped(send1, 1)
    (send2,) = call(relay_kernel, [shape(second)], "relay_rest", keep2, got2)
    relayed2 = swapped(send2, 1)
    own1, exact1, squares = call(
        first_factor_kernel,
        [shape(first), shape(first, F32), shape(1, F32)],
        "factor",
        keep1,
        got1,
        relayed1,
        old,
    )
    near1 = swapped(own1, 1)
    own2, exact2 = call(
        second_factor_kernel,
        [shape(second + digits), shape(half, F32)],
        "factor_rest",
        keep2,
        got2,
        relayed2,
        old,
        squares,
    )
    near2 = swapped(own2, 1)
    (pair1,) = call(pair_kernel, [shape(2 * first)], "pair", own1, near1)
    far1 = swapped(pair1, 0)
    (pair2,) = call(pair_kernel, [shape(2 * (second + digits))], "pair_rest", own2, near2, after=[pair1])
    far2 = swapped(pair2, 0)
    known, diagonal = call(
        matrix_kernel, [shape(order, BF16, order), shape(1, F32, order)], "matrix", pair1, pair2, far1
    )
    (factor,) = call(
        new_rows_kernel, [shape(share, F32, order)], "new_rows", exact1, exact2, far1, pair2, after=[diagonal]
    )
    root, step = call(
        functools.partial(root_kernel, replicas),
        [shape(share, BF16, order), shape(grows)],
        "root",
        iter_count,
        known,
        diagonal,
        pair2,
        far2,
        old_root[0, 0],
        in_smem=[0],
        scratch=[
            pltpu.VMEM((share, order), BF16),
            pltpu.VMEM((share, order), F32),
            pltpu.VMEM((grows, order), BF16),
            pltpu.VMEM((grows, share), BF16),
        ],
    )
    return (factor[None, None], root[None, None], step[None, None])


def ring_plan(acts, out_grad, old_factor, old_root, iter_count):
    inputs = acts[0]
    replicas = lax.axis_size("dp")
    tokens_all = inputs.shape[0] * replicas
    order = inputs.shape[1]
    share = order // replicas
    offset = lax.axis_index("dp") * share
    received = passed_along(out_grad, "pipe", -1)[0]
    partial_grad = jnp.dot(received.T, inputs, preferred_element_type=F32) / math.sqrt(tokens_all)
    batch = lax.psum_scatter(
        jnp.dot(inputs.T, inputs, preferred_element_type=F32) / tokens_all,
        "dp",
        scatter_dimension=0,
        tiled=True,
    )
    eye_rows = eye_of(share, order, offset)
    factor = DECAY * old_factor[0, 0] + (1.0 - DECAY) * batch + DAMPING * eye_rows
    grad16 = lax.psum(partial_grad, "dp").astype(BF16)
    scale = jnp.sqrt(lax.psum(jnp.sum(factor * factor), "dp") / order + EPSILON)
    step = lax.dot_general(
        grad16, old_root[0, 0], (((1,), (1,)), ((), ())), preferred_element_type=F32
    ).astype(BF16)
    first = lax.all_gather((factor / scale).astype(BF16), "dp", axis=0, tiled=True)
    turn_one = (1.5 * eye_of(order, order) - 0.5 * first.astype(F32)).astype(BF16)
    turn_rows = lax.dynamic_slice_in_dim(turn_one, offset, share, 0)
    second = jnp.dot(turn_rows, first, preferred_element_type=F32).astype(BF16)
    product = jnp.dot(second, turn_one, preferred_element_type=F32)
    turn_two = (1.5 * eye_rows - 0.5 * product).astype(BF16)
    inverse_rows = jnp.dot(turn_two, turn_one, preferred_element_type=F32)
    chosen = jnp.where(iter_count[0, 0] == 1, turn_rows.astype(F32), inverse_rows)
    root = (chosen / jnp.sqrt(scale)).astype(BF16)
    return (factor[None, None], root[None, None], step[None, None])


def solution(mesh):
    return jax.shard_map(
        square_plan if mesh.shape["dp"] == 4 and mesh.shape["pipe"] == 2 else ring_plan,
        mesh=mesh,
        in_specs=(
            P("pipe", "dp", "tensor"),
            P("pipe", "dp", "tensor"),
            P("pipe", "tensor", "dp", None),
            P("pipe", "tensor", "dp", None),
            P("pipe", "tensor"),
        ),
        out_specs=(
            P("pipe", "tensor", "dp", None),
            P("pipe", "tensor", "dp", None),
            P("pipe", "tensor", None, "dp"),
        ),
        check_vma=False,
    )
```

```python
import functools
import math

import jax
import jax.numpy as jnp
from jax import lax
from jax.experimental import pallas as pl
from jax.experimental.pallas import tpu as pltpu
from jax.sharding import PartitionSpec as P

DECAY = 0.75
DAMPING = 0.1
EPSILON = 1e-06
BF16 = jnp.bfloat16
F32 = jnp.float32
VMEM_LIMIT = 28 * 1024 * 1024


def passed_along(block, axis, distance):
    devices = range(lax.axis_size(axis))
    route = [((i - distance) % len(devices), i) for i in devices]
    return lax.ppermute(block, axis, route)


def swapped(block, offset):
    return lax.ppermute(block, "dp", [(i, i ^ offset) for i in range(lax.axis_size("dp"))])


def along(turn):
    return jnp.where(lax.axis_index("pipe") == turn, 1, 2)


def swapped_along(block, turn):
    replicas = lax.axis_size("dp")
    route = []
    for section in range(lax.axis_size("pipe")):
        offset = 1 if section == turn else 2
        route += [(section * replicas + i, section * replicas + (i ^ offset)) for i in range(replicas)]
    return lax.ppermute(block, ("pipe", "dp"), route)


def eye_of(rows, cols, shift=0):
    row_ids = lax.broadcasted_iota(jnp.int32, (rows, cols), 0) + shift
    col_ids = lax.broadcasted_iota(jnp.int32, (rows, cols), 1)
    return (row_ids == col_ids).astype(F32)


def whole(count):
    return [pl.BlockSpec(memory_space=pltpu.VMEM)] * count


def transposed(block):
    return block.astype(F32).T.astype(block.dtype)


OVER_ROWS = (((0,), (0,)), ((), ()))


def chunk_starts(share):
    half = share // 2
    return (0, half) + tuple(half + half // 2 + half * i for i in range(4))


def shared_half(owner, offset, share):
    other = owner ^ offset
    low, high = jnp.minimum(owner, other), jnp.maximum(owner, other)
    row = low * share + jnp.where(owner > other, share // 2, 0)
    return pl.multiple_of(row, share // 2), pl.multiple_of(high * share, share)


def band(index, size):
    return pl.ds(pl.multiple_of(index * size, size), size)


def side_by_side(low):
    half = low.shape[0] // 2
    return jnp.concatenate([low[0:half], low[half:]], axis=1)


def stacked(packed):
    half = packed.shape[1] // 2
    return jnp.concatenate([packed[:, 0:half], packed[:, half:]], axis=0)


def store_chunk(pieces, length, upper, lower):
    for start, piece in pieces:
        stop = start + piece.shape[0]
        for target, low, high in ((upper, 0, length), (lower, length, stop)):
            first, last = max(start, low), min(stop, high)
            if first < last:
                ref, at = target
                ref[at + first - low : at + last - low, :] = piece[first - start : last - start].astype(ref.dtype)


def batch_kernel(replicas, tokens_all, acts, send_x, send_y, keep, batch):
    order = acts.shape[1]
    share = order // replicas
    half = share // 2
    starts = chunk_starts(share)
    length = send_x.shape[0] // 2
    mine = lax.axis_index("dp")
    for i in range(replicas):
        rows = slice(i * share, (i + 1) * share)
        batch[rows, i * share :] = lax.dot_general(
            acts[:, rows], acts[:, i * share :], OVER_ROWS, preferred_element_type=F32
        ) * (1.0 / tokens_all)

    def pieces(offset):
        owner = mine ^ offset
        corner = pl.ds(pl.multiple_of(owner * share + half, half), half)
        yield starts[0], batch[pl.ds(pl.multiple_of(owner * share, share), half), band(owner, share)]
        yield starts[1], side_by_side(batch[corner, corner])
        for step in range(1, replicas):
            row, col = shared_half(owner, step, share)
            yield starts[1 + step], batch[pl.ds(row, half), pl.ds(col, share)]

    store_chunk(pieces(3), length, (send_x, 0), (send_y, 0))
    store_chunk(pieces(1), length, (send_x, length), (keep, 3 * length))
    store_chunk(pieces(2), length, (keep, 2 * length), (send_y, length))
    store_chunk(pieces(0), length, (keep, 0), (keep, length))


def relay_kernel(keep, got_x, got_y, send_x, send_y):
    length = send_x.shape[0]
    send_y[...] = (keep[2 * length : 3 * length, :] + got_x[0:length, :].astype(F32)).astype(BF16)
    send_x[...] = (keep[3 * length :, :] + got_y[0:length, :].astype(F32)).astype(BF16)


def grad_kernel(replicas, tokens_all, acts, grads, send, keep, total):
    share = acts.shape[1] // replicas
    strip = grads.shape[1] // replicas
    mine = lax.axis_index("dp")
    total[...] = lax.dot_general(grads[...], acts[...], OVER_ROWS, preferred_element_type=F32) * (
        1.0 / math.sqrt(tokens_all)
    )
    for ref, offsets in ((send, (along(0), 3)), (keep, (0, along(1)))):
        for i, offset in enumerate(offsets):
            for part in range(replicas):
                start = (i * replicas + part) * strip
                piece = total[band(mine ^ offset, strip), part * share : (part + 1) * share]
                ref[start : start + strip, :] = piece.astype(ref.dtype)


def strip_relay_kernel(keep, got, send):
    length = send.shape[0]
    send[...] = (keep[length:, :] + got[length:, :].astype(F32)).astype(BF16)


def strip_kernel(keep, got, relayed, strip):
    length = strip.shape[0]
    strip[...] = (keep[0:length, :] + got[0:length, :].astype(F32) + relayed[...].astype(F32)).astype(BF16)


def pair_kernel(own, got, send):
    length = own.shape[0]
    send[0:length, :] = own[...]
    send[length:, :] = got[...]


def factor_kernel(keep, got_x, got_y, relay_x, relay_y, old, chunk, exact):
    share = old.shape[0]
    half = share // 2
    starts = chunk_starts(share)
    length = relay_x.shape[0]
    mine = lax.axis_index("dp")
    upper = keep[0:length, :] + got_x[length:, :].astype(F32) + relay_y[...].astype(F32)
    lower = keep[length : 2 * length, :] + got_y[length:, :].astype(F32) + relay_x[...].astype(F32)
    total = jnp.concatenate([upper, lower], axis=0)
    diagonal = old[:, band(mine, share)]
    terms = [
        DECAY * diagonal[0:half] + DAMPING * eye_of(half, share),
        side_by_side(DECAY * diagonal[half:, half:] + DAMPING * eye_of(half, half)),
    ]
    for offset in range(1, 4):
        block = old[:, band(mine ^ offset, share)]
        terms.append(DECAY * jnp.where(mine < mine ^ offset, block[0:half], block[:, half:].T))
    column = lax.broadcasted_iota(jnp.int32, (1, share), 1)
    weights = [jnp.where(column < half, 1.0, 2.0), 1.0, 2.0, 2.0, 2.0]
    sums = jnp.zeros((1, share), F32)
    for start, term, weight in zip(starts, terms, weights):
        rows = slice(start, start + term.shape[0])
        value = term + (1.0 - DECAY) * total[rows]
        exact[rows, :] = value
        chunk[rows, :] = value.astype(BF16)
        sums = sums + weight * jnp.sum(value * value, axis=0, keepdims=True)
    high = sums.astype(BF16).astype(F32)
    middle = (sums - high).astype(BF16).astype(F32)
    rest = sums - high - middle
    spot = lax.broadcasted_iota(jnp.int32, (chunk.shape[0] - 2 * length, share), 0)
    digits = jnp.where(spot == 0, high, jnp.where(spot == 1, middle, jnp.where(spot == 2, rest, 0.0)))
    chunk[2 * length :, :] = digits.astype(BF16)


def halves_kernel(got_x, got_y, send_x, send_y):
    length = send_y.shape[0]
    send_y[...] = got_x[0:length, :]
    send_x[...] = got_y[length:, :]


def place(factor, diagonal, owner, read, share):
    half = share // 2
    starts = chunk_starts(share)
    base = pl.ds(pl.multiple_of(owner * share, share), half)
    corner = pl.ds(pl.multiple_of(owner * share + half, half), half)
    top = read(starts[0], half)
    low = stacked(read(starts[1], half // 2))
    factor[base, band(owner, share)] = top
    factor[corner, base] = transposed(top[:, half:])
    factor[corner, corner] = low
    eye = eye_of(half, half)
    diagonal[:, base] = jnp.sum(top[:, 0:half].astype(F32) * eye, axis=0, keepdims=True)
    diagonal[:, corner] = jnp.sum(low.astype(F32) * eye, axis=0, keepdims=True)
    for offset in range(1, 4):
        row, col = shared_half(owner, offset, share)
        block = read(starts[1 + offset], half)
        factor[pl.ds(row, half), pl.ds(col, share)] = block
        factor[pl.ds(col, share), pl.ds(row, half)] = transposed(block)


def rows_of(upper, lower=None):
    def read(start, count):
        if lower is None:
            return upper[start : start + count, :]
        length = upper.shape[0]
        if start + count <= length:
            return upper[start : start + count, :]
        if start >= length:
            return lower[start - length : start - length + count, :]
        return jnp.concatenate([upper[start:, :], lower[0 : start + count - length, :]], axis=0)

    return read


def store_shared(target, columns, own_is_upper, own, theirs):
    half = own.shape[0]

    @pl.when(own_is_upper)
    def _():
        target[0:half, columns] = own
        target[half:, columns] = theirs

    @pl.when(jnp.logical_not(own_is_upper))
    def _():
        target[:, columns] = jnp.concatenate([theirs.T, own.T], axis=1)


def matrix_kernel(exact, chunk, near, side, old_root, factor, diagonal, squares, rows, old_columns):
    share = exact.shape[1]
    half = share // 2
    starts = chunk_starts(share)
    mine = lax.axis_index("dp")
    factor[...] = jnp.zeros_like(factor)
    diagonal[...] = jnp.zeros_like(diagonal)
    sums = jnp.zeros((chunk.shape[0] - starts[-1], share), F32)
    for offset, ref in enumerate((chunk, near, side)):
        place(factor, diagonal, mine ^ offset, rows_of(ref), share)
        sums = sums + ref[starts[-1] :, :].astype(F32)
    squares[...] = sums
    top = exact[0:half, :]
    low = stacked(exact[starts[1] : starts[2], :])
    rows[0:half, band(mine, share)] = top
    rows[half:, band(mine, share)] = jnp.concatenate([top[:, half:].T, low], axis=1)
    for offset, ref in ((1, near), (2, side)):
        part = slice(starts[1 + offset], starts[1 + offset] + half)
        other = mine ^ offset
        store_shared(rows, band(other, share), mine < other, exact[part, :], ref[part, :].astype(F32))
    rows[:, band(mine ^ 3, share)] = jnp.zeros((share, share), F32)
    old_columns[...] = transposed(old_root[...])


def root_kernel(
    count, known, known_diagonal, squares, rows, exact, upper, lower, factor_out, root_out, finished, factor, diagonal,
    shared, sent,
):
    share, order = root_out.shape
    half = share // 2
    starts = chunk_starts(share)
    mine = lax.axis_index("dp")
    read = rows_of(upper, lower)
    last = slice(starts[4], starts[5])
    store_shared(shared, slice(None), mine < mine ^ 3, exact[last, :], read(starts[4], half).astype(F32))
    copies = []
    for offset in range(4):
        columns = band(mine ^ offset, share)
        source = shared if offset == 3 else rows.at[:, columns]
        copies.append(pltpu.make_async_copy(source, factor_out.at[:, columns], sent.at[offset]))
        copies[-1].start()

    factor[...] = known[...]
    diagonal[...] = known_diagonal[...]
    place(factor, diagonal, mine ^ 3, read, share)
    total = squares[...] + lower[lower.shape[0] - squares.shape[0] :, :].astype(F32)
    scale = jnp.sqrt(jnp.sum(total, keepdims=True) / order + EPSILON)
    inverse = 1.0 / scale
    ones = (diagonal[...] * inverse).astype(BF16).astype(F32)
    lift = (1.5 - 0.5 * ones).astype(BF16).astype(F32) + 0.5 * (diagonal[...] * inverse)
    eye = eye_of(share, order, mine * share)
    first = (factor[band(mine, share), :].astype(F32) * inverse).astype(BF16).astype(F32)
    turn = (1.5 * eye - 0.5 * first).astype(BF16)
    second = (jnp.dot(turn, factor[...], preferred_element_type=F32) * inverse).astype(BF16)
    product = (-0.5 * inverse) * jnp.dot(second, factor[...], preferred_element_type=F32) + second.astype(F32) * lift
    turn_two = (1.5 * eye - 0.5 * product).astype(BF16)
    inverse_rows = (-0.5 * inverse) * jnp.dot(
        turn_two, factor[...], preferred_element_type=F32
    ) + turn_two.astype(F32) * lift
    chosen = jnp.where(count[0, 0] == 1, turn.astype(F32), inverse_rows)
    root_out[...] = (chosen * lax.rsqrt(scale)).astype(BF16)
    finished[...] = jnp.zeros_like(finished)
    for copy in copies:
        copy.wait()


def step_kernel(replicas, pair, far, old_columns, step_out, grads, result):
    share = old_columns.shape[1]
    strip = step_out.shape[0] // replicas
    length = pair.shape[0] // 2
    mine = lax.axis_index("dp")
    strips = [(pair, 0, 0), (pair, length, along(1)), (far, 0, along(0)), (far, length, 3)]
    for i, (ref, at, _) in enumerate(strips):
        for part in range(replicas):
            start = at + part * strip
            grads[i * strip : (i + 1) * strip, part * share : (part + 1) * share] = ref[start : start + strip, :]
    result[...] = jnp.dot(grads[...], old_columns[...], preferred_element_type=F32).astype(BF16)
    for i, (_, _, offset) in enumerate(strips):
        step_out[band(mine ^ offset, strip), :] = result[i * strip : (i + 1) * strip, :]


def square_plan(acts, out_grad, old_factor, old_root, iter_count):
    replicas = lax.axis_size("dp")
    inputs = acts[0]
    tokens, order = inputs.shape
    share = order // replicas
    grows = out_grad.shape[2]
    params = pltpu.CompilerParams(vmem_limit_bytes=VMEM_LIMIT)
    length = chunk_starts(share)[-1]
    digits = 16

    def shape(rows, kind=BF16, columns=share):
        return jax.ShapeDtypeStruct((rows, columns), kind)

    def call(kernel, outs, name, *operands, flops=0, scalar=False, first_out=None, after=(), scratch=()):
        in_specs = whole(len(operands)) + [pl.BlockSpec(memory_space=pl.ANY)] * len(after)
        out_specs = whole(len(outs))
        if scalar:
            in_specs[0] = pl.BlockSpec(memory_space=pltpu.SMEM)
        if first_out is not None:
            out_specs[0] = pl.BlockSpec(memory_space=first_out)

        def body(*refs):
            kernel(*refs[: len(operands)], *refs[len(operands) + len(after) :])

        return pl.pallas_call(
            body,
            out_shape=outs,
            in_specs=in_specs,
            out_specs=out_specs,
            scratch_shapes=scratch,
            compiler_params=params,
            cost_estimate=pl.CostEstimate(
                flops=flops,
                bytes_accessed=sum(x.size * x.dtype.itemsize for x in (*operands, *outs)),
                transcendentals=0,
            ),
            name=name,
        )(*operands, *after)

    def both(x, y):
        return swapped(x, 1), swapped(y, 2)

    received = passed_along(out_grad, "pipe", -1)[0]
    send_x, send_y, keep = call(
        functools.partial(batch_kernel, replicas, tokens * replicas),
        [shape(length)] * 2 + [shape(2 * length, F32)],
        "batch",
        inputs,
        flops=5 * tokens * order * order // 4,
        scratch=[pltpu.VMEM((order, order), F32)],
    )
    got_x, got_y = both(send_x, send_y)
    on_x, on_y = call(relay_kernel, [shape(length // 2)] * 2, "relay", keep, got_x, got_y)
    relay_x, relay_y = both(on_x, on_y)
    strips, strips_keep = call(
        functools.partial(grad_kernel, replicas, tokens * replicas),
        [shape(2 * grows), shape(2 * grows, F32)],
        "grad",
        inputs,
        received,
        flops=2 * tokens * order * grows,
        scratch=[pltpu.VMEM((grows, order), F32)],
    )
    strips_got = swapped_along(strips, 0)
    chunk, exact = call(
        factor_kernel,
        [shape(length + digits), shape(length, F32)],
        "factor",
        keep,
        got_x,
        got_y,
        relay_x,
        relay_y,
        old_factor[0, 0],
    )
    near, side = both(chunk, chunk)
    (strip_on,) = call(strip_relay_kernel, [shape(grows)], "strip_relay", strips_keep, strips_got, after=[chunk])
    strip_relayed = swapped_along(strip_on, 1)
    (strip,) = call(strip_kernel, [shape(grows)], "strip", strips_keep, strips_got, strip_relayed)
    strip_near = swapped_along(strip, 1)
    on_x, on_y = call(halves_kernel, [shape(length // 2 + digits), shape(length // 2)], "halves", near, side)
    lower, upper = both(on_x, on_y)
    known, diagonal, squares, rows, old_columns = call(
        matrix_kernel,
        [shape(order, BF16, order), shape(1, F32, order), shape(digits, F32), shape(share, F32, order), shape(order)],
        "matrix",
        exact,
        chunk,
        near,
        side,
        old_root[0, 0],
        after=[on_x],
    )
    (pair,) = call(pair_kernel, [shape(2 * grows)], "pair", strip, strip_near, after=[diagonal])
    pair_far = swapped_along(pair, 0)
    factor, root, finished = call(
        root_kernel,
        [shape(share, F32, order), shape(share, BF16, order), shape(8, F32, 128)],
        "root",
        iter_count,
        known,
        diagonal,
        squares,
        rows,
        exact,
        upper,
        lower,
        flops=6 * share * order * order,
        scalar=True,
        first_out=pl.ANY,
        scratch=[
            pltpu.VMEM((order, order), BF16),
            pltpu.VMEM((1, order), F32),
            pltpu.VMEM((share, share), F32),
            pltpu.SemaphoreType.DMA((replicas,)),
        ],
    )
    (step,) = call(
        functools.partial(step_kernel, replicas),
        [shape(grows)],
        "step",
        pair,
        pair_far,
        old_columns,
        flops=2 * grows * order * share,
        after=[finished],
        scratch=[pltpu.VMEM((grows, order), BF16), pltpu.VMEM((grows, share), BF16)],
    )
    return (factor[None, None], root[None, None], step[None, None])


def ring_plan(acts, out_grad, old_factor, old_root, iter_count):
    inputs = acts[0]
    replicas = lax.axis_size("dp")
    tokens_all = inputs.shape[0] * replicas
    order = inputs.shape[1]
    share = order // replicas
    offset = lax.axis_index("dp") * share
    received = passed_along(out_grad, "pipe", -1)[0]
    partial_grad = jnp.dot(received.T, inputs, preferred_element_type=F32) / math.sqrt(tokens_all)
    batch = lax.psum_scatter(
        jnp.dot(inputs.T, inputs, preferred_element_type=F32) / tokens_all,
        "dp",
        scatter_dimension=0,
        tiled=True,
    )
    eye_rows = eye_of(share, order, offset)
    factor = DECAY * old_factor[0, 0] + (1.0 - DECAY) * batch + DAMPING * eye_rows
    grad16 = lax.psum(partial_grad, "dp").astype(BF16)
    scale = jnp.sqrt(lax.psum(jnp.sum(factor * factor), "dp") / order + EPSILON)
    step = lax.dot_general(
        grad16, old_root[0, 0], (((1,), (1,)), ((), ())), preferred_element_type=F32
    ).astype(BF16)
    first = lax.all_gather((factor / scale).astype(BF16), "dp", axis=0, tiled=True)
    turn_one = (1.5 * eye_of(order, order) - 0.5 * first.astype(F32)).astype(BF16)
    turn_rows = lax.dynamic_slice_in_dim(turn_one, offset, share, 0)
    second = jnp.dot(turn_rows, first, preferred_element_type=F32).astype(BF16)
    product = jnp.dot(second, turn_one, preferred_element_type=F32)
    turn_two = (1.5 * eye_rows - 0.5 * product).astype(BF16)
    inverse_rows = jnp.dot(turn_two, turn_one, preferred_element_type=F32)
    chosen = jnp.where(iter_count[0, 0] == 1, turn_rows.astype(F32), inverse_rows)
    root = (chosen / jnp.sqrt(scale)).astype(BF16)
    return (factor[None, None], root[None, None], step[None, None])


def solution(mesh):
    return jax.shard_map(
        square_plan if mesh.shape["dp"] == 4 and mesh.shape["pipe"] == 2 else ring_plan,
        mesh=mesh,
        in_specs=(
            P("pipe", "dp", "tensor"),
            P("pipe", "dp", "tensor"),
            P("pipe", "tensor", "dp", None),
            P("pipe", "tensor", "dp", None),
            P("pipe", "tensor"),
        ),
        out_specs=(
            P("pipe", "tensor", "dp", None),
            P("pipe", "tensor", "dp", None),
            P("pipe", "tensor", None, "dp"),
        ),
        check_vma=False,
    )
```

```python
import functools
import math

import jax
import jax.numpy as jnp
from jax import lax
from jax.experimental import pallas as pl
from jax.experimental.pallas import tpu as pltpu
from jax.sharding import PartitionSpec as P

DECAY = 0.75
DAMPING = 0.1
EPSILON = 1e-06
BF16 = jnp.bfloat16
F32 = jnp.float32
VMEM_LIMIT = 28 * 1024 * 1024


def passed_along(block, axis, distance):
    devices = range(lax.axis_size(axis))
    route = [((i - distance) % len(devices), i) for i in devices]
    return lax.ppermute(block, axis, route)


def swapped(block, offset):
    return lax.ppermute(block, "dp", [(i, i ^ offset) for i in range(lax.axis_size("dp"))])


def along(turn):
    return jnp.where(lax.axis_index("pipe") == turn, 1, 2)


def swapped_along(block, turn):
    replicas = lax.axis_size("dp")
    route = []
    for section in range(lax.axis_size("pipe")):
        offset = 1 if section == turn else 2
        route += [(section * replicas + i, section * replicas + (i ^ offset)) for i in range(replicas)]
    return lax.ppermute(block, ("pipe", "dp"), route)


def eye_of(rows, cols, shift=0):
    row_ids = lax.broadcasted_iota(jnp.int32, (rows, cols), 0) + shift
    col_ids = lax.broadcasted_iota(jnp.int32, (rows, cols), 1)
    return (row_ids == col_ids).astype(F32)


def whole(count):
    return [pl.BlockSpec(memory_space=pltpu.VMEM)] * count


def transposed(block):
    return block.astype(F32).T.astype(block.dtype)


OVER_ROWS = (((0,), (0,)), ((), ()))


def chunk_starts(share):
    half = share // 2
    return (0, half) + tuple(half + half // 2 + half * i for i in range(4))


def shared_half(owner, offset, share):
    other = owner ^ offset
    low, high = jnp.minimum(owner, other), jnp.maximum(owner, other)
    row = low * share + jnp.where(owner > other, share // 2, 0)
    return pl.multiple_of(row, share // 2), pl.multiple_of(high * share, share)


def band(index, size):
    return pl.ds(pl.multiple_of(index * size, size), size)


def side_by_side(low):
    half = low.shape[0] // 2
    return jnp.concatenate([low[0:half], low[half:]], axis=1)


def stacked(packed):
    half = packed.shape[1] // 2
    return jnp.concatenate([packed[:, 0:half], packed[:, half:]], axis=0)


def store_chunk(pieces, length, upper, lower):
    for start, piece in pieces:
        stop = start + piece.shape[0]
        for target, low, high in ((upper, 0, length), (lower, length, stop)):
            first, last = max(start, low), min(stop, high)
            if first < last:
                ref, at = target
                ref[at + first - low : at + last - low, :] = piece[first - start : last - start].astype(ref.dtype)


def batch_kernel(replicas, tokens_all, acts, relay_x, relay_y, direct_x, direct_y, keep, batch):
    order = acts.shape[1]
    share = order // replicas
    half = share // 2
    starts = chunk_starts(share)
    length = relay_x.shape[0]
    mine = lax.axis_index("dp")
    for i in range(replicas):
        rows = slice(i * share, (i + 1) * share)
        batch[rows, i * share :] = lax.dot_general(
            acts[:, rows], acts[:, i * share :], OVER_ROWS, preferred_element_type=F32
        ) * (1.0 / tokens_all)

    def pieces(offset):
        owner = mine ^ offset
        corner = pl.ds(pl.multiple_of(owner * share + half, half), half)
        yield starts[0], batch[pl.ds(pl.multiple_of(owner * share, share), half), band(owner, share)]
        yield starts[1], side_by_side(batch[corner, corner])
        for step in range(1, replicas):
            row, col = shared_half(owner, step, share)
            yield starts[1 + step], batch[pl.ds(row, half), pl.ds(col, share)]

    store_chunk(pieces(3), length, (relay_x, 0), (relay_y, 0))
    store_chunk(pieces(1), length, (direct_x, 0), (keep, 3 * length))
    store_chunk(pieces(2), length, (keep, 2 * length), (direct_y, 0))
    store_chunk(pieces(0), length, (keep, 0), (keep, length))


def relay_kernel(keep, got_x, got_y, send_x, send_y):
    length = send_x.shape[0]
    send_y[...] = (keep[2 * length : 3 * length, :] + got_x[...].astype(F32)).astype(BF16)
    send_x[...] = (keep[3 * length :, :] + got_y[...].astype(F32)).astype(BF16)


def grad_kernel(replicas, tokens_all, acts, grads, send, keep, total):
    share = acts.shape[1] // replicas
    strip = grads.shape[1] // replicas
    mine = lax.axis_index("dp")
    total[...] = lax.dot_general(grads[...], acts[...], OVER_ROWS, preferred_element_type=F32) * (
        1.0 / math.sqrt(tokens_all)
    )
    for ref, offsets in ((send, (along(0), 3)), (keep, (0, along(1)))):
        for i, offset in enumerate(offsets):
            for part in range(replicas):
                start = (i * replicas + part) * strip
                piece = total[band(mine ^ offset, strip), part * share : (part + 1) * share]
                ref[start : start + strip, :] = piece.astype(ref.dtype)


def copy_kernel(source, target):
    target[...] = source[...]


def strip_relay_kernel(keep, got, send):
    length = send.shape[0]
    send[...] = (keep[length:, :] + got[length:, :].astype(F32)).astype(BF16)


def strip_kernel(keep, got, relayed, strip):
    length = strip.shape[0]
    strip[...] = (keep[0:length, :] + got[0:length, :].astype(F32) + relayed[...].astype(F32)).astype(BF16)


def pair_kernel(own, got, send):
    length = own.shape[0]
    send[0:length, :] = own[...]
    send[length:, :] = got[...]


def factor_kernel(keep, direct_x, direct_y, relay_x, relay_y, old, chunk_upper, chunk_lower, exact):
    share = old.shape[0]
    half = share // 2
    starts = chunk_starts(share)
    length = relay_x.shape[0]
    mine = lax.axis_index("dp")
    upper = keep[0:length, :] + direct_x[...].astype(F32) + relay_y[...].astype(F32)
    lower = keep[length : 2 * length, :] + direct_y[...].astype(F32) + relay_x[...].astype(F32)
    total = jnp.concatenate([upper, lower], axis=0)
    diagonal = old[:, band(mine, share)]
    terms = [
        DECAY * diagonal[0:half] + DAMPING * eye_of(half, share),
        side_by_side(DECAY * diagonal[half:, half:] + DAMPING * eye_of(half, half)),
    ]
    for offset in range(1, 4):
        block = old[:, band(mine ^ offset, share)]
        terms.append(DECAY * jnp.where(mine < mine ^ offset, block[0:half], block[:, half:].T))
    column = lax.broadcasted_iota(jnp.int32, (1, share), 1)
    weights = [jnp.where(column < half, 1.0, 2.0), 1.0, 2.0, 2.0, 2.0]
    sums = jnp.zeros((1, share), F32)
    for start, term, weight in zip(starts, terms, weights):
        rows = slice(start, start + term.shape[0])
        value = term + (1.0 - DECAY) * total[rows]
        exact[rows, :] = value
        sums = sums + weight * jnp.sum(value * value, axis=0, keepdims=True)
    high = sums.astype(BF16).astype(F32)
    middle = (sums - high).astype(BF16).astype(F32)
    rest = sums - high - middle
    spot = lax.broadcasted_iota(jnp.int32, (chunk_lower.shape[0] - length, share), 0)
    digits = jnp.where(spot == 0, high, jnp.where(spot == 1, middle, jnp.where(spot == 2, rest, 0.0)))
    chunk_upper[...] = exact[0:length, :].astype(BF16)
    chunk_lower[0:length, :] = exact[length:, :].astype(BF16)
    chunk_lower[length:, :] = digits.astype(BF16)


def place(factor, diagonal, owner, read, share):
    half = share // 2
    starts = chunk_starts(share)
    base = pl.ds(pl.multiple_of(owner * share, share), half)
    corner = pl.ds(pl.multiple_of(owner * share + half, half), half)
    top = read(starts[0], half)
    low = stacked(read(starts[1], half // 2))
    factor[base, band(owner, share)] = top
    factor[corner, base] = transposed(top[:, half:])
    factor[corner, corner] = low
    eye = eye_of(half, half)
    diagonal[:, base] = jnp.sum(top[:, 0:half].astype(F32) * eye, axis=0, keepdims=True)
    diagonal[:, corner] = jnp.sum(low.astype(F32) * eye, axis=0, keepdims=True)
    for offset in range(1, 4):
        row, col = shared_half(owner, offset, share)
        block = read(starts[1 + offset], half)
        factor[pl.ds(row, half), pl.ds(col, share)] = block
        factor[pl.ds(col, share), pl.ds(row, half)] = transposed(block)


def rows_of(upper, lower):
    def read(start, count):
        length = upper.shape[0]
        if start + count <= length:
            return upper[start : start + count, :]
        if start >= length:
            return lower[start - length : start - length + count, :]
        return jnp.concatenate([upper[start:, :], lower[0 : start + count - length, :]], axis=0)

    return read


def store_shared(target, columns, own_is_upper, own, theirs):
    half = own.shape[0]

    @pl.when(own_is_upper)
    def _():
        target[0:half, columns] = own
        target[half:, columns] = theirs

    @pl.when(jnp.logical_not(own_is_upper))
    def _():
        target[:, columns] = jnp.concatenate([theirs.T, own.T], axis=1)


def matrix_kernel(
    exact, own_upper, own_lower, near_upper, near_lower, side_upper, side_lower, old_root, factor, diagonal, squares, rows,
    old_columns,
):
    share = exact.shape[1]
    half = share // 2
    starts = chunk_starts(share)
    mine = lax.axis_index("dp")
    factor[...] = jnp.zeros_like(factor)
    diagonal[...] = jnp.zeros_like(diagonal)
    count = squares.shape[0]
    reads = [rows_of(own_upper, own_lower), rows_of(near_upper, near_lower), rows_of(side_upper, side_lower)]
    sums = jnp.zeros((count, share), F32)
    for offset, read in enumerate(reads):
        place(factor, diagonal, mine ^ offset, read, share)
        sums = sums + read(starts[-1], count).astype(F32)
    squares[...] = sums
    top = exact[0:half, :]
    low = stacked(exact[starts[1] : starts[2], :])
    rows[0:half, band(mine, share)] = top
    rows[half:, band(mine, share)] = jnp.concatenate([top[:, half:].T, low], axis=1)
    for offset in (1, 2):
        start = starts[1 + offset]
        other = mine ^ offset
        theirs = reads[offset](start, half).astype(F32)
        store_shared(rows, band(other, share), mine < other, exact[start : start + half, :], theirs)
    rows[:, band(mine ^ 3, share)] = jnp.zeros((share, share), F32)
    old_columns[...] = transposed(old_root[...])


def root_kernel(
    count, known, known_diagonal, squares, rows, exact, upper, lower, factor_out, root_out, finished, factor, diagonal,
    shared, sent,
):
    share, order = root_out.shape
    half = share // 2
    starts = chunk_starts(share)
    mine = lax.axis_index("dp")
    read = rows_of(upper, lower)
    last = slice(starts[4], starts[5])
    store_shared(shared, slice(None), mine < mine ^ 3, exact[last, :], read(starts[4], half).astype(F32))
    copies = []
    for offset in range(4):
        columns = band(mine ^ offset, share)
        source = shared if offset == 3 else rows.at[:, columns]
        copies.append(pltpu.make_async_copy(source, factor_out.at[:, columns], sent.at[offset]))
        copies[-1].start()

    factor[...] = known[...]
    diagonal[...] = known_diagonal[...]
    place(factor, diagonal, mine ^ 3, read, share)
    total = squares[...] + lower[lower.shape[0] - squares.shape[0] :, :].astype(F32)
    scale = jnp.sqrt(jnp.sum(total, keepdims=True) / order + EPSILON)
    inverse = 1.0 / scale
    ones = (diagonal[...] * inverse).astype(BF16).astype(F32)
    lift = (1.5 - 0.5 * ones).astype(BF16).astype(F32) + 0.5 * (diagonal[...] * inverse)
    eye = eye_of(share, order, mine * share)
    first = (factor[band(mine, share), :].astype(F32) * inverse).astype(BF16).astype(F32)
    turn = (1.5 * eye - 0.5 * first).astype(BF16)
    second = (jnp.dot(turn, factor[...], preferred_element_type=F32) * inverse).astype(BF16)
    product = (-0.5 * inverse) * jnp.dot(second, factor[...], preferred_element_type=F32) + second.astype(F32) * lift
    turn_two = (1.5 * eye - 0.5 * product).astype(BF16)
    inverse_rows = (-0.5 * inverse) * jnp.dot(
        turn_two, factor[...], preferred_element_type=F32
    ) + turn_two.astype(F32) * lift
    chosen = jnp.where(count[0, 0] == 1, turn.astype(F32), inverse_rows)
    root_out[...] = (chosen * lax.rsqrt(scale)).astype(BF16)
    finished[...] = jnp.zeros_like(finished)
    for copy in copies:
        copy.wait()


def step_kernel(replicas, pair, far, old_columns, step_out, grads, result):
    share = old_columns.shape[1]
    strip = step_out.shape[0] // replicas
    length = pair.shape[0] // 2
    mine = lax.axis_index("dp")
    strips = [(pair, 0, 0), (pair, length, along(1)), (far, 0, along(0)), (far, length, 3)]
    for i, (ref, at, _) in enumerate(strips):
        for part in range(replicas):
            start = at + part * strip
            grads[i * strip : (i + 1) * strip, part * share : (part + 1) * share] = ref[start : start + strip, :]
    result[...] = jnp.dot(grads[...], old_columns[...], preferred_element_type=F32).astype(BF16)
    for i, (_, _, offset) in enumerate(strips):
        step_out[band(mine ^ offset, strip), :] = result[i * strip : (i + 1) * strip, :]


def square_plan(acts, out_grad, old_factor, old_root, iter_count):
    replicas = lax.axis_size("dp")
    inputs = acts[0]
    tokens, order = inputs.shape
    share = order // replicas
    grows = out_grad.shape[2]
    params = pltpu.CompilerParams(vmem_limit_bytes=VMEM_LIMIT)
    length = chunk_starts(share)[-1]
    digits = 16

    def shape(rows, kind=BF16, columns=share):
        return jax.ShapeDtypeStruct((rows, columns), kind)

    def call(kernel, outs, name, *operands, flops=0, scalar=False, first_out=None, after=(), scratch=()):
        in_specs = whole(len(operands)) + [pl.BlockSpec(memory_space=pl.ANY)] * len(after)
        out_specs = whole(len(outs))
        if scalar:
            in_specs[0] = pl.BlockSpec(memory_space=pltpu.SMEM)
        if first_out is not None:
            out_specs[0] = pl.BlockSpec(memory_space=first_out)

        def body(*refs):
            kernel(*refs[: len(operands)], *refs[len(operands) + len(after) :])

        return pl.pallas_call(
            body,
            out_shape=outs,
            in_specs=in_specs,
            out_specs=out_specs,
            scratch_shapes=scratch,
            compiler_params=params,
            cost_estimate=pl.CostEstimate(
                flops=flops,
                bytes_accessed=sum(x.size * x.dtype.itemsize for x in (*operands, *outs)),
                transcendentals=0,
            )
            if flops
            else None,
            name=name,
        )(*operands, *after)

    def both(x, y):
        return swapped(x, 1), swapped(y, 2)

    received = passed_along(out_grad, "pipe", -1)[0]
    relay_x, relay_y, direct_x, direct_y, keep = call(
        functools.partial(batch_kernel, replicas, tokens * replicas),
        [shape(length // 2)] * 4 + [shape(2 * length, F32)],
        "batch",
        inputs,
        scratch=[pltpu.VMEM((order, order), F32)],
    )
    relay_x, relay_y = both(relay_x, relay_y)
    direct_x, direct_y = both(direct_x, direct_y)
    on_x, on_y = call(relay_kernel, [shape(length // 2)] * 2, "relay", keep, relay_x, relay_y)
    relay_x, relay_y = both(on_x, on_y)
    strips, strips_keep = call(
        functools.partial(grad_kernel, replicas, tokens * replicas),
        [shape(2 * grows), shape(2 * grows, F32)],
        "grad",
        inputs,
        received,
        scratch=[pltpu.VMEM((grows, order), F32)],
    )
    (strips_now,) = call(copy_kernel, [shape(2 * grows)], "release", strips, after=[relay_x, relay_y, direct_x, direct_y])
    strips_got = swapped_along(strips_now, 0)
    upper, lower, exact = call(
        factor_kernel,
        [shape(length // 2), shape(length // 2 + digits), shape(length, F32)],
        "factor",
        keep,
        direct_x,
        direct_y,
        relay_x,
        relay_y,
        old_factor[0, 0],
    )
    near_upper, side_lower = both(upper, lower)
    near_lower, side_upper = both(lower, upper)
    far_lower, far_upper = both(side_lower, near_upper)
    (strip_on,) = call(strip_relay_kernel, [shape(grows)], "strip_relay", strips_keep, strips_got, after=[upper])
    strip_relayed = swapped_along(strip_on, 1)
    (strip,) = call(strip_kernel, [shape(grows)], "strip", strips_keep, strips_got, strip_relayed)
    strip_near = swapped_along(strip, 1)
    known, diagonal, squares, rows, old_columns = call(
        matrix_kernel,
        [shape(order, BF16, order), shape(1, F32, order), shape(digits, F32), shape(share, F32, order), shape(order)],
        "matrix",
        exact,
        upper,
        lower,
        near_upper,
        near_lower,
        side_upper,
        side_lower,
        old_root[0, 0],
        flops=order * order,
    )
    (pair,) = call(pair_kernel, [shape(2 * grows)], "pair", strip, strip_near, after=[diagonal, far_lower, far_upper])
    pair_far = swapped_along(pair, 0)
    factor, root, finished = call(
        root_kernel,
        [shape(share, F32, order), shape(share, BF16, order), shape(8, F32, 128)],
        "root",
        iter_count,
        known,
        diagonal,
        squares,
        rows,
        exact,
        far_upper,
        far_lower,
        flops=6 * share * order * order,
        scalar=True,
        first_out=pl.ANY,
        scratch=[
            pltpu.VMEM((order, order), BF16),
            pltpu.VMEM((1, order), F32),
            pltpu.VMEM((share, share), F32),
            pltpu.SemaphoreType.DMA((replicas,)),
        ],
    )
    (step,) = call(
        functools.partial(step_kernel, replicas),
        [shape(grows)],
        "step",
        pair,
        pair_far,
        old_columns,
        after=[finished],
        scratch=[pltpu.VMEM((grows, order), BF16), pltpu.VMEM((grows, share), BF16)],
    )
    return (factor[None, None], root[None, None], step[None, None])


def ring_plan(acts, out_grad, old_factor, old_root, iter_count):
    inputs = acts[0]
    replicas = lax.axis_size("dp")
    tokens_all = inputs.shape[0] * replicas
    order = inputs.shape[1]
    share = order // replicas
    offset = lax.axis_index("dp") * share
    received = passed_along(out_grad, "pipe", -1)[0]
    partial_grad = jnp.dot(received.T, inputs, preferred_element_type=F32) / math.sqrt(tokens_all)
    batch = lax.psum_scatter(
        jnp.dot(inputs.T, inputs, preferred_element_type=F32) / tokens_all,
        "dp",
        scatter_dimension=0,
        tiled=True,
    )
    eye_rows = eye_of(share, order, offset)
    factor = DECAY * old_factor[0, 0] + (1.0 - DECAY) * batch + DAMPING * eye_rows
    grad16 = lax.psum(partial_grad, "dp").astype(BF16)
    scale = jnp.sqrt(lax.psum(jnp.sum(factor * factor), "dp") / order + EPSILON)
    step = lax.dot_general(
        grad16, old_root[0, 0], (((1,), (1,)), ((), ())), preferred_element_type=F32
    ).astype(BF16)
    first = lax.all_gather((factor / scale).astype(BF16), "dp", axis=0, tiled=True)
    turn_one = (1.5 * eye_of(order, order) - 0.5 * first.astype(F32)).astype(BF16)
    turn_rows = lax.dynamic_slice_in_dim(turn_one, offset, share, 0)
    second = jnp.dot(turn_rows, first, preferred_element_type=F32).astype(BF16)
    product = jnp.dot(second, turn_one, preferred_element_type=F32)
    turn_two = (1.5 * eye_rows - 0.5 * product).astype(BF16)
    inverse_rows = jnp.dot(turn_two, turn_one, preferred_element_type=F32)
    chosen = jnp.where(iter_count[0, 0] == 1, turn_rows.astype(F32), inverse_rows)
    root = (chosen / jnp.sqrt(scale)).astype(BF16)
    return (factor[None, None], root[None, None], step[None, None])


def solution(mesh):
    return jax.shard_map(
        square_plan if mesh.shape["dp"] == 4 and mesh.shape["pipe"] == 2 else ring_plan,
        mesh=mesh,
        in_specs=(
            P("pipe", "dp", "tensor"),
            P("pipe", "dp", "tensor"),
            P("pipe", "tensor", "dp", None),
            P("pipe", "tensor", "dp", None),
            P("pipe", "tensor"),
        ),
        out_specs=(
            P("pipe", "tensor", "dp", None),
            P("pipe", "tensor", "dp", None),
            P("pipe", "tensor", None, "dp"),
        ),
        check_vma=False,
    )
```

```python
import functools
import math

import jax
import jax.numpy as jnp
from jax import lax
from jax.experimental import pallas as pl
from jax.experimental.pallas import tpu as pltpu
from jax.sharding import PartitionSpec as P

DECAY = 0.75
DAMPING = 0.1
EPSILON = 1e-06
BF16 = jnp.bfloat16
F32 = jnp.float32
VMEM_LIMIT = 28 * 1024 * 1024


def passed_along(block, axis, distance):
    devices = range(lax.axis_size(axis))
    route = [((i - distance) % len(devices), i) for i in devices]
    return lax.ppermute(block, axis, route)


def along(turn):
    return jnp.where(lax.axis_index("pipe") == turn, 1, 2)


def swapped(block, turn):
    replicas = lax.axis_size("dp")
    route = []
    for section in range(lax.axis_size("pipe")):
        offset = 1 if section == turn else 2
        route += [(section * replicas + i, section * replicas + (i ^ offset)) for i in range(replicas)]
    return lax.ppermute(block, ("pipe", "dp"), route)


def swapped_across(block):
    return lax.ppermute(block, "dp", [(i, i ^ 3) for i in range(lax.axis_size("dp"))])


def eye_of(rows, cols, shift=0):
    row_ids = lax.broadcasted_iota(jnp.int32, (rows, cols), 0) + shift
    col_ids = lax.broadcasted_iota(jnp.int32, (rows, cols), 1)
    return (row_ids == col_ids).astype(F32)


def whole(count):
    return [pl.BlockSpec(memory_space=pltpu.VMEM)] * count


def transposed(block):
    return block.astype(F32).T.astype(block.dtype)


def offsets():
    return 0, along(0), along(1), 3


def chunk_rows(share):
    half = share // 2
    return [0, half, half + half // 2] + [half + half // 2 + half * i for i in range(1, 4)]


def shared_half(owner, offset, share):
    other = owner ^ offset
    low, high = jnp.minimum(owner, other), jnp.maximum(owner, other)
    row = low * share + jnp.where(owner > other, share // 2, 0)
    return pl.multiple_of(row, share // 2), pl.multiple_of(high * share, share)


def store_chunk(pieces, length, upper, lower):
    for start, piece in pieces:
        stop = start + piece.shape[0]
        for target, low, high in ((upper, 0, length), (lower, length, stop)):
            first, last = max(start, low), min(stop, high)
            if target is not None and first < last:
                ref, at = target
                ref[at + first - low : at + last - low, :] = piece[first - start : last - start].astype(ref.dtype)


def batch_kernel(replicas, tokens_all, acts, relay_x, relay_y, direct_x, direct_y, keep, batch):
    order = acts.shape[1]
    share = order // replicas
    half = share // 2
    starts = chunk_rows(share)
    length = relay_x.shape[0]
    mine = lax.axis_index("dp")
    for i in range(replicas):
        band = slice(i * share, (i + 1) * share)
        batch[band, i * share :] = lax.dot_general(
            acts[:, band], acts[:, i * share :], (((0,), (0,)), ((), ())), preferred_element_type=F32
        ) * (1.0 / tokens_all)

    def pieces(offset):
        owner = mine ^ offset
        base = pl.multiple_of(owner * share, share)
        corner = pl.multiple_of(owner * share + half, half)
        yield 0, batch[pl.ds(base, half), pl.ds(base, share)]
        low = batch[pl.ds(corner, half), pl.ds(corner, half)]
        yield starts[1], jnp.concatenate([low[0 : half // 2], low[half // 2 :]], axis=1)
        for start, step in zip(starts[2:], offsets()[1:]):
            row, col = shared_half(owner, step, share)
            yield start, batch[pl.ds(row, half), pl.ds(col, share)]

    store_chunk(pieces(3), length, (relay_x, 0), (relay_y, 0))
    store_chunk(pieces(along(0)), length, (direct_x, 0), (keep, 3 * length))
    store_chunk(pieces(along(1)), length, (keep, 2 * length), (direct_y, 0))
    store_chunk(pieces(0), length, (keep, 0), (keep, length))


def grad_kernel(replicas, tokens_all, acts, grads, send_x, send_y, keep, total):
    order = acts.shape[1]
    share = order // replicas
    strip = grads.shape[1] // replicas
    length = send_x.shape[0] // 2
    mine = lax.axis_index("dp")
    total[...] = lax.dot_general(
        grads[...], acts[...], (((0,), (0,)), ((), ())), preferred_element_type=F32
    ) * (1.0 / math.sqrt(tokens_all))

    def pieces(offset):
        rows = pl.ds(pl.multiple_of((mine ^ offset) * strip, strip), strip)
        for part in range(replicas):
            yield part * strip, total[rows, part * share : (part + 1) * share]

    store_chunk(pieces(3), length, (send_x, 0), (send_y, 0))
    store_chunk(pieces(along(0)), length, (send_x, length), (keep, 3 * length))
    store_chunk(pieces(along(1)), length, (keep, 2 * length), (send_y, length))
    store_chunk(pieces(0), length, (keep, 0), (keep, length))


def relay_kernel(keep, got_x, got_y, send_x, send_y):
    length = send_x.shape[0]
    send_y[...] = (keep[2 * length : 3 * length, :] + got_x[...].astype(F32)).astype(BF16)
    send_x[...] = (keep[3 * length :, :] + got_y[...].astype(F32)).astype(BF16)


def grad_relay_kernel(keep, got_x, got_y, send_x, send_y):
    length = send_x.shape[0]
    send_y[...] = (keep[2 * length : 3 * length, :] + got_x[0:length, :].astype(F32)).astype(BF16)
    send_x[...] = (keep[3 * length :, :] + got_y[0:length, :].astype(F32)).astype(BF16)


def grad_total_kernel(keep, got_x, got_y, relay_x, relay_y, chunk):
    length = relay_x.shape[0]
    chunk[0:length, :] = (
        keep[0:length, :] + got_x[length:, :].astype(F32) + relay_y[...].astype(F32)
    ).astype(BF16)
    chunk[length:, :] = (
        keep[length : 2 * length, :] + got_y[length:, :].astype(F32) + relay_x[...].astype(F32)
    ).astype(BF16)


def factor_kernel(replicas, keep, direct_x, direct_y, relay_x, relay_y, old, upper, lower, exact):
    share, order = old.shape
    half = share // 2
    starts = chunk_rows(share)
    length = upper.shape[0]
    mine = lax.axis_index("dp")
    total = jnp.concatenate(
        [
            keep[0:length, :] + direct_x[...].astype(F32) + relay_y[...].astype(F32),
            keep[length : 2 * length, :] + direct_y[...].astype(F32) + relay_x[...].astype(F32),
        ],
        axis=0,
    )
    diagonal = old[:, pl.ds(pl.multiple_of(mine * share, share), share)]
    eye = eye_of(half, share)
    low_eye = eye_of(half, half)

    def packed(low):
        return jnp.concatenate([low[0 : half // 2], low[half // 2 :]], axis=1)

    terms = [
        DECAY * diagonal[0:half] + DAMPING * eye,
        packed(DECAY * diagonal[half:, half:] + DAMPING * low_eye),
    ]
    for step in offsets()[1:]:
        other = mine ^ step
        block = old[:, pl.ds(pl.multiple_of(other * share, share), share)]
        terms.append(DECAY * jnp.where(mine < other, block[0:half], block[:, half:].T))
    column = lax.broadcasted_iota(jnp.int32, (1, share), 1)
    squares = jnp.zeros((1, share), F32)
    values = []
    for position, (start, term) in enumerate(zip(starts, terms)):
        value = term + (1.0 - DECAY) * total[start : start + term.shape[0]]
        exact[start : start + term.shape[0], :] = value
        summed = jnp.sum(value * value, axis=0, keepdims=True)
        if position == 0:
            summed = jnp.where(column < half, summed, 2.0 * summed)
        squares = squares + (summed if position < 2 else 2.0 * summed)
        values.append(value.astype(BF16))
    high = squares.astype(BF16).astype(F32)
    middle = (squares - high).astype(BF16).astype(F32)
    rest = squares - high - middle
    spot = lax.broadcasted_iota(jnp.int32, (16, share), 0)
    digits = jnp.where(spot == 0, high, jnp.where(spot == 1, middle, jnp.where(spot == 2, rest, 0.0)))
    values.append(digits.astype(BF16))
    chunk = jnp.concatenate(values, axis=0)
    upper[...] = chunk[0:length]
    lower[...] = chunk[length:]


def root_kernel(count, exact, *rest):
    chunks = [rest[2 * i : 2 * i + 2] for i in range(4)]
    factor_out, root_out, finished, factor, diagonal, rows, sent = rest[8:]
    share, order = root_out.shape
    half = share // 2
    starts = chunk_rows(share)
    length = chunks[0][0].shape[0]
    mine = lax.axis_index("dp")

    def rows_of(position, start, count):
        upper, lower = chunks[position]
        if start + count <= length:
            return upper[start : start + count, :]
        if start >= length:
            return lower[start - length : start - length + count, :]
        return jnp.concatenate([upper[start:length, :], lower[0 : start + count - length, :]], axis=0)

    top = exact[0:half, :]
    low = exact[starts[1] : starts[2], :]
    low = jnp.concatenate([low[:, 0:half], low[:, half:]], axis=0)
    copies = []
    for position, step in enumerate(offsets()):
        other = mine ^ step
        target = rows.at[position]
        if position == 0:
            target[0:half, :] = top
            target[half:, :] = jnp.concatenate([top[:, half:].T, low], axis=1)
        else:
            start = starts[1 + position]
            own = exact[start : start + half, :]
            theirs = rows_of(position, start, half).astype(F32)

            @pl.when(mine < other)
            def _():
                target[0:half, :] = own
                target[half:, :] = theirs

            @pl.when(mine > other)
            def _():
                target[...] = jnp.concatenate([theirs.T, own.T], axis=1)

        columns = pl.ds(pl.multiple_of(other * share, share), share)
        copies.append(pltpu.make_async_copy(target, factor_out.at[:, columns], sent.at[position]))
        copies[-1].start()

    squares = jnp.zeros((16, share), F32)
    low_eye = eye_of(half, half)
    for position, offset in enumerate(offsets()):
        owner = mine ^ offset
        base = pl.multiple_of(owner * share, share)
        corner = pl.multiple_of(owner * share + half, half)
        top = rows_of(position, 0, half)
        low = rows_of(position, starts[1], half // 2)
        low = jnp.concatenate([low[:, 0:half], low[:, half:]], axis=0)
        factor[pl.ds(base, half), pl.ds(base, share)] = top
        factor[pl.ds(corner, half), pl.ds(base, half)] = transposed(top[:, half:])
        factor[pl.ds(corner, half), pl.ds(corner, half)] = low
        diagonal[:, pl.ds(base, half)] = jnp.sum(top[:, 0:half].astype(F32) * low_eye, axis=0, keepdims=True)
        diagonal[:, pl.ds(corner, half)] = jnp.sum(low.astype(F32) * low_eye, axis=0, keepdims=True)
        for start, step in zip(starts[2:], offsets()[1:]):
            row, col = shared_half(owner, step, share)
            block = rows_of(position, start, half)
            factor[pl.ds(row, half), pl.ds(col, share)] = block
            factor[pl.ds(col, share), pl.ds(row, half)] = transposed(block)
        squares = squares + rows_of(position, starts[-1], 16).astype(F32)

    scale = jnp.sqrt(jnp.sum(squares, keepdims=True) / order + EPSILON)
    inverse = 1.0 / scale
    ones = (diagonal[...] * inverse).astype(BF16).astype(F32)
    lift = (1.5 - 0.5 * ones).astype(BF16).astype(F32) + 0.5 * (diagonal[...] * inverse)
    eye = eye_of(share, order, mine * share)
    my_rows = pl.ds(pl.multiple_of(mine * share, share), share)
    first = (factor[my_rows, :].astype(F32) * inverse).astype(BF16).astype(F32)
    turn = (1.5 * eye - 0.5 * first).astype(BF16)
    second = (jnp.dot(turn, factor[...], preferred_element_type=F32) * inverse).astype(BF16)
    product = (-0.5 * inverse) * jnp.dot(second, factor[...], preferred_element_type=F32) + second.astype(F32) * lift
    turn_two = (1.5 * eye - 0.5 * product).astype(BF16)
    inverse_rows = (-0.5 * inverse) * jnp.dot(
        turn_two, factor[...], preferred_element_type=F32
    ) + turn_two.astype(F32) * lift
    chosen = jnp.where(count[0, 0] == 1, turn.astype(F32), inverse_rows)
    root_out[...] = (chosen * lax.rsqrt(scale)).astype(BF16)
    finished[...] = jnp.zeros_like(finished)
    for copy in copies:
        copy.wait()


def step_kernel(replicas, *refs):
    chunks = refs[:replicas]
    old_root, step_out, grads, result = refs[replicas:]
    share = old_root.shape[0]
    strip = step_out.shape[0] // replicas
    mine = lax.axis_index("dp")
    for offset, chunk in enumerate(chunks):
        for part in range(replicas):
            grads[offset * strip : (offset + 1) * strip, part * share : (part + 1) * share] = chunk[
                part * strip : (part + 1) * strip, :
            ]
    result[...] = lax.dot_general(
        grads[...], old_root[...], (((1,), (1,)), ((), ())), preferred_element_type=F32
    ).astype(BF16)
    for position, offset in enumerate(offsets()):
        rows = pl.ds(pl.multiple_of((mine ^ offset) * strip, strip), strip)
        step_out[rows, :] = result[position * strip : (position + 1) * strip, :]


def square_plan(acts, out_grad, old_factor, old_root, iter_count):
    replicas = lax.axis_size("dp")
    inputs = acts[0]
    tokens, order = inputs.shape
    share = order // replicas
    grows = out_grad.shape[2]
    params = pltpu.CompilerParams(vmem_limit_bytes=VMEM_LIMIT)
    whole_rows = chunk_rows(share)[-1]
    length = whole_rows // 2

    def shape(rows, kind=BF16, columns=share):
        return jax.ShapeDtypeStruct((rows, columns), kind)

    def call(kernel, outs, name, *operands, first=None, first_out=None, after=(), scratch=()):
        in_specs = whole(len(operands)) + [pl.BlockSpec(memory_space=pl.ANY)] * len(after)
        if first is not None:
            in_specs[0] = pl.BlockSpec(memory_space=first)
        out_specs = whole(len(outs))
        if first_out is not None:
            out_specs[0] = pl.BlockSpec(memory_space=first_out)

        def body(*refs):
            kernel(*refs[: len(operands)], *refs[len(operands) + len(after) :])

        return pl.pallas_call(
            body,
            out_shape=outs,
            in_specs=in_specs,
            out_specs=out_specs,
            scratch_shapes=scratch,
            compiler_params=params,
            name=name,
        )(*operands, *after)

    received = passed_along(out_grad, "pipe", -1)[0]
    relay_x, relay_y, direct_x, direct_y, keep = call(
        functools.partial(batch_kernel, replicas, tokens * replicas),
        [shape(length)] * 4 + [shape(4 * length, F32)],
        "batch",
        inputs,
        scratch=[pltpu.VMEM((order, order), F32)],
    )
    relay_x, relay_y = swapped(relay_x, 0), swapped(relay_y, 1)
    direct_x, direct_y = swapped(direct_x, 0), swapped(direct_y, 1)
    relay_x, relay_y = call(relay_kernel, [shape(length)] * 2, "relay", keep, relay_x, relay_y)
    grad_x, grad_y, grad_keep = call(
        functools.partial(grad_kernel, replicas, tokens * replicas),
        [shape(grows)] * 2 + [shape(2 * grows, F32)],
        "grad",
        inputs,
        received,
        after=[relay_x, relay_y],
        scratch=[pltpu.VMEM((grows, order), F32)],
    )
    relay_x, relay_y = swapped(relay_x, 0), swapped(relay_y, 1)
    grad_x, grad_y = swapped(grad_x, 0), swapped(grad_y, 1)
    upper, lower, exact = call(
        functools.partial(factor_kernel, replicas),
        [shape(length), shape(length + 16), shape(whole_rows, F32)],
        "factor",
        keep,
        direct_x,
        direct_y,
        relay_x,
        relay_y,
        old_factor[0, 0],
    )
    upper_x, lower_y = swapped(upper, 0), swapped(lower, 1)
    lower_x, upper_y = swapped(lower, 0), swapped(upper, 1)
    strip_x, strip_y = call(
        grad_relay_kernel, [shape(grows // 2)] * 2, "grad_relay", grad_keep, grad_x, grad_y, after=[upper, lower]
    )
    strip_x, strip_y = swapped(strip_x, 0), swapped(strip_y, 1)
    upper_far, lower_far = swapped(upper_x, 1), swapped(lower_y, 0)
    (strip,) = call(
        grad_total_kernel,
        [shape(grows)],
        "grad_total",
        grad_keep,
        grad_x,
        grad_y,
        strip_x,
        strip_y,
        after=[upper_x, lower_y],
    )
    strips = [strip, swapped(strip, 0), swapped(strip, 1), swapped_across(strip)]
    factor, root, finished = call(
        root_kernel,
        [shape(share, F32, order), shape(share, BF16, order), shape(8, F32, 128)],
        "root",
        iter_count,
        exact,
        upper,
        lower,
        upper_x,
        lower_x,
        upper_y,
        lower_y,
        upper_far,
        lower_far,
        first=pltpu.SMEM,
        first_out=pl.ANY,
        scratch=[
            pltpu.VMEM((order, order), BF16),
            pltpu.VMEM((1, order), F32),
            pltpu.VMEM((replicas, share, share), F32),
            pltpu.SemaphoreType.DMA((replicas,)),
        ],
    )
    (step,) = call(
        functools.partial(step_kernel, replicas),
        [shape(grows, BF16, share)],
        "step",
        *strips,
        old_root[0, 0],
        after=[finished],
        scratch=[pltpu.VMEM((grows, order), BF16), pltpu.VMEM((grows, share), BF16)],
    )
    return (factor[None, None], root[None, None], step[None, None])


def ring_plan(acts, out_grad, old_factor, old_root, iter_count):
    inputs = acts[0]
    replicas = lax.axis_size("dp")
    tokens_all = inputs.shape[0] * replicas
    order = inputs.shape[1]
    share = order // replicas
    offset = lax.axis_index("dp") * share
    received = passed_along(out_grad, "pipe", -1)[0]
    partial_grad = jnp.dot(received.T, inputs, preferred_element_type=F32) / math.sqrt(tokens_all)
    batch = lax.psum_scatter(
        jnp.dot(inputs.T, inputs, preferred_element_type=F32) / tokens_all,
        "dp",
        scatter_dimension=0,
        tiled=True,
    )
    eye_rows = eye_of(share, order, offset)
    factor = DECAY * old_factor[0, 0] + (1.0 - DECAY) * batch + DAMPING * eye_rows
    grad16 = lax.psum(partial_grad, "dp").astype(BF16)
    scale = jnp.sqrt(lax.psum(jnp.sum(factor * factor), "dp") / order + EPSILON)
    step = lax.dot_general(
        grad16, old_root[0, 0], (((1,), (1,)), ((), ())), preferred_element_type=F32
    ).astype(BF16)
    first = lax.all_gather((factor / scale).astype(BF16), "dp", axis=0, tiled=True)
    turn_one = (1.5 * eye_of(order, order) - 0.5 * first.astype(F32)).astype(BF16)
    turn_rows = lax.dynamic_slice_in_dim(turn_one, offset, share, 0)
    second = jnp.dot(turn_rows, first, preferred_element_type=F32).astype(BF16)
    product = jnp.dot(second, turn_one, preferred_element_type=F32)
    turn_two = (1.5 * eye_rows - 0.5 * product).astype(BF16)
    inverse_rows = jnp.dot(turn_two, turn_one, preferred_element_type=F32)
    chosen = jnp.where(iter_count[0, 0] == 1, turn_rows.astype(F32), inverse_rows)
    root = (chosen / jnp.sqrt(scale)).astype(BF16)
    return (factor[None, None], root[None, None], step[None, None])


def solution(mesh):
    return jax.shard_map(
        square_plan if mesh.shape["dp"] == 4 and mesh.shape["pipe"] == 2 else ring_plan,
        mesh=mesh,
        in_specs=(
            P("pipe", "dp", "tensor"),
            P("pipe", "dp", "tensor"),
            P("pipe", "tensor", "dp", None),
            P("pipe", "tensor", "dp", None),
            P("pipe", "tensor"),
        ),
        out_specs=(
            P("pipe", "tensor", "dp", None),
            P("pipe", "tensor", "dp", None),
            P("pipe", "tensor", None, "dp"),
        ),
        check_vma=False,
    )
```

```python
import functools
import math

import jax
import jax.numpy as jnp
from jax import lax
from jax.experimental import pallas as pl
from jax.experimental.pallas import tpu as pltpu
from jax.sharding import PartitionSpec as P

DECAY = 0.75
DAMPING = 0.1
EPSILON = 1e-06
BF16 = jnp.bfloat16
F32 = jnp.float32
VMEM_LIMIT = 28 * 1024 * 1024


def passed_along(block, axis, distance):
    devices = range(lax.axis_size(axis))
    route = [((i - distance) % len(devices), i) for i in devices]
    return lax.ppermute(block, axis, route)


def along(turn):
    return jnp.where(lax.axis_index("pipe") == turn, 1, 2)


def swapped(block, turn):
    replicas = lax.axis_size("dp")
    route = []
    for section in range(lax.axis_size("pipe")):
        offset = 1 if section == turn else 2
        route += [(section * replicas + i, section * replicas + (i ^ offset)) for i in range(replicas)]
    return lax.ppermute(block, ("pipe", "dp"), route)


def swapped_across(block):
    return lax.ppermute(block, "dp", [(i, i ^ 3) for i in range(lax.axis_size("dp"))])


def eye_of(rows, cols, shift=0):
    row_ids = lax.broadcasted_iota(jnp.int32, (rows, cols), 0) + shift
    col_ids = lax.broadcasted_iota(jnp.int32, (rows, cols), 1)
    return (row_ids == col_ids).astype(F32)


def whole(count):
    return [pl.BlockSpec(memory_space=pltpu.VMEM)] * count


def transposed(block):
    return block.astype(F32).T.astype(block.dtype)


def offsets():
    return 0, along(0), along(1), 3


def chunk_rows(share):
    half = share // 2
    return [0, half, half + half // 2] + [half + half // 2 + half * i for i in range(1, 4)]


def shared_half(owner, offset, share):
    other = owner ^ offset
    low, high = jnp.minimum(owner, other), jnp.maximum(owner, other)
    row = low * share + jnp.where(owner > other, share // 2, 0)
    return pl.multiple_of(row, share // 2), pl.multiple_of(high * share, share)


def store_chunk(pieces, length, upper, lower):
    for start, piece in pieces:
        stop = start + piece.shape[0]
        for target, low, high in ((upper, 0, length), (lower, length, stop)):
            first, last = max(start, low), min(stop, high)
            if target is not None and first < last:
                ref, at = target
                ref[at + first - low : at + last - low, :] = piece[first - start : last - start].astype(ref.dtype)


def batch_kernel(replicas, tokens_all, acts, relay_x, relay_y, direct_x, direct_y, keep, batch):
    order = acts.shape[1]
    share = order // replicas
    half = share // 2
    starts = chunk_rows(share)
    length = relay_x.shape[0]
    mine = lax.axis_index("dp")
    for i in range(replicas):
        band = slice(i * share, (i + 1) * share)
        batch[band, i * share :] = lax.dot_general(
            acts[:, band], acts[:, i * share :], (((0,), (0,)), ((), ())), preferred_element_type=F32
        ) * (1.0 / tokens_all)

    def pieces(offset):
        owner = mine ^ offset
        base = pl.multiple_of(owner * share, share)
        corner = pl.multiple_of(owner * share + half, half)
        yield 0, batch[pl.ds(base, half), pl.ds(base, share)]
        low = batch[pl.ds(corner, half), pl.ds(corner, half)]
        yield starts[1], jnp.concatenate([low[0 : half // 2], low[half // 2 :]], axis=1)
        for start, step in zip(starts[2:], offsets()[1:]):
            row, col = shared_half(owner, step, share)
            yield start, batch[pl.ds(row, half), pl.ds(col, share)]

    store_chunk(pieces(3), length, (relay_x, 0), (relay_y, 0))
    store_chunk(pieces(along(0)), length, (direct_x, 0), (keep, 3 * length))
    store_chunk(pieces(along(1)), length, (keep, 2 * length), (direct_y, 0))
    store_chunk(pieces(0), length, (keep, 0), (keep, length))


def grad_kernel(replicas, tokens_all, acts, grads, send_x, send_y, keep, total):
    order = acts.shape[1]
    share = order // replicas
    strip = grads.shape[1] // replicas
    length = send_x.shape[0] // 2
    mine = lax.axis_index("dp")
    total[...] = lax.dot_general(
        grads[...], acts[...], (((0,), (0,)), ((), ())), preferred_element_type=F32
    ) * (1.0 / math.sqrt(tokens_all))

    def pieces(offset):
        rows = pl.ds(pl.multiple_of((mine ^ offset) * strip, strip), strip)
        for part in range(replicas):
            yield part * strip, total[rows, part * share : (part + 1) * share]

    store_chunk(pieces(3), length, (send_x, 0), (send_y, 0))
    store_chunk(pieces(along(0)), length, (send_x, length), (keep, 3 * length))
    store_chunk(pieces(along(1)), length, (keep, 2 * length), (send_y, length))
    store_chunk(pieces(0), length, (keep, 0), (keep, length))


def relay_kernel(keep, got_x, got_y, send_x, send_y):
    length = send_x.shape[0]
    send_y[...] = (keep[2 * length : 3 * length, :] + got_x[...].astype(F32)).astype(BF16)
    send_x[...] = (keep[3 * length :, :] + got_y[...].astype(F32)).astype(BF16)


def gather_kernel(keep, got_x, got_y, upper, lower, send_x, send_y):
    length = got_x.shape[0] // 2
    send_x[0 : upper.shape[0], :] = upper[...]
    send_x[upper.shape[0] :, :] = (keep[3 * length :, :] + got_y[0:length, :].astype(F32)).astype(BF16)
    send_y[0 : lower.shape[0], :] = lower[...]
    send_y[lower.shape[0] :, :] = (keep[2 * length : 3 * length, :] + got_x[0:length, :].astype(F32)).astype(BF16)


def halves_kernel(got_x, got_y, send_x, send_y):
    send_y[...] = got_x[0 : send_y.shape[0], :]
    send_x[...] = got_y[0 : send_x.shape[0], :]


def strip_kernel(keep, got_x, got_y, relay_x, relay_y, strip):
    length = got_x.shape[0] // 2
    first_x, first_y = relay_x.shape[0] - length, relay_y.shape[0] - length
    strip[0:length, :] = (
        keep[0:length, :] + got_x[length:, :].astype(F32) + relay_y[first_y:, :].astype(F32)
    ).astype(BF16)
    strip[length:, :] = (
        keep[length : 2 * length, :] + got_y[length:, :].astype(F32) + relay_x[first_x:, :].astype(F32)
    ).astype(BF16)


def factor_kernel(replicas, keep, direct_x, direct_y, relay_x, relay_y, old, upper, lower, exact):
    share, order = old.shape
    half = share // 2
    starts = chunk_rows(share)
    length = upper.shape[0]
    mine = lax.axis_index("dp")
    total = jnp.concatenate(
        [
            keep[0:length, :] + direct_x[...].astype(F32) + relay_y[...].astype(F32),
            keep[length : 2 * length, :] + direct_y[...].astype(F32) + relay_x[...].astype(F32),
        ],
        axis=0,
    )
    diagonal = old[:, pl.ds(pl.multiple_of(mine * share, share), share)]
    eye = eye_of(half, share)
    low_eye = eye_of(half, half)

    def packed(low):
        return jnp.concatenate([low[0 : half // 2], low[half // 2 :]], axis=1)

    terms = [
        DECAY * diagonal[0:half] + DAMPING * eye,
        packed(DECAY * diagonal[half:, half:] + DAMPING * low_eye),
    ]
    for step in offsets()[1:]:
        other = mine ^ step
        block = old[:, pl.ds(pl.multiple_of(other * share, share), share)]
        terms.append(DECAY * jnp.where(mine < other, block[0:half], block[:, half:].T))
    column = lax.broadcasted_iota(jnp.int32, (1, share), 1)
    squares = jnp.zeros((1, share), F32)
    values = []
    for position, (start, term) in enumerate(zip(starts, terms)):
        value = term + (1.0 - DECAY) * total[start : start + term.shape[0]]
        exact[start : start + term.shape[0], :] = value
        summed = jnp.sum(value * value, axis=0, keepdims=True)
        if position == 0:
            summed = jnp.where(column < half, summed, 2.0 * summed)
        squares = squares + (summed if position < 2 else 2.0 * summed)
        values.append(value.astype(BF16))
    high = squares.astype(BF16).astype(F32)
    middle = (squares - high).astype(BF16).astype(F32)
    rest = squares - high - middle
    spot = lax.broadcasted_iota(jnp.int32, (16, share), 0)
    digits = jnp.where(spot == 0, high, jnp.where(spot == 1, middle, jnp.where(spot == 2, rest, 0.0)))
    values.append(digits.astype(BF16))
    chunk = jnp.concatenate(values, axis=0)
    upper[...] = chunk[0:length]
    lower[...] = chunk[length:]


def root_kernel(count, exact, *rest):
    chunks = [rest[2 * i : 2 * i + 2] for i in range(4)]
    factor_out, root_out, finished, factor, diagonal, rows, sent = rest[8:]
    share, order = root_out.shape
    half = share // 2
    starts = chunk_rows(share)
    length = chunks[0][0].shape[0]
    mine = lax.axis_index("dp")

    def rows_of(position, start, count):
        upper, lower = chunks[position]
        if start + count <= length:
            return upper[start : start + count, :]
        if start >= length:
            return lower[start - length : start - length + count, :]
        return jnp.concatenate([upper[start:length, :], lower[0 : start + count - length, :]], axis=0)

    top = exact[0:half, :]
    low = exact[starts[1] : starts[2], :]
    low = jnp.concatenate([low[:, 0:half], low[:, half:]], axis=0)
    copies = []
    for position, step in enumerate(offsets()):
        other = mine ^ step
        target = rows.at[position]
        if position == 0:
            target[0:half, :] = top
            target[half:, :] = jnp.concatenate([top[:, half:].T, low], axis=1)
        else:
            start = starts[1 + position]
            own = exact[start : start + half, :]
            theirs = rows_of(position, start, half).astype(F32)

            @pl.when(mine < other)
            def _():
                target[0:half, :] = own
                target[half:, :] = theirs

            @pl.when(mine > other)
            def _():
                target[...] = jnp.concatenate([theirs.T, own.T], axis=1)

        columns = pl.ds(pl.multiple_of(other * share, share), share)
        copies.append(pltpu.make_async_copy(target, factor_out.at[:, columns], sent.at[position]))
        copies[-1].start()

    squares = jnp.zeros((16, share), F32)
    low_eye = eye_of(half, half)
    for position, offset in enumerate(offsets()):
        owner = mine ^ offset
        base = pl.multiple_of(owner * share, share)
        corner = pl.multiple_of(owner * share + half, half)
        top = rows_of(position, 0, half)
        low = rows_of(position, starts[1], half // 2)
        low = jnp.concatenate([low[:, 0:half], low[:, half:]], axis=0)
        factor[pl.ds(base, half), pl.ds(base, share)] = top
        factor[pl.ds(corner, half), pl.ds(base, half)] = transposed(top[:, half:])
        factor[pl.ds(corner, half), pl.ds(corner, half)] = low
        diagonal[:, pl.ds(base, half)] = jnp.sum(top[:, 0:half].astype(F32) * low_eye, axis=0, keepdims=True)
        diagonal[:, pl.ds(corner, half)] = jnp.sum(low.astype(F32) * low_eye, axis=0, keepdims=True)
        for start, step in zip(starts[2:], offsets()[1:]):
            row, col = shared_half(owner, step, share)
            block = rows_of(position, start, half)
            factor[pl.ds(row, half), pl.ds(col, share)] = block
            factor[pl.ds(col, share), pl.ds(row, half)] = transposed(block)
        squares = squares + rows_of(position, starts[-1], 16).astype(F32)

    scale = jnp.sqrt(jnp.sum(squares, keepdims=True) / order + EPSILON)
    inverse = 1.0 / scale
    ones = (diagonal[...] * inverse).astype(BF16).astype(F32)
    lift = (1.5 - 0.5 * ones).astype(BF16).astype(F32) + 0.5 * (diagonal[...] * inverse)
    eye = eye_of(share, order, mine * share)
    my_rows = pl.ds(pl.multiple_of(mine * share, share), share)
    first = (factor[my_rows, :].astype(F32) * inverse).astype(BF16).astype(F32)
    turn = (1.5 * eye - 0.5 * first).astype(BF16)
    second = (jnp.dot(turn, factor[...], preferred_element_type=F32) * inverse).astype(BF16)
    product = (-0.5 * inverse) * jnp.dot(second, factor[...], preferred_element_type=F32) + second.astype(F32) * lift
    turn_two = (1.5 * eye - 0.5 * product).astype(BF16)
    inverse_rows = (-0.5 * inverse) * jnp.dot(
        turn_two, factor[...], preferred_element_type=F32
    ) + turn_two.astype(F32) * lift
    chosen = jnp.where(count[0, 0] == 1, turn.astype(F32), inverse_rows)
    root_out[...] = (chosen * lax.rsqrt(scale)).astype(BF16)
    finished[...] = jnp.zeros_like(finished)
    for copy in copies:
        copy.wait()


def step_kernel(replicas, *refs):
    chunks = refs[:replicas]
    old_root, step_out, grads, result = refs[replicas:]
    share = old_root.shape[0]
    strip = step_out.shape[0] // replicas
    mine = lax.axis_index("dp")
    for offset, chunk in enumerate(chunks):
        for part in range(replicas):
            grads[offset * strip : (offset + 1) * strip, part * share : (part + 1) * share] = chunk[
                part * strip : (part + 1) * strip, :
            ]
    result[...] = lax.dot_general(
        grads[...], old_root[...], (((1,), (1,)), ((), ())), preferred_element_type=F32
    ).astype(BF16)
    for position, offset in enumerate(offsets()):
        rows = pl.ds(pl.multiple_of((mine ^ offset) * strip, strip), strip)
        step_out[rows, :] = result[position * strip : (position + 1) * strip, :]


def square_plan(acts, out_grad, old_factor, old_root, iter_count):
    replicas = lax.axis_size("dp")
    inputs = acts[0]
    tokens, order = inputs.shape
    share = order // replicas
    grows = out_grad.shape[2]
    params = pltpu.CompilerParams(vmem_limit_bytes=VMEM_LIMIT)
    whole_rows = chunk_rows(share)[-1]
    length = whole_rows // 2

    def shape(rows, kind=BF16, columns=share):
        return jax.ShapeDtypeStruct((rows, columns), kind)

    def call(kernel, outs, name, *operands, first=None, first_out=None, after=(), scratch=()):
        in_specs = whole(len(operands)) + [pl.BlockSpec(memory_space=pl.ANY)] * len(after)
        if first is not None:
            in_specs[0] = pl.BlockSpec(memory_space=first)
        out_specs = whole(len(outs))
        if first_out is not None:
            out_specs[0] = pl.BlockSpec(memory_space=first_out)

        def body(*refs):
            kernel(*refs[: len(operands)], *refs[len(operands) + len(after) :])

        return pl.pallas_call(
            body,
            out_shape=outs,
            in_specs=in_specs,
            out_specs=out_specs,
            scratch_shapes=scratch,
            compiler_params=params,
            name=name,
        )(*operands, *after)

    received = passed_along(out_grad, "pipe", -1)[0]
    relay_x, relay_y, direct_x, direct_y, keep = call(
        functools.partial(batch_kernel, replicas, tokens * replicas),
        [shape(length)] * 4 + [shape(4 * length, F32)],
        "batch",
        inputs,
        scratch=[pltpu.VMEM((order, order), F32)],
    )
    relay_x, relay_y = swapped(relay_x, 0), swapped(relay_y, 1)
    direct_x, direct_y = swapped(direct_x, 0), swapped(direct_y, 1)
    relay_x, relay_y = call(relay_kernel, [shape(length)] * 2, "relay", keep, relay_x, relay_y)
    grad_x, grad_y, grad_keep = call(
        functools.partial(grad_kernel, replicas, tokens * replicas),
        [shape(grows)] * 2 + [shape(2 * grows, F32)],
        "grad",
        inputs,
        received,
        after=[relay_x, relay_y],
        scratch=[pltpu.VMEM((grows, order), F32)],
    )
    relay_x, relay_y = swapped(relay_x, 0), swapped(relay_y, 1)
    grad_x, grad_y = swapped(grad_x, 0), swapped(grad_y, 1)
    upper, lower, exact = call(
        functools.partial(factor_kernel, replicas),
        [shape(length), shape(length + 16), shape(whole_rows, F32)],
        "factor",
        keep,
        direct_x,
        direct_y,
        relay_x,
        relay_y,
        old_factor[0, 0],
    )
    on_x, on_y = call(
        gather_kernel,
        [shape(length + grows // 2), shape(length + 16 + grows // 2)],
        "gather",
        grad_keep,
        grad_x,
        grad_y,
        upper,
        lower,
    )
    upper_x, lower_y = swapped(on_x, 0), swapped(on_y, 1)
    lower_x, upper_y = swapped(lower, 0), swapped(upper, 1)
    on_x, on_y = call(halves_kernel, [shape(length + 16), shape(length)], "halves", upper_x, lower_y)
    lower_far, upper_far = swapped(on_x, 0), swapped(on_y, 1)
    (strip,) = call(
        strip_kernel, [shape(grows)], "strip", grad_keep, grad_x, grad_y, upper_x, lower_y, after=[on_x]
    )
    strips = [strip, swapped(strip, 0), swapped(strip, 1), swapped_across(strip)]
    factor, root, finished = call(
        root_kernel,
        [shape(share, F32, order), shape(share, BF16, order), shape(8, F32, 128)],
        "root",
        iter_count,
        exact,
        upper,
        lower,
        upper_x,
        lower_x,
        upper_y,
        lower_y,
        upper_far,
        lower_far,
        first=pltpu.SMEM,
        first_out=pl.ANY,
        scratch=[
            pltpu.VMEM((order, order), BF16),
            pltpu.VMEM((1, order), F32),
            pltpu.VMEM((replicas, share, share), F32),
            pltpu.SemaphoreType.DMA((replicas,)),
        ],
    )
    (step,) = call(
        functools.partial(step_kernel, replicas),
        [shape(grows, BF16, share)],
        "step",
        *strips,
        old_root[0, 0],
        after=[finished],
        scratch=[pltpu.VMEM((grows, order), BF16), pltpu.VMEM((grows, share), BF16)],
    )
    return (factor[None, None], root[None, None], step[None, None])


def ring_plan(acts, out_grad, old_factor, old_root, iter_count):
    inputs = acts[0]
    replicas = lax.axis_size("dp")
    tokens_all = inputs.shape[0] * replicas
    order = inputs.shape[1]
    share = order // replicas
    offset = lax.axis_index("dp") * share
    received = passed_along(out_grad, "pipe", -1)[0]
    partial_grad = jnp.dot(received.T, inputs, preferred_element_type=F32) / math.sqrt(tokens_all)
    batch = lax.psum_scatter(
        jnp.dot(inputs.T, inputs, preferred_element_type=F32) / tokens_all,
        "dp",
        scatter_dimension=0,
        tiled=True,
    )
    eye_rows = eye_of(share, order, offset)
    factor = DECAY * old_factor[0, 0] + (1.0 - DECAY) * batch + DAMPING * eye_rows
    grad16 = lax.psum(partial_grad, "dp").astype(BF16)
    scale = jnp.sqrt(lax.psum(jnp.sum(factor * factor), "dp") / order + EPSILON)
    step = lax.dot_general(
        grad16, old_root[0, 0], (((1,), (1,)), ((), ())), preferred_element_type=F32
    ).astype(BF16)
    first = lax.all_gather((factor / scale).astype(BF16), "dp", axis=0, tiled=True)
    turn_one = (1.5 * eye_of(order, order) - 0.5 * first.astype(F32)).astype(BF16)
    turn_rows = lax.dynamic_slice_in_dim(turn_one, offset, share, 0)
    second = jnp.dot(turn_rows, first, preferred_element_type=F32).astype(BF16)
    product = jnp.dot(second, turn_one, preferred_element_type=F32)
    turn_two = (1.5 * eye_rows - 0.5 * product).astype(BF16)
    inverse_rows = jnp.dot(turn_two, turn_one, preferred_element_type=F32)
    chosen = jnp.where(iter_count[0, 0] == 1, turn_rows.astype(F32), inverse_rows)
    root = (chosen / jnp.sqrt(scale)).astype(BF16)
    return (factor[None, None], root[None, None], step[None, None])


def solution(mesh):
    return jax.shard_map(
        square_plan if mesh.shape["dp"] == 4 and mesh.shape["pipe"] == 2 else ring_plan,
        mesh=mesh,
        in_specs=(
            P("pipe", "dp", "tensor"),
            P("pipe", "dp", "tensor"),
            P("pipe", "tensor", "dp", None),
            P("pipe", "tensor", "dp", None),
            P("pipe", "tensor"),
        ),
        out_specs=(
            P("pipe", "tensor", "dp", None),
            P("pipe", "tensor", "dp", None),
            P("pipe", "tensor", None, "dp"),
        ),
        check_vma=False,
    )
```

```python
import functools
import math

import jax
import jax.numpy as jnp
from jax import lax
from jax.experimental import pallas as pl
from jax.experimental.pallas import tpu as pltpu
from jax.sharding import PartitionSpec as P

DECAY = 0.75
DAMPING = 0.1
EPSILON = 1e-06
BF16 = jnp.bfloat16
F32 = jnp.float32
VMEM_LIMIT = 28 * 1024 * 1024


def passed_along(block, axis, distance):
    devices = range(lax.axis_size(axis))
    route = [((i - distance) % len(devices), i) for i in devices]
    return lax.ppermute(block, axis, route)


def along(turn):
    return jnp.where(lax.axis_index("pipe") == turn, 1, 2)


def swapped(block, turn):
    replicas = lax.axis_size("dp")
    route = []
    for section in range(lax.axis_size("pipe")):
        offset = 1 if section == turn else 2
        route += [(section * replicas + i, section * replicas + (i ^ offset)) for i in range(replicas)]
    return lax.ppermute(block, ("pipe", "dp"), route)


def swapped_across(block):
    return lax.ppermute(block, "dp", [(i, i ^ 3) for i in range(lax.axis_size("dp"))])


def eye_of(rows, cols, shift=0):
    row_ids = lax.broadcasted_iota(jnp.int32, (rows, cols), 0) + shift
    col_ids = lax.broadcasted_iota(jnp.int32, (rows, cols), 1)
    return (row_ids == col_ids).astype(F32)


def whole(count):
    return [pl.BlockSpec(memory_space=pltpu.VMEM)] * count


def transposed(block):
    return block.astype(F32).T.astype(block.dtype)


def offsets():
    return 0, along(0), along(1), 3


def chunk_rows(share):
    half, packed = share // 2, 5 * share // 8
    return [0] + [packed + half * i for i in range(4)]


def packed_upper(block):
    quarter = block.shape[0] // 4
    column = lax.broadcasted_iota(jnp.int32, (quarter, 4 * quarter), 1)
    second = pltpu.roll(block[quarter : 2 * quarter], 3 * quarter, 1)
    third = block[2 * quarter : 3 * quarter, 2 * quarter :]
    return jnp.concatenate(
        [
            block[0:quarter],
            jnp.where(column < 3 * quarter, second, block[3 * quarter :]),
            jnp.concatenate([third[0 : quarter // 2], third[quarter // 2 :]], axis=1),
        ],
        axis=0,
    )


def unpacked(packed):
    share = packed.shape[1]
    quarter = share // 4
    column = lax.broadcasted_iota(jnp.int32, (quarter, share), 1)
    second = packed[quarter : 2 * quarter]
    third = packed[2 * quarter :]
    third = jnp.concatenate([third[:, 0 : 2 * quarter], third[:, 2 * quarter :]], axis=0)
    upper = jnp.concatenate(
        [
            packed[0:quarter],
            jnp.where(column < quarter, 0.0, pltpu.roll(second, quarter, 1)),
            jnp.concatenate([jnp.zeros((quarter, 2 * quarter), F32), third], axis=1),
            jnp.where(column < 3 * quarter, 0.0, second),
        ],
        axis=0,
    )
    rows = lax.broadcasted_iota(jnp.int32, (share, share), 0) // quarter
    columns = lax.broadcasted_iota(jnp.int32, (share, share), 1) // quarter
    return upper + jnp.where(rows == columns, 0.0, upper).T


def shared_half(owner, offset, share):
    other = owner ^ offset
    low, high = jnp.minimum(owner, other), jnp.maximum(owner, other)
    row = low * share + jnp.where(owner > other, share // 2, 0)
    return pl.multiple_of(row, share // 2), pl.multiple_of(high * share, share)


def store_chunk(pieces, length, upper, lower):
    for start, piece in pieces:
        stop = start + piece.shape[0]
        for target, low, high in ((upper, 0, length), (lower, length, stop)):
            first, last = max(start, low), min(stop, high)
            if target is not None and first < last:
                ref, at = target
                ref[at + first - low : at + last - low, :] = piece[first - start : last - start].astype(ref.dtype)


def batch_kernel(replicas, tokens_all, acts, relay_x, relay_y, direct_x, direct_y, keep, batch):
    order = acts.shape[1]
    share = order // replicas
    half = share // 2
    starts = chunk_rows(share)
    length = relay_x.shape[0]
    mine = lax.axis_index("dp")
    for i in range(replicas):
        band = slice(i * share, (i + 1) * share)
        batch[band, i * share :] = lax.dot_general(
            acts[:, band], acts[:, i * share :], (((0,), (0,)), ((), ())), preferred_element_type=F32
        ) * (1.0 / tokens_all)

    def pieces(offset):
        owner = mine ^ offset
        base = pl.multiple_of(owner * share, share)
        yield 0, packed_upper(batch[pl.ds(base, share), pl.ds(base, share)])
        for start, step in zip(starts[1:], offsets()[1:]):
            row, col = shared_half(owner, step, share)
            yield start, batch[pl.ds(row, half), pl.ds(col, share)]

    store_chunk(pieces(3), length, (relay_x, 0), (relay_y, 0))
    store_chunk(pieces(along(0)), length, (direct_x, 0), (keep, 3 * length))
    store_chunk(pieces(along(1)), length, (keep, 2 * length), (direct_y, 0))
    store_chunk(pieces(0), length, (keep, 0), (keep, length))


def grad_kernel(replicas, tokens_all, acts, grads, send_x, send_y, keep, total):
    order = acts.shape[1]
    share = order // replicas
    strip = grads.shape[1] // replicas
    length = send_x.shape[0] // 2
    mine = lax.axis_index("dp")
    total[...] = lax.dot_general(
        grads[...], acts[...], (((0,), (0,)), ((), ())), preferred_element_type=F32
    ) * (1.0 / math.sqrt(tokens_all))

    def pieces(offset):
        rows = pl.ds(pl.multiple_of((mine ^ offset) * strip, strip), strip)
        for part in range(replicas):
            yield part * strip, total[rows, part * share : (part + 1) * share]

    store_chunk(pieces(3), length, (send_x, 0), (send_y, 0))
    store_chunk(pieces(along(0)), length, (send_x, length), (keep, 3 * length))
    store_chunk(pieces(along(1)), length, (keep, 2 * length), (send_y, length))
    store_chunk(pieces(0), length, (keep, 0), (keep, length))


def relay_kernel(keep, got_x, got_y, send_x, send_y):
    length = send_x.shape[0]
    send_y[...] = (keep[2 * length : 3 * length, :] + got_x[...].astype(F32)).astype(BF16)
    send_x[...] = (keep[3 * length :, :] + got_y[...].astype(F32)).astype(BF16)


def grad_relay_kernel(keep, got_x, got_y, send_x, send_y):
    length = send_x.shape[0]
    send_y[...] = (keep[2 * length : 3 * length, :] + got_x[0:length, :].astype(F32)).astype(BF16)
    send_x[...] = (keep[3 * length :, :] + got_y[0:length, :].astype(F32)).astype(BF16)


def grad_total_kernel(keep, got_x, got_y, relay_x, relay_y, chunk):
    length = relay_x.shape[0]
    chunk[0:length, :] = (
        keep[0:length, :] + got_x[length:, :].astype(F32) + relay_y[...].astype(F32)
    ).astype(BF16)
    chunk[length:, :] = (
        keep[length : 2 * length, :] + got_y[length:, :].astype(F32) + relay_x[...].astype(F32)
    ).astype(BF16)


def factor_kernel(replicas, keep, direct_x, direct_y, relay_x, relay_y, old, upper, lower, exact):
    share, order = old.shape
    half = share // 2
    starts = chunk_rows(share)
    length = upper.shape[0]
    mine = lax.axis_index("dp")
    total = jnp.concatenate(
        [
            keep[0:length, :] + direct_x[...].astype(F32) + relay_y[...].astype(F32),
            keep[length : 2 * length, :] + direct_y[...].astype(F32) + relay_x[...].astype(F32),
        ],
        axis=0,
    )
    diagonal = old[:, pl.ds(pl.multiple_of(mine * share, share), share)]
    block_sum = unpacked(total[0 : starts[1]])
    value = DECAY * diagonal + (1.0 - DECAY) * block_sum + DAMPING * eye_of(share, share)
    exact[0:share, :] = value
    squares = jnp.sum(value * value, axis=0, keepdims=True)
    values = [packed_upper(value).astype(BF16)]
    for position, step in enumerate(offsets()[1:]):
        other = mine ^ step
        block = old[:, pl.ds(pl.multiple_of(other * share, share), share)]
        term = DECAY * jnp.where(mine < other, block[0:half], block[:, half:].T)
        start = starts[1 + position]
        value = term + (1.0 - DECAY) * total[start : start + half]
        exact[share + position * half : share + (position + 1) * half, :] = value
        squares = squares + 2.0 * jnp.sum(value * value, axis=0, keepdims=True)
        values.append(value.astype(BF16))
    high = squares.astype(BF16).astype(F32)
    middle = (squares - high).astype(BF16).astype(F32)
    rest = squares - high - middle
    spot = lax.broadcasted_iota(jnp.int32, (16, share), 0)
    digits = jnp.where(spot == 0, high, jnp.where(spot == 1, middle, jnp.where(spot == 2, rest, 0.0)))
    values.append(digits.astype(BF16))
    chunk = jnp.concatenate(values, axis=0)
    upper[...] = chunk[0:length]
    lower[...] = chunk[length:]


def root_kernel(count, exact, *rest):
    chunks = [rest[2 * i : 2 * i + 2] for i in range(4)]
    factor_out, root_out, finished, factor, diagonal, rows, sent = rest[8:]
    share, order = root_out.shape
    half = share // 2
    starts = chunk_rows(share)
    length = chunks[0][0].shape[0]
    mine = lax.axis_index("dp")

    def rows_of(position, start, count):
        upper, lower = chunks[position]
        if start + count <= length:
            return upper[start : start + count, :]
        if start >= length:
            return lower[start - length : start - length + count, :]
        return jnp.concatenate([upper[start:length, :], lower[0 : start + count - length, :]], axis=0)

    copies = []
    for position, step in enumerate(offsets()):
        other = mine ^ step
        target = rows.at[position]
        if position == 0:
            target[...] = exact[0:share, :]
        else:
            start = starts[position]
            own = exact[share + (position - 1) * half : share + position * half, :]
            theirs = rows_of(position, start, half).astype(F32)

            @pl.when(mine < other)
            def _():
                target[0:half, :] = own
                target[half:, :] = theirs

            @pl.when(mine > other)
            def _():
                target[...] = jnp.concatenate([theirs.T, own.T], axis=1)

        columns = pl.ds(pl.multiple_of(other * share, share), share)
        copies.append(pltpu.make_async_copy(target, factor_out.at[:, columns], sent.at[position]))
        copies[-1].start()

    squares = jnp.zeros((16, share), F32)
    block_eye = eye_of(share, share)
    for position, offset in enumerate(offsets()):
        owner = mine ^ offset
        own_band = pl.ds(pl.multiple_of(owner * share, share), share)
        block = unpacked(rows_of(position, 0, starts[1]).astype(F32))
        factor[own_band, own_band] = block.astype(BF16)
        diagonal[:, own_band] = jnp.sum(block * block_eye, axis=0, keepdims=True)
        for start, step in zip(starts[1:], offsets()[1:]):
            row, col = shared_half(owner, step, share)
            block = rows_of(position, start, half)
            factor[pl.ds(row, half), pl.ds(col, share)] = block
            factor[pl.ds(col, share), pl.ds(row, half)] = transposed(block)
        squares = squares + rows_of(position, starts[-1], 16).astype(F32)

    scale = jnp.sqrt(jnp.sum(squares, keepdims=True) / order + EPSILON)
    inverse = 1.0 / scale
    ones = (diagonal[...] * inverse).astype(BF16).astype(F32)
    lift = (1.5 - 0.5 * ones).astype(BF16).astype(F32) + 0.5 * (diagonal[...] * inverse)
    eye = eye_of(share, order, mine * share)
    my_rows = pl.ds(pl.multiple_of(mine * share, share), share)
    first = (factor[my_rows, :].astype(F32) * inverse).astype(BF16).astype(F32)
    turn = (1.5 * eye - 0.5 * first).astype(BF16)
    second = (jnp.dot(turn, factor[...], preferred_element_type=F32) * inverse).astype(BF16)
    product = (-0.5 * inverse) * jnp.dot(second, factor[...], preferred_element_type=F32) + second.astype(F32) * lift
    turn_two = (1.5 * eye - 0.5 * product).astype(BF16)
    inverse_rows = (-0.5 * inverse) * jnp.dot(
        turn_two, factor[...], preferred_element_type=F32
    ) + turn_two.astype(F32) * lift
    chosen = jnp.where(count[0, 0] == 1, turn.astype(F32), inverse_rows)
    root_out[...] = (chosen * lax.rsqrt(scale)).astype(BF16)
    finished[...] = jnp.zeros_like(finished)
    for copy in copies:
        copy.wait()


def step_kernel(replicas, *refs):
    chunks = refs[:replicas]
    old_root, step_out, grads, result = refs[replicas:]
    share = old_root.shape[0]
    strip = step_out.shape[0] // replicas
    mine = lax.axis_index("dp")
    for offset, chunk in enumerate(chunks):
        for part in range(replicas):
            grads[offset * strip : (offset + 1) * strip, part * share : (part + 1) * share] = chunk[
                part * strip : (part + 1) * strip, :
            ]
    result[...] = lax.dot_general(
        grads[...], old_root[...], (((1,), (1,)), ((), ())), preferred_element_type=F32
    ).astype(BF16)
    for position, offset in enumerate(offsets()):
        rows = pl.ds(pl.multiple_of((mine ^ offset) * strip, strip), strip)
        step_out[rows, :] = result[position * strip : (position + 1) * strip, :]


def square_plan(acts, out_grad, old_factor, old_root, iter_count):
    replicas = lax.axis_size("dp")
    inputs = acts[0]
    tokens, order = inputs.shape
    share = order // replicas
    grows = out_grad.shape[2]
    params = pltpu.CompilerParams(vmem_limit_bytes=VMEM_LIMIT)
    whole_rows = chunk_rows(share)[-1]
    length = whole_rows // 2

    def shape(rows, kind=BF16, columns=share):
        return jax.ShapeDtypeStruct((rows, columns), kind)

    def call(kernel, outs, name, *operands, first=None, first_out=None, after=(), scratch=()):
        in_specs = whole(len(operands)) + [pl.BlockSpec(memory_space=pl.ANY)] * len(after)
        if first is not None:
            in_specs[0] = pl.BlockSpec(memory_space=first)
        out_specs = whole(len(outs))
        if first_out is not None:
            out_specs[0] = pl.BlockSpec(memory_space=first_out)

        def body(*refs):
            kernel(*refs[: len(operands)], *refs[len(operands) + len(after) :])

        return pl.pallas_call(
            body,
            out_shape=outs,
            in_specs=in_specs,
            out_specs=out_specs,
            scratch_shapes=scratch,
            compiler_params=params,
            name=name,
        )(*operands, *after)

    received = passed_along(out_grad, "pipe", -1)[0]
    relay_x, relay_y, direct_x, direct_y, keep = call(
        functools.partial(batch_kernel, replicas, tokens * replicas),
        [shape(length)] * 4 + [shape(4 * length, F32)],
        "batch",
        inputs,
        scratch=[pltpu.VMEM((order, order), F32)],
    )
    relay_x, relay_y = swapped(relay_x, 0), swapped(relay_y, 1)
    direct_x, direct_y = swapped(direct_x, 0), swapped(direct_y, 1)
    relay_x, relay_y = call(relay_kernel, [shape(length)] * 2, "relay", keep, relay_x, relay_y)
    grad_x, grad_y, grad_keep = call(
        functools.partial(grad_kernel, replicas, tokens * replicas),
        [shape(grows)] * 2 + [shape(2 * grows, F32)],
        "grad",
        inputs,
        received,
        after=[relay_x, relay_y],
        scratch=[pltpu.VMEM((grows, order), F32)],
    )
    relay_x, relay_y = swapped(relay_x, 0), swapped(relay_y, 1)
    grad_x, grad_y = swapped(grad_x, 0), swapped(grad_y, 1)
    upper, lower, exact = call(
        functools.partial(factor_kernel, replicas),
        [shape(length), shape(length + 16), shape(5 * share // 2, F32)],
        "factor",
        keep,
        direct_x,
        direct_y,
        relay_x,
        relay_y,
        old_factor[0, 0],
    )
    upper_x, lower_y = swapped(upper, 0), swapped(lower, 1)
    lower_x, upper_y = swapped(lower, 0), swapped(upper, 1)
    strip_x, strip_y = call(
        grad_relay_kernel, [shape(grows // 2)] * 2, "grad_relay", grad_keep, grad_x, grad_y, after=[upper, lower]
    )
    strip_x, strip_y = swapped(strip_x, 0), swapped(strip_y, 1)
    upper_far, lower_far = swapped(upper_x, 1), swapped(lower_y, 0)
    (strip,) = call(
        grad_total_kernel,
        [shape(grows)],
        "grad_total",
        grad_keep,
        grad_x,
        grad_y,
        strip_x,
        strip_y,
        after=[lower_x, upper_y],
    )
    strips = [strip, swapped(strip, 0), swapped(strip, 1), swapped_across(strip)]
    factor, root, finished = call(
        root_kernel,
        [shape(share, F32, order), shape(share, BF16, order), shape(8, F32, 128)],
        "root",
        iter_count,
        exact,
        upper,
        lower,
        upper_x,
        lower_x,
        upper_y,
        lower_y,
        upper_far,
        lower_far,
        first=pltpu.SMEM,
        first_out=pl.ANY,
        scratch=[
            pltpu.VMEM((order, order), BF16),
            pltpu.VMEM((1, order), F32),
            pltpu.VMEM((replicas, share, share), F32),
            pltpu.SemaphoreType.DMA((replicas,)),
        ],
    )
    (step,) = call(
        functools.partial(step_kernel, replicas),
        [shape(grows, BF16, share)],
        "step",
        *strips,
        old_root[0, 0],
        after=[finished],
        scratch=[pltpu.VMEM((grows, order), BF16), pltpu.VMEM((grows, share), BF16)],
    )
    return (factor[None, None], root[None, None], step[None, None])


def ring_plan(acts, out_grad, old_factor, old_root, iter_count):
    inputs = acts[0]
    replicas = lax.axis_size("dp")
    tokens_all = inputs.shape[0] * replicas
    order = inputs.shape[1]
    share = order // replicas
    offset = lax.axis_index("dp") * share
    received = passed_along(out_grad, "pipe", -1)[0]
    partial_grad = jnp.dot(received.T, inputs, preferred_element_type=F32) / math.sqrt(tokens_all)
    batch = lax.psum_scatter(
        jnp.dot(inputs.T, inputs, preferred_element_type=F32) / tokens_all,
        "dp",
        scatter_dimension=0,
        tiled=True,
    )
    eye_rows = eye_of(share, order, offset)
    factor = DECAY * old_factor[0, 0] + (1.0 - DECAY) * batch + DAMPING * eye_rows
    grad16 = lax.psum(partial_grad, "dp").astype(BF16)
    scale = jnp.sqrt(lax.psum(jnp.sum(factor * factor), "dp") / order + EPSILON)
    step = lax.dot_general(
        grad16, old_root[0, 0], (((1,), (1,)), ((), ())), preferred_element_type=F32
    ).astype(BF16)
    first = lax.all_gather((factor / scale).astype(BF16), "dp", axis=0, tiled=True)
    turn_one = (1.5 * eye_of(order, order) - 0.5 * first.astype(F32)).astype(BF16)
    turn_rows = lax.dynamic_slice_in_dim(turn_one, offset, share, 0)
    second = jnp.dot(turn_rows, first, preferred_element_type=F32).astype(BF16)
    product = jnp.dot(second, turn_one, preferred_element_type=F32)
    turn_two = (1.5 * eye_rows - 0.5 * product).astype(BF16)
    inverse_rows = jnp.dot(turn_two, turn_one, preferred_element_type=F32)
    chosen = jnp.where(iter_count[0, 0] == 1, turn_rows.astype(F32), inverse_rows)
    root = (chosen / jnp.sqrt(scale)).astype(BF16)
    return (factor[None, None], root[None, None], step[None, None])


def solution(mesh):
    return jax.shard_map(
        square_plan if mesh.shape["dp"] == 4 and mesh.shape["pipe"] == 2 else ring_plan,
        mesh=mesh,
        in_specs=(
            P("pipe", "dp", "tensor"),
            P("pipe", "dp", "tensor"),
            P("pipe", "tensor", "dp", None),
            P("pipe", "tensor", "dp", None),
            P("pipe", "tensor"),
        ),
        out_specs=(
            P("pipe", "tensor", "dp", None),
            P("pipe", "tensor", "dp", None),
            P("pipe", "tensor", None, "dp"),
        ),
        check_vma=False,
    )
```

```python
import functools
import math

import jax
import jax.numpy as jnp
from jax import lax
from jax.experimental import pallas as pl
from jax.experimental.pallas import tpu as pltpu
from jax.sharding import PartitionSpec as P

DECAY = 0.75
DAMPING = 0.1
EPSILON = 1e-06
BF16 = jnp.bfloat16
F32 = jnp.float32
VMEM_LIMIT = 28 * 1024 * 1024


def passed_along(block, axis, distance):
    devices = range(lax.axis_size(axis))
    route = [((i - distance) % len(devices), i) for i in devices]
    return lax.ppermute(block, axis, route)


def along(turn):
    return jnp.where(lax.axis_index("pipe") == turn, 1, 2)


def swapped(block, turn):
    replicas = lax.axis_size("dp")
    route = []
    for section in range(lax.axis_size("pipe")):
        offset = 1 if section == turn else 2
        route += [(section * replicas + i, section * replicas + (i ^ offset)) for i in range(replicas)]
    return lax.ppermute(block, ("pipe", "dp"), route)


def swapped_across(block):
    return lax.ppermute(block, "dp", [(i, i ^ 3) for i in range(lax.axis_size("dp"))])


def eye_of(rows, cols, shift=0):
    row_ids = lax.broadcasted_iota(jnp.int32, (rows, cols), 0) + shift
    col_ids = lax.broadcasted_iota(jnp.int32, (rows, cols), 1)
    return (row_ids == col_ids).astype(F32)


def whole(count):
    return [pl.BlockSpec(memory_space=pltpu.VMEM)] * count


def transposed(block):
    return block.astype(F32).T.astype(block.dtype)


def offsets():
    return 0, along(0), along(1), 3


def chunk_rows(share):
    half, packed = share // 2, 5 * share // 8
    return [0] + [packed + half * i for i in range(4)]


def packed_upper(block):
    quarter = block.shape[0] // 4
    column = lax.broadcasted_iota(jnp.int32, (quarter, 4 * quarter), 1)
    second = pltpu.roll(block[quarter : 2 * quarter], 3 * quarter, 1)
    third = block[2 * quarter : 3 * quarter, 2 * quarter :]
    return jnp.concatenate(
        [
            block[0:quarter],
            jnp.where(column < 3 * quarter, second, block[3 * quarter :]),
            jnp.concatenate([third[0 : quarter // 2], third[quarter // 2 :]], axis=1),
        ],
        axis=0,
    )


def unpacked(packed):
    share = packed.shape[1]
    quarter = share // 4
    column = lax.broadcasted_iota(jnp.int32, (quarter, share), 1)
    second = packed[quarter : 2 * quarter]
    third = packed[2 * quarter :]
    third = jnp.concatenate([third[:, 0 : 2 * quarter], third[:, 2 * quarter :]], axis=0)
    upper = jnp.concatenate(
        [
            packed[0:quarter],
            jnp.where(column < quarter, 0.0, pltpu.roll(second, quarter, 1)),
            jnp.concatenate([jnp.zeros((quarter, 2 * quarter), F32), third], axis=1),
            jnp.where(column < 3 * quarter, 0.0, second),
        ],
        axis=0,
    )
    rows = lax.broadcasted_iota(jnp.int32, (share, share), 0) // quarter
    columns = lax.broadcasted_iota(jnp.int32, (share, share), 1) // quarter
    return upper + jnp.where(rows == columns, 0.0, upper).T


def shared_half(owner, offset, share):
    other = owner ^ offset
    low, high = jnp.minimum(owner, other), jnp.maximum(owner, other)
    row = low * share + jnp.where(owner > other, share // 2, 0)
    return pl.multiple_of(row, share // 2), pl.multiple_of(high * share, share)


def store_chunk(pieces, length, upper, lower):
    for start, piece in pieces:
        stop = start + piece.shape[0]
        for target, low, high in ((upper, 0, length), (lower, length, stop)):
            first, last = max(start, low), min(stop, high)
            if target is not None and first < last:
                ref, at = target
                ref[at + first - low : at + last - low, :] = piece[first - start : last - start].astype(ref.dtype)


def batch_kernel(replicas, tokens_all, acts, relay_x, relay_y, direct_x, direct_y, keep, batch):
    order = acts.shape[1]
    share = order // replicas
    half = share // 2
    starts = chunk_rows(share)
    length = relay_x.shape[0]
    mine = lax.axis_index("dp")
    for i in range(replicas):
        band = slice(i * share, (i + 1) * share)
        batch[band, i * share :] = lax.dot_general(
            acts[:, band], acts[:, i * share :], (((0,), (0,)), ((), ())), preferred_element_type=F32
        ) * (1.0 / tokens_all)

    def pieces(offset):
        owner = mine ^ offset
        base = pl.multiple_of(owner * share, share)
        yield 0, packed_upper(batch[pl.ds(base, share), pl.ds(base, share)])
        for start, step in zip(starts[1:], offsets()[1:]):
            row, col = shared_half(owner, step, share)
            yield start, batch[pl.ds(row, half), pl.ds(col, share)]

    store_chunk(pieces(3), length, (relay_x, 0), (relay_y, 0))
    store_chunk(pieces(along(0)), length, (direct_x, 0), (keep, 3 * length))
    store_chunk(pieces(along(1)), length, (keep, 2 * length), (direct_y, 0))
    store_chunk(pieces(0), length, (keep, 0), (keep, length))


def grad_kernel(replicas, tokens_all, acts, grads, send_x, send_y, keep, total):
    order = acts.shape[1]
    share = order // replicas
    strip = grads.shape[1] // replicas
    length = send_x.shape[0] // 2
    mine = lax.axis_index("dp")
    total[...] = lax.dot_general(
        grads[...], acts[...], (((0,), (0,)), ((), ())), preferred_element_type=F32
    ) * (1.0 / math.sqrt(tokens_all))

    def pieces(offset):
        rows = pl.ds(pl.multiple_of((mine ^ offset) * strip, strip), strip)
        for part in range(replicas):
            yield part * strip, total[rows, part * share : (part + 1) * share]

    store_chunk(pieces(3), length, (send_x, 0), (send_y, 0))
    store_chunk(pieces(along(0)), length, (send_x, length), (keep, 3 * length))
    store_chunk(pieces(along(1)), length, (keep, 2 * length), (send_y, length))
    store_chunk(pieces(0), length, (keep, 0), (keep, length))


def relay_kernel(keep, got_x, got_y, send_x, send_y):
    length = send_x.shape[0]
    send_y[...] = (keep[2 * length : 3 * length, :] + got_x[...].astype(F32)).astype(BF16)
    send_x[...] = (keep[3 * length :, :] + got_y[...].astype(F32)).astype(BF16)


def grad_relay_kernel(keep, got_x, got_y, send_x, send_y):
    length = send_x.shape[0]
    send_y[...] = (keep[2 * length : 3 * length, :] + got_x[0:length, :].astype(F32)).astype(BF16)
    send_x[...] = (keep[3 * length :, :] + got_y[0:length, :].astype(F32)).astype(BF16)


def grad_total_kernel(keep, got_x, got_y, relay_x, relay_y, chunk):
    length = relay_x.shape[0]
    chunk[0:length, :] = (
        keep[0:length, :] + got_x[length:, :].astype(F32) + relay_y[...].astype(F32)
    ).astype(BF16)
    chunk[length:, :] = (
        keep[length : 2 * length, :] + got_y[length:, :].astype(F32) + relay_x[...].astype(F32)
    ).astype(BF16)


def factor_kernel(replicas, keep, direct_x, direct_y, relay_x, relay_y, old, upper, lower, exact):
    share, order = old.shape
    half = share // 2
    starts = chunk_rows(share)
    length = upper.shape[0]
    mine = lax.axis_index("dp")
    total = jnp.concatenate(
        [
            keep[0:length, :] + direct_x[...].astype(F32) + relay_y[...].astype(F32),
            keep[length : 2 * length, :] + direct_y[...].astype(F32) + relay_x[...].astype(F32),
        ],
        axis=0,
    )
    diagonal = old[:, pl.ds(pl.multiple_of(mine * share, share), share)]
    block_sum = unpacked(total[0 : starts[1]])
    value = DECAY * diagonal + (1.0 - DECAY) * block_sum + DAMPING * eye_of(share, share)
    exact[0:share, :] = value
    squares = jnp.sum(value * value, axis=0, keepdims=True)
    values = [packed_upper(value).astype(BF16)]
    for position, step in enumerate(offsets()[1:]):
        other = mine ^ step
        block = old[:, pl.ds(pl.multiple_of(other * share, share), share)]
        term = DECAY * jnp.where(mine < other, block[0:half], block[:, half:].T)
        start = starts[1 + position]
        value = term + (1.0 - DECAY) * total[start : start + half]
        exact[share + position * half : share + (position + 1) * half, :] = value
        squares = squares + 2.0 * jnp.sum(value * value, axis=0, keepdims=True)
        values.append(value.astype(BF16))
    high = squares.astype(BF16).astype(F32)
    middle = (squares - high).astype(BF16).astype(F32)
    rest = squares - high - middle
    spot = lax.broadcasted_iota(jnp.int32, (16, share), 0)
    digits = jnp.where(spot == 0, high, jnp.where(spot == 1, middle, jnp.where(spot == 2, rest, 0.0)))
    values.append(digits.astype(BF16))
    chunk = jnp.concatenate(values, axis=0)
    upper[...] = chunk[0:length]
    lower[...] = chunk[length:]


def root_kernel(count, exact, *rest):
    chunks = [rest[2 * i : 2 * i + 2] for i in range(4)]
    factor_out, root_out, finished, factor, diagonal, rows, sent = rest[8:]
    share, order = root_out.shape
    half = share // 2
    starts = chunk_rows(share)
    length = chunks[0][0].shape[0]
    mine = lax.axis_index("dp")

    def rows_of(position, start, count):
        upper, lower = chunks[position]
        if start + count <= length:
            return upper[start : start + count, :]
        if start >= length:
            return lower[start - length : start - length + count, :]
        return jnp.concatenate([upper[start:length, :], lower[0 : start + count - length, :]], axis=0)

    copies = []
    for position, step in enumerate(offsets()):
        other = mine ^ step
        target = rows.at[position]
        if position == 0:
            target[...] = exact[0:share, :]
        else:
            start = starts[position]
            own = exact[share + (position - 1) * half : share + position * half, :]
            theirs = rows_of(position, start, half).astype(F32)

            @pl.when(mine < other)
            def _():
                target[0:half, :] = own
                target[half:, :] = theirs

            @pl.when(mine > other)
            def _():
                target[...] = jnp.concatenate([theirs.T, own.T], axis=1)

        columns = pl.ds(pl.multiple_of(other * share, share), share)
        copies.append(pltpu.make_async_copy(target, factor_out.at[:, columns], sent.at[position]))
        copies[-1].start()

    squares = jnp.zeros((16, share), F32)
    block_eye = eye_of(share, share)
    for position, offset in enumerate(offsets()):
        owner = mine ^ offset
        own_band = pl.ds(pl.multiple_of(owner * share, share), share)
        block = unpacked(rows_of(position, 0, starts[1]).astype(F32))
        factor[own_band, own_band] = block.astype(BF16)
        diagonal[:, own_band] = jnp.sum(block * block_eye, axis=0, keepdims=True)
        for start, step in zip(starts[1:], offsets()[1:]):
            row, col = shared_half(owner, step, share)
            block = rows_of(position, start, half)
            factor[pl.ds(row, half), pl.ds(col, share)] = block
            factor[pl.ds(col, share), pl.ds(row, half)] = transposed(block)
        squares = squares + rows_of(position, starts[-1], 16).astype(F32)

    scale = jnp.sqrt(jnp.sum(squares, keepdims=True) / order + EPSILON)
    inverse = 1.0 / scale
    ones = (diagonal[...] * inverse).astype(BF16).astype(F32)
    lift = (1.5 - 0.5 * ones).astype(BF16).astype(F32) + 0.5 * (diagonal[...] * inverse)
    eye = eye_of(share, order, mine * share)
    my_rows = pl.ds(pl.multiple_of(mine * share, share), share)
    first = (factor[my_rows, :].astype(F32) * inverse).astype(BF16).astype(F32)
    turn = (1.5 * eye - 0.5 * first).astype(BF16)
    second = (jnp.dot(turn, factor[...], preferred_element_type=F32) * inverse).astype(BF16)
    product = (-0.5 * inverse) * jnp.dot(second, factor[...], preferred_element_type=F32) + second.astype(F32) * lift
    turn_two = (1.5 * eye - 0.5 * product).astype(BF16)
    inverse_rows = (-0.5 * inverse) * jnp.dot(
        turn_two, factor[...], preferred_element_type=F32
    ) + turn_two.astype(F32) * lift
    chosen = jnp.where(count[0, 0] == 1, turn.astype(F32), inverse_rows)
    root_out[...] = (chosen * lax.rsqrt(scale)).astype(BF16)
    finished[...] = jnp.zeros_like(finished)
    for copy in copies:
        copy.wait()


def step_kernel(replicas, *refs):
    chunks = refs[:replicas]
    old_root, step_out, grads, result = refs[replicas:]
    share = old_root.shape[0]
    strip = step_out.shape[0] // replicas
    mine = lax.axis_index("dp")
    for offset, chunk in enumerate(chunks):
        for part in range(replicas):
            grads[offset * strip : (offset + 1) * strip, part * share : (part + 1) * share] = chunk[
                part * strip : (part + 1) * strip, :
            ]
    result[...] = lax.dot_general(
        grads[...], old_root[...], (((1,), (1,)), ((), ())), preferred_element_type=F32
    ).astype(BF16)
    for position, offset in enumerate(offsets()):
        rows = pl.ds(pl.multiple_of((mine ^ offset) * strip, strip), strip)
        step_out[rows, :] = result[position * strip : (position + 1) * strip, :]


def square_plan(acts, out_grad, old_factor, old_root, iter_count):
    replicas = lax.axis_size("dp")
    inputs = acts[0]
    tokens, order = inputs.shape
    share = order // replicas
    grows = out_grad.shape[2]
    params = pltpu.CompilerParams(vmem_limit_bytes=VMEM_LIMIT)
    whole_rows = chunk_rows(share)[-1]
    length = whole_rows // 2

    def shape(rows, kind=BF16, columns=share):
        return jax.ShapeDtypeStruct((rows, columns), kind)

    def call(kernel, outs, name, *operands, first=None, first_out=None, after=(), scratch=()):
        in_specs = whole(len(operands)) + [pl.BlockSpec(memory_space=pl.ANY)] * len(after)
        if first is not None:
            in_specs[0] = pl.BlockSpec(memory_space=first)
        out_specs = whole(len(outs))
        if first_out is not None:
            out_specs[0] = pl.BlockSpec(memory_space=first_out)

        def body(*refs):
            kernel(*refs[: len(operands)], *refs[len(operands) + len(after) :])

        return pl.pallas_call(
            body,
            out_shape=outs,
            in_specs=in_specs,
            out_specs=out_specs,
            scratch_shapes=scratch,
            compiler_params=params,
            name=name,
        )(*operands, *after)

    received = passed_along(out_grad, "pipe", -1)[0]
    relay_x, relay_y, direct_x, direct_y, keep = call(
        functools.partial(batch_kernel, replicas, tokens * replicas),
        [shape(length)] * 4 + [shape(4 * length, F32)],
        "batch",
        inputs,
        scratch=[pltpu.VMEM((order, order), F32)],
    )
    relay_x, relay_y = swapped(relay_x, 0), swapped(relay_y, 1)
    direct_x, direct_y = swapped(direct_x, 0), swapped(direct_y, 1)
    relay_x, relay_y = call(relay_kernel, [shape(length)] * 2, "relay", keep, relay_x, relay_y)
    grad_x, grad_y, grad_keep = call(
        functools.partial(grad_kernel, replicas, tokens * replicas),
        [shape(grows)] * 2 + [shape(2 * grows, F32)],
        "grad",
        inputs,
        received,
        scratch=[pltpu.VMEM((grows, order), F32)],
    )
    relay_x, relay_y = swapped(relay_x, 0), swapped(relay_y, 1)
    grad_x, grad_y = swapped(grad_x, 0), swapped(grad_y, 1)
    strip_x, strip_y = call(
        grad_relay_kernel, [shape(grows // 2)] * 2, "grad_relay", grad_keep, grad_x, grad_y
    )
    strip_x, strip_y = swapped(strip_x, 0), swapped(strip_y, 1)
    upper, lower, exact = call(
        functools.partial(factor_kernel, replicas),
        [shape(length), shape(length + 16), shape(5 * share // 2, F32)],
        "factor",
        keep,
        direct_x,
        direct_y,
        relay_x,
        relay_y,
        old_factor[0, 0],
        after=[strip_x, strip_y],
    )
    upper_x, lower_y = swapped(upper, 0), swapped(lower, 1)
    lower_x, upper_y = swapped(lower, 0), swapped(upper, 1)
    upper_far, lower_far = swapped(upper_x, 1), swapped(lower_y, 0)
    (strip,) = call(
        grad_total_kernel,
        [shape(grows)],
        "grad_total",
        grad_keep,
        grad_x,
        grad_y,
        strip_x,
        strip_y,
        after=[upper_x, lower_y],
    )
    strips = [strip, swapped(strip, 0), swapped(strip, 1), swapped_across(strip)]
    factor, root, finished = call(
        root_kernel,
        [shape(share, F32, order), shape(share, BF16, order), shape(8, F32, 128)],
        "root",
        iter_count,
        exact,
        upper,
        lower,
        upper_x,
        lower_x,
        upper_y,
        lower_y,
        upper_far,
        lower_far,
        first=pltpu.SMEM,
        first_out=pl.ANY,
        scratch=[
            pltpu.VMEM((order, order), BF16),
            pltpu.VMEM((1, order), F32),
            pltpu.VMEM((replicas, share, share), F32),
            pltpu.SemaphoreType.DMA((replicas,)),
        ],
    )
    (step,) = call(
        functools.partial(step_kernel, replicas),
        [shape(grows, BF16, share)],
        "step",
        *strips,
        old_root[0, 0],
        after=[finished],
        scratch=[pltpu.VMEM((grows, order), BF16), pltpu.VMEM((grows, share), BF16)],
    )
    return (factor[None, None], root[None, None], step[None, None])


def ring_plan(acts, out_grad, old_factor, old_root, iter_count):
    inputs = acts[0]
    replicas = lax.axis_size("dp")
    tokens_all = inputs.shape[0] * replicas
    order = inputs.shape[1]
    share = order // replicas
    offset = lax.axis_index("dp") * share
    received = passed_along(out_grad, "pipe", -1)[0]
    partial_grad = jnp.dot(received.T, inputs, preferred_element_type=F32) / math.sqrt(tokens_all)
    batch = lax.psum_scatter(
        jnp.dot(inputs.T, inputs, preferred_element_type=F32) / tokens_all,
        "dp",
        scatter_dimension=0,
        tiled=True,
    )
    eye_rows = eye_of(share, order, offset)
    factor = DECAY * old_factor[0, 0] + (1.0 - DECAY) * batch + DAMPING * eye_rows
    grad16 = lax.psum(partial_grad, "dp").astype(BF16)
    scale = jnp.sqrt(lax.psum(jnp.sum(factor * factor), "dp") / order + EPSILON)
    step = lax.dot_general(
        grad16, old_root[0, 0], (((1,), (1,)), ((), ())), preferred_element_type=F32
    ).astype(BF16)
    first = lax.all_gather((factor / scale).astype(BF16), "dp", axis=0, tiled=True)
    turn_one = (1.5 * eye_of(order, order) - 0.5 * first.astype(F32)).astype(BF16)
    turn_rows = lax.dynamic_slice_in_dim(turn_one, offset, share, 0)
    second = jnp.dot(turn_rows, first, preferred_element_type=F32).astype(BF16)
    product = jnp.dot(second, turn_one, preferred_element_type=F32)
    turn_two = (1.5 * eye_rows - 0.5 * product).astype(BF16)
    inverse_rows = jnp.dot(turn_two, turn_one, preferred_element_type=F32)
    chosen = jnp.where(iter_count[0, 0] == 1, turn_rows.astype(F32), inverse_rows)
    root = (chosen / jnp.sqrt(scale)).astype(BF16)
    return (factor[None, None], root[None, None], step[None, None])


def solution(mesh):
    return jax.shard_map(
        square_plan if mesh.shape["dp"] == 4 and mesh.shape["pipe"] == 2 else ring_plan,
        mesh=mesh,
        in_specs=(
            P("pipe", "dp", "tensor"),
            P("pipe", "dp", "tensor"),
            P("pipe", "tensor", "dp", None),
            P("pipe", "tensor", "dp", None),
            P("pipe", "tensor"),
        ),
        out_specs=(
            P("pipe", "tensor", "dp", None),
            P("pipe", "tensor", "dp", None),
            P("pipe", "tensor", None, "dp"),
        ),
        check_vma=False,
    )
```

```python
import functools
import math

import jax
import jax.numpy as jnp
from jax import lax
from jax.experimental import pallas as pl
from jax.experimental.pallas import tpu as pltpu
from jax.sharding import PartitionSpec as P

DECAY = 0.75
DAMPING = 0.1
EPSILON = 1e-06
BF16 = jnp.bfloat16
F32 = jnp.float32
VMEM_LIMIT = 28 * 1024 * 1024


def passed_along(block, axis, distance):
    devices = range(lax.axis_size(axis))
    route = [((i - distance) % len(devices), i) for i in devices]
    return lax.ppermute(block, axis, route)


def along(turn):
    return jnp.where(lax.axis_index("pipe") == turn, 1, 2)


def swapped(block, turn):
    replicas = lax.axis_size("dp")
    route = []
    for section in range(lax.axis_size("pipe")):
        offset = 1 if section == turn else 2
        route += [(section * replicas + i, section * replicas + (i ^ offset)) for i in range(replicas)]
    return lax.ppermute(block, ("pipe", "dp"), route)


def eye_of(rows, cols, shift=0):
    row_ids = lax.broadcasted_iota(jnp.int32, (rows, cols), 0) + shift
    col_ids = lax.broadcasted_iota(jnp.int32, (rows, cols), 1)
    return (row_ids == col_ids).astype(F32)


def whole(count):
    return [pl.BlockSpec(memory_space=pltpu.VMEM)] * count


def transposed(block):
    return block.astype(F32).T.astype(block.dtype)


def offsets():
    return 0, along(0), along(1), 3


def chunk_rows(share):
    half, packed = share // 2, 5 * share // 8
    return [0] + [packed + half * i for i in range(4)]


def packed_upper(block):
    quarter = block.shape[0] // 4
    column = lax.broadcasted_iota(jnp.int32, (quarter, 4 * quarter), 1)
    second = pltpu.roll(block[quarter : 2 * quarter], 3 * quarter, 1)
    third = block[2 * quarter : 3 * quarter, 2 * quarter :]
    return jnp.concatenate(
        [
            block[0:quarter],
            jnp.where(column < 3 * quarter, second, block[3 * quarter :]),
            jnp.concatenate([third[0 : quarter // 2], third[quarter // 2 :]], axis=1),
        ],
        axis=0,
    )


def unpacked(packed):
    share = packed.shape[1]
    quarter = share // 4
    column = lax.broadcasted_iota(jnp.int32, (quarter, share), 1)
    second = packed[quarter : 2 * quarter]
    third = packed[2 * quarter :]
    third = jnp.concatenate([third[:, 0 : 2 * quarter], third[:, 2 * quarter :]], axis=0)
    upper = jnp.concatenate(
        [
            packed[0:quarter],
            jnp.where(column < quarter, 0.0, pltpu.roll(second, quarter, 1)),
            jnp.concatenate([jnp.zeros((quarter, 2 * quarter), F32), third], axis=1),
            jnp.where(column < 3 * quarter, 0.0, second),
        ],
        axis=0,
    )
    rows = lax.broadcasted_iota(jnp.int32, (share, share), 0) // quarter
    columns = lax.broadcasted_iota(jnp.int32, (share, share), 1) // quarter
    return upper + jnp.where(rows == columns, 0.0, upper).T


def shared_half(owner, offset, share):
    other = owner ^ offset
    low, high = jnp.minimum(owner, other), jnp.maximum(owner, other)
    row = low * share + jnp.where(owner > other, share // 2, 0)
    return pl.multiple_of(row, share // 2), pl.multiple_of(high * share, share)


def store_chunk(pieces, length, upper, lower):
    for start, piece in pieces:
        stop = start + piece.shape[0]
        for target, low, high in ((upper, 0, length), (lower, length, stop)):
            first, last = max(start, low), min(stop, high)
            if target is not None and first < last:
                ref, at = target
                ref[at + first - low : at + last - low, :] = piece[first - start : last - start].astype(ref.dtype)


def batch_kernel(replicas, tokens_all, acts, relay_x, relay_y, direct_x, direct_y, keep, batch):
    order = acts.shape[1]
    share = order // replicas
    half = share // 2
    starts = chunk_rows(share)
    length = relay_x.shape[0]
    mine = lax.axis_index("dp")
    for i in range(replicas):
        band = slice(i * share, (i + 1) * share)
        batch[band, i * share :] = lax.dot_general(
            acts[:, band], acts[:, i * share :], (((0,), (0,)), ((), ())), preferred_element_type=F32
        ) * (1.0 / tokens_all)

    def pieces(offset):
        owner = mine ^ offset
        base = pl.multiple_of(owner * share, share)
        yield 0, packed_upper(batch[pl.ds(base, share), pl.ds(base, share)])
        for start, step in zip(starts[1:], offsets()[1:]):
            row, col = shared_half(owner, step, share)
            yield start, batch[pl.ds(row, half), pl.ds(col, share)]

    store_chunk(pieces(3), length, (relay_x, 0), (relay_y, 0))
    store_chunk(pieces(along(0)), length, (direct_x, 0), (keep, 3 * length))
    store_chunk(pieces(along(1)), length, (keep, 2 * length), (direct_y, 0))
    store_chunk(pieces(0), length, (keep, 0), (keep, length))


def band(index, size):
    return pl.ds(pl.multiple_of(index * size, size), size)


def grad_kernel(replicas, tokens_all, acts, grads, send, keep, total):
    share = acts.shape[1] // replicas
    strip = grads.shape[1] // replicas
    mine = lax.axis_index("dp")
    total[...] = lax.dot_general(grads[...], acts[...], (((0,), (0,)), ((), ())), preferred_element_type=F32) * (
        1.0 / math.sqrt(tokens_all)
    )
    for ref, offsets in ((send, (along(0), 3)), (keep, (0, along(1)))):
        for i, offset in enumerate(offsets):
            for part in range(replicas):
                start = (i * replicas + part) * strip
                piece = total[band(mine ^ offset, strip), part * share : (part + 1) * share]
                ref[start : start + strip, :] = piece.astype(ref.dtype)


def relay_kernel(keep, got_x, got_y, send_x, send_y):
    length = send_x.shape[0]
    send_y[...] = (keep[2 * length : 3 * length, :] + got_x[...].astype(F32)).astype(BF16)
    send_x[...] = (keep[3 * length :, :] + got_y[...].astype(F32)).astype(BF16)


def strip_relay_kernel(keep, got, send):
    length = send.shape[0]
    send[...] = (keep[length:, :] + got[length:, :].astype(F32)).astype(BF16)


def strip_kernel(keep, got, relayed, strip):
    length = strip.shape[0]
    strip[...] = (keep[0:length, :] + got[0:length, :].astype(F32) + relayed[...].astype(F32)).astype(BF16)


def pair_kernel(own, got, send):
    length = own.shape[0]
    send[0:length, :] = own[...]
    send[length:, :] = got[...]


def factor_kernel(replicas, keep, direct_x, direct_y, relay_x, relay_y, old, upper, lower, exact):
    share, order = old.shape
    half = share // 2
    starts = chunk_rows(share)
    length = upper.shape[0]
    mine = lax.axis_index("dp")
    total = jnp.concatenate(
        [
            keep[0:length, :] + direct_x[...].astype(F32) + relay_y[...].astype(F32),
            keep[length : 2 * length, :] + direct_y[...].astype(F32) + relay_x[...].astype(F32),
        ],
        axis=0,
    )
    diagonal = old[:, pl.ds(pl.multiple_of(mine * share, share), share)]
    block_sum = unpacked(total[0 : starts[1]])
    value = DECAY * diagonal + (1.0 - DECAY) * block_sum + DAMPING * eye_of(share, share)
    exact[0:share, :] = value
    squares = jnp.sum(value * value, axis=0, keepdims=True)
    values = [packed_upper(value).astype(BF16)]
    for position, step in enumerate(offsets()[1:]):
        other = mine ^ step
        block = old[:, pl.ds(pl.multiple_of(other * share, share), share)]
        term = DECAY * jnp.where(mine < other, block[0:half], block[:, half:].T)
        start = starts[1 + position]
        value = term + (1.0 - DECAY) * total[start : start + half]
        exact[share + position * half : share + (position + 1) * half, :] = value
        squares = squares + 2.0 * jnp.sum(value * value, axis=0, keepdims=True)
        values.append(value.astype(BF16))
    high = squares.astype(BF16).astype(F32)
    middle = (squares - high).astype(BF16).astype(F32)
    rest = squares - high - middle
    spot = lax.broadcasted_iota(jnp.int32, (16, share), 0)
    digits = jnp.where(spot == 0, high, jnp.where(spot == 1, middle, jnp.where(spot == 2, rest, 0.0)))
    values.append(digits.astype(BF16))
    chunk = jnp.concatenate(values, axis=0)
    upper[...] = chunk[0:length]
    lower[...] = chunk[length:]


def root_kernel(count, exact, *rest):
    chunks = [rest[2 * i : 2 * i + 2] for i in range(4)]
    factor_out, root_out, finished, factor, diagonal, rows, sent = rest[8:]
    share, order = root_out.shape
    half = share // 2
    starts = chunk_rows(share)
    length = chunks[0][0].shape[0]
    mine = lax.axis_index("dp")

    def rows_of(position, start, count):
        upper, lower = chunks[position]
        if start + count <= length:
            return upper[start : start + count, :]
        if start >= length:
            return lower[start - length : start - length + count, :]
        return jnp.concatenate([upper[start:length, :], lower[0 : start + count - length, :]], axis=0)

    copies = []
    for position, step in enumerate(offsets()):
        other = mine ^ step
        target = rows.at[position]
        if position == 0:
            target[...] = exact[0:share, :]
        else:
            start = starts[position]
            own = exact[share + (position - 1) * half : share + position * half, :]
            theirs = rows_of(position, start, half).astype(F32)

            @pl.when(mine < other)
            def _():
                target[0:half, :] = own
                target[half:, :] = theirs

            @pl.when(mine > other)
            def _():
                target[...] = jnp.concatenate([theirs.T, own.T], axis=1)

        columns = pl.ds(pl.multiple_of(other * share, share), share)
        copies.append(pltpu.make_async_copy(target, factor_out.at[:, columns], sent.at[position]))
        copies[-1].start()

    squares = jnp.zeros((16, share), F32)
    block_eye = eye_of(share, share)
    for position, offset in enumerate(offsets()):
        owner = mine ^ offset
        own_band = pl.ds(pl.multiple_of(owner * share, share), share)
        block = unpacked(rows_of(position, 0, starts[1]).astype(F32))
        factor[own_band, own_band] = block.astype(BF16)
        diagonal[:, own_band] = jnp.sum(block * block_eye, axis=0, keepdims=True)
        for start, step in zip(starts[1:], offsets()[1:]):
            row, col = shared_half(owner, step, share)
            block = rows_of(position, start, half)
            factor[pl.ds(row, half), pl.ds(col, share)] = block
            factor[pl.ds(col, share), pl.ds(row, half)] = transposed(block)
        squares = squares + rows_of(position, starts[-1], 16).astype(F32)

    scale = jnp.sqrt(jnp.sum(squares, keepdims=True) / order + EPSILON)
    inverse = 1.0 / scale
    ones = (diagonal[...] * inverse).astype(BF16).astype(F32)
    lift = (1.5 - 0.5 * ones).astype(BF16).astype(F32) + 0.5 * (diagonal[...] * inverse)
    eye = eye_of(share, order, mine * share)
    my_rows = pl.ds(pl.multiple_of(mine * share, share), share)
    first = (factor[my_rows, :].astype(F32) * inverse).astype(BF16).astype(F32)
    turn = (1.5 * eye - 0.5 * first).astype(BF16)
    second = (jnp.dot(turn, factor[...], preferred_element_type=F32) * inverse).astype(BF16)
    product = (-0.5 * inverse) * jnp.dot(second, factor[...], preferred_element_type=F32) + second.astype(F32) * lift
    turn_two = (1.5 * eye - 0.5 * product).astype(BF16)
    inverse_rows = (-0.5 * inverse) * jnp.dot(
        turn_two, factor[...], preferred_element_type=F32
    ) + turn_two.astype(F32) * lift
    chosen = jnp.where(count[0, 0] == 1, turn.astype(F32), inverse_rows)
    root_out[...] = (chosen * lax.rsqrt(scale)).astype(BF16)
    finished[...] = jnp.zeros_like(finished)
    for copy in copies:
        copy.wait()


def step_kernel(replicas, pair, far, old_root, step_out, grads, result):
    share = old_root.shape[0]
    strip = step_out.shape[0] // replicas
    length = pair.shape[0] // 2
    mine = lax.axis_index("dp")
    strips = [(pair, 0, 0), (pair, length, along(1)), (far, 0, along(0)), (far, length, 3)]
    for i, (ref, at, _) in enumerate(strips):
        for part in range(replicas):
            start = at + part * strip
            grads[i * strip : (i + 1) * strip, part * share : (part + 1) * share] = ref[start : start + strip, :]
    result[...] = lax.dot_general(
        grads[...], old_root[...], (((1,), (1,)), ((), ())), preferred_element_type=F32
    ).astype(BF16)
    for i, (_, _, offset) in enumerate(strips):
        step_out[band(mine ^ offset, strip), :] = result[i * strip : (i + 1) * strip, :]


def square_plan(acts, out_grad, old_factor, old_root, iter_count):
    replicas = lax.axis_size("dp")
    inputs = acts[0]
    tokens, order = inputs.shape
    share = order // replicas
    grows = out_grad.shape[2]
    params = pltpu.CompilerParams(vmem_limit_bytes=VMEM_LIMIT)
    whole_rows = chunk_rows(share)[-1]
    length = whole_rows // 2

    def shape(rows, kind=BF16, columns=share):
        return jax.ShapeDtypeStruct((rows, columns), kind)

    def call(kernel, outs, name, *operands, first=None, first_out=None, after=(), scratch=()):
        in_specs = whole(len(operands)) + [pl.BlockSpec(memory_space=pl.ANY)] * len(after)
        if first is not None:
            in_specs[0] = pl.BlockSpec(memory_space=first)
        out_specs = whole(len(outs))
        if first_out is not None:
            out_specs[0] = pl.BlockSpec(memory_space=first_out)

        def body(*refs):
            kernel(*refs[: len(operands)], *refs[len(operands) + len(after) :])

        return pl.pallas_call(
            body,
            out_shape=outs,
            in_specs=in_specs,
            out_specs=out_specs,
            scratch_shapes=scratch,
            compiler_params=params,
            name=name,
        )(*operands, *after)

    received = passed_along(out_grad, "pipe", -1)[0]
    relay_x, relay_y, direct_x, direct_y, keep = call(
        functools.partial(batch_kernel, replicas, tokens * replicas),
        [shape(length)] * 4 + [shape(4 * length, F32)],
        "batch",
        inputs,
        scratch=[pltpu.VMEM((order, order), F32)],
    )
    relay_x, relay_y = swapped(relay_x, 0), swapped(relay_y, 1)
    direct_x, direct_y = swapped(direct_x, 0), swapped(direct_y, 1)
    relay_x, relay_y = call(relay_kernel, [shape(length)] * 2, "relay", keep, relay_x, relay_y)
    strips, strips_keep = call(
        functools.partial(grad_kernel, replicas, tokens * replicas),
        [shape(2 * grows), shape(2 * grows, F32)],
        "grad",
        inputs,
        received,
        scratch=[pltpu.VMEM((grows, order), F32)],
    )
    relay_x, relay_y = swapped(relay_x, 0), swapped(relay_y, 1)
    strips_got = swapped(strips, 0)
    (strip_on,) = call(strip_relay_kernel, [shape(grows)], "strip_relay", strips_keep, strips_got)
    strip_relayed = swapped(strip_on, 1)
    upper, lower, exact = call(
        functools.partial(factor_kernel, replicas),
        [shape(length), shape(length + 16), shape(5 * share // 2, F32)],
        "factor",
        keep,
        direct_x,
        direct_y,
        relay_x,
        relay_y,
        old_factor[0, 0],
        after=[strip_relayed],
    )
    upper_x, lower_y = swapped(upper, 0), swapped(lower, 1)
    lower_x, upper_y = swapped(lower, 0), swapped(upper, 1)
    upper_far, lower_far = swapped(upper_x, 1), swapped(lower_y, 0)
    (strip,) = call(
        strip_kernel, [shape(grows)], "strip", strips_keep, strips_got, strip_relayed, after=[upper_x, lower_y, lower_x, upper_y]
    )
    strip_near = swapped(strip, 1)
    (pair,) = call(pair_kernel, [shape(2 * grows)], "pair", strip, strip_near, after=[upper_far, lower_far])
    pair_far = swapped(pair, 0)
    factor, root, finished = call(
        root_kernel,
        [shape(share, F32, order), shape(share, BF16, order), shape(8, F32, 128)],
        "root",
        iter_count,
        exact,
        upper,
        lower,
        upper_x,
        lower_x,
        upper_y,
        lower_y,
        upper_far,
        lower_far,
        first=pltpu.SMEM,
        first_out=pl.ANY,
        scratch=[
            pltpu.VMEM((order, order), BF16),
            pltpu.VMEM((1, order), F32),
            pltpu.VMEM((replicas, share, share), F32),
            pltpu.SemaphoreType.DMA((replicas,)),
        ],
    )
    (step,) = call(
        functools.partial(step_kernel, replicas),
        [shape(grows, BF16, share)],
        "step",
        pair,
        pair_far,
        old_root[0, 0],
        after=[finished],
        scratch=[pltpu.VMEM((grows, order), BF16), pltpu.VMEM((grows, share), BF16)],
    )
    return (factor[None, None], root[None, None], step[None, None])


def ring_plan(acts, out_grad, old_factor, old_root, iter_count):
    inputs = acts[0]
    replicas = lax.axis_size("dp")
    tokens_all = inputs.shape[0] * replicas
    order = inputs.shape[1]
    share = order // replicas
    offset = lax.axis_index("dp") * share
    received = passed_along(out_grad, "pipe", -1)[0]
    partial_grad = jnp.dot(received.T, inputs, preferred_element_type=F32) / math.sqrt(tokens_all)
    batch = lax.psum_scatter(
        jnp.dot(inputs.T, inputs, preferred_element_type=F32) / tokens_all,
        "dp",
        scatter_dimension=0,
        tiled=True,
    )
    eye_rows = eye_of(share, order, offset)
    factor = DECAY * old_factor[0, 0] + (1.0 - DECAY) * batch + DAMPING * eye_rows
    grad16 = lax.psum(partial_grad, "dp").astype(BF16)
    scale = jnp.sqrt(lax.psum(jnp.sum(factor * factor), "dp") / order + EPSILON)
    step = lax.dot_general(
        grad16, old_root[0, 0], (((1,), (1,)), ((), ())), preferred_element_type=F32
    ).astype(BF16)
    first = lax.all_gather((factor / scale).astype(BF16), "dp", axis=0, tiled=True)
    turn_one = (1.5 * eye_of(order, order) - 0.5 * first.astype(F32)).astype(BF16)
    turn_rows = lax.dynamic_slice_in_dim(turn_one, offset, share, 0)
    second = jnp.dot(turn_rows, first, preferred_element_type=F32).astype(BF16)
    product = jnp.dot(second, turn_one, preferred_element_type=F32)
    turn_two = (1.5 * eye_rows - 0.5 * product).astype(BF16)
    inverse_rows = jnp.dot(turn_two, turn_one, preferred_element_type=F32)
    chosen = jnp.where(iter_count[0, 0] == 1, turn_rows.astype(F32), inverse_rows)
    root = (chosen / jnp.sqrt(scale)).astype(BF16)
    return (factor[None, None], root[None, None], step[None, None])


def solution(mesh):
    return jax.shard_map(
        square_plan if mesh.shape["dp"] == 4 and mesh.shape["pipe"] == 2 else ring_plan,
        mesh=mesh,
        in_specs=(
            P("pipe", "dp", "tensor"),
            P("pipe", "dp", "tensor"),
            P("pipe", "tensor", "dp", None),
            P("pipe", "tensor", "dp", None),
            P("pipe", "tensor"),
        ),
        out_specs=(
            P("pipe", "tensor", "dp", None),
            P("pipe", "tensor", "dp", None),
            P("pipe", "tensor", None, "dp"),
        ),
        check_vma=False,
    )
```

```python
import functools
import math

import jax
import jax.numpy as jnp
from jax import lax
from jax.experimental import pallas as pl
from jax.experimental.pallas import tpu as pltpu
from jax.sharding import PartitionSpec as P

DECAY = 0.75
DAMPING = 0.1
EPSILON = 1e-06
BF16 = jnp.bfloat16
F32 = jnp.float32
VMEM_LIMIT = 28 * 1024 * 1024


def passed_along(block, axis, distance):
    devices = range(lax.axis_size(axis))
    route = [((i - distance) % len(devices), i) for i in devices]
    return lax.ppermute(block, axis, route)


def along(turn):
    return jnp.where(lax.axis_index("pipe") == turn, 1, 2)


def swapped(block, turn):
    replicas = lax.axis_size("dp")
    route = []
    for section in range(lax.axis_size("pipe")):
        offset = 1 if section == turn else 2
        route += [(section * replicas + i, section * replicas + (i ^ offset)) for i in range(replicas)]
    return lax.ppermute(block, ("pipe", "dp"), route)


def eye_of(rows, cols, shift=0):
    row_ids = lax.broadcasted_iota(jnp.int32, (rows, cols), 0) + shift
    col_ids = lax.broadcasted_iota(jnp.int32, (rows, cols), 1)
    return (row_ids == col_ids).astype(F32)


def whole(count):
    return [pl.BlockSpec(memory_space=pltpu.VMEM)] * count


def transposed(block):
    return block.astype(F32).T.astype(block.dtype)


def offsets():
    return 0, along(0), along(1), 3


def chunk_rows(share):
    half, packed = share // 2, 5 * share // 8
    return [0] + [packed + half * i for i in range(4)]


def packed_upper(block):
    quarter = block.shape[0] // 4
    column = lax.broadcasted_iota(jnp.int32, (quarter, 4 * quarter), 1)
    second = pltpu.roll(block[quarter : 2 * quarter], 3 * quarter, 1)
    third = block[2 * quarter : 3 * quarter, 2 * quarter :]
    return jnp.concatenate(
        [
            block[0:quarter],
            jnp.where(column < 3 * quarter, second, block[3 * quarter :]),
            jnp.concatenate([third[0 : quarter // 2], third[quarter // 2 :]], axis=1),
        ],
        axis=0,
    )


def unpacked(packed):
    share = packed.shape[1]
    quarter = share // 4
    column = lax.broadcasted_iota(jnp.int32, (quarter, share), 1)
    second = packed[quarter : 2 * quarter]
    third = packed[2 * quarter :]
    third = jnp.concatenate([third[:, 0 : 2 * quarter], third[:, 2 * quarter :]], axis=0)
    upper = jnp.concatenate(
        [
            packed[0:quarter],
            jnp.where(column < quarter, 0.0, pltpu.roll(second, quarter, 1)),
            jnp.concatenate([jnp.zeros((quarter, 2 * quarter), F32), third], axis=1),
            jnp.where(column < 3 * quarter, 0.0, second),
        ],
        axis=0,
    )
    rows = lax.broadcasted_iota(jnp.int32, (share, share), 0) // quarter
    columns = lax.broadcasted_iota(jnp.int32, (share, share), 1) // quarter
    return upper + jnp.where(rows == columns, 0.0, upper).T


def shared_half(owner, offset, share):
    other = owner ^ offset
    low, high = jnp.minimum(owner, other), jnp.maximum(owner, other)
    row = low * share + jnp.where(owner > other, share // 2, 0)
    return pl.multiple_of(row, share // 2), pl.multiple_of(high * share, share)


def store_chunk(pieces, length, upper, lower):
    for start, piece in pieces:
        stop = start + piece.shape[0]
        for target, low, high in ((upper, 0, length), (lower, length, stop)):
            first, last = max(start, low), min(stop, high)
            if target is not None and first < last:
                ref, at = target
                ref[at + first - low : at + last - low, :] = piece[first - start : last - start].astype(ref.dtype)


def batch_kernel(replicas, tokens_all, acts, relay_x, relay_y, direct_x, direct_y, keep, batch):
    order = acts.shape[1]
    share = order // replicas
    half = share // 2
    starts = chunk_rows(share)
    length = relay_x.shape[0]
    mine = lax.axis_index("dp")
    for i in range(replicas):
        band = slice(i * share, (i + 1) * share)
        batch[band, i * share :] = lax.dot_general(
            acts[:, band], acts[:, i * share :], (((0,), (0,)), ((), ())), preferred_element_type=F32
        ) * (1.0 / tokens_all)

    def pieces(offset):
        owner = mine ^ offset
        base = pl.multiple_of(owner * share, share)
        yield 0, packed_upper(batch[pl.ds(base, share), pl.ds(base, share)])
        for start, step in zip(starts[1:], offsets()[1:]):
            row, col = shared_half(owner, step, share)
            yield start, batch[pl.ds(row, half), pl.ds(col, share)]

    store_chunk(pieces(3), length, (relay_x, 0), (relay_y, 0))
    store_chunk(pieces(along(0)), length, (direct_x, 0), (keep, 3 * length))
    store_chunk(pieces(along(1)), length, (keep, 2 * length), (direct_y, 0))
    store_chunk(pieces(0), length, (keep, 0), (keep, length))


def grad_kernel(replicas, tokens_all, acts, grads, send_x, send_y, keep, total):
    order = acts.shape[1]
    share = order // replicas
    strip = grads.shape[1] // replicas
    length = send_x.shape[0] // 2
    mine = lax.axis_index("dp")
    total[...] = lax.dot_general(
        grads[...], acts[...], (((0,), (0,)), ((), ())), preferred_element_type=F32
    ) * (1.0 / math.sqrt(tokens_all))

    def pieces(offset):
        rows = pl.ds(pl.multiple_of((mine ^ offset) * strip, strip), strip)
        for part in range(replicas):
            yield part * strip, total[rows, part * share : (part + 1) * share]

    store_chunk(pieces(3), length, (send_x, 0), (send_y, 0))
    store_chunk(pieces(along(0)), length, (send_x, length), (keep, 3 * length))
    store_chunk(pieces(along(1)), length, (keep, 2 * length), (send_y, length))
    store_chunk(pieces(0), length, (keep, 0), (keep, length))


def relay_kernel(keep, got_x, got_y, send_x, send_y):
    length = send_x.shape[0]
    send_y[...] = (keep[2 * length : 3 * length, :] + got_x[...].astype(F32)).astype(BF16)
    send_x[...] = (keep[3 * length :, :] + got_y[...].astype(F32)).astype(BF16)


def grad_relay_kernel(keep, got_x, got_y, send_x, send_y):
    length = send_x.shape[0]
    send_y[...] = (keep[2 * length : 3 * length, :] + got_x[0:length, :].astype(F32)).astype(BF16)
    send_x[...] = (keep[3 * length :, :] + got_y[0:length, :].astype(F32)).astype(BF16)


def grad_total_kernel(keep, got_x, got_y, relay_x, relay_y, chunk):
    length = relay_x.shape[0]
    chunk[0:length, :] = (
        keep[0:length, :] + got_x[length:, :].astype(F32) + relay_y[...].astype(F32)
    ).astype(BF16)
    chunk[length:, :] = (
        keep[length : 2 * length, :] + got_y[length:, :].astype(F32) + relay_x[...].astype(F32)
    ).astype(BF16)


def band(index, size):
    return pl.ds(pl.multiple_of(index * size, size), size)


def pair_kernel(own, got, send):
    length = own.shape[0]
    send[0:length, :] = own[...]
    send[length:, :] = got[...]


def second_kernel(upper, lower, got_x, got_y, send_x, send_y):
    send_x[0 : lower.shape[0], :] = lower[...]
    send_x[lower.shape[0] :, :] = got_y[...]
    send_y[0 : upper.shape[0], :] = upper[...]
    send_y[upper.shape[0] :, :] = got_x[...]


def factor_kernel(replicas, keep, direct_x, direct_y, relay_x, relay_y, old, upper, lower, exact):
    share, order = old.shape
    half = share // 2
    starts = chunk_rows(share)
    length = upper.shape[0]
    mine = lax.axis_index("dp")
    total = jnp.concatenate(
        [
            keep[0:length, :] + direct_x[...].astype(F32) + relay_y[...].astype(F32),
            keep[length : 2 * length, :] + direct_y[...].astype(F32) + relay_x[...].astype(F32),
        ],
        axis=0,
    )
    diagonal = old[:, pl.ds(pl.multiple_of(mine * share, share), share)]
    block_sum = unpacked(total[0 : starts[1]])
    value = DECAY * diagonal + (1.0 - DECAY) * block_sum + DAMPING * eye_of(share, share)
    exact[0:share, :] = value
    squares = jnp.sum(value * value, axis=0, keepdims=True)
    values = [packed_upper(value).astype(BF16)]
    for position, step in enumerate(offsets()[1:]):
        other = mine ^ step
        block = old[:, pl.ds(pl.multiple_of(other * share, share), share)]
        term = DECAY * jnp.where(mine < other, block[0:half], block[:, half:].T)
        start = starts[1 + position]
        value = term + (1.0 - DECAY) * total[start : start + half]
        exact[share + position * half : share + (position + 1) * half, :] = value
        squares = squares + 2.0 * jnp.sum(value * value, axis=0, keepdims=True)
        values.append(value.astype(BF16))
    high = squares.astype(BF16).astype(F32)
    middle = (squares - high).astype(BF16).astype(F32)
    rest = squares - high - middle
    spot = lax.broadcasted_iota(jnp.int32, (16, share), 0)
    digits = jnp.where(spot == 0, high, jnp.where(spot == 1, middle, jnp.where(spot == 2, rest, 0.0)))
    values.append(digits.astype(BF16))
    chunk = jnp.concatenate(values, axis=0)
    upper[...] = chunk[0:length]
    lower[...] = chunk[length:]


def root_kernel(count, exact, *rest):
    upper, lower, upper_x, lower_y, second_x, second_y = rest[:6]
    factor_out, root_out, finished, factor, diagonal, rows, sent = rest[6:]
    share, order = root_out.shape
    half = share // 2
    starts = chunk_rows(share)
    length, rest_length = upper.shape[0], lower.shape[0]
    mine = lax.axis_index("dp")
    chunks = [
        ((upper, 0), (lower, 0)),
        ((upper_x, 0), (second_x, 0)),
        ((second_y, 0), (lower_y, 0)),
        ((second_y, length), (second_x, rest_length)),
    ]

    def rows_of(position, start, count):
        parts = []
        for (ref, at), low, high in zip(chunks[position], (0, length), (length, length + rest_length)):
            first, last = max(start, low), min(start + count, high)
            if first < last:
                parts.append(ref[at + first - low : at + last - low, :])
        return parts[0] if len(parts) == 1 else jnp.concatenate(parts, axis=0)

    copies = []
    for position, step in enumerate(offsets()):
        other = mine ^ step
        target = rows.at[position]
        if position == 0:
            target[...] = exact[0:share, :]
        else:
            start = starts[position]
            own = exact[share + (position - 1) * half : share + position * half, :]
            theirs = rows_of(position, start, half).astype(F32)

            @pl.when(mine < other)
            def _():
                target[0:half, :] = own
                target[half:, :] = theirs

            @pl.when(mine > other)
            def _():
                target[...] = jnp.concatenate([theirs.T, own.T], axis=1)

        columns = pl.ds(pl.multiple_of(other * share, share), share)
        copies.append(pltpu.make_async_copy(target, factor_out.at[:, columns], sent.at[position]))
        copies[-1].start()

    squares = jnp.zeros((16, share), F32)
    block_eye = eye_of(share, share)
    for position, offset in enumerate(offsets()):
        owner = mine ^ offset
        own_band = pl.ds(pl.multiple_of(owner * share, share), share)
        block = unpacked(rows_of(position, 0, starts[1]).astype(F32))
        factor[own_band, own_band] = block.astype(BF16)
        diagonal[:, own_band] = jnp.sum(block * block_eye, axis=0, keepdims=True)
        for start, step in zip(starts[1:], offsets()[1:]):
            row, col = shared_half(owner, step, share)
            block = rows_of(position, start, half)
            factor[pl.ds(row, half), pl.ds(col, share)] = block
            factor[pl.ds(col, share), pl.ds(row, half)] = transposed(block)
        squares = squares + rows_of(position, starts[-1], 16).astype(F32)

    scale = jnp.sqrt(jnp.sum(squares, keepdims=True) / order + EPSILON)
    inverse = 1.0 / scale
    ones = (diagonal[...] * inverse).astype(BF16).astype(F32)
    lift = (1.5 - 0.5 * ones).astype(BF16).astype(F32) + 0.5 * (diagonal[...] * inverse)
    eye = eye_of(share, order, mine * share)
    my_rows = pl.ds(pl.multiple_of(mine * share, share), share)
    first = (factor[my_rows, :].astype(F32) * inverse).astype(BF16).astype(F32)
    turn = (1.5 * eye - 0.5 * first).astype(BF16)
    second = (jnp.dot(turn, factor[...], preferred_element_type=F32) * inverse).astype(BF16)
    product = (-0.5 * inverse) * jnp.dot(second, factor[...], preferred_element_type=F32) + second.astype(F32) * lift
    turn_two = (1.5 * eye - 0.5 * product).astype(BF16)
    inverse_rows = (-0.5 * inverse) * jnp.dot(
        turn_two, factor[...], preferred_element_type=F32
    ) + turn_two.astype(F32) * lift
    chosen = jnp.where(count[0, 0] == 1, turn.astype(F32), inverse_rows)
    root_out[...] = (chosen * lax.rsqrt(scale)).astype(BF16)
    finished[...] = jnp.zeros_like(finished)
    for copy in copies:
        copy.wait()


def step_kernel(replicas, pair, far, old_root, step_out, grads, result):
    share = old_root.shape[0]
    strip = step_out.shape[0] // replicas
    length = pair.shape[0] // 2
    mine = lax.axis_index("dp")
    strips = [(pair, 0, 0), (pair, length, along(1)), (far, 0, along(0)), (far, length, 3)]
    for i, (ref, at, _) in enumerate(strips):
        for part in range(replicas):
            start = at + part * strip
            grads[i * strip : (i + 1) * strip, part * share : (part + 1) * share] = ref[start : start + strip, :]
    result[...] = lax.dot_general(
        grads[...], old_root[...], (((1,), (1,)), ((), ())), preferred_element_type=F32
    ).astype(BF16)
    for i, (_, _, offset) in enumerate(strips):
        step_out[band(mine ^ offset, strip), :] = result[i * strip : (i + 1) * strip, :]


def square_plan(acts, out_grad, old_factor, old_root, iter_count):
    replicas = lax.axis_size("dp")
    inputs = acts[0]
    tokens, order = inputs.shape
    share = order // replicas
    grows = out_grad.shape[2]
    params = pltpu.CompilerParams(vmem_limit_bytes=VMEM_LIMIT)
    whole_rows = chunk_rows(share)[-1]
    length = whole_rows // 2

    def shape(rows, kind=BF16, columns=share):
        return jax.ShapeDtypeStruct((rows, columns), kind)

    def call(kernel, outs, name, *operands, first=None, first_out=None, after=(), scratch=()):
        in_specs = whole(len(operands)) + [pl.BlockSpec(memory_space=pl.ANY)] * len(after)
        if first is not None:
            in_specs[0] = pl.BlockSpec(memory_space=first)
        out_specs = whole(len(outs))
        if first_out is not None:
            out_specs[0] = pl.BlockSpec(memory_space=first_out)

        def body(*refs):
            kernel(*refs[: len(operands)], *refs[len(operands) + len(after) :])

        return pl.pallas_call(
            body,
            out_shape=outs,
            in_specs=in_specs,
            out_specs=out_specs,
            scratch_shapes=scratch,
            compiler_params=params,
            name=name,
        )(*operands, *after)

    received = passed_along(out_grad, "pipe", -1)[0]
    relay_x, relay_y, direct_x, direct_y, keep = call(
        functools.partial(batch_kernel, replicas, tokens * replicas),
        [shape(length)] * 4 + [shape(4 * length, F32)],
        "batch",
        inputs,
        scratch=[pltpu.VMEM((order, order), F32)],
    )
    relay_x, relay_y = swapped(relay_x, 0), swapped(relay_y, 1)
    direct_x, direct_y = swapped(direct_x, 0), swapped(direct_y, 1)
    relay_x, relay_y = call(relay_kernel, [shape(length)] * 2, "relay", keep, relay_x, relay_y)
    grad_x, grad_y, grad_keep = call(
        functools.partial(grad_kernel, replicas, tokens * replicas),
        [shape(grows)] * 2 + [shape(2 * grows, F32)],
        "grad",
        inputs,
        received,
        after=[relay_x, relay_y],
        scratch=[pltpu.VMEM((grows, order), F32)],
    )
    relay_x, relay_y = swapped(relay_x, 0), swapped(relay_y, 1)
    grad_x, grad_y = swapped(grad_x, 0), swapped(grad_y, 1)
    upper, lower, exact = call(
        functools.partial(factor_kernel, replicas),
        [shape(length), shape(length + 16), shape(5 * share // 2, F32)],
        "factor",
        keep,
        direct_x,
        direct_y,
        relay_x,
        relay_y,
        old_factor[0, 0],
    )
    upper_x, lower_y = swapped(upper, 0), swapped(lower, 1)
    strip_x, strip_y = call(
        grad_relay_kernel, [shape(grows // 2)] * 2, "grad_relay", grad_keep, grad_x, grad_y, after=[upper, lower]
    )
    strip_x, strip_y = swapped(strip_x, 0), swapped(strip_y, 1)
    on_x, on_y = call(
        second_kernel, [shape(2 * length + 32), shape(2 * length)], "second", upper, lower, upper_x, lower_y
    )
    second_x, second_y = swapped(on_x, 0), swapped(on_y, 1)
    (strip,) = call(
        grad_total_kernel,
        [shape(grows)],
        "grad_total",
        grad_keep,
        grad_x,
        grad_y,
        strip_x,
        strip_y,
        after=[on_x],
    )
    strip_near = swapped(strip, 1)
    (pair,) = call(pair_kernel, [shape(2 * grows)], "pair", strip, strip_near, after=[second_x, second_y])
    pair_far = swapped(pair, 0)
    factor, root, finished = call(
        root_kernel,
        [shape(share, F32, order), shape(share, BF16, order), shape(8, F32, 128)],
        "root",
        iter_count,
        exact,
        upper,
        lower,
        upper_x,
        lower_y,
        second_x,
        second_y,
        first=pltpu.SMEM,
        first_out=pl.ANY,
        scratch=[
            pltpu.VMEM((order, order), BF16),
            pltpu.VMEM((1, order), F32),
            pltpu.VMEM((replicas, share, share), F32),
            pltpu.SemaphoreType.DMA((replicas,)),
        ],
    )
    (step,) = call(
        functools.partial(step_kernel, replicas),
        [shape(grows, BF16, share)],
        "step",
        pair,
        pair_far,
        old_root[0, 0],
        after=[finished],
        scratch=[pltpu.VMEM((grows, order), BF16), pltpu.VMEM((grows, share), BF16)],
    )
    return (factor[None, None], root[None, None], step[None, None])


def ring_plan(acts, out_grad, old_factor, old_root, iter_count):
    inputs = acts[0]
    replicas = lax.axis_size("dp")
    tokens_all = inputs.shape[0] * replicas
    order = inputs.shape[1]
    share = order // replicas
    offset = lax.axis_index("dp") * share
    received = passed_along(out_grad, "pipe", -1)[0]
    partial_grad = jnp.dot(received.T, inputs, preferred_element_type=F32) / math.sqrt(tokens_all)
    batch = lax.psum_scatter(
        jnp.dot(inputs.T, inputs, preferred_element_type=F32) / tokens_all,
        "dp",
        scatter_dimension=0,
        tiled=True,
    )
    eye_rows = eye_of(share, order, offset)
    factor = DECAY * old_factor[0, 0] + (1.0 - DECAY) * batch + DAMPING * eye_rows
    grad16 = lax.psum(partial_grad, "dp").astype(BF16)
    scale = jnp.sqrt(lax.psum(jnp.sum(factor * factor), "dp") / order + EPSILON)
    step = lax.dot_general(
        grad16, old_root[0, 0], (((1,), (1,)), ((), ())), preferred_element_type=F32
    ).astype(BF16)
    first = lax.all_gather((factor / scale).astype(BF16), "dp", axis=0, tiled=True)
    turn_one = (1.5 * eye_of(order, order) - 0.5 * first.astype(F32)).astype(BF16)
    turn_rows = lax.dynamic_slice_in_dim(turn_one, offset, share, 0)
    second = jnp.dot(turn_rows, first, preferred_element_type=F32).astype(BF16)
    product = jnp.dot(second, turn_one, preferred_element_type=F32)
    turn_two = (1.5 * eye_rows - 0.5 * product).astype(BF16)
    inverse_rows = jnp.dot(turn_two, turn_one, preferred_element_type=F32)
    chosen = jnp.where(iter_count[0, 0] == 1, turn_rows.astype(F32), inverse_rows)
    root = (chosen / jnp.sqrt(scale)).astype(BF16)
    return (factor[None, None], root[None, None], step[None, None])


def solution(mesh):
    return jax.shard_map(
        square_plan if mesh.shape["dp"] == 4 and mesh.shape["pipe"] == 2 else ring_plan,
        mesh=mesh,
        in_specs=(
            P("pipe", "dp", "tensor"),
            P("pipe", "dp", "tensor"),
            P("pipe", "tensor", "dp", None),
            P("pipe", "tensor", "dp", None),
            P("pipe", "tensor"),
        ),
        out_specs=(
            P("pipe", "tensor", "dp", None),
            P("pipe", "tensor", "dp", None),
            P("pipe", "tensor", None, "dp"),
        ),
        check_vma=False,
    )
```

```python
import functools
import math

import jax
import jax.numpy as jnp
from jax import lax
from jax.experimental import pallas as pl
from jax.experimental.pallas import tpu as pltpu
from jax.sharding import PartitionSpec as P

DECAY = 0.75
DAMPING = 0.1
EPSILON = 1e-06
BF16 = jnp.bfloat16
F32 = jnp.float32
VMEM_LIMIT = 28 * 1024 * 1024


def passed_along(block, axis, distance):
    devices = range(lax.axis_size(axis))
    route = [((i - distance) % len(devices), i) for i in devices]
    return lax.ppermute(block, axis, route)


def along(turn):
    return jnp.where(lax.axis_index("pipe") == turn, 1, 2)


def swapped(block, turn):
    replicas = lax.axis_size("dp")
    route = []
    for section in range(lax.axis_size("pipe")):
        offset = 1 if section == turn else 2
        route += [(section * replicas + i, section * replicas + (i ^ offset)) for i in range(replicas)]
    return lax.ppermute(block, ("pipe", "dp"), route)


def eye_of(rows, cols, shift=0):
    row_ids = lax.broadcasted_iota(jnp.int32, (rows, cols), 0) + shift
    col_ids = lax.broadcasted_iota(jnp.int32, (rows, cols), 1)
    return (row_ids == col_ids).astype(F32)


def whole(count):
    return [pl.BlockSpec(memory_space=pltpu.VMEM)] * count


def transposed(block):
    return block.astype(F32).T.astype(block.dtype)


def offsets():
    return 0, along(0), along(1), 3


def chunk_rows(share):
    half, packed = share // 2, 5 * share // 8
    return [0] + [packed + half * i for i in range(4)]


def packed_upper(block):
    quarter = block.shape[0] // 4
    column = lax.broadcasted_iota(jnp.int32, (quarter, 4 * quarter), 1)
    second = pltpu.roll(block[quarter : 2 * quarter], 3 * quarter, 1)
    third = block[2 * quarter : 3 * quarter, 2 * quarter :]
    return jnp.concatenate(
        [
            block[0:quarter],
            jnp.where(column < 3 * quarter, second, block[3 * quarter :]),
            jnp.concatenate([third[0 : quarter // 2], third[quarter // 2 :]], axis=1),
        ],
        axis=0,
    )


def unpacked(packed):
    share = packed.shape[1]
    quarter = share // 4
    column = lax.broadcasted_iota(jnp.int32, (quarter, share), 1)
    second = packed[quarter : 2 * quarter]
    third = packed[2 * quarter :]
    third = jnp.concatenate([third[:, 0 : 2 * quarter], third[:, 2 * quarter :]], axis=0)
    upper = jnp.concatenate(
        [
            packed[0:quarter],
            jnp.where(column < quarter, 0.0, pltpu.roll(second, quarter, 1)),
            jnp.concatenate([jnp.zeros((quarter, 2 * quarter), F32), third], axis=1),
            jnp.where(column < 3 * quarter, 0.0, second),
        ],
        axis=0,
    )
    rows = lax.broadcasted_iota(jnp.int32, (share, share), 0) // quarter
    columns = lax.broadcasted_iota(jnp.int32, (share, share), 1) // quarter
    return upper + jnp.where(rows == columns, 0.0, upper).T


def shared_half(owner, offset, share):
    other = owner ^ offset
    low, high = jnp.minimum(owner, other), jnp.maximum(owner, other)
    row = low * share + jnp.where(owner > other, share // 2, 0)
    return pl.multiple_of(row, share // 2), pl.multiple_of(high * share, share)


def store_chunk(pieces, length, upper, lower):
    for start, piece in pieces:
        stop = start + piece.shape[0]
        for target, low, high in ((upper, 0, length), (lower, length, stop)):
            first, last = max(start, low), min(stop, high)
            if target is not None and first < last:
                ref, at = target
                ref[at + first - low : at + last - low, :] = piece[first - start : last - start].astype(ref.dtype)


def batch_kernel(replicas, tokens_all, acts, relay_x, relay_y, direct_x, direct_y, keep, batch):
    order = acts.shape[1]
    share = order // replicas
    half = share // 2
    starts = chunk_rows(share)
    length = relay_x.shape[0]
    mine = lax.axis_index("dp")
    for i in range(replicas):
        band = slice(i * share, (i + 1) * share)
        batch[band, i * share :] = lax.dot_general(
            acts[:, band], acts[:, i * share :], (((0,), (0,)), ((), ())), preferred_element_type=F32
        ) * (1.0 / tokens_all)

    def pieces(offset):
        owner = mine ^ offset
        base = pl.multiple_of(owner * share, share)
        yield 0, packed_upper(batch[pl.ds(base, share), pl.ds(base, share)])
        for start, step in zip(starts[1:], offsets()[1:]):
            row, col = shared_half(owner, step, share)
            yield start, batch[pl.ds(row, half), pl.ds(col, share)]

    store_chunk(pieces(3), length, (relay_x, 0), (relay_y, 0))
    store_chunk(pieces(along(0)), length, (direct_x, 0), (keep, 3 * length))
    store_chunk(pieces(along(1)), length, (keep, 2 * length), (direct_y, 0))
    store_chunk(pieces(0), length, (keep, 0), (keep, length))


def grad_kernel(replicas, tokens_all, acts, grads, send_x, send_y, keep, total):
    order = acts.shape[1]
    share = order // replicas
    strip = grads.shape[1] // replicas
    length = send_x.shape[0] // 2
    mine = lax.axis_index("dp")
    total[...] = lax.dot_general(
        grads[...], acts[...], (((0,), (0,)), ((), ())), preferred_element_type=F32
    ) * (1.0 / math.sqrt(tokens_all))

    def pieces(offset):
        rows = pl.ds(pl.multiple_of((mine ^ offset) * strip, strip), strip)
        for part in range(replicas):
            yield part * strip, total[rows, part * share : (part + 1) * share]

    store_chunk(pieces(3), length, (send_x, 0), (send_y, 0))
    store_chunk(pieces(along(0)), length, (send_x, length), (keep, 3 * length))
    store_chunk(pieces(along(1)), length, (keep, 2 * length), (send_y, length))
    store_chunk(pieces(0), length, (keep, 0), (keep, length))


def relay_kernel(keep, got_x, got_y, send_x, send_y):
    length = send_x.shape[0]
    send_y[...] = (keep[2 * length : 3 * length, :] + got_x[...].astype(F32)).astype(BF16)
    send_x[...] = (keep[3 * length :, :] + got_y[...].astype(F32)).astype(BF16)


def grad_relay_kernel(keep, got_x, got_y, send_x, send_y):
    length = send_x.shape[0]
    send_y[...] = (keep[2 * length : 3 * length, :] + got_x[0:length, :].astype(F32)).astype(BF16)
    send_x[...] = (keep[3 * length :, :] + got_y[0:length, :].astype(F32)).astype(BF16)


def grad_total_kernel(keep, got_x, got_y, relay_x, relay_y, chunk):
    length = relay_x.shape[0]
    chunk[0:length, :] = (
        keep[0:length, :] + got_x[length:, :].astype(F32) + relay_y[...].astype(F32)
    ).astype(BF16)
    chunk[length:, :] = (
        keep[length : 2 * length, :] + got_y[length:, :].astype(F32) + relay_x[...].astype(F32)
    ).astype(BF16)


def band(index, size):
    return pl.ds(pl.multiple_of(index * size, size), size)


def pair_kernel(own, got, send):
    length = own.shape[0]
    send[0:length, :] = own[...]
    send[length:, :] = got[...]


def factor_kernel(replicas, keep, direct_x, direct_y, relay_x, relay_y, old, upper, lower, exact):
    share, order = old.shape
    half = share // 2
    starts = chunk_rows(share)
    length = upper.shape[0]
    mine = lax.axis_index("dp")
    total = jnp.concatenate(
        [
            keep[0:length, :] + direct_x[...].astype(F32) + relay_y[...].astype(F32),
            keep[length : 2 * length, :] + direct_y[...].astype(F32) + relay_x[...].astype(F32),
        ],
        axis=0,
    )
    diagonal = old[:, pl.ds(pl.multiple_of(mine * share, share), share)]
    block_sum = unpacked(total[0 : starts[1]])
    value = DECAY * diagonal + (1.0 - DECAY) * block_sum + DAMPING * eye_of(share, share)
    exact[0:share, :] = value
    squares = jnp.sum(value * value, axis=0, keepdims=True)
    values = [packed_upper(value).astype(BF16)]
    for position, step in enumerate(offsets()[1:]):
        other = mine ^ step
        block = old[:, pl.ds(pl.multiple_of(other * share, share), share)]
        term = DECAY * jnp.where(mine < other, block[0:half], block[:, half:].T)
        start = starts[1 + position]
        value = term + (1.0 - DECAY) * total[start : start + half]
        exact[share + position * half : share + (position + 1) * half, :] = value
        squares = squares + 2.0 * jnp.sum(value * value, axis=0, keepdims=True)
        values.append(value.astype(BF16))
    high = squares.astype(BF16).astype(F32)
    middle = (squares - high).astype(BF16).astype(F32)
    rest = squares - high - middle
    spot = lax.broadcasted_iota(jnp.int32, (16, share), 0)
    digits = jnp.where(spot == 0, high, jnp.where(spot == 1, middle, jnp.where(spot == 2, rest, 0.0)))
    values.append(digits.astype(BF16))
    chunk = jnp.concatenate(values, axis=0)
    upper[...] = chunk[0:length]
    lower[...] = chunk[length:]


def root_kernel(count, exact, *rest):
    chunks = [rest[2 * i : 2 * i + 2] for i in range(4)]
    factor_out, root_out, finished, factor, diagonal, rows, sent = rest[8:]
    share, order = root_out.shape
    half = share // 2
    starts = chunk_rows(share)
    length = chunks[0][0].shape[0]
    mine = lax.axis_index("dp")

    def rows_of(position, start, count):
        upper, lower = chunks[position]
        if start + count <= length:
            return upper[start : start + count, :]
        if start >= length:
            return lower[start - length : start - length + count, :]
        return jnp.concatenate([upper[start:length, :], lower[0 : start + count - length, :]], axis=0)

    copies = []
    for position, step in enumerate(offsets()):
        other = mine ^ step
        target = rows.at[position]
        if position == 0:
            target[...] = exact[0:share, :]
        else:
            start = starts[position]
            own = exact[share + (position - 1) * half : share + position * half, :]
            theirs = rows_of(position, start, half).astype(F32)

            @pl.when(mine < other)
            def _():
                target[0:half, :] = own
                target[half:, :] = theirs

            @pl.when(mine > other)
            def _():
                target[...] = jnp.concatenate([theirs.T, own.T], axis=1)

        columns = pl.ds(pl.multiple_of(other * share, share), share)
        copies.append(pltpu.make_async_copy(target, factor_out.at[:, columns], sent.at[position]))
        copies[-1].start()

    squares = jnp.zeros((16, share), F32)
    block_eye = eye_of(share, share)
    for position, offset in enumerate(offsets()):
        owner = mine ^ offset
        own_band = pl.ds(pl.multiple_of(owner * share, share), share)
        block = unpacked(rows_of(position, 0, starts[1]).astype(F32))
        factor[own_band, own_band] = block.astype(BF16)
        diagonal[:, own_band] = jnp.sum(block * block_eye, axis=0, keepdims=True)
        for start, step in zip(starts[1:], offsets()[1:]):
            row, col = shared_half(owner, step, share)
            block = rows_of(position, start, half)
            factor[pl.ds(row, half), pl.ds(col, share)] = block
            factor[pl.ds(col, share), pl.ds(row, half)] = transposed(block)
        squares = squares + rows_of(position, starts[-1], 16).astype(F32)

    scale = jnp.sqrt(jnp.sum(squares, keepdims=True) / order + EPSILON)
    inverse = 1.0 / scale
    ones = (diagonal[...] * inverse).astype(BF16).astype(F32)
    lift = (1.5 - 0.5 * ones).astype(BF16).astype(F32) + 0.5 * (diagonal[...] * inverse)
    eye = eye_of(share, order, mine * share)
    my_rows = pl.ds(pl.multiple_of(mine * share, share), share)
    first = (factor[my_rows, :].astype(F32) * inverse).astype(BF16).astype(F32)
    turn = (1.5 * eye - 0.5 * first).astype(BF16)
    second = (jnp.dot(turn, factor[...], preferred_element_type=F32) * inverse).astype(BF16)
    product = (-0.5 * inverse) * jnp.dot(second, factor[...], preferred_element_type=F32) + second.astype(F32) * lift
    turn_two = (1.5 * eye - 0.5 * product).astype(BF16)
    inverse_rows = (-0.5 * inverse) * jnp.dot(
        turn_two, factor[...], preferred_element_type=F32
    ) + turn_two.astype(F32) * lift
    chosen = jnp.where(count[0, 0] == 1, turn.astype(F32), inverse_rows)
    root_out[...] = (chosen * lax.rsqrt(scale)).astype(BF16)
    finished[...] = jnp.zeros_like(finished)
    for copy in copies:
        copy.wait()


def step_kernel(replicas, pair, far, old_root, step_out, grads, result):
    share = old_root.shape[0]
    strip = step_out.shape[0] // replicas
    length = pair.shape[0] // 2
    mine = lax.axis_index("dp")
    strips = [(pair, 0, 0), (pair, length, along(1)), (far, 0, along(0)), (far, length, 3)]
    for i, (ref, at, _) in enumerate(strips):
        for part in range(replicas):
            start = at + part * strip
            grads[i * strip : (i + 1) * strip, part * share : (part + 1) * share] = ref[start : start + strip, :]
    result[...] = lax.dot_general(
        grads[...], old_root[...], (((1,), (1,)), ((), ())), preferred_element_type=F32
    ).astype(BF16)
    for i, (_, _, offset) in enumerate(strips):
        step_out[band(mine ^ offset, strip), :] = result[i * strip : (i + 1) * strip, :]


def square_plan(acts, out_grad, old_factor, old_root, iter_count):
    replicas = lax.axis_size("dp")
    inputs = acts[0]
    tokens, order = inputs.shape
    share = order // replicas
    grows = out_grad.shape[2]
    params = pltpu.CompilerParams(vmem_limit_bytes=VMEM_LIMIT)
    whole_rows = chunk_rows(share)[-1]
    length = whole_rows // 2

    def shape(rows, kind=BF16, columns=share):
        return jax.ShapeDtypeStruct((rows, columns), kind)

    def call(kernel, outs, name, *operands, first=None, first_out=None, after=(), scratch=()):
        in_specs = whole(len(operands)) + [pl.BlockSpec(memory_space=pl.ANY)] * len(after)
        if first is not None:
            in_specs[0] = pl.BlockSpec(memory_space=first)
        out_specs = whole(len(outs))
        if first_out is not None:
            out_specs[0] = pl.BlockSpec(memory_space=first_out)

        def body(*refs):
            kernel(*refs[: len(operands)], *refs[len(operands) + len(after) :])

        return pl.pallas_call(
            body,
            out_shape=outs,
            in_specs=in_specs,
            out_specs=out_specs,
            scratch_shapes=scratch,
            compiler_params=params,
            name=name,
        )(*operands, *after)

    received = passed_along(out_grad, "pipe", -1)[0]
    relay_x, relay_y, direct_x, direct_y, keep = call(
        functools.partial(batch_kernel, replicas, tokens * replicas),
        [shape(length)] * 4 + [shape(4 * length, F32)],
        "batch",
        inputs,
        scratch=[pltpu.VMEM((order, order), F32)],
    )
    relay_x, relay_y = swapped(relay_x, 0), swapped(relay_y, 1)
    direct_x, direct_y = swapped(direct_x, 0), swapped(direct_y, 1)
    relay_x, relay_y = call(relay_kernel, [shape(length)] * 2, "relay", keep, relay_x, relay_y)
    grad_x, grad_y, grad_keep = call(
        functools.partial(grad_kernel, replicas, tokens * replicas),
        [shape(grows)] * 2 + [shape(2 * grows, F32)],
        "grad",
        inputs,
        received,
        scratch=[pltpu.VMEM((grows, order), F32)],
    )
    relay_x, relay_y = swapped(relay_x, 0), swapped(relay_y, 1)
    grad_x, grad_y = swapped(grad_x, 0), swapped(grad_y, 1)
    strip_x, strip_y = call(
        grad_relay_kernel, [shape(grows // 2)] * 2, "grad_relay", grad_keep, grad_x, grad_y
    )
    strip_x, strip_y = swapped(strip_x, 0), swapped(strip_y, 1)
    upper, lower, exact = call(
        functools.partial(factor_kernel, replicas),
        [shape(length), shape(length + 16), shape(5 * share // 2, F32)],
        "factor",
        keep,
        direct_x,
        direct_y,
        relay_x,
        relay_y,
        old_factor[0, 0],
        after=[strip_x, strip_y],
    )
    upper_x, lower_y = swapped(upper, 0), swapped(lower, 1)
    lower_x, upper_y = swapped(lower, 0), swapped(upper, 1)
    upper_far, lower_far = swapped(upper_x, 1), swapped(lower_y, 0)
    (strip,) = call(
        grad_total_kernel,
        [shape(grows)],
        "grad_total",
        grad_keep,
        grad_x,
        grad_y,
        strip_x,
        strip_y,
        after=[upper],
    )
    strip_near = swapped(strip, 1)
    (pair,) = call(pair_kernel, [shape(2 * grows)], "pair", strip, strip_near, after=[upper_far, lower_far, lower_x, upper_y])
    pair_far = swapped(pair, 0)
    factor, root, finished = call(
        root_kernel,
        [shape(share, F32, order), shape(share, BF16, order), shape(8, F32, 128)],
        "root",
        iter_count,
        exact,
        upper,
        lower,
        upper_x,
        lower_x,
        upper_y,
        lower_y,
        upper_far,
        lower_far,
        first=pltpu.SMEM,
        first_out=pl.ANY,
        scratch=[
            pltpu.VMEM((order, order), BF16),
            pltpu.VMEM((1, order), F32),
            pltpu.VMEM((replicas, share, share), F32),
            pltpu.SemaphoreType.DMA((replicas,)),
        ],
    )
    (step,) = call(
        functools.partial(step_kernel, replicas),
        [shape(grows, BF16, share)],
        "step",
        pair,
        pair_far,
        old_root[0, 0],
        after=[finished],
        scratch=[pltpu.VMEM((grows, order), BF16), pltpu.VMEM((grows, share), BF16)],
    )
    return (factor[None, None], root[None, None], step[None, None])


def ring_plan(acts, out_grad, old_factor, old_root, iter_count):
    inputs = acts[0]
    replicas = lax.axis_size("dp")
    tokens_all = inputs.shape[0] * replicas
    order = inputs.shape[1]
    share = order // replicas
    offset = lax.axis_index("dp") * share
    received = passed_along(out_grad, "pipe", -1)[0]
    partial_grad = jnp.dot(received.T, inputs, preferred_element_type=F32) / math.sqrt(tokens_all)
    batch = lax.psum_scatter(
        jnp.dot(inputs.T, inputs, preferred_element_type=F32) / tokens_all,
        "dp",
        scatter_dimension=0,
        tiled=True,
    )
    eye_rows = eye_of(share, order, offset)
    factor = DECAY * old_factor[0, 0] + (1.0 - DECAY) * batch + DAMPING * eye_rows
    grad16 = lax.psum(partial_grad, "dp").astype(BF16)
    scale = jnp.sqrt(lax.psum(jnp.sum(factor * factor), "dp") / order + EPSILON)
    step = lax.dot_general(
        grad16, old_root[0, 0], (((1,), (1,)), ((), ())), preferred_element_type=F32
    ).astype(BF16)
    first = lax.all_gather((factor / scale).astype(BF16), "dp", axis=0, tiled=True)
    turn_one = (1.5 * eye_of(order, order) - 0.5 * first.astype(F32)).astype(BF16)
    turn_rows = lax.dynamic_slice_in_dim(turn_one, offset, share, 0)
    second = jnp.dot(turn_rows, first, preferred_element_type=F32).astype(BF16)
    product = jnp.dot(second, turn_one, preferred_element_type=F32)
    turn_two = (1.5 * eye_rows - 0.5 * product).astype(BF16)
    inverse_rows = jnp.dot(turn_two, turn_one, preferred_element_type=F32)
    chosen = jnp.where(iter_count[0, 0] == 1, turn_rows.astype(F32), inverse_rows)
    root = (chosen / jnp.sqrt(scale)).astype(BF16)
    return (factor[None, None], root[None, None], step[None, None])


def solution(mesh):
    return jax.shard_map(
        square_plan if mesh.shape["dp"] == 4 and mesh.shape["pipe"] == 2 else ring_plan,
        mesh=mesh,
        in_specs=(
            P("pipe", "dp", "tensor"),
            P("pipe", "dp", "tensor"),
            P("pipe", "tensor", "dp", None),
            P("pipe", "tensor", "dp", None),
            P("pipe", "tensor"),
        ),
        out_specs=(
            P("pipe", "tensor", "dp", None),
            P("pipe", "tensor", "dp", None),
            P("pipe", "tensor", None, "dp"),
        ),
        check_vma=False,
    )
```

```python
import functools
import math

import jax
import jax.numpy as jnp
from jax import lax
from jax.experimental import pallas as pl
from jax.experimental.pallas import tpu as pltpu
from jax.sharding import PartitionSpec as P

DECAY = 0.75
DAMPING = 0.1
EPSILON = 1e-06
BF16 = jnp.bfloat16
F32 = jnp.float32
VMEM_LIMIT = 28 * 1024 * 1024


def passed_along(block, axis, distance):
    devices = range(lax.axis_size(axis))
    route = [((i - distance) % len(devices), i) for i in devices]
    return lax.ppermute(block, axis, route)


def swapped(block, offset):
    return lax.ppermute(block, "dp", [(i, i ^ offset) for i in range(lax.axis_size("dp"))])


def eye_of(rows, cols, shift=0):
    row_ids = lax.broadcasted_iota(jnp.int32, (rows, cols), 0) + shift
    col_ids = lax.broadcasted_iota(jnp.int32, (rows, cols), 1)
    return (row_ids == col_ids).astype(F32)


def whole(count):
    return [pl.BlockSpec(memory_space=pltpu.VMEM)] * count


def transposed(block):
    return block.astype(F32).T.astype(block.dtype)


OFFSETS = (0, 1, 2, 3)


def chunk_rows(share):
    half, packed = share // 2, 5 * share // 8
    return [0] + [packed + half * i for i in range(4)]


def packed_upper(block):
    quarter = block.shape[0] // 4
    column = lax.broadcasted_iota(jnp.int32, (quarter, 4 * quarter), 1)
    second = pltpu.roll(block[quarter : 2 * quarter], 3 * quarter, 1)
    third = block[2 * quarter : 3 * quarter, 2 * quarter :]
    return jnp.concatenate(
        [
            block[0:quarter],
            jnp.where(column < 3 * quarter, second, block[3 * quarter :]),
            jnp.concatenate([third[0 : quarter // 2], third[quarter // 2 :]], axis=1),
        ],
        axis=0,
    )


def unpacked(packed):
    share = packed.shape[1]
    quarter = share // 4
    column = lax.broadcasted_iota(jnp.int32, (quarter, share), 1)
    second = packed[quarter : 2 * quarter]
    third = packed[2 * quarter :]
    third = jnp.concatenate([third[:, 0 : 2 * quarter], third[:, 2 * quarter :]], axis=0)
    upper = jnp.concatenate(
        [
            packed[0:quarter],
            jnp.where(column < quarter, 0.0, pltpu.roll(second, quarter, 1)),
            jnp.concatenate([jnp.zeros((quarter, 2 * quarter), F32), third], axis=1),
            jnp.where(column < 3 * quarter, 0.0, second),
        ],
        axis=0,
    )
    rows = lax.broadcasted_iota(jnp.int32, (share, share), 0) // quarter
    columns = lax.broadcasted_iota(jnp.int32, (share, share), 1) // quarter
    return upper + jnp.where(rows == columns, 0.0, upper).T


def shared_half(owner, offset, share):
    other = owner ^ offset
    low, high = jnp.minimum(owner, other), jnp.maximum(owner, other)
    row = low * share + jnp.where(owner > other, share // 2, 0)
    return pl.multiple_of(row, share // 2), pl.multiple_of(high * share, share)


def store_chunk(pieces, length, upper, lower):
    for start, piece in pieces:
        stop = start + piece.shape[0]
        for target, low, high in ((upper, 0, length), (lower, length, stop)):
            first, last = max(start, low), min(stop, high)
            if target is not None and first < last:
                ref, at = target
                ref[at + first - low : at + last - low, :] = piece[first - start : last - start].astype(ref.dtype)


def batch_kernel(replicas, tokens_all, acts, relay_x, relay_y, direct_x, direct_y, keep, batch):
    order = acts.shape[1]
    share = order // replicas
    half = share // 2
    starts = chunk_rows(share)
    length = relay_x.shape[0]
    mine = lax.axis_index("dp")
    for i in range(replicas):
        band = slice(i * share, (i + 1) * share)
        batch[band, i * share :] = lax.dot_general(
            acts[:, band], acts[:, i * share :], (((0,), (0,)), ((), ())), preferred_element_type=F32
        ) * (1.0 / tokens_all)

    def pieces(offset):
        owner = mine ^ offset
        base = pl.multiple_of(owner * share, share)
        yield 0, packed_upper(batch[pl.ds(base, share), pl.ds(base, share)])
        for start, step in zip(starts[1:], OFFSETS[1:]):
            row, col = shared_half(owner, step, share)
            yield start, batch[pl.ds(row, half), pl.ds(col, share)]

    store_chunk(pieces(3), length, (relay_x, 0), (relay_y, 0))
    store_chunk(pieces(1), length, (direct_x, 0), (keep, 3 * length))
    store_chunk(pieces(2), length, (keep, 2 * length), (direct_y, 0))
    store_chunk(pieces(0), length, (keep, 0), (keep, length))


def grad_kernel(replicas, tokens_all, acts, grads, send_x, send_y, keep, total):
    order = acts.shape[1]
    share = order // replicas
    strip = grads.shape[1] // replicas
    length = send_x.shape[0] // 2
    mine = lax.axis_index("dp")
    total[...] = lax.dot_general(
        grads[...], acts[...], (((0,), (0,)), ((), ())), preferred_element_type=F32
    ) * (1.0 / math.sqrt(tokens_all))

    def pieces(offset):
        rows = pl.ds(pl.multiple_of((mine ^ offset) * strip, strip), strip)
        for part in range(replicas):
            yield part * strip, total[rows, part * share : (part + 1) * share]

    store_chunk(pieces(3), length, (send_x, 0), (send_y, 0))
    store_chunk(pieces(1), length, (send_x, length), (keep, 3 * length))
    store_chunk(pieces(2), length, (keep, 2 * length), (send_y, length))
    store_chunk(pieces(0), length, (keep, 0), (keep, length))


def relay_kernel(keep, got_x, got_y, send_x, send_y):
    length = send_x.shape[0]
    send_y[...] = (keep[2 * length : 3 * length, :] + got_x[...].astype(F32)).astype(BF16)
    send_x[...] = (keep[3 * length :, :] + got_y[...].astype(F32)).astype(BF16)


def grad_relay_kernel(keep, got_x, got_y, send_x, send_y):
    length = send_x.shape[0]
    send_y[...] = (keep[2 * length : 3 * length, :] + got_x[0:length, :].astype(F32)).astype(BF16)
    send_x[...] = (keep[3 * length :, :] + got_y[0:length, :].astype(F32)).astype(BF16)


def grad_total_kernel(keep, got_x, got_y, relay_x, relay_y, chunk):
    length = relay_x.shape[0]
    chunk[0:length, :] = (
        keep[0:length, :] + got_x[length:, :].astype(F32) + relay_y[...].astype(F32)
    ).astype(BF16)
    chunk[length:, :] = (
        keep[length : 2 * length, :] + got_y[length:, :].astype(F32) + relay_x[...].astype(F32)
    ).astype(BF16)


def factor_kernel(replicas, keep, direct_x, direct_y, relay_x, relay_y, old, upper, lower, exact):
    share, order = old.shape
    half = share // 2
    starts = chunk_rows(share)
    length = upper.shape[0]
    mine = lax.axis_index("dp")
    total = jnp.concatenate(
        [
            keep[0:length, :] + direct_x[...].astype(F32) + relay_y[...].astype(F32),
            keep[length : 2 * length, :] + direct_y[...].astype(F32) + relay_x[...].astype(F32),
        ],
        axis=0,
    )
    diagonal = old[:, pl.ds(pl.multiple_of(mine * share, share), share)]
    block_sum = unpacked(total[0 : starts[1]])
    value = DECAY * diagonal + (1.0 - DECAY) * block_sum + DAMPING * eye_of(share, share)
    exact[0:share, :] = value
    squares = jnp.sum(value * value, axis=0, keepdims=True)
    values = [packed_upper(value).astype(BF16)]
    for position, step in enumerate(OFFSETS[1:]):
        other = mine ^ step
        block = old[:, pl.ds(pl.multiple_of(other * share, share), share)]
        term = DECAY * jnp.where(mine < other, block[0:half], block[:, half:].T)
        start = starts[1 + position]
        value = term + (1.0 - DECAY) * total[start : start + half]
        exact[share + position * half : share + (position + 1) * half, :] = value
        squares = squares + 2.0 * jnp.sum(value * value, axis=0, keepdims=True)
        values.append(value.astype(BF16))
    high = squares.astype(BF16).astype(F32)
    middle = (squares - high).astype(BF16).astype(F32)
    rest = squares - high - middle
    spot = lax.broadcasted_iota(jnp.int32, (16, share), 0)
    digits = jnp.where(spot == 0, high, jnp.where(spot == 1, middle, jnp.where(spot == 2, rest, 0.0)))
    values.append(digits.astype(BF16))
    chunk = jnp.concatenate(values, axis=0)
    upper[...] = chunk[0:length]
    lower[...] = chunk[length:]


def root_kernel(count, exact, *rest):
    chunks = [rest[2 * i : 2 * i + 2] for i in range(4)]
    factor_out, root_out, finished, factor, diagonal, rows, sent = rest[8:]
    share, order = root_out.shape
    half = share // 2
    starts = chunk_rows(share)
    length = chunks[0][0].shape[0]
    mine = lax.axis_index("dp")

    def rows_of(position, start, count):
        upper, lower = chunks[position]
        if start + count <= length:
            return upper[start : start + count, :]
        if start >= length:
            return lower[start - length : start - length + count, :]
        return jnp.concatenate([upper[start:length, :], lower[0 : start + count - length, :]], axis=0)

    copies = []
    for position, step in enumerate(OFFSETS):
        other = mine ^ step
        target = rows.at[position]
        if position == 0:
            target[...] = exact[0:share, :]
        else:
            start = starts[position]
            own = exact[share + (position - 1) * half : share + position * half, :]
            theirs = rows_of(position, start, half).astype(F32)

            @pl.when(mine < other)
            def _():
                target[0:half, :] = own
                target[half:, :] = theirs

            @pl.when(mine > other)
            def _():
                target[...] = jnp.concatenate([theirs.T, own.T], axis=1)

        columns = pl.ds(pl.multiple_of(other * share, share), share)
        copies.append(pltpu.make_async_copy(target, factor_out.at[:, columns], sent.at[position]))
        copies[-1].start()

    squares = jnp.zeros((16, share), F32)
    block_eye = eye_of(share, share)
    for position, offset in enumerate(OFFSETS):
        owner = mine ^ offset
        own_band = pl.ds(pl.multiple_of(owner * share, share), share)
        block = unpacked(rows_of(position, 0, starts[1]).astype(F32))
        factor[own_band, own_band] = block.astype(BF16)
        diagonal[:, own_band] = jnp.sum(block * block_eye, axis=0, keepdims=True)
        for start, step in zip(starts[1:], OFFSETS[1:]):
            row, col = shared_half(owner, step, share)
            block = rows_of(position, start, half)
            factor[pl.ds(row, half), pl.ds(col, share)] = block
            factor[pl.ds(col, share), pl.ds(row, half)] = transposed(block)
        squares = squares + rows_of(position, starts[-1], 16).astype(F32)

    scale = jnp.sqrt(jnp.sum(squares, keepdims=True) / order + EPSILON)
    inverse = 1.0 / scale
    ones = (diagonal[...] * inverse).astype(BF16).astype(F32)
    lift = (1.5 - 0.5 * ones).astype(BF16).astype(F32) + 0.5 * (diagonal[...] * inverse)
    eye = eye_of(share, order, mine * share)
    my_rows = pl.ds(pl.multiple_of(mine * share, share), share)
    first = (factor[my_rows, :].astype(F32) * inverse).astype(BF16).astype(F32)
    turn = (1.5 * eye - 0.5 * first).astype(BF16)
    second = (jnp.dot(turn, factor[...], preferred_element_type=F32) * inverse).astype(BF16)
    product = (-0.5 * inverse) * jnp.dot(second, factor[...], preferred_element_type=F32) + second.astype(F32) * lift
    turn_two = (1.5 * eye - 0.5 * product).astype(BF16)
    inverse_rows = (-0.5 * inverse) * jnp.dot(
        turn_two, factor[...], preferred_element_type=F32
    ) + turn_two.astype(F32) * lift
    chosen = jnp.where(count[0, 0] == 1, turn.astype(F32), inverse_rows)
    root_out[...] = (chosen * lax.rsqrt(scale)).astype(BF16)
    finished[...] = jnp.zeros_like(finished)
    for copy in copies:
        copy.wait()


def step_kernel(replicas, *refs):
    chunks = refs[:replicas]
    old_root, step_out, grads, result = refs[replicas:]
    share = old_root.shape[0]
    strip = step_out.shape[0] // replicas
    mine = lax.axis_index("dp")
    for offset, chunk in enumerate(chunks):
        for part in range(replicas):
            grads[offset * strip : (offset + 1) * strip, part * share : (part + 1) * share] = chunk[
                part * strip : (part + 1) * strip, :
            ]
    result[...] = lax.dot_general(
        grads[...], old_root[...], (((1,), (1,)), ((), ())), preferred_element_type=F32
    ).astype(BF16)
    for position, offset in enumerate(OFFSETS):
        rows = pl.ds(pl.multiple_of((mine ^ offset) * strip, strip), strip)
        step_out[rows, :] = result[position * strip : (position + 1) * strip, :]


def square_plan(acts, out_grad, old_factor, old_root, iter_count):
    replicas = lax.axis_size("dp")
    inputs = acts[0]
    tokens, order = inputs.shape
    share = order // replicas
    grows = out_grad.shape[2]
    params = pltpu.CompilerParams(vmem_limit_bytes=VMEM_LIMIT)
    whole_rows = chunk_rows(share)[-1]
    length = whole_rows // 2

    def shape(rows, kind=BF16, columns=share):
        return jax.ShapeDtypeStruct((rows, columns), kind)

    def call(kernel, outs, name, *operands, first=None, first_out=None, after=(), scratch=()):
        in_specs = whole(len(operands)) + [pl.BlockSpec(memory_space=pl.ANY)] * len(after)
        if first is not None:
            in_specs[0] = pl.BlockSpec(memory_space=first)
        out_specs = whole(len(outs))
        if first_out is not None:
            out_specs[0] = pl.BlockSpec(memory_space=first_out)

        def body(*refs):
            kernel(*refs[: len(operands)], *refs[len(operands) + len(after) :])

        return pl.pallas_call(
            body,
            out_shape=outs,
            in_specs=in_specs,
            out_specs=out_specs,
            scratch_shapes=scratch,
            compiler_params=params,
            name=name,
        )(*operands, *after)

    received = passed_along(out_grad, "pipe", -1)[0]
    relay_x, relay_y, direct_x, direct_y, keep = call(
        functools.partial(batch_kernel, replicas, tokens * replicas),
        [shape(length)] * 4 + [shape(4 * length, F32)],
        "batch",
        inputs,
        scratch=[pltpu.VMEM((order, order), F32)],
    )
    relay_x, relay_y = swapped(relay_x, 1), swapped(relay_y, 2)
    direct_x, direct_y = swapped(direct_x, 1), swapped(direct_y, 2)
    relay_x, relay_y = call(relay_kernel, [shape(length)] * 2, "relay", keep, relay_x, relay_y)
    grad_x, grad_y, grad_keep = call(
        functools.partial(grad_kernel, replicas, tokens * replicas),
        [shape(grows)] * 2 + [shape(2 * grows, F32)],
        "grad",
        inputs,
        received,
        after=[relay_x, relay_y],
        scratch=[pltpu.VMEM((grows, order), F32)],
    )
    relay_x, relay_y = swapped(relay_x, 1), swapped(relay_y, 2)
    grad_x, grad_y = swapped(grad_x, 1), swapped(grad_y, 2)
    upper, lower, exact = call(
        functools.partial(factor_kernel, replicas),
        [shape(length), shape(length + 16), shape(5 * share // 2, F32)],
        "factor",
        keep,
        direct_x,
        direct_y,
        relay_x,
        relay_y,
        old_factor[0, 0],
    )
    upper_x, lower_y = swapped(upper, 1), swapped(lower, 2)
    lower_x, upper_y = swapped(lower, 1), swapped(upper, 2)
    strip_x, strip_y = call(
        grad_relay_kernel, [shape(grows // 2)] * 2, "grad_relay", grad_keep, grad_x, grad_y, after=[upper, lower]
    )
    strip_x, strip_y = swapped(strip_x, 1), swapped(strip_y, 2)
    upper_far, lower_far = swapped(upper_x, 2), swapped(lower_y, 1)
    (strip,) = call(
        grad_total_kernel,
        [shape(grows)],
        "grad_total",
        grad_keep,
        grad_x,
        grad_y,
        strip_x,
        strip_y,
        after=[upper_x, lower_y],
    )
    strips = [strip, swapped(strip, 1), swapped(strip, 2), swapped(strip, 3)]
    factor, root, finished = call(
        root_kernel,
        [shape(share, F32, order), shape(share, BF16, order), shape(8, F32, 128)],
        "root",
        iter_count,
        exact,
        upper,
        lower,
        upper_x,
        lower_x,
        upper_y,
        lower_y,
        upper_far,
        lower_far,
        first=pltpu.SMEM,
        first_out=pl.ANY,
        scratch=[
            pltpu.VMEM((order, order), BF16),
            pltpu.VMEM((1, order), F32),
            pltpu.VMEM((replicas, share, share), F32),
            pltpu.SemaphoreType.DMA((replicas,)),
        ],
    )
    (step,) = call(
        functools.partial(step_kernel, replicas),
        [shape(grows, BF16, share)],
        "step",
        *strips,
        old_root[0, 0],
        after=[finished],
        scratch=[pltpu.VMEM((grows, order), BF16), pltpu.VMEM((grows, share), BF16)],
    )
    return (factor[None, None], root[None, None], step[None, None])


def ring_plan(acts, out_grad, old_factor, old_root, iter_count):
    inputs = acts[0]
    replicas = lax.axis_size("dp")
    tokens_all = inputs.shape[0] * replicas
    order = inputs.shape[1]
    share = order // replicas
    offset = lax.axis_index("dp") * share
    received = passed_along(out_grad, "pipe", -1)[0]
    partial_grad = jnp.dot(received.T, inputs, preferred_element_type=F32) / math.sqrt(tokens_all)
    batch = lax.psum_scatter(
        jnp.dot(inputs.T, inputs, preferred_element_type=F32) / tokens_all,
        "dp",
        scatter_dimension=0,
        tiled=True,
    )
    eye_rows = eye_of(share, order, offset)
    factor = DECAY * old_factor[0, 0] + (1.0 - DECAY) * batch + DAMPING * eye_rows
    grad16 = lax.psum(partial_grad, "dp").astype(BF16)
    scale = jnp.sqrt(lax.psum(jnp.sum(factor * factor), "dp") / order + EPSILON)
    step = lax.dot_general(
        grad16, old_root[0, 0], (((1,), (1,)), ((), ())), preferred_element_type=F32
    ).astype(BF16)
    first = lax.all_gather((factor / scale).astype(BF16), "dp", axis=0, tiled=True)
    turn_one = (1.5 * eye_of(order, order) - 0.5 * first.astype(F32)).astype(BF16)
    turn_rows = lax.dynamic_slice_in_dim(turn_one, offset, share, 0)
    second = jnp.dot(turn_rows, first, preferred_element_type=F32).astype(BF16)
    product = jnp.dot(second, turn_one, preferred_element_type=F32)
    turn_two = (1.5 * eye_rows - 0.5 * product).astype(BF16)
    inverse_rows = jnp.dot(turn_two, turn_one, preferred_element_type=F32)
    chosen = jnp.where(iter_count[0, 0] == 1, turn_rows.astype(F32), inverse_rows)
    root = (chosen / jnp.sqrt(scale)).astype(BF16)
    return (factor[None, None], root[None, None], step[None, None])


def solution(mesh):
    return jax.shard_map(
        square_plan if mesh.shape["dp"] == 4 else ring_plan,
        mesh=mesh,
        in_specs=(
            P("pipe", "dp", "tensor"),
            P("pipe", "dp", "tensor"),
            P("pipe", "tensor", "dp", None),
            P("pipe", "tensor", "dp", None),
            P("pipe", "tensor"),
        ),
        out_specs=(
            P("pipe", "tensor", "dp", None),
            P("pipe", "tensor", "dp", None),
            P("pipe", "tensor", None, "dp"),
        ),
        check_vma=False,
    )
```

```python
import functools
import math

import jax
import jax.numpy as jnp
from jax import lax
from jax.experimental import pallas as pl
from jax.experimental.pallas import tpu as pltpu
from jax.sharding import PartitionSpec as P

DECAY = 0.75
DAMPING = 0.1
EPSILON = 1e-06
BF16 = jnp.bfloat16
F32 = jnp.float32
VMEM_LIMIT = 28 * 1024 * 1024


def passed_along(block, axis, distance):
    devices = range(lax.axis_size(axis))
    route = [((i - distance) % len(devices), i) for i in devices]
    return lax.ppermute(block, axis, route)


def swapped(block, offset):
    return lax.ppermute(block, "dp", [(i, i ^ offset) for i in range(lax.axis_size("dp"))])


def eye_of(rows, cols, shift=0):
    row_ids = lax.broadcasted_iota(jnp.int32, (rows, cols), 0) + shift
    col_ids = lax.broadcasted_iota(jnp.int32, (rows, cols), 1)
    return (row_ids == col_ids).astype(F32)


def whole(count):
    return [pl.BlockSpec(memory_space=pltpu.VMEM)] * count


def transposed(block):
    return block.astype(F32).T.astype(block.dtype)


OFFSETS = (0, 1, 2, 3)


def chunk_rows(share):
    half, packed = share // 2, 5 * share // 8
    return [0] + [packed + half * i for i in range(4)]


def packed_upper(block):
    quarter = block.shape[0] // 4
    column = lax.broadcasted_iota(jnp.int32, (quarter, 4 * quarter), 1)
    second = pltpu.roll(block[quarter : 2 * quarter], 3 * quarter, 1)
    third = block[2 * quarter : 3 * quarter, 2 * quarter :]
    return jnp.concatenate(
        [
            block[0:quarter],
            jnp.where(column < 3 * quarter, second, block[3 * quarter :]),
            jnp.concatenate([third[0 : quarter // 2], third[quarter // 2 :]], axis=1),
        ],
        axis=0,
    )


def unpacked(packed):
    share = packed.shape[1]
    quarter = share // 4
    column = lax.broadcasted_iota(jnp.int32, (quarter, share), 1)
    second = packed[quarter : 2 * quarter]
    third = packed[2 * quarter :]
    third = jnp.concatenate([third[:, 0 : 2 * quarter], third[:, 2 * quarter :]], axis=0)
    upper = jnp.concatenate(
        [
            packed[0:quarter],
            jnp.where(column < quarter, 0.0, pltpu.roll(second, quarter, 1)),
            jnp.concatenate([jnp.zeros((quarter, 2 * quarter), F32), third], axis=1),
            jnp.where(column < 3 * quarter, 0.0, second),
        ],
        axis=0,
    )
    rows = lax.broadcasted_iota(jnp.int32, (share, share), 0) // quarter
    columns = lax.broadcasted_iota(jnp.int32, (share, share), 1) // quarter
    return upper + jnp.where(rows == columns, 0.0, upper).T


def shared_half(owner, offset, share):
    other = owner ^ offset
    low, high = jnp.minimum(owner, other), jnp.maximum(owner, other)
    row = low * share + jnp.where(owner > other, share // 2, 0)
    return pl.multiple_of(row, share // 2), pl.multiple_of(high * share, share)


def store_chunk(pieces, length, upper, lower):
    for start, piece in pieces:
        stop = start + piece.shape[0]
        for target, low, high in ((upper, 0, length), (lower, length, stop)):
            first, last = max(start, low), min(stop, high)
            if target is not None and first < last:
                ref, at = target
                ref[at + first - low : at + last - low, :] = piece[first - start : last - start].astype(ref.dtype)


def across_kernel(tokens_all, acts, relay_x, relay_y):
    share = relay_x.shape[1]
    half = share // 2
    starts = chunk_rows(share)
    owner = lax.axis_index("dp") ^ 3

    def product(left, right):
        return lax.dot_general(
            acts[:, left], acts[:, right], (((0,), (0,)), ((), ())), preferred_element_type=F32
        ) * (1.0 / tokens_all)

    columns = pl.ds(pl.multiple_of(owner * share, share), share)
    pieces = [(0, packed_upper(product(columns, columns)))]
    for start, step in zip(starts[1:], OFFSETS[1:]):
        row, col = shared_half(owner, step, share)
        pieces.append((start, product(pl.ds(row, half), pl.ds(col, share))))
    store_chunk(pieces, relay_x.shape[0], (relay_x, 0), (relay_y, 0))


def batch_kernel(replicas, tokens_all, acts, direct_x, direct_y, keep, batch):
    order = acts.shape[1]
    share = order // replicas
    half = share // 2
    starts = chunk_rows(share)
    length = direct_x.shape[0]
    mine = lax.axis_index("dp")
    for i in range(replicas):
        band = slice(i * share, (i + 1) * share)
        batch[band, i * share :] = lax.dot_general(
            acts[:, band], acts[:, i * share :], (((0,), (0,)), ((), ())), preferred_element_type=F32
        ) * (1.0 / tokens_all)

    def pieces(offset):
        owner = mine ^ offset
        base = pl.multiple_of(owner * share, share)
        yield 0, packed_upper(batch[pl.ds(base, share), pl.ds(base, share)])
        for start, step in zip(starts[1:], OFFSETS[1:]):
            row, col = shared_half(owner, step, share)
            yield start, batch[pl.ds(row, half), pl.ds(col, share)]

    store_chunk(pieces(1), length, (direct_x, 0), (keep, 3 * length))
    store_chunk(pieces(2), length, (keep, 2 * length), (direct_y, 0))
    store_chunk(pieces(0), length, (keep, 0), (keep, length))


def grad_kernel(replicas, tokens_all, acts, grads, send_x, send_y, keep, total):
    order = acts.shape[1]
    share = order // replicas
    strip = grads.shape[1] // replicas
    length = send_x.shape[0] // 2
    mine = lax.axis_index("dp")
    total[...] = lax.dot_general(
        grads[...], acts[...], (((0,), (0,)), ((), ())), preferred_element_type=F32
    ) * (1.0 / math.sqrt(tokens_all))

    def pieces(offset):
        rows = pl.ds(pl.multiple_of((mine ^ offset) * strip, strip), strip)
        for part in range(replicas):
            yield part * strip, total[rows, part * share : (part + 1) * share]

    store_chunk(pieces(3), length, (send_x, 0), (send_y, 0))
    store_chunk(pieces(1), length, (send_x, length), (keep, 3 * length))
    store_chunk(pieces(2), length, (keep, 2 * length), (send_y, length))
    store_chunk(pieces(0), length, (keep, 0), (keep, length))


def relay_kernel(keep, got_x, got_y, send_x, send_y):
    length = send_x.shape[0]
    send_y[...] = (keep[2 * length : 3 * length, :] + got_x[...].astype(F32)).astype(BF16)
    send_x[...] = (keep[3 * length :, :] + got_y[...].astype(F32)).astype(BF16)


def grad_relay_kernel(keep, got_x, got_y, send_x, send_y):
    length = send_x.shape[0]
    send_y[...] = (keep[2 * length : 3 * length, :] + got_x[0:length, :].astype(F32)).astype(BF16)
    send_x[...] = (keep[3 * length :, :] + got_y[0:length, :].astype(F32)).astype(BF16)


def grad_total_kernel(keep, got_x, got_y, relay_x, relay_y, chunk):
    length = relay_x.shape[0]
    chunk[0:length, :] = (
        keep[0:length, :] + got_x[length:, :].astype(F32) + relay_y[...].astype(F32)
    ).astype(BF16)
    chunk[length:, :] = (
        keep[length : 2 * length, :] + got_y[length:, :].astype(F32) + relay_x[...].astype(F32)
    ).astype(BF16)


def factor_kernel(replicas, keep, direct_x, direct_y, relay_x, relay_y, old, upper, lower, exact):
    share, order = old.shape
    half = share // 2
    starts = chunk_rows(share)
    length = upper.shape[0]
    mine = lax.axis_index("dp")
    total = jnp.concatenate(
        [
            keep[0:length, :] + direct_x[...].astype(F32) + relay_y[...].astype(F32),
            keep[length : 2 * length, :] + direct_y[...].astype(F32) + relay_x[...].astype(F32),
        ],
        axis=0,
    )
    diagonal = old[:, pl.ds(pl.multiple_of(mine * share, share), share)]
    block_sum = unpacked(total[0 : starts[1]])
    value = DECAY * diagonal + (1.0 - DECAY) * block_sum + DAMPING * eye_of(share, share)
    exact[0:share, :] = value
    squares = jnp.sum(value * value, axis=0, keepdims=True)
    values = [packed_upper(value).astype(BF16)]
    for position, step in enumerate(OFFSETS[1:]):
        other = mine ^ step
        block = old[:, pl.ds(pl.multiple_of(other * share, share), share)]
        term = DECAY * jnp.where(mine < other, block[0:half], block[:, half:].T)
        start = starts[1 + position]
        value = term + (1.0 - DECAY) * total[start : start + half]
        exact[share + position * half : share + (position + 1) * half, :] = value
        squares = squares + 2.0 * jnp.sum(value * value, axis=0, keepdims=True)
        values.append(value.astype(BF16))
    high = squares.astype(BF16).astype(F32)
    middle = (squares - high).astype(BF16).astype(F32)
    rest = squares - high - middle
    spot = lax.broadcasted_iota(jnp.int32, (16, share), 0)
    digits = jnp.where(spot == 0, high, jnp.where(spot == 1, middle, jnp.where(spot == 2, rest, 0.0)))
    values.append(digits.astype(BF16))
    chunk = jnp.concatenate(values, axis=0)
    upper[...] = chunk[0:length]
    lower[...] = chunk[length:]


def root_kernel(count, exact, *rest):
    chunks = [rest[2 * i : 2 * i + 2] for i in range(4)]
    factor_out, root_out, finished, factor, diagonal, rows, sent = rest[8:]
    share, order = root_out.shape
    half = share // 2
    starts = chunk_rows(share)
    length = chunks[0][0].shape[0]
    mine = lax.axis_index("dp")

    def rows_of(position, start, count):
        upper, lower = chunks[position]
        if start + count <= length:
            return upper[start : start + count, :]
        if start >= length:
            return lower[start - length : start - length + count, :]
        return jnp.concatenate([upper[start:length, :], lower[0 : start + count - length, :]], axis=0)

    copies = []
    for position, step in enumerate(OFFSETS):
        other = mine ^ step
        target = rows.at[position]
        if position == 0:
            target[...] = exact[0:share, :]
        else:
            start = starts[position]
            own = exact[share + (position - 1) * half : share + position * half, :]
            theirs = rows_of(position, start, half).astype(F32)

            @pl.when(mine < other)
            def _():
                target[0:half, :] = own
                target[half:, :] = theirs

            @pl.when(mine > other)
            def _():
                target[...] = jnp.concatenate([theirs.T, own.T], axis=1)

        columns = pl.ds(pl.multiple_of(other * share, share), share)
        copies.append(pltpu.make_async_copy(target, factor_out.at[:, columns], sent.at[position]))
        copies[-1].start()

    squares = jnp.zeros((16, share), F32)
    block_eye = eye_of(share, share)
    for position, offset in enumerate(OFFSETS):
        owner = mine ^ offset
        own_band = pl.ds(pl.multiple_of(owner * share, share), share)
        block = unpacked(rows_of(position, 0, starts[1]).astype(F32))
        factor[own_band, own_band] = block.astype(BF16)
        diagonal[:, own_band] = jnp.sum(block * block_eye, axis=0, keepdims=True)
        for start, step in zip(starts[1:], OFFSETS[1:]):
            row, col = shared_half(owner, step, share)
            block = rows_of(position, start, half)
            factor[pl.ds(row, half), pl.ds(col, share)] = block
            factor[pl.ds(col, share), pl.ds(row, half)] = transposed(block)
        squares = squares + rows_of(position, starts[-1], 16).astype(F32)

    scale = jnp.sqrt(jnp.sum(squares, keepdims=True) / order + EPSILON)
    inverse = 1.0 / scale
    ones = (diagonal[...] * inverse).astype(BF16).astype(F32)
    lift = (1.5 - 0.5 * ones).astype(BF16).astype(F32) + 0.5 * (diagonal[...] * inverse)
    eye = eye_of(share, order, mine * share)
    my_rows = pl.ds(pl.multiple_of(mine * share, share), share)
    first = (factor[my_rows, :].astype(F32) * inverse).astype(BF16).astype(F32)
    turn = (1.5 * eye - 0.5 * first).astype(BF16)
    second = (jnp.dot(turn, factor[...], preferred_element_type=F32) * inverse).astype(BF16)
    product = (-0.5 * inverse) * jnp.dot(second, factor[...], preferred_element_type=F32) + second.astype(F32) * lift
    turn_two = (1.5 * eye - 0.5 * product).astype(BF16)
    inverse_rows = (-0.5 * inverse) * jnp.dot(
        turn_two, factor[...], preferred_element_type=F32
    ) + turn_two.astype(F32) * lift
    chosen = jnp.where(count[0, 0] == 1, turn.astype(F32), inverse_rows)
    root_out[...] = (chosen * lax.rsqrt(scale)).astype(BF16)
    finished[...] = jnp.zeros_like(finished)
    for copy in copies:
        copy.wait()


def step_kernel(replicas, *refs):
    chunks = refs[:replicas]
    old_root, step_out, grads, result = refs[replicas:]
    share = old_root.shape[0]
    strip = step_out.shape[0] // replicas
    mine = lax.axis_index("dp")
    for offset, chunk in enumerate(chunks):
        for part in range(replicas):
            grads[offset * strip : (offset + 1) * strip, part * share : (part + 1) * share] = chunk[
                part * strip : (part + 1) * strip, :
            ]
    result[...] = lax.dot_general(
        grads[...], old_root[...], (((1,), (1,)), ((), ())), preferred_element_type=F32
    ).astype(BF16)
    for position, offset in enumerate(OFFSETS):
        rows = pl.ds(pl.multiple_of((mine ^ offset) * strip, strip), strip)
        step_out[rows, :] = result[position * strip : (position + 1) * strip, :]


def square_plan(acts, out_grad, old_factor, old_root, iter_count):
    replicas = lax.axis_size("dp")
    inputs = acts[0]
    tokens, order = inputs.shape
    share = order // replicas
    grows = out_grad.shape[2]
    params = pltpu.CompilerParams(vmem_limit_bytes=VMEM_LIMIT)
    whole_rows = chunk_rows(share)[-1]
    length = whole_rows // 2

    def shape(rows, kind=BF16, columns=share):
        return jax.ShapeDtypeStruct((rows, columns), kind)

    def call(kernel, outs, name, *operands, first=None, first_out=None, after=(), scratch=()):
        in_specs = whole(len(operands)) + [pl.BlockSpec(memory_space=pl.ANY)] * len(after)
        if first is not None:
            in_specs[0] = pl.BlockSpec(memory_space=first)
        out_specs = whole(len(outs))
        if first_out is not None:
            out_specs[0] = pl.BlockSpec(memory_space=first_out)

        def body(*refs):
            kernel(*refs[: len(operands)], *refs[len(operands) + len(after) :])

        return pl.pallas_call(
            body,
            out_shape=outs,
            in_specs=in_specs,
            out_specs=out_specs,
            scratch_shapes=scratch,
            compiler_params=params,
            name=name,
        )(*operands, *after)

    received = passed_along(out_grad, "pipe", -1)[0]
    relay_x, relay_y = call(
        functools.partial(across_kernel, tokens * replicas), [shape(length)] * 2, "across", inputs
    )
    direct_x, direct_y, keep = call(
        functools.partial(batch_kernel, replicas, tokens * replicas),
        [shape(length)] * 2 + [shape(4 * length, F32)],
        "batch",
        inputs,
        after=[relay_x],
        scratch=[pltpu.VMEM((order, order), F32)],
    )
    relay_x, relay_y = swapped(relay_x, 1), swapped(relay_y, 2)
    direct_x, direct_y = swapped(direct_x, 1), swapped(direct_y, 2)
    relay_x, relay_y = call(relay_kernel, [shape(length)] * 2, "relay", keep, relay_x, relay_y)
    grad_x, grad_y, grad_keep = call(
        functools.partial(grad_kernel, replicas, tokens * replicas),
        [shape(grows)] * 2 + [shape(2 * grows, F32)],
        "grad",
        inputs,
        received,
        after=[relay_x, relay_y],
        scratch=[pltpu.VMEM((grows, order), F32)],
    )
    relay_x, relay_y = swapped(relay_x, 1), swapped(relay_y, 2)
    grad_x, grad_y = swapped(grad_x, 1), swapped(grad_y, 2)
    upper, lower, exact = call(
        functools.partial(factor_kernel, replicas),
        [shape(length), shape(length + 16), shape(5 * share // 2, F32)],
        "factor",
        keep,
        direct_x,
        direct_y,
        relay_x,
        relay_y,
        old_factor[0, 0],
    )
    upper_x, lower_y = swapped(upper, 1), swapped(lower, 2)
    lower_x, upper_y = swapped(lower, 1), swapped(upper, 2)
    strip_x, strip_y = call(
        grad_relay_kernel, [shape(grows // 2)] * 2, "grad_relay", grad_keep, grad_x, grad_y, after=[upper, lower]
    )
    strip_x, strip_y = swapped(strip_x, 1), swapped(strip_y, 2)
    upper_far, lower_far = swapped(upper_x, 2), swapped(lower_y, 1)
    (strip,) = call(
        grad_total_kernel,
        [shape(grows)],
        "grad_total",
        grad_keep,
        grad_x,
        grad_y,
        strip_x,
        strip_y,
        after=[upper_x, lower_y],
    )
    strips = [strip, swapped(strip, 1), swapped(strip, 2), swapped(strip, 3)]
    factor, root, finished = call(
        root_kernel,
        [shape(share, F32, order), shape(share, BF16, order), shape(8, F32, 128)],
        "root",
        iter_count,
        exact,
        upper,
        lower,
        upper_x,
        lower_x,
        upper_y,
        lower_y,
        upper_far,
        lower_far,
        first=pltpu.SMEM,
        first_out=pl.ANY,
        scratch=[
            pltpu.VMEM((order, order), BF16),
            pltpu.VMEM((1, order), F32),
            pltpu.VMEM((replicas, share, share), F32),
            pltpu.SemaphoreType.DMA((replicas,)),
        ],
    )
    (step,) = call(
        functools.partial(step_kernel, replicas),
        [shape(grows, BF16, share)],
        "step",
        *strips,
        old_root[0, 0],
        after=[finished],
        scratch=[pltpu.VMEM((grows, order), BF16), pltpu.VMEM((grows, share), BF16)],
    )
    return (factor[None, None], root[None, None], step[None, None])


def ring_plan(acts, out_grad, old_factor, old_root, iter_count):
    inputs = acts[0]
    replicas = lax.axis_size("dp")
    tokens_all = inputs.shape[0] * replicas
    order = inputs.shape[1]
    share = order // replicas
    offset = lax.axis_index("dp") * share
    received = passed_along(out_grad, "pipe", -1)[0]
    partial_grad = jnp.dot(received.T, inputs, preferred_element_type=F32) / math.sqrt(tokens_all)
    batch = lax.psum_scatter(
        jnp.dot(inputs.T, inputs, preferred_element_type=F32) / tokens_all,
        "dp",
        scatter_dimension=0,
        tiled=True,
    )
    eye_rows = eye_of(share, order, offset)
    factor = DECAY * old_factor[0, 0] + (1.0 - DECAY) * batch + DAMPING * eye_rows
    grad16 = lax.psum(partial_grad, "dp").astype(BF16)
    scale = jnp.sqrt(lax.psum(jnp.sum(factor * factor), "dp") / order + EPSILON)
    step = lax.dot_general(
        grad16, old_root[0, 0], (((1,), (1,)), ((), ())), preferred_element_type=F32
    ).astype(BF16)
    first = lax.all_gather((factor / scale).astype(BF16), "dp", axis=0, tiled=True)
    turn_one = (1.5 * eye_of(order, order) - 0.5 * first.astype(F32)).astype(BF16)
    turn_rows = lax.dynamic_slice_in_dim(turn_one, offset, share, 0)
    second = jnp.dot(turn_rows, first, preferred_element_type=F32).astype(BF16)
    product = jnp.dot(second, turn_one, preferred_element_type=F32)
    turn_two = (1.5 * eye_rows - 0.5 * product).astype(BF16)
    inverse_rows = jnp.dot(turn_two, turn_one, preferred_element_type=F32)
    chosen = jnp.where(iter_count[0, 0] == 1, turn_rows.astype(F32), inverse_rows)
    root = (chosen / jnp.sqrt(scale)).astype(BF16)
    return (factor[None, None], root[None, None], step[None, None])


def solution(mesh):
    return jax.shard_map(
        square_plan if mesh.shape["dp"] == 4 else ring_plan,
        mesh=mesh,
        in_specs=(
            P("pipe", "dp", "tensor"),
            P("pipe", "dp", "tensor"),
            P("pipe", "tensor", "dp", None),
            P("pipe", "tensor", "dp", None),
            P("pipe", "tensor"),
        ),
        out_specs=(
            P("pipe", "tensor", "dp", None),
            P("pipe", "tensor", "dp", None),
            P("pipe", "tensor", None, "dp"),
        ),
        check_vma=False,
    )
```

```python
import functools
import math

import jax
import jax.numpy as jnp
from jax import lax
from jax.experimental import pallas as pl
from jax.experimental.pallas import tpu as pltpu
from jax.sharding import PartitionSpec as P

DECAY = 0.75
DAMPING = 0.1
EPSILON = 1e-06
BF16 = jnp.bfloat16
F32 = jnp.float32
VMEM_LIMIT = 28 * 1024 * 1024


def passed_along(block, axis, distance):
    devices = range(lax.axis_size(axis))
    route = [((i - distance) % len(devices), i) for i in devices]
    return lax.ppermute(block, axis, route)


def swapped(block, offset):
    return lax.ppermute(block, "dp", [(i, i ^ offset) for i in range(lax.axis_size("dp"))])


def eye_of(rows, cols, shift=0):
    row_ids = lax.broadcasted_iota(jnp.int32, (rows, cols), 0) + shift
    col_ids = lax.broadcasted_iota(jnp.int32, (rows, cols), 1)
    return (row_ids == col_ids).astype(F32)


def whole(count):
    return [pl.BlockSpec(memory_space=pltpu.VMEM)] * count


def transposed(block):
    return block.T


OFFSETS = (0, 1, 2, 3)


def chunk_rows(share):
    half, packed = share // 2, 5 * share // 8
    return [0] + [packed + half * i for i in range(4)]


def packed_upper(block):
    quarter = block.shape[0] // 4
    column = lax.broadcasted_iota(jnp.int32, (quarter, 4 * quarter), 1)
    second = pltpu.roll(block[quarter : 2 * quarter], 3 * quarter, 1)
    third = block[2 * quarter : 3 * quarter, 2 * quarter :]
    return jnp.concatenate(
        [
            block[0:quarter],
            jnp.where(column < 3 * quarter, second, block[3 * quarter :]),
            jnp.concatenate([third[0 : quarter // 2], third[quarter // 2 :]], axis=1),
        ],
        axis=0,
    )


def unpacked(packed):
    share = packed.shape[1]
    quarter = share // 4
    column = lax.broadcasted_iota(jnp.int32, (quarter, share), 1)
    second = packed[quarter : 2 * quarter]
    third = packed[2 * quarter :]
    third = jnp.concatenate([third[:, 0 : 2 * quarter], third[:, 2 * quarter :]], axis=0)
    upper = jnp.concatenate(
        [
            packed[0:quarter],
            jnp.where(column < quarter, 0.0, pltpu.roll(second, quarter, 1)),
            jnp.concatenate([jnp.zeros((quarter, 2 * quarter), F32), third], axis=1),
            jnp.where(column < 3 * quarter, 0.0, second),
        ],
        axis=0,
    )
    rows = lax.broadcasted_iota(jnp.int32, (share, share), 0) // quarter
    columns = lax.broadcasted_iota(jnp.int32, (share, share), 1) // quarter
    return upper + jnp.where(rows == columns, 0.0, upper).T


def shared_half(owner, offset, share):
    other = owner ^ offset
    low, high = jnp.minimum(owner, other), jnp.maximum(owner, other)
    row = low * share + jnp.where(owner > other, share // 2, 0)
    return pl.multiple_of(row, share // 2), pl.multiple_of(high * share, share)


def store_chunk(pieces, length, upper, lower):
    for start, piece in pieces:
        stop = start + piece.shape[0]
        for target, low, high in ((upper, 0, length), (lower, length, stop)):
            first, last = max(start, low), min(stop, high)
            if target is not None and first < last:
                ref, at = target
                ref[at + first - low : at + last - low, :] = piece[first - start : last - start].astype(ref.dtype)


def across_kernel(tokens_all, acts, relay_x, relay_y):
    share = relay_x.shape[1]
    half = share // 2
    starts = chunk_rows(share)
    owner = lax.axis_index("dp") ^ 3

    def product(left, right):
        return lax.dot_general(
            acts[:, left], acts[:, right], (((0,), (0,)), ((), ())), preferred_element_type=F32
        ) * (1.0 / tokens_all)

    columns = pl.ds(pl.multiple_of(owner * share, share), share)
    pieces = [(0, packed_upper(product(columns, columns)))]
    for start, step in zip(starts[1:], OFFSETS[1:]):
        row, col = shared_half(owner, step, share)
        pieces.append((start, product(pl.ds(row, half), pl.ds(col, share))))
    store_chunk(pieces, relay_x.shape[0], (relay_x, 0), (relay_y, 0))


def batch_kernel(replicas, tokens_all, acts, direct_x, direct_y, keep, batch):
    order = acts.shape[1]
    share = order // replicas
    half = share // 2
    starts = chunk_rows(share)
    length = direct_x.shape[0]
    mine = lax.axis_index("dp")
    for i in range(replicas):
        band = slice(i * share, (i + 1) * share)
        batch[band, i * share :] = lax.dot_general(
            acts[:, band], acts[:, i * share :], (((0,), (0,)), ((), ())), preferred_element_type=F32
        ) * (1.0 / tokens_all)

    def pieces(offset):
        owner = mine ^ offset
        base = pl.multiple_of(owner * share, share)
        yield 0, packed_upper(batch[pl.ds(base, share), pl.ds(base, share)])
        for start, step in zip(starts[1:], OFFSETS[1:]):
            row, col = shared_half(owner, step, share)
            yield start, batch[pl.ds(row, half), pl.ds(col, share)]

    store_chunk(pieces(1), length, (direct_x, 0), (keep, 3 * length))
    store_chunk(pieces(2), length, (keep, 2 * length), (direct_y, 0))
    store_chunk(pieces(0), length, (keep, 0), (keep, length))


def grad_kernel(replicas, tokens_all, acts, grads, old_root, send_x, send_y, keep, old_columns, total):
    old_columns[...] = old_root[...].T
    order = acts.shape[1]
    share = order // replicas
    strip = grads.shape[1] // replicas
    length = send_x.shape[0] // 2
    mine = lax.axis_index("dp")
    total[...] = lax.dot_general(
        grads[...], acts[...], (((0,), (0,)), ((), ())), preferred_element_type=F32
    ) * (1.0 / math.sqrt(tokens_all))

    def pieces(offset):
        rows = pl.ds(pl.multiple_of((mine ^ offset) * strip, strip), strip)
        for part in range(replicas):
            yield part * strip, total[rows, part * share : (part + 1) * share]

    store_chunk(pieces(3), length, (send_x, 0), (send_y, 0))
    store_chunk(pieces(1), length, (send_x, length), (keep, 3 * length))
    store_chunk(pieces(2), length, (keep, 2 * length), (send_y, length))
    store_chunk(pieces(0), length, (keep, 0), (keep, length))


def relay_kernel(keep, got_x, got_y, send_x, send_y):
    length = send_x.shape[0]
    send_y[...] = (keep[2 * length : 3 * length, :] + got_x[...].astype(F32)).astype(BF16)
    send_x[...] = (keep[3 * length :, :] + got_y[...].astype(F32)).astype(BF16)


def grad_relay_kernel(keep, got_x, got_y, send_x, send_y):
    length = send_x.shape[0]
    send_y[...] = (keep[2 * length : 3 * length, :] + got_x[0:length, :].astype(F32)).astype(BF16)
    send_x[...] = (keep[3 * length :, :] + got_y[0:length, :].astype(F32)).astype(BF16)


def grad_total_kernel(keep, got_x, got_y, relay_x, relay_y, chunk):
    length = relay_x.shape[0]
    chunk[0:length, :] = (
        keep[0:length, :] + got_x[length:, :].astype(F32) + relay_y[...].astype(F32)
    ).astype(BF16)
    chunk[length:, :] = (
        keep[length : 2 * length, :] + got_y[length:, :].astype(F32) + relay_x[...].astype(F32)
    ).astype(BF16)


def factor_kernel(replicas, keep, direct_x, direct_y, relay_x, relay_y, old, upper, lower, exact):
    share, order = old.shape
    half = share // 2
    starts = chunk_rows(share)
    length = upper.shape[0]
    mine = lax.axis_index("dp")
    total = jnp.concatenate(
        [
            keep[0:length, :] + direct_x[...].astype(F32) + relay_y[...].astype(F32),
            keep[length : 2 * length, :] + direct_y[...].astype(F32) + relay_x[...].astype(F32),
        ],
        axis=0,
    )
    diagonal = old[:, pl.ds(pl.multiple_of(mine * share, share), share)]
    block_sum = unpacked(total[0 : starts[1]])
    value = DECAY * diagonal + (1.0 - DECAY) * block_sum + DAMPING * eye_of(share, share)
    exact[0:share, :] = value
    squares = jnp.sum(value * value, axis=0, keepdims=True)
    values = [packed_upper(value).astype(BF16)]
    for position, step in enumerate(OFFSETS[1:]):
        other = mine ^ step
        block = old[:, pl.ds(pl.multiple_of(other * share, share), share)]
        term = DECAY * jnp.where(mine < other, block[0:half], block[:, half:].T)
        start = starts[1 + position]
        value = term + (1.0 - DECAY) * total[start : start + half]
        exact[share + position * half : share + (position + 1) * half, :] = value
        squares = squares + 2.0 * jnp.sum(value * value, axis=0, keepdims=True)
        values.append(value.astype(BF16))
    high = squares.astype(BF16).astype(F32)
    middle = (squares - high).astype(BF16).astype(F32)
    rest = squares - high - middle
    spot = lax.broadcasted_iota(jnp.int32, (16, share), 0)
    digits = jnp.where(spot == 0, high, jnp.where(spot == 1, middle, jnp.where(spot == 2, rest, 0.0)))
    values.append(digits.astype(BF16))
    chunk = jnp.concatenate(values, axis=0)
    upper[...] = chunk[0:length]
    lower[...] = chunk[length:]


def root_kernel(count, exact, *rest):
    chunks = [rest[2 * i : 2 * i + 2] for i in range(4)]
    factor_out, root_out, finished, factor, diagonal, rows, sent = rest[8:]
    share, order = root_out.shape
    half = share // 2
    starts = chunk_rows(share)
    length = chunks[0][0].shape[0]
    mine = lax.axis_index("dp")

    def rows_of(position, start, count):
        upper, lower = chunks[position]
        if start + count <= length:
            return upper[start : start + count, :]
        if start >= length:
            return lower[start - length : start - length + count, :]
        return jnp.concatenate([upper[start:length, :], lower[0 : start + count - length, :]], axis=0)

    copies = []
    for position, step in enumerate(OFFSETS):
        other = mine ^ step
        target = rows.at[position]
        if position == 0:
            target[...] = exact[0:share, :]
        else:
            start = starts[position]
            own = exact[share + (position - 1) * half : share + position * half, :]
            theirs = rows_of(position, start, half).astype(F32)

            @pl.when(mine < other)
            def _():
                target[0:half, :] = own
                target[half:, :] = theirs

            @pl.when(mine > other)
            def _():
                target[...] = jnp.concatenate([theirs.T, own.T], axis=1)

        columns = pl.ds(pl.multiple_of(other * share, share), share)
        copies.append(pltpu.make_async_copy(target, factor_out.at[:, columns], sent.at[position]))
        copies[-1].start()

    squares = jnp.zeros((16, share), F32)
    block_eye = eye_of(share, share)
    for position, offset in enumerate(OFFSETS):
        owner = mine ^ offset
        own_band = pl.ds(pl.multiple_of(owner * share, share), share)
        block = unpacked(rows_of(position, 0, starts[1]).astype(F32))
        factor[own_band, own_band] = block.astype(BF16)
        diagonal[:, own_band] = jnp.sum(block * block_eye, axis=0, keepdims=True)
        for start, step in zip(starts[1:], OFFSETS[1:]):
            row, col = shared_half(owner, step, share)
            block = rows_of(position, start, half)
            factor[pl.ds(row, half), pl.ds(col, share)] = block
            factor[pl.ds(col, share), pl.ds(row, half)] = transposed(block)
        squares = squares + rows_of(position, starts[-1], 16).astype(F32)

    scale = jnp.sqrt(jnp.sum(squares, keepdims=True) / order + EPSILON)
    inverse = 1.0 / scale
    ones = (diagonal[...] * inverse).astype(BF16).astype(F32)
    lift = (1.5 - 0.5 * ones).astype(BF16).astype(F32) + 0.5 * (diagonal[...] * inverse)
    eye = eye_of(share, order, mine * share)
    my_rows = pl.ds(pl.multiple_of(mine * share, share), share)
    first = (factor[my_rows, :].astype(F32) * inverse).astype(BF16).astype(F32)
    turn = (1.5 * eye - 0.5 * first).astype(BF16)
    second = (jnp.dot(turn, factor[...], preferred_element_type=F32) * inverse).astype(BF16)
    product = (-0.5 * inverse) * jnp.dot(second, factor[...], preferred_element_type=F32) + second.astype(F32) * lift
    turn_two = (1.5 * eye - 0.5 * product).astype(BF16)
    inverse_rows = (-0.5 * inverse) * jnp.dot(
        turn_two, factor[...], preferred_element_type=F32
    ) + turn_two.astype(F32) * lift
    chosen = jnp.where(count[0, 0] == 1, turn.astype(F32), inverse_rows)
    root_out[...] = (chosen * lax.rsqrt(scale)).astype(BF16)
    finished[...] = jnp.zeros_like(finished)
    for copy in copies:
        copy.wait()


def step_kernel(replicas, *refs):
    chunks = refs[:replicas]
    old_columns, step_out, grads, result = refs[replicas:]
    share = old_columns.shape[1]
    strip = step_out.shape[0] // replicas
    mine = lax.axis_index("dp")
    for offset, chunk in enumerate(chunks):
        for part in range(replicas):
            grads[offset * strip : (offset + 1) * strip, part * share : (part + 1) * share] = chunk[
                part * strip : (part + 1) * strip, :
            ]
    result[...] = jnp.dot(grads[...], old_columns[...], preferred_element_type=F32).astype(BF16)
    for position, offset in enumerate(OFFSETS):
        rows = pl.ds(pl.multiple_of((mine ^ offset) * strip, strip), strip)
        step_out[rows, :] = result[position * strip : (position + 1) * strip, :]


def square_plan(acts, out_grad, old_factor, old_root, iter_count):
    replicas = lax.axis_size("dp")
    inputs = acts[0]
    tokens, order = inputs.shape
    share = order // replicas
    grows = out_grad.shape[2]
    params = pltpu.CompilerParams(vmem_limit_bytes=VMEM_LIMIT)
    whole_rows = chunk_rows(share)[-1]
    length = whole_rows // 2

    def shape(rows, kind=BF16, columns=share):
        return jax.ShapeDtypeStruct((rows, columns), kind)

    def call(kernel, outs, name, *operands, first=None, first_out=None, after=(), scratch=()):
        in_specs = whole(len(operands)) + [pl.BlockSpec(memory_space=pl.ANY)] * len(after)
        if first is not None:
            in_specs[0] = pl.BlockSpec(memory_space=first)
        out_specs = whole(len(outs))
        if first_out is not None:
            out_specs[0] = pl.BlockSpec(memory_space=first_out)

        def body(*refs):
            kernel(*refs[: len(operands)], *refs[len(operands) + len(after) :])

        return pl.pallas_call(
            body,
            out_shape=outs,
            in_specs=in_specs,
            out_specs=out_specs,
            scratch_shapes=scratch,
            compiler_params=params,
            name=name,
        )(*operands, *after)

    received = passed_along(out_grad, "pipe", -1)[0]
    relay_x, relay_y = call(
        functools.partial(across_kernel, tokens * replicas), [shape(length)] * 2, "across", inputs
    )
    direct_x, direct_y, keep = call(
        functools.partial(batch_kernel, replicas, tokens * replicas),
        [shape(length)] * 2 + [shape(4 * length, F32)],
        "batch",
        inputs,
        after=[relay_x],
        scratch=[pltpu.VMEM((order, order), F32)],
    )
    relay_x, relay_y = swapped(relay_x, 1), swapped(relay_y, 2)
    direct_x, direct_y = swapped(direct_x, 1), swapped(direct_y, 2)
    relay_x, relay_y = call(relay_kernel, [shape(length)] * 2, "relay", keep, relay_x, relay_y)
    grad_x, grad_y, grad_keep, old_columns = call(
        functools.partial(grad_kernel, replicas, tokens * replicas),
        [shape(grows)] * 2 + [shape(2 * grows, F32), shape(order)],
        "grad",
        inputs,
        received,
        old_root[0, 0],
        after=[relay_x, relay_y],
        scratch=[pltpu.VMEM((grows, order), F32)],
    )
    relay_x, relay_y = swapped(relay_x, 1), swapped(relay_y, 2)
    grad_x, grad_y = swapped(grad_x, 1), swapped(grad_y, 2)
    upper, lower, exact = call(
        functools.partial(factor_kernel, replicas),
        [shape(length), shape(length + 16), shape(5 * share // 2, F32)],
        "factor",
        keep,
        direct_x,
        direct_y,
        relay_x,
        relay_y,
        old_factor[0, 0],
    )
    upper_x, lower_y = swapped(upper, 1), swapped(lower, 2)
    lower_x, upper_y = swapped(lower, 1), swapped(upper, 2)
    strip_x, strip_y = call(
        grad_relay_kernel, [shape(grows // 2)] * 2, "grad_relay", grad_keep, grad_x, grad_y, after=[upper, lower]
    )
    strip_x, strip_y = swapped(strip_x, 1), swapped(strip_y, 2)
    upper_far, lower_far = swapped(upper_x, 2), swapped(lower_y, 1)
    (strip,) = call(
        grad_total_kernel,
        [shape(grows)],
        "grad_total",
        grad_keep,
        grad_x,
        grad_y,
        strip_x,
        strip_y,
        after=[upper_x, lower_y],
    )
    strips = [strip, swapped(strip, 1), swapped(strip, 2), swapped(strip, 3)]
    factor, root, finished = call(
        root_kernel,
        [shape(share, F32, order), shape(share, BF16, order), shape(8, F32, 128)],
        "root",
        iter_count,
        exact,
        upper,
        lower,
        upper_x,
        lower_x,
        upper_y,
        lower_y,
        upper_far,
        lower_far,
        first=pltpu.SMEM,
        first_out=pl.ANY,
        scratch=[
            pltpu.VMEM((order, order), BF16),
            pltpu.VMEM((1, order), F32),
            pltpu.VMEM((replicas, share, share), F32),
            pltpu.SemaphoreType.DMA((replicas,)),
        ],
    )
    (step,) = call(
        functools.partial(step_kernel, replicas),
        [shape(grows, BF16, share)],
        "step",
        *strips,
        old_columns,
        after=[finished],
        scratch=[pltpu.VMEM((grows, order), BF16), pltpu.VMEM((grows, share), BF16)],
    )
    return (factor[None, None], root[None, None], step[None, None])


def ring_plan(acts, out_grad, old_factor, old_root, iter_count):
    inputs = acts[0]
    replicas = lax.axis_size("dp")
    tokens_all = inputs.shape[0] * replicas
    order = inputs.shape[1]
    share = order // replicas
    offset = lax.axis_index("dp") * share
    received = passed_along(out_grad, "pipe", -1)[0]
    partial_grad = jnp.dot(received.T, inputs, preferred_element_type=F32) / math.sqrt(tokens_all)
    batch = lax.psum_scatter(
        jnp.dot(inputs.T, inputs, preferred_element_type=F32) / tokens_all,
        "dp",
        scatter_dimension=0,
        tiled=True,
    )
    eye_rows = eye_of(share, order, offset)
    factor = DECAY * old_factor[0, 0] + (1.0 - DECAY) * batch + DAMPING * eye_rows
    grad16 = lax.psum(partial_grad, "dp").astype(BF16)
    scale = jnp.sqrt(lax.psum(jnp.sum(factor * factor), "dp") / order + EPSILON)
    step = lax.dot_general(
        grad16, old_root[0, 0], (((1,), (1,)), ((), ())), preferred_element_type=F32
    ).astype(BF16)
    first = lax.all_gather((factor / scale).astype(BF16), "dp", axis=0, tiled=True)
    turn_one = (1.5 * eye_of(order, order) - 0.5 * first.astype(F32)).astype(BF16)
    turn_rows = lax.dynamic_slice_in_dim(turn_one, offset, share, 0)
    second = jnp.dot(turn_rows, first, preferred_element_type=F32).astype(BF16)
    product = jnp.dot(second, turn_one, preferred_element_type=F32)
    turn_two = (1.5 * eye_rows - 0.5 * product).astype(BF16)
    inverse_rows = jnp.dot(turn_two, turn_one, preferred_element_type=F32)
    chosen = jnp.where(iter_count[0, 0] == 1, turn_rows.astype(F32), inverse_rows)
    root = (chosen / jnp.sqrt(scale)).astype(BF16)
    return (factor[None, None], root[None, None], step[None, None])


def solution(mesh):
    return jax.shard_map(
        square_plan if mesh.shape["dp"] == 4 else ring_plan,
        mesh=mesh,
        in_specs=(
            P("pipe", "dp", "tensor"),
            P("pipe", "dp", "tensor"),
            P("pipe", "tensor", "dp", None),
            P("pipe", "tensor", "dp", None),
            P("pipe", "tensor"),
        ),
        out_specs=(
            P("pipe", "tensor", "dp", None),
            P("pipe", "tensor", "dp", None),
            P("pipe", "tensor", None, "dp"),
        ),
        check_vma=False,
    )
```

```python
import functools
import math

import jax
import jax.numpy as jnp
from jax import lax
from jax.experimental import pallas as pl
from jax.experimental.pallas import tpu as pltpu
from jax.sharding import PartitionSpec as P

DECAY = 0.75
DAMPING = 0.1
EPSILON = 1e-06
BF16 = jnp.bfloat16
F32 = jnp.float32
VMEM_LIMIT = 28 * 1024 * 1024


def passed_along(block, axis, distance):
    devices = range(lax.axis_size(axis))
    route = [((i - distance) % len(devices), i) for i in devices]
    return lax.ppermute(block, axis, route)


def swapped(block, offset):
    return lax.ppermute(block, "dp", [(i, i ^ offset) for i in range(lax.axis_size("dp"))])


def eye_of(rows, cols, shift=0):
    row_ids = lax.broadcasted_iota(jnp.int32, (rows, cols), 0) + shift
    col_ids = lax.broadcasted_iota(jnp.int32, (rows, cols), 1)
    return (row_ids == col_ids).astype(F32)


def whole(count):
    return [pl.BlockSpec(memory_space=pltpu.VMEM)] * count


def transposed(block):
    return block.astype(F32).T.astype(block.dtype)


OFFSETS = (0, 1, 2, 3)


def chunk_rows(share):
    half, packed = share // 2, 5 * share // 8
    return [0] + [packed + half * i for i in range(4)]


def packed_upper(block):
    quarter = block.shape[0] // 4
    column = lax.broadcasted_iota(jnp.int32, (quarter, 4 * quarter), 1)
    second = pltpu.roll(block[quarter : 2 * quarter], 3 * quarter, 1)
    third = block[2 * quarter : 3 * quarter, 2 * quarter :]
    return jnp.concatenate(
        [
            block[0:quarter],
            jnp.where(column < 3 * quarter, second, block[3 * quarter :]),
            jnp.concatenate([third[0 : quarter // 2], third[quarter // 2 :]], axis=1),
        ],
        axis=0,
    )


def unpacked(packed):
    share = packed.shape[1]
    quarter = share // 4
    column = lax.broadcasted_iota(jnp.int32, (quarter, share), 1)
    second = packed[quarter : 2 * quarter]
    third = packed[2 * quarter :]
    third = jnp.concatenate([third[:, 0 : 2 * quarter], third[:, 2 * quarter :]], axis=0)
    upper = jnp.concatenate(
        [
            packed[0:quarter],
            jnp.where(column < quarter, 0.0, pltpu.roll(second, quarter, 1)),
            jnp.concatenate([jnp.zeros((quarter, 2 * quarter), F32), third], axis=1),
            jnp.where(column < 3 * quarter, 0.0, second),
        ],
        axis=0,
    )
    rows = lax.broadcasted_iota(jnp.int32, (share, share), 0) // quarter
    columns = lax.broadcasted_iota(jnp.int32, (share, share), 1) // quarter
    return upper + jnp.where(rows == columns, 0.0, upper).T


def shared_half(owner, offset, share):
    other = owner ^ offset
    low, high = jnp.minimum(owner, other), jnp.maximum(owner, other)
    row = low * share + jnp.where(owner > other, share // 2, 0)
    return pl.multiple_of(row, share // 2), pl.multiple_of(high * share, share)


def store_chunk(pieces, length, upper, lower):
    for start, piece in pieces:
        stop = start + piece.shape[0]
        for target, low, high in ((upper, 0, length), (lower, length, stop)):
            first, last = max(start, low), min(stop, high)
            if target is not None and first < last:
                ref, at = target
                ref[at + first - low : at + last - low, :] = piece[first - start : last - start].astype(ref.dtype)


def across_kernel(tokens_all, acts, relay_x, relay_y):
    share = relay_x.shape[1]
    half = share // 2
    starts = chunk_rows(share)
    owner = lax.axis_index("dp") ^ 3

    def product(left, right):
        return lax.dot_general(
            acts[:, left], acts[:, right], (((0,), (0,)), ((), ())), preferred_element_type=F32
        ) * (1.0 / tokens_all)

    columns = pl.ds(pl.multiple_of(owner * share, share), share)
    pieces = [(0, packed_upper(product(columns, columns)))]
    for start, step in zip(starts[1:], OFFSETS[1:]):
        row, col = shared_half(owner, step, share)
        pieces.append((start, product(pl.ds(row, half), pl.ds(col, share))))
    store_chunk(pieces, relay_x.shape[0], (relay_x, 0), (relay_y, 0))


def batch_kernel(replicas, tokens_all, acts, direct_x, direct_y, keep, batch):
    order = acts.shape[1]
    share = order // replicas
    half = share // 2
    starts = chunk_rows(share)
    length = direct_x.shape[0]
    mine = lax.axis_index("dp")
    for i in range(replicas):
        band = slice(i * share, (i + 1) * share)
        batch[band, i * share :] = lax.dot_general(
            acts[:, band], acts[:, i * share :], (((0,), (0,)), ((), ())), preferred_element_type=F32
        ) * (1.0 / tokens_all)

    def pieces(offset):
        owner = mine ^ offset
        base = pl.multiple_of(owner * share, share)
        yield 0, packed_upper(batch[pl.ds(base, share), pl.ds(base, share)])
        for start, step in zip(starts[1:], OFFSETS[1:]):
            row, col = shared_half(owner, step, share)
            yield start, batch[pl.ds(row, half), pl.ds(col, share)]

    store_chunk(pieces(1), length, (direct_x, 0), (keep, 3 * length))
    store_chunk(pieces(2), length, (keep, 2 * length), (direct_y, 0))
    store_chunk(pieces(0), length, (keep, 0), (keep, length))


def grad_kernel(replicas, tokens_all, acts, grads, send_x, send_y, keep, total):
    order = acts.shape[1]
    share = order // replicas
    strip = grads.shape[1] // replicas
    length = send_x.shape[0] // 2
    mine = lax.axis_index("dp")
    total[...] = lax.dot_general(
        grads[...], acts[...], (((0,), (0,)), ((), ())), preferred_element_type=F32
    ) * (1.0 / math.sqrt(tokens_all))

    def pieces(offset):
        rows = pl.ds(pl.multiple_of((mine ^ offset) * strip, strip), strip)
        for part in range(replicas):
            yield part * strip, total[rows, part * share : (part + 1) * share]

    store_chunk(pieces(3), length, (send_x, 0), (send_y, 0))
    store_chunk(pieces(1), length, (send_x, length), (keep, 3 * length))
    store_chunk(pieces(2), length, (keep, 2 * length), (send_y, length))
    store_chunk(pieces(0), length, (keep, 0), (keep, length))


def relay_kernel(keep, got_x, got_y, send_x, send_y):
    length = send_x.shape[0]
    send_y[...] = (keep[2 * length : 3 * length, :] + got_x[...].astype(F32)).astype(BF16)
    send_x[...] = (keep[3 * length :, :] + got_y[...].astype(F32)).astype(BF16)


def grad_relay_kernel(keep, got_x, got_y, send_x, send_y):
    length = send_x.shape[0]
    send_y[...] = (keep[2 * length : 3 * length, :] + got_x[0:length, :].astype(F32)).astype(BF16)
    send_x[...] = (keep[3 * length :, :] + got_y[0:length, :].astype(F32)).astype(BF16)


def grad_total_kernel(keep, got_x, got_y, relay_x, relay_y, chunk):
    length = relay_x.shape[0]
    chunk[0:length, :] = (
        keep[0:length, :] + got_x[length:, :].astype(F32) + relay_y[...].astype(F32)
    ).astype(BF16)
    chunk[length:, :] = (
        keep[length : 2 * length, :] + got_y[length:, :].astype(F32) + relay_x[...].astype(F32)
    ).astype(BF16)


def factor_kernel(replicas, keep, direct_x, direct_y, relay_x, relay_y, old, upper, lower, exact):
    share, order = old.shape
    half = share // 2
    starts = chunk_rows(share)
    length = upper.shape[0]
    mine = lax.axis_index("dp")
    total = jnp.concatenate(
        [
            keep[0:length, :] + direct_x[...].astype(F32) + relay_y[...].astype(F32),
            keep[length : 2 * length, :] + direct_y[...].astype(F32) + relay_x[...].astype(F32),
        ],
        axis=0,
    )
    diagonal = old[:, pl.ds(pl.multiple_of(mine * share, share), share)]
    block_sum = unpacked(total[0 : starts[1]])
    value = DECAY * diagonal + (1.0 - DECAY) * block_sum + DAMPING * eye_of(share, share)
    exact[0:share, :] = value
    squares = jnp.sum(value * value, axis=0, keepdims=True)
    values = [packed_upper(value).astype(BF16)]
    for position, step in enumerate(OFFSETS[1:]):
        other = mine ^ step
        block = old[:, pl.ds(pl.multiple_of(other * share, share), share)]
        term = DECAY * jnp.where(mine < other, block[0:half], block[:, half:].T)
        start = starts[1 + position]
        value = term + (1.0 - DECAY) * total[start : start + half]
        exact[share + position * half : share + (position + 1) * half, :] = value
        squares = squares + 2.0 * jnp.sum(value * value, axis=0, keepdims=True)
        values.append(value.astype(BF16))
    high = squares.astype(BF16).astype(F32)
    middle = (squares - high).astype(BF16).astype(F32)
    rest = squares - high - middle
    spot = lax.broadcasted_iota(jnp.int32, (16, share), 0)
    digits = jnp.where(spot == 0, high, jnp.where(spot == 1, middle, jnp.where(spot == 2, rest, 0.0)))
    values.append(digits.astype(BF16))
    chunk = jnp.concatenate(values, axis=0)
    upper[...] = chunk[0:length]
    lower[...] = chunk[length:]


def root_kernel(count, exact, *rest):
    chunks = [rest[2 * i : 2 * i + 2] for i in range(4)]
    factor_out, root_out, finished, factor, diagonal, rows, roots, sent, root_sent = rest[8:]
    share, order = root_out.shape
    half = share // 2
    starts = chunk_rows(share)
    length = chunks[0][0].shape[0]
    mine = lax.axis_index("dp")

    def rows_of(position, start, count):
        upper, lower = chunks[position]
        if start + count <= length:
            return upper[start : start + count, :]
        if start >= length:
            return lower[start - length : start - length + count, :]
        return jnp.concatenate([upper[start:length, :], lower[0 : start + count - length, :]], axis=0)

    copies = []
    for position, step in enumerate(OFFSETS):
        other = mine ^ step
        target = rows.at[position]
        if position == 0:
            target[...] = exact[0:share, :]
        else:
            start = starts[position]
            own = exact[share + (position - 1) * half : share + position * half, :]
            theirs = rows_of(position, start, half).astype(F32)

            @pl.when(mine < other)
            def _():
                target[0:half, :] = own
                target[half:, :] = theirs

            @pl.when(mine > other)
            def _():
                target[...] = jnp.concatenate([theirs.T, own.T], axis=1)

        columns = pl.ds(pl.multiple_of(other * share, share), share)
        copies.append(pltpu.make_async_copy(target, factor_out.at[:, columns], sent.at[position]))
        copies[-1].start()

    squares = jnp.zeros((16, share), F32)
    block_eye = eye_of(share, share)
    for position, offset in enumerate(OFFSETS):
        owner = mine ^ offset
        own_band = pl.ds(pl.multiple_of(owner * share, share), share)
        block = unpacked(rows_of(position, 0, starts[1]).astype(F32))
        factor[own_band, own_band] = block.astype(BF16)
        diagonal[:, own_band] = jnp.sum(block * block_eye, axis=0, keepdims=True)
        for start, step in zip(starts[1:], OFFSETS[1:]):
            row, col = shared_half(owner, step, share)
            block = rows_of(position, start, half)
            factor[pl.ds(row, half), pl.ds(col, share)] = block
            factor[pl.ds(col, share), pl.ds(row, half)] = transposed(block)
        squares = squares + rows_of(position, starts[-1], 16).astype(F32)

    scale = jnp.sqrt(jnp.sum(squares, keepdims=True) / order + EPSILON)
    inverse = 1.0 / scale
    ones = (diagonal[...] * inverse).astype(BF16).astype(F32)
    lift = (1.5 - 0.5 * ones).astype(BF16).astype(F32) + 0.5 * (diagonal[...] * inverse)
    eye = eye_of(share, order, mine * share)
    my_rows = pl.ds(pl.multiple_of(mine * share, share), share)
    first = (factor[my_rows, :].astype(F32) * inverse).astype(BF16).astype(F32)
    turn = (1.5 * eye - 0.5 * first).astype(BF16)
    second = (jnp.dot(turn, factor[...], preferred_element_type=F32) * inverse).astype(BF16)
    product = (-0.5 * inverse) * jnp.dot(second, factor[...], preferred_element_type=F32) + second.astype(F32) * lift
    turn_two = (1.5 * eye - 0.5 * product).astype(BF16)
    root_scale = lax.rsqrt(scale)
    for i in range(order // share):
        part = slice(i * share, (i + 1) * share)
        inverse_rows = (-0.5 * inverse) * jnp.dot(
            turn_two, factor[:, part], preferred_element_type=F32
        ) + turn_two[:, part].astype(F32) * lift[:, part]
        chosen = jnp.where(count[0, 0] == 1, turn[:, part].astype(F32), inverse_rows)
        roots[i] = (chosen * root_scale).astype(BF16)
        copies.append(pltpu.make_async_copy(roots.at[i], root_out.at[:, part], root_sent.at[i]))
        copies[-1].start()
    finished[...] = jnp.zeros_like(finished)
    for copy in copies:
        copy.wait()


def step_kernel(replicas, *refs):
    chunks = refs[:replicas]
    old_root, step_out, grads, result = refs[replicas:]
    share = old_root.shape[0]
    strip = step_out.shape[0] // replicas
    mine = lax.axis_index("dp")
    for offset, chunk in enumerate(chunks):
        for part in range(replicas):
            grads[offset * strip : (offset + 1) * strip, part * share : (part + 1) * share] = chunk[
                part * strip : (part + 1) * strip, :
            ]
    result[...] = lax.dot_general(
        grads[...], old_root[...], (((1,), (1,)), ((), ())), preferred_element_type=F32
    ).astype(BF16)
    for position, offset in enumerate(OFFSETS):
        rows = pl.ds(pl.multiple_of((mine ^ offset) * strip, strip), strip)
        step_out[rows, :] = result[position * strip : (position + 1) * strip, :]


def square_plan(acts, out_grad, old_factor, old_root, iter_count):
    replicas = lax.axis_size("dp")
    inputs = acts[0]
    tokens, order = inputs.shape
    share = order // replicas
    grows = out_grad.shape[2]
    params = pltpu.CompilerParams(vmem_limit_bytes=VMEM_LIMIT)
    whole_rows = chunk_rows(share)[-1]
    length = whole_rows // 2

    def shape(rows, kind=BF16, columns=share):
        return jax.ShapeDtypeStruct((rows, columns), kind)

    def call(kernel, outs, name, *operands, first=None, copied_out=0, after=(), scratch=()):
        in_specs = whole(len(operands)) + [pl.BlockSpec(memory_space=pl.ANY)] * len(after)
        if first is not None:
            in_specs[0] = pl.BlockSpec(memory_space=first)
        out_specs = whole(len(outs))
        out_specs[:copied_out] = [pl.BlockSpec(memory_space=pl.ANY)] * copied_out

        def body(*refs):
            kernel(*refs[: len(operands)], *refs[len(operands) + len(after) :])

        return pl.pallas_call(
            body,
            out_shape=outs,
            in_specs=in_specs,
            out_specs=out_specs,
            scratch_shapes=scratch,
            compiler_params=params,
            name=name,
        )(*operands, *after)

    received = passed_along(out_grad, "pipe", -1)[0]
    relay_x, relay_y = call(
        functools.partial(across_kernel, tokens * replicas), [shape(length)] * 2, "across", inputs
    )
    direct_x, direct_y, keep = call(
        functools.partial(batch_kernel, replicas, tokens * replicas),
        [shape(length)] * 2 + [shape(4 * length, F32)],
        "batch",
        inputs,
        after=[relay_x],
        scratch=[pltpu.VMEM((order, order), F32)],
    )
    relay_x, relay_y = swapped(relay_x, 1), swapped(relay_y, 2)
    direct_x, direct_y = swapped(direct_x, 1), swapped(direct_y, 2)
    relay_x, relay_y = call(relay_kernel, [shape(length)] * 2, "relay", keep, relay_x, relay_y)
    grad_x, grad_y, grad_keep = call(
        functools.partial(grad_kernel, replicas, tokens * replicas),
        [shape(grows)] * 2 + [shape(2 * grows, F32)],
        "grad",
        inputs,
        received,
        after=[relay_x, relay_y],
        scratch=[pltpu.VMEM((grows, order), F32)],
    )
    relay_x, relay_y = swapped(relay_x, 1), swapped(relay_y, 2)
    grad_x, grad_y = swapped(grad_x, 1), swapped(grad_y, 2)
    upper, lower, exact = call(
        functools.partial(factor_kernel, replicas),
        [shape(length), shape(length + 16), shape(5 * share // 2, F32)],
        "factor",
        keep,
        direct_x,
        direct_y,
        relay_x,
        relay_y,
        old_factor[0, 0],
    )
    upper_x, lower_y = swapped(upper, 1), swapped(lower, 2)
    lower_x, upper_y = swapped(lower, 1), swapped(upper, 2)
    strip_x, strip_y = call(
        grad_relay_kernel, [shape(grows // 2)] * 2, "grad_relay", grad_keep, grad_x, grad_y, after=[upper, lower]
    )
    strip_x, strip_y = swapped(strip_x, 1), swapped(strip_y, 2)
    upper_far, lower_far = swapped(upper_x, 2), swapped(lower_y, 1)
    (strip,) = call(
        grad_total_kernel,
        [shape(grows)],
        "grad_total",
        grad_keep,
        grad_x,
        grad_y,
        strip_x,
        strip_y,
        after=[upper_x, lower_y],
    )
    strips = [strip, swapped(strip, 1), swapped(strip, 2), swapped(strip, 3)]
    factor, root, finished = call(
        root_kernel,
        [shape(share, F32, order), shape(share, BF16, order), shape(8, F32, 128)],
        "root",
        iter_count,
        exact,
        upper,
        lower,
        upper_x,
        lower_x,
        upper_y,
        lower_y,
        upper_far,
        lower_far,
        first=pltpu.SMEM,
        copied_out=2,
        scratch=[
            pltpu.VMEM((order, order), BF16),
            pltpu.VMEM((1, order), F32),
            pltpu.VMEM((replicas, share, share), F32),
            pltpu.VMEM((replicas, share, share), BF16),
            pltpu.SemaphoreType.DMA((replicas,)),
            pltpu.SemaphoreType.DMA((replicas,)),
        ],
    )
    (step,) = call(
        functools.partial(step_kernel, replicas),
        [shape(grows, BF16, share)],
        "step",
        *strips,
        old_root[0, 0],
        after=[finished],
        scratch=[pltpu.VMEM((grows, order), BF16), pltpu.VMEM((grows, share), BF16)],
    )
    return (factor[None, None], root[None, None], step[None, None])


def ring_plan(acts, out_grad, old_factor, old_root, iter_count):
    inputs = acts[0]
    replicas = lax.axis_size("dp")
    tokens_all = inputs.shape[0] * replicas
    order = inputs.shape[1]
    share = order // replicas
    offset = lax.axis_index("dp") * share
    received = passed_along(out_grad, "pipe", -1)[0]
    partial_grad = jnp.dot(received.T, inputs, preferred_element_type=F32) / math.sqrt(tokens_all)
    batch = lax.psum_scatter(
        jnp.dot(inputs.T, inputs, preferred_element_type=F32) / tokens_all,
        "dp",
        scatter_dimension=0,
        tiled=True,
    )
    eye_rows = eye_of(share, order, offset)
    factor = DECAY * old_factor[0, 0] + (1.0 - DECAY) * batch + DAMPING * eye_rows
    grad16 = lax.psum(partial_grad, "dp").astype(BF16)
    scale = jnp.sqrt(lax.psum(jnp.sum(factor * factor), "dp") / order + EPSILON)
    step = lax.dot_general(
        grad16, old_root[0, 0], (((1,), (1,)), ((), ())), preferred_element_type=F32
    ).astype(BF16)
    first = lax.all_gather((factor / scale).astype(BF16), "dp", axis=0, tiled=True)
    turn_one = (1.5 * eye_of(order, order) - 0.5 * first.astype(F32)).astype(BF16)
    turn_rows = lax.dynamic_slice_in_dim(turn_one, offset, share, 0)
    second = jnp.dot(turn_rows, first, preferred_element_type=F32).astype(BF16)
    product = jnp.dot(second, turn_one, preferred_element_type=F32)
    turn_two = (1.5 * eye_rows - 0.5 * product).astype(BF16)
    inverse_rows = jnp.dot(turn_two, turn_one, preferred_element_type=F32)
    chosen = jnp.where(iter_count[0, 0] == 1, turn_rows.astype(F32), inverse_rows)
    root = (chosen / jnp.sqrt(scale)).astype(BF16)
    return (factor[None, None], root[None, None], step[None, None])


def solution(mesh):
    return jax.shard_map(
        square_plan if mesh.shape["dp"] == 4 else ring_plan,
        mesh=mesh,
        in_specs=(
            P("pipe", "dp", "tensor"),
            P("pipe", "dp", "tensor"),
            P("pipe", "tensor", "dp", None),
            P("pipe", "tensor", "dp", None),
            P("pipe", "tensor"),
        ),
        out_specs=(
            P("pipe", "tensor", "dp", None),
            P("pipe", "tensor", "dp", None),
            P("pipe", "tensor", None, "dp"),
        ),
        check_vma=False,
    )
```

```python
import functools
import math

import jax
import jax.numpy as jnp
from jax import lax
from jax.experimental import pallas as pl
from jax.experimental.pallas import tpu as pltpu
from jax.sharding import PartitionSpec as P

DECAY = 0.75
DAMPING = 0.1
EPSILON = 1e-06
BF16 = jnp.bfloat16
F32 = jnp.float32
VMEM_LIMIT = 28 * 1024 * 1024


def passed_along(block, axis, distance):
    devices = range(lax.axis_size(axis))
    route = [((i - distance) % len(devices), i) for i in devices]
    return lax.ppermute(block, axis, route)


def swapped(block, offset):
    return lax.ppermute(block, "dp", [(i, i ^ offset) for i in range(lax.axis_size("dp"))])


def eye_of(rows, cols, shift=0):
    row_ids = lax.broadcasted_iota(jnp.int32, (rows, cols), 0) + shift
    col_ids = lax.broadcasted_iota(jnp.int32, (rows, cols), 1)
    return (row_ids == col_ids).astype(F32)


def whole(count):
    return [pl.BlockSpec(memory_space=pltpu.VMEM)] * count


def transposed(block):
    return block.astype(F32).T.astype(block.dtype)


OFFSETS = (0, 1, 2, 3)


def chunk_rows(share):
    half, packed = share // 2, 5 * share // 8
    return [0] + [packed + half * i for i in range(4)]


def packed_upper(block):
    quarter = block.shape[0] // 4
    column = lax.broadcasted_iota(jnp.int32, (quarter, 4 * quarter), 1)
    second = pltpu.roll(block[quarter : 2 * quarter], 3 * quarter, 1)
    third = block[2 * quarter : 3 * quarter, 2 * quarter :]
    return jnp.concatenate(
        [
            block[0:quarter],
            jnp.where(column < 3 * quarter, second, block[3 * quarter :]),
            jnp.concatenate([third[0 : quarter // 2], third[quarter // 2 :]], axis=1),
        ],
        axis=0,
    )


def unpacked(packed):
    share = packed.shape[1]
    quarter = share // 4
    column = lax.broadcasted_iota(jnp.int32, (quarter, share), 1)
    second = packed[quarter : 2 * quarter]
    third = packed[2 * quarter :]
    third = jnp.concatenate([third[:, 0 : 2 * quarter], third[:, 2 * quarter :]], axis=0)
    upper = jnp.concatenate(
        [
            packed[0:quarter],
            jnp.where(column < quarter, 0.0, pltpu.roll(second, quarter, 1)),
            jnp.concatenate([jnp.zeros((quarter, 2 * quarter), F32), third], axis=1),
            jnp.where(column < 3 * quarter, 0.0, second),
        ],
        axis=0,
    )
    rows = lax.broadcasted_iota(jnp.int32, (share, share), 0) // quarter
    columns = lax.broadcasted_iota(jnp.int32, (share, share), 1) // quarter
    return upper + jnp.where(rows == columns, 0.0, upper).T


def shared_half(owner, offset, share):
    other = owner ^ offset
    low, high = jnp.minimum(owner, other), jnp.maximum(owner, other)
    row = low * share + jnp.where(owner > other, share // 2, 0)
    return pl.multiple_of(row, share // 2), pl.multiple_of(high * share, share)


def store_chunk(pieces, length, upper, lower):
    for start, piece in pieces:
        stop = start + piece.shape[0]
        for target, low, high in ((upper, 0, length), (lower, length, stop)):
            first, last = max(start, low), min(stop, high)
            if target is not None and first < last:
                ref, at = target
                ref[at + first - low : at + last - low, :] = piece[first - start : last - start].astype(ref.dtype)


def across_kernel(tokens_all, acts, relay_x, relay_y):
    share = relay_x.shape[1]
    half = share // 2
    starts = chunk_rows(share)
    owner = lax.axis_index("dp") ^ 3

    def product(left, right):
        return lax.dot_general(
            acts[:, left], acts[:, right], (((0,), (0,)), ((), ())), preferred_element_type=F32
        ) * (1.0 / tokens_all)

    columns = pl.ds(pl.multiple_of(owner * share, share), share)
    pieces = [(0, packed_upper(product(columns, columns)))]
    for start, step in zip(starts[1:], OFFSETS[1:]):
        row, col = shared_half(owner, step, share)
        pieces.append((start, product(pl.ds(row, half), pl.ds(col, share))))
    store_chunk(pieces, relay_x.shape[0], (relay_x, 0), (relay_y, 0))


def batch_kernel(replicas, tokens_all, acts, direct_x, direct_y, keep, batch):
    order = acts.shape[1]
    share = order // replicas
    half = share // 2
    starts = chunk_rows(share)
    length = direct_x.shape[0]
    mine = lax.axis_index("dp")
    for i in range(replicas):
        band = slice(i * share, (i + 1) * share)
        batch[band, i * share :] = lax.dot_general(
            acts[:, band], acts[:, i * share :], (((0,), (0,)), ((), ())), preferred_element_type=F32
        ) * (1.0 / tokens_all)

    def pieces(offset):
        owner = mine ^ offset
        base = pl.multiple_of(owner * share, share)
        yield 0, packed_upper(batch[pl.ds(base, share), pl.ds(base, share)])
        for start, step in zip(starts[1:], OFFSETS[1:]):
            row, col = shared_half(owner, step, share)
            yield start, batch[pl.ds(row, half), pl.ds(col, share)]

    store_chunk(pieces(1), length, (direct_x, 0), (keep, 3 * length))
    store_chunk(pieces(2), length, (keep, 2 * length), (direct_y, 0))
    store_chunk(pieces(0), length, (keep, 0), (keep, length))


def grad_kernel(replicas, tokens_all, acts, grads, send_x, send_y, keep, total):
    order = acts.shape[1]
    share = order // replicas
    strip = grads.shape[1] // replicas
    length = send_x.shape[0] // 2
    mine = lax.axis_index("dp")
    total[...] = lax.dot_general(
        grads[...], acts[...], (((0,), (0,)), ((), ())), preferred_element_type=F32
    ) * (1.0 / math.sqrt(tokens_all))

    def pieces(offset):
        rows = pl.ds(pl.multiple_of((mine ^ offset) * strip, strip), strip)
        for part in range(replicas):
            yield part * strip, total[rows, part * share : (part + 1) * share]

    store_chunk(pieces(3), length, (send_x, 0), (send_y, 0))
    store_chunk(pieces(1), length, (send_x, length), (keep, 3 * length))
    store_chunk(pieces(2), length, (keep, 2 * length), (send_y, length))
    store_chunk(pieces(0), length, (keep, 0), (keep, length))


def relay_kernel(keep, got_x, got_y, send_x, send_y):
    length = send_x.shape[0]
    send_y[...] = (keep[2 * length : 3 * length, :] + got_x[...].astype(F32)).astype(BF16)
    send_x[...] = (keep[3 * length :, :] + got_y[...].astype(F32)).astype(BF16)


def grad_relay_kernel(keep, got_x, got_y, send_x, send_y):
    length = send_x.shape[0]
    send_y[...] = (keep[2 * length : 3 * length, :] + got_x[0:length, :].astype(F32)).astype(BF16)
    send_x[...] = (keep[3 * length :, :] + got_y[0:length, :].astype(F32)).astype(BF16)


def grad_total_kernel(keep, got_x, got_y, relay_x, relay_y, chunk):
    length = relay_x.shape[0]
    chunk[0:length, :] = (
        keep[0:length, :] + got_x[length:, :].astype(F32) + relay_y[...].astype(F32)
    ).astype(BF16)
    chunk[length:, :] = (
        keep[length : 2 * length, :] + got_y[length:, :].astype(F32) + relay_x[...].astype(F32)
    ).astype(BF16)


def factor_kernel(replicas, keep, direct_x, direct_y, relay_x, relay_y, old, upper, lower, exact):
    share, order = old.shape
    half = share // 2
    starts = chunk_rows(share)
    length = upper.shape[0]
    mine = lax.axis_index("dp")
    total = jnp.concatenate(
        [
            keep[0:length, :] + direct_x[...].astype(F32) + relay_y[...].astype(F32),
            keep[length : 2 * length, :] + direct_y[...].astype(F32) + relay_x[...].astype(F32),
        ],
        axis=0,
    )
    diagonal = old[:, pl.ds(pl.multiple_of(mine * share, share), share)]
    block_sum = unpacked(total[0 : starts[1]])
    value = DECAY * diagonal + (1.0 - DECAY) * block_sum + DAMPING * eye_of(share, share)
    exact[0:share, :] = value
    squares = jnp.sum(value * value, axis=0, keepdims=True)
    values = [packed_upper(value).astype(BF16)]
    for position, step in enumerate(OFFSETS[1:]):
        other = mine ^ step
        block = old[:, pl.ds(pl.multiple_of(other * share, share), share)]
        term = DECAY * jnp.where(mine < other, block[0:half], block[:, half:].T)
        start = starts[1 + position]
        value = term + (1.0 - DECAY) * total[start : start + half]
        exact[share + position * half : share + (position + 1) * half, :] = value
        squares = squares + 2.0 * jnp.sum(value * value, axis=0, keepdims=True)
        values.append(value.astype(BF16))
    high = squares.astype(BF16).astype(F32)
    middle = (squares - high).astype(BF16).astype(F32)
    rest = squares - high - middle
    spot = lax.broadcasted_iota(jnp.int32, (16, share), 0)
    digits = jnp.where(spot == 0, high, jnp.where(spot == 1, middle, jnp.where(spot == 2, rest, 0.0)))
    values.append(digits.astype(BF16))
    chunk = jnp.concatenate(values, axis=0)
    upper[...] = chunk[0:length]
    lower[...] = chunk[length:]


def root_kernel(count, exact, *rest):
    chunks = [rest[2 * i : 2 * i + 2] for i in range(4)]
    factor_out, root_out, finished, factor, diagonal, rows, sent = rest[8:]
    share, order = root_out.shape
    half = share // 2
    starts = chunk_rows(share)
    length = chunks[0][0].shape[0]
    mine = lax.axis_index("dp")

    def rows_of(position, start, count):
        upper, lower = chunks[position]
        if start + count <= length:
            return upper[start : start + count, :]
        if start >= length:
            return lower[start - length : start - length + count, :]
        return jnp.concatenate([upper[start:length, :], lower[0 : start + count - length, :]], axis=0)

    copies = []
    for position, step in enumerate(OFFSETS):
        other = mine ^ step
        target = rows.at[position]
        if position == 0:
            target[...] = exact[0:share, :]
        else:
            start = starts[position]
            own = exact[share + (position - 1) * half : share + position * half, :]
            theirs = rows_of(position, start, half).astype(F32)

            @pl.when(mine < other)
            def _():
                target[0:half, :] = own
                target[half:, :] = theirs

            @pl.when(mine > other)
            def _():
                target[...] = jnp.concatenate([theirs.T, own.T], axis=1)

        columns = pl.ds(pl.multiple_of(other * share, share), share)
        copies.append(pltpu.make_async_copy(target, factor_out.at[:, columns], sent.at[position]))
        copies[-1].start()

    squares = jnp.zeros((16, share), F32)
    block_eye = eye_of(share, share)
    for position, offset in enumerate(OFFSETS):
        owner = mine ^ offset
        own_band = pl.ds(pl.multiple_of(owner * share, share), share)
        block = unpacked(rows_of(position, 0, starts[1]).astype(F32))
        factor[own_band, own_band] = block.astype(BF16)
        diagonal[:, own_band] = jnp.sum(block * block_eye, axis=0, keepdims=True)
        for start, step in zip(starts[1:], OFFSETS[1:]):
            row, col = shared_half(owner, step, share)
            block = rows_of(position, start, half)
            factor[pl.ds(row, half), pl.ds(col, share)] = block
            factor[pl.ds(col, share), pl.ds(row, half)] = transposed(block)
        squares = squares + rows_of(position, starts[-1], 16).astype(F32)

    scale = jnp.sqrt(jnp.sum(squares, keepdims=True) / order + EPSILON)
    inverse = 1.0 / scale
    ones = (diagonal[...] * inverse).astype(BF16).astype(F32)
    lift = (1.5 - 0.5 * ones).astype(BF16).astype(F32) + 0.5 * (diagonal[...] * inverse)
    eye = eye_of(share, order, mine * share)
    my_rows = pl.ds(pl.multiple_of(mine * share, share), share)
    first = (factor[my_rows, :].astype(F32) * inverse).astype(BF16).astype(F32)
    turn = (1.5 * eye - 0.5 * first).astype(BF16)
    second = (jnp.dot(turn, factor[...], preferred_element_type=F32) * inverse).astype(BF16)
    product = (-0.5 * inverse) * jnp.dot(second, factor[...], preferred_element_type=F32) + second.astype(F32) * lift
    turn_two = (1.5 * eye - 0.5 * product).astype(BF16)
    inverse_rows = (-0.5 * inverse) * jnp.dot(
        turn_two, factor[...], preferred_element_type=F32
    ) + turn_two.astype(F32) * lift
    chosen = jnp.where(count[0, 0] == 1, turn.astype(F32), inverse_rows)
    root_out[...] = (chosen * lax.rsqrt(scale)).astype(BF16)
    finished[...] = jnp.zeros_like(finished)
    for copy in copies:
        copy.wait()


def step_kernel(replicas, *refs):
    chunks = refs[:replicas]
    old_root, step_out, grads, result = refs[replicas:]
    share = old_root.shape[0]
    strip = step_out.shape[0] // replicas
    mine = lax.axis_index("dp")
    for offset, chunk in enumerate(chunks):
        for part in range(replicas):
            grads[offset * strip : (offset + 1) * strip, part * share : (part + 1) * share] = chunk[
                part * strip : (part + 1) * strip, :
            ]
    result[...] = lax.dot_general(
        grads[...], old_root[...], (((1,), (1,)), ((), ())), preferred_element_type=F32
    ).astype(BF16)
    for position, offset in enumerate(OFFSETS):
        rows = pl.ds(pl.multiple_of((mine ^ offset) * strip, strip), strip)
        step_out[rows, :] = result[position * strip : (position + 1) * strip, :]


def square_plan(acts, out_grad, old_factor, old_root, iter_count):
    replicas = lax.axis_size("dp")
    inputs = acts[0]
    tokens, order = inputs.shape
    share = order // replicas
    grows = out_grad.shape[2]
    params = pltpu.CompilerParams(vmem_limit_bytes=VMEM_LIMIT)
    whole_rows = chunk_rows(share)[-1]
    length = whole_rows // 2

    def shape(rows, kind=BF16, columns=share):
        return jax.ShapeDtypeStruct((rows, columns), kind)

    def call(kernel, outs, name, *operands, first=None, first_out=None, after=(), scratch=()):
        in_specs = whole(len(operands)) + [pl.BlockSpec(memory_space=pl.ANY)] * len(after)
        if first is not None:
            in_specs[0] = pl.BlockSpec(memory_space=first)
        out_specs = whole(len(outs))
        if first_out is not None:
            out_specs[0] = pl.BlockSpec(memory_space=first_out)

        def body(*refs):
            kernel(*refs[: len(operands)], *refs[len(operands) + len(after) :])

        return pl.pallas_call(
            body,
            out_shape=outs,
            in_specs=in_specs,
            out_specs=out_specs,
            scratch_shapes=scratch,
            compiler_params=params,
            name=name,
        )(*operands, *after)

    received = passed_along(out_grad, "pipe", -1)[0]
    relay_x, relay_y = call(
        functools.partial(across_kernel, tokens * replicas), [shape(length)] * 2, "across", inputs
    )
    direct_x, direct_y, keep = call(
        functools.partial(batch_kernel, replicas, tokens * replicas),
        [shape(length)] * 2 + [shape(4 * length, F32)],
        "batch",
        inputs,
        after=[relay_x],
        scratch=[pltpu.VMEM((order, order), F32)],
    )
    relay_x, relay_y = swapped(relay_x, 1), swapped(relay_y, 2)
    direct_x, direct_y = swapped(direct_x, 1), swapped(direct_y, 2)
    relay_x, relay_y = call(relay_kernel, [shape(length)] * 2, "relay", keep, relay_x, relay_y)
    grad_x, grad_y, grad_keep = call(
        functools.partial(grad_kernel, replicas, tokens * replicas),
        [shape(grows)] * 2 + [shape(2 * grows, F32)],
        "grad",
        inputs,
        received,
        after=[relay_x, relay_y],
        scratch=[pltpu.VMEM((grows, order), F32)],
    )
    relay_x, relay_y = swapped(relay_x, 1), swapped(relay_y, 2)
    grad_x, grad_y = swapped(grad_x, 1), swapped(grad_y, 2)
    upper, lower, exact = call(
        functools.partial(factor_kernel, replicas),
        [shape(length), shape(length + 16), shape(5 * share // 2, F32)],
        "factor",
        keep,
        direct_x,
        direct_y,
        relay_x,
        relay_y,
        old_factor[0, 0],
    )
    upper_x, lower_y = swapped(upper, 1), swapped(lower, 2)
    lower_x, upper_y = swapped(lower, 1), swapped(upper, 2)
    strip_x, strip_y = call(
        grad_relay_kernel, [shape(grows // 2)] * 2, "grad_relay", grad_keep, grad_x, grad_y, after=[upper, lower]
    )
    strip_x, strip_y = swapped(strip_x, 1), swapped(strip_y, 2)
    upper_far, lower_far = swapped(upper_x, 2), swapped(lower_y, 1)
    (strip,) = call(
        grad_total_kernel,
        [shape(grows)],
        "grad_total",
        grad_keep,
        grad_x,
        grad_y,
        strip_x,
        strip_y,
        after=[upper_x, lower_y],
    )
    from_across = swapped(strip, 3)
    strips = [strip, swapped(strip, 1), swapped(strip, 2), from_across]
    factor, root, finished = call(
        root_kernel,
        [shape(share, F32, order), shape(share, BF16, order), shape(8, F32, 128)],
        "root",
        iter_count,
        exact,
        upper,
        lower,
        upper_x,
        lower_x,
        upper_y,
        lower_y,
        upper_far,
        lower_far,
        first=pltpu.SMEM,
        first_out=pl.ANY,
        scratch=[
            pltpu.VMEM((order, order), BF16),
            pltpu.VMEM((1, order), F32),
            pltpu.VMEM((replicas, share, share), F32),
            pltpu.SemaphoreType.DMA((replicas,)),
        ],
    )
    (step,) = call(
        functools.partial(step_kernel, replicas),
        [shape(grows, BF16, share)],
        "step",
        *strips,
        old_root[0, 0],
        after=[finished],
        scratch=[pltpu.VMEM((grows, order), BF16), pltpu.VMEM((grows, share), BF16)],
    )
    return (factor[None, None], root[None, None], step[None, None])


def ring_plan(acts, out_grad, old_factor, old_root, iter_count):
    inputs = acts[0]
    replicas = lax.axis_size("dp")
    tokens_all = inputs.shape[0] * replicas
    order = inputs.shape[1]
    share = order // replicas
    offset = lax.axis_index("dp") * share
    received = passed_along(out_grad, "pipe", -1)[0]
    partial_grad = jnp.dot(received.T, inputs, preferred_element_type=F32) / math.sqrt(tokens_all)
    batch = lax.psum_scatter(
        jnp.dot(inputs.T, inputs, preferred_element_type=F32) / tokens_all,
        "dp",
        scatter_dimension=0,
        tiled=True,
    )
    eye_rows = eye_of(share, order, offset)
    factor = DECAY * old_factor[0, 0] + (1.0 - DECAY) * batch + DAMPING * eye_rows
    grad16 = lax.psum(partial_grad, "dp").astype(BF16)
    scale = jnp.sqrt(lax.psum(jnp.sum(factor * factor), "dp") / order + EPSILON)
    step = lax.dot_general(
        grad16, old_root[0, 0], (((1,), (1,)), ((), ())), preferred_element_type=F32
    ).astype(BF16)
    first = lax.all_gather((factor / scale).astype(BF16), "dp", axis=0, tiled=True)
    turn_one = (1.5 * eye_of(order, order) - 0.5 * first.astype(F32)).astype(BF16)
    turn_rows = lax.dynamic_slice_in_dim(turn_one, offset, share, 0)
    second = jnp.dot(turn_rows, first, preferred_element_type=F32).astype(BF16)
    product = jnp.dot(second, turn_one, preferred_element_type=F32)
    turn_two = (1.5 * eye_rows - 0.5 * product).astype(BF16)
    inverse_rows = jnp.dot(turn_two, turn_one, preferred_element_type=F32)
    chosen = jnp.where(iter_count[0, 0] == 1, turn_rows.astype(F32), inverse_rows)
    root = (chosen / jnp.sqrt(scale)).astype(BF16)
    return (factor[None, None], root[None, None], step[None, None])


def solution(mesh):
    return jax.shard_map(
        square_plan if mesh.shape["dp"] == 4 else ring_plan,
        mesh=mesh,
        in_specs=(
            P("pipe", "dp", "tensor"),
            P("pipe", "dp", "tensor"),
            P("pipe", "tensor", "dp", None),
            P("pipe", "tensor", "dp", None),
            P("pipe", "tensor"),
        ),
        out_specs=(
            P("pipe", "tensor", "dp", None),
            P("pipe", "tensor", "dp", None),
            P("pipe", "tensor", None, "dp"),
        ),
        check_vma=False,
    )
```
